128 devices in a mesh: lon: 16 (over y_lo, z, core), lat: 8 (over x, y_hi).
Axes of the slice: x: 4, y: 4 (y_hi: 2, y_lo: 2; y = y_hi * 2 + y_lo), z: 4, core: 2. Of those that a mesh axis runs over, the one named last changes fastest.
Arguments:
- fields: bfloat16 [2, 4, 48, 384, 192], P(None, None, 'lat', 'lon'), may hold values from -6 to 6
- merge_cotangent: bfloat16 [192, 2, 4, 24, 384], P(None, None, None, 'lat', 'lon'), may hold values from -6 to 6
- attend_gain: float32 [192], replicated, may hold values from 0.1 to 1.9
- triple_weight: bfloat16 [192, 576], replicated, may hold values from -0.4375 to 0.4375
- bias_table: float32 [8, 2, 6, 3312], P('lat'), may hold values from -320 to 320
- output_weight: bfloat16 [192, 192], replicated, may hold values from -0.4375 to 0.4375
- feed_gain: float32 [192], replicated, may hold values from 0.1 to 1.9
- expand_weight: bfloat16 [192, 768], replicated, may hold values from -0.4375 to 0.4375
- shrink_weight: bfloat16 [768, 192], replicated, may hold values from -0.21875 to 0.21875
- merge_gain: float32 [768], replicated, may hold values from 0.1 to 1.9
- merge_weight: bfloat16 [768, 384], P(None, 'lon'), may hold values from -0.21875 to 0.21875
Outputs:
- grad_fields: bfloat16 [2, 4, 48, 384, 192], P(None, None, 'lat', 'lon')
- grad_triple: float32 [192, 576], replicated
- grad_output: float32 [192, 192], replicated
- grad_expand: float32 [192, 768], replicated
- grad_shrink: float32 [768, 192], replicated
- grad_attend_gain: float32 [192], replicated
- grad_feed_gain: float32 [192], replicated
- grad_table: float32 [8, 2, 6, 3312], P('lat')
The draws below stay inside these ranges and needn't reach their ends.
All inputs are finite; a program needn't handle non-finite values.
Results may differ from the reference program's by a relative error of at most 0.035.
Values may be sent and summed in bfloat16 or wider, within the bound.
A program may use at most 128 MiB of HBM per device.

```python
import math
import jax
import jax.numpy as jnp
import numpy as np
from jax import lax

C = 192
HEADS = 6
FF = 768
C2 = 384
WIN_LEV = 2
WIN_LAT = 6
WIN_LON = 12
LEV = 4
BATCH = 2
LAT = 48
LON = 384
LAT2 = 24
LON2 = 192
LATW = 8
LEVW = 2
POS = 3312
C2B = 24
N_LON = 16


def draw_bias_table(key, part):
    key = jax.random.fold_in(key, 7)
    keys = jax.random.split(key, 1)
    shape = (LATW, LEVW, HEADS, POS)
    base = jnp.clip(jax.random.normal(keys[0], shape, jnp.float32), -6.0, 6.0)
    return base


def with_spikes(array, rng, source, target, parts, factor):
    owner, partner = [(jnp.arange(array.shape[position]) // (array.shape[position] // parts)).reshape([-1 if axis == position else 1 for axis in range(array.ndim)]) for position in (source, target)]
    chosen = jax.random.permutation(rng, parts)[partner]
    strong = (owner == chosen) | (owner == (partner + parts // 2) % parts)
    return jnp.where(strong, factor * array, array)


def block_scale(stream_key, dims, cuts, smallest, top_value):
    loudness = 1.0
    for dim, parts in cuts:
        steps = jax.random.uniform(jax.random.fold_in(jax.random.fold_in(stream_key, 6), dim), (parts,), jnp.float32, smallest / len(cuts), top_value / len(cuts))
        loudness = loudness * jnp.repeat(jnp.exp(steps), dims[dim] // parts).reshape((-1,) + (1,) * (len(dims) - 1 - dim))
    return loudness


def normal_values(own_key, extent, deviation, limit, shards=(), kind=jnp.bfloat16):
    entries = deviation * jax.random.normal(own_key, extent, jnp.float32)
    if shards:
        entries = entries * block_scale(own_key, extent, shards, -0.22, 0.18)
    return jnp.clip(entries, -limit, limit).astype(kind)


def heavy_noise(key, extent, scale, most, cuts, heavy, kind=jnp.bfloat16):
    values = scale * jax.random.normal(key, extent, jnp.float32)
    if cuts:
        values = values * block_scale(key, extent, cuts, -0.22, 0.18)
    return jnp.clip(with_spikes(values, jax.random.fold_in(key, 3), *heavy), -most, most).astype(kind)


def setup_inputs(seed: int = 0) -> dict:
    key_of = jax.random.split(jax.random.key(seed), 12)
    fields = normal_values(key_of[0], (BATCH, LEV, LAT, LON, C), 1.0, 6.0, ((2, 8), (3, 16)))
    merge_cotangent = heavy_noise(key_of[1], (LON2, BATCH, LEV, LAT2, C2), 1.0, 6.0, ((3, 8), (4, 16)), (4, 0, 16, 2.0))
    attend_gain = jnp.clip(1.0 + 0.18 * jax.random.normal(key_of[2], (C,), jnp.float32), 0.1, 1.9)
    triple_weight = normal_values(key_of[3], (C, 3 * C), C ** -0.5, 0.4375)
    bias_table = draw_bias_table(jax.random.fold_in(key_of[11], 71), 0)
    output_weight = normal_values(key_of[5], (C, C), C ** -0.5, 0.4375)
    feed_gain = jnp.clip(1.0 + 0.18 * jax.random.normal(key_of[6], (C,), jnp.float32), 0.1, 1.9)
    expand_weight = normal_values(key_of[7], (C, FF), C ** -0.5, 0.4375)
    shrink_weight = normal_values(key_of[8], (FF, C), FF ** -0.5, 0.21875)
    merge_gain = jnp.clip(1.0 + 0.18 * jax.random.normal(key_of[9], (4 * C,), jnp.float32), 0.1, 1.9)
    merge_weight = normal_values(key_of[10], (4 * C, C2), (4 * C) ** -0.5, 0.21875, ((1, 16),))
    return {"fields": fields, "merge_cotangent": merge_cotangent, "attend_gain": attend_gain, "triple_weight": triple_weight, "bias_table": bias_table, "output_weight": output_weight, "feed_gain": feed_gain, "expand_weight": expand_weight, "shrink_weight": shrink_weight, "merge_gain": merge_gain, "merge_weight": merge_weight}


EPS = 1e-05
MASKED = -1000000000.0

def multiply(pattern, first_op, second_op):
    return jnp.einsum(pattern, first_op.astype(jnp.float32), second_op.astype(jnp.float32), precision=lax.Precision.HIGHEST)

def contract(first_op, second_op):
    flat_first = first_op.reshape(-1, first_op.shape[-1])
    flat_second = second_op.reshape(-1, second_op.shape[-1])
    return lax.dot_general(flat_first, flat_second, (((0,), (0,)), ((), ())), preferred_element_type=jnp.float32)

def backmul(upstream, weight):
    return lax.dot_general(upstream, weight, (((upstream.ndim - 1,), (1,)), ((), ())), preferred_element_type=jnp.float32)

def statistics(values):
    centred = values - lax.optimization_barrier(jnp.mean(values, axis=-1, keepdims=True))
    inverse = lax.rsqrt(lax.optimization_barrier(jnp.mean(centred * centred, axis=-1, keepdims=True)) + EPS)
    return (centred * inverse, inverse)

def norm_back(values, gain_vec, upstream):
    normed, inverse = statistics(values)
    scaled = upstream * gain_vec
    centre_term = lax.optimization_barrier(jnp.mean(scaled, axis=-1, keepdims=True))
    projected = lax.optimization_barrier(jnp.mean(scaled * normed, axis=-1, keepdims=True))
    return (inverse * (scaled - centre_term - normed * projected), normed)

def gelu_exact(values):
    return 0.5 * values * (1.0 + jax.scipy.special.erf(values * (1.0 / math.sqrt(2.0))))

def gelu_slope(values):
    cumulative = 0.5 * (1.0 + jax.scipy.special.erf(values * (1.0 / math.sqrt(2.0))))
    return cumulative + values * jnp.exp(-0.5 * values * values) * (1.0 / math.sqrt(2.0 * math.pi))

def lon_offsets():
    span_ids = np.arange(WIN_LON)
    return (span_ids[:, None] - span_ids[None, :] + WIN_LON - 1).astype(np.int32)

def diagonal_table():
    offsets = lon_offsets().reshape(-1)
    return (offsets[:, None] == np.arange(2 * WIN_LON - 1)[None, :]).astype(np.float32)

def expand(bias_part):
    leading = bias_part.shape[:3]
    grid_view = bias_part.reshape(leading + (WIN_LEV, WIN_LEV, WIN_LAT, WIN_LAT, 2 * WIN_LON - 1))
    spread = jnp.take(grid_view, jnp.asarray(lon_offsets()), axis=-1)
    spread = spread.transpose(0, 1, 2, 3, 5, 7, 4, 6, 8)
    window_size = WIN_LEV * WIN_LAT * WIN_LON
    return spread.reshape(leading + (window_size, window_size))

def fold_bias(grad_full):
    leading = grad_full.shape[:3]
    grid_view = grad_full.reshape(leading + (WIN_LEV, WIN_LAT, WIN_LON, WIN_LEV, WIN_LAT, WIN_LON))
    grid_view = grid_view.transpose(0, 1, 2, 3, 6, 4, 7, 5, 8)
    grid_view = grid_view.reshape(leading + (WIN_LEV, WIN_LEV, WIN_LAT, WIN_LAT, WIN_LON * WIN_LON))
    summed = jnp.einsum('...r,rs->...s', grid_view, jnp.asarray(diagonal_table()), precision=lax.Precision.HIGHEST)
    return summed.reshape(leading + (-1,))

def windows(grid_field):
    shape = grid_field.shape
    split = grid_field.reshape(shape[0], shape[1] // WIN_LEV, WIN_LEV, shape[2] // WIN_LAT, WIN_LAT, shape[3] // WIN_LON, WIN_LON, shape[4])
    split = split.transpose(0, 1, 3, 5, 2, 4, 6, 7)
    return split.reshape(split.shape[:4] + (WIN_LEV * WIN_LAT * WIN_LON, shape[4]))

def unwindows(window_field):
    shape = window_field.shape
    split = window_field.reshape(shape[:4] + (WIN_LEV, WIN_LAT, WIN_LON, shape[5]))
    split = split.transpose(0, 1, 4, 2, 5, 3, 6, 7)
    return split.reshape(shape[0], shape[1] * WIN_LEV, shape[2] * WIN_LAT, shape[3] * WIN_LON, shape[5])

def zone_mask(level_windows, lat_windows, lat_start, lat_total):
    levels = level_windows * WIN_LEV
    level_ids = jnp.arange(levels, dtype=jnp.int32).reshape(level_windows, WIN_LEV)
    level_zone = (level_ids >= levels - WIN_LEV).astype(jnp.int32) + (level_ids >= levels - WIN_LEV // 2).astype(jnp.int32)
    lat_ids = lat_start + jnp.arange(lat_windows * WIN_LAT, dtype=jnp.int32).reshape(lat_windows, WIN_LAT)
    lat_zone = (lat_ids >= lat_total - WIN_LAT).astype(jnp.int32) + (lat_ids >= lat_total - WIN_LAT // 2).astype(jnp.int32)
    zone_id = level_zone[:, None, :, None, None] * 3 + lat_zone[None, :, None, :, None]
    zone_id = jnp.broadcast_to(zone_id, (level_windows, lat_windows, WIN_LEV, WIN_LAT, WIN_LON)).reshape(level_windows, lat_windows, -1)
    return zone_id[..., :, None] == zone_id[..., None, :]

def forward(grid_field, lat_start, lat_total, bias_part, params):
    attend_gain, triple_weight, output_weight, feed_gain, expand_weight, shrink_weight = params
    tokens = windows(grid_field)
    channels = tokens.shape[-1]
    head_count = bias_part.shape[2]
    head_size = channels // head_count
    factor = head_size ** (-0.5)
    normed_in = (statistics(tokens.astype(jnp.float32))[0] * attend_gain).astype(jnp.bfloat16)
    triple = jnp.dot(normed_in, triple_weight, preferred_element_type=jnp.float32).astype(jnp.bfloat16)
    sections = triple.reshape(triple.shape[:-1] + (3, head_count, head_size))
    queries = sections[..., 0, :, :]
    lookups = sections[..., 1, :, :]
    contents = sections[..., 2, :, :]
    raw_scores = multiply('...qhd,...khd->...hqk', queries, lookups)
    offsets = jnp.swapaxes(expand(bias_part), 0, 1)[None, :, :, None]
    same_zone = zone_mask(tokens.shape[1], tokens.shape[2], lat_start, lat_total)[None, :, :, None, None]
    scores = jnp.where(same_zone, raw_scores * factor + offsets, MASKED)
    highest = lax.optimization_barrier(jnp.max(scores, axis=-1, keepdims=True))
    exponent = jnp.exp(scores - highest)
    chances = exponent / lax.optimization_barrier(jnp.sum(exponent, axis=-1, keepdims=True))
    chances_half = chances.astype(jnp.bfloat16)
    attended = multiply('...hqk,...khd->...qhd', chances_half, contents).astype(jnp.bfloat16)
    attended = attended.reshape(attended.shape[:-2] + (channels,))
    middle = tokens.astype(jnp.float32) + jnp.dot(attended, output_weight, preferred_element_type=jnp.float32)
    normed_mid = (statistics(middle)[0] * feed_gain).astype(jnp.bfloat16)
    hidden_pre = jnp.dot(normed_mid, expand_weight, preferred_element_type=jnp.float32)
    hidden_act = gelu_exact(hidden_pre).astype(jnp.bfloat16)
    result = (middle + jnp.dot(hidden_act, shrink_weight, preferred_element_type=jnp.float32)).astype(jnp.bfloat16)
    stored = (tokens, normed_in, triple, chances, chances_half, attended, middle, normed_mid, hidden_pre, hidden_act)
    return (unwindows(result), stored)

def backward(upstream_field, stored, params, head_count):
    attend_gain, triple_weight, output_weight, feed_gain, expand_weight, shrink_weight = params
    tokens, normed_in, triple, chances, chances_half, attended, middle, normed_mid, hidden_pre, hidden_act = stored
    channels = tokens.shape[-1]
    head_size = channels // head_count
    factor = head_size ** (-0.5)
    grad_out = windows(upstream_field)
    grad_shrink = contract(hidden_act, grad_out)
    grad_hidden = (backmul(grad_out, shrink_weight) * gelu_slope(hidden_pre)).astype(jnp.bfloat16)
    grad_expand = contract(normed_mid, grad_hidden)
    grad_normed_mid = backmul(grad_hidden, expand_weight)
    back_mid, unit_mid = norm_back(middle, feed_gain, grad_normed_mid)
    grad_feed_gain = lax.optimization_barrier(jnp.sum((grad_normed_mid * unit_mid).reshape(-1, channels), axis=0))
    grad_middle = grad_out.astype(jnp.float32) + back_mid
    grad_middle_half = grad_middle.astype(jnp.bfloat16)
    grad_output = contract(attended, grad_middle_half)
    grad_attended = backmul(grad_middle_half, output_weight).astype(jnp.bfloat16)
    grad_attended = grad_attended.reshape(grad_attended.shape[:-1] + (head_count, head_size))
    sections = triple.reshape(triple.shape[:-1] + (3, head_count, head_size))
    queries = sections[..., 0, :, :]
    lookups = sections[..., 1, :, :]
    contents = sections[..., 2, :, :]
    grad_chances = multiply('...qhd,...khd->...hqk', grad_attended, contents)
    grad_contents = multiply('...hqk,...qhd->...khd', chances_half, grad_attended)
    grad_scores = chances * (grad_chances - lax.optimization_barrier(jnp.sum(chances * grad_chances, axis=-1, keepdims=True)))
    grad_bias = fold_bias(jnp.swapaxes(lax.optimization_barrier(jnp.sum(grad_scores, axis=(0, 3))), 0, 1))
    grad_scores_half = grad_scores.astype(jnp.bfloat16)
    grad_queries = multiply('...hqk,...khd->...qhd', grad_scores_half, lookups) * factor
    grad_lookups = multiply('...hqk,...qhd->...khd', grad_scores_half, queries) * factor
    grad_triple_in = jnp.stack([grad_queries, grad_lookups, grad_contents], axis=-3).astype(jnp.bfloat16)
    grad_triple_in = grad_triple_in.reshape(grad_triple_in.shape[:-3] + (3 * channels,))
    grad_triple = contract(normed_in, grad_triple_in)
    grad_normed_in = backmul(grad_triple_in, triple_weight)
    back_in, unit_in = norm_back(tokens.astype(jnp.float32), attend_gain, grad_normed_in)
    grad_attend_gain = lax.optimization_barrier(jnp.sum((grad_normed_in * unit_in).reshape(-1, channels), axis=0))
    grad_tokens = (grad_middle + back_in).astype(jnp.bfloat16)
    grads = (grad_triple, grad_output, grad_expand, grad_shrink, grad_attend_gain, grad_feed_gain)
    return (unwindows(grad_tokens), grads, grad_bias)

def merge_cells(grid_field):
    shape = grid_field.shape
    split = grid_field.reshape(shape[0], shape[1], shape[2] // 2, 2, shape[3] // 2, 2, shape[4])
    split = split.transpose(0, 1, 2, 4, 3, 5, 6)
    return split.reshape(shape[0], shape[1], shape[2] // 2, shape[3] // 2, 4 * shape[4])

def split_cells(merged_field):
    shape = merged_field.shape
    channels = shape[4] // 4
    split = merged_field.reshape(shape[0], shape[1], shape[2], shape[3], 2, 2, channels)
    split = split.transpose(0, 1, 2, 4, 3, 5, 6)
    return split.reshape(shape[0], shape[1], 2 * shape[2], 2 * shape[3], channels)

def to_bands(grid_field):
    shape = grid_field.shape
    split = grid_field.reshape(shape[0], shape[1], shape[2] // WIN_LAT, WIN_LAT, shape[3], shape[4])
    return split.transpose(2, 0, 1, 3, 4, 5)

def from_bands(band_field):
    shape = band_field.shape
    joined = band_field.transpose(1, 2, 0, 3, 4, 5)
    return joined.reshape(shape[1], shape[2], shape[0] * shape[3], shape[4], shape[5])

def reference(fields, merge_cotangent, attend_gain, triple_weight, bias_table, output_weight, feed_gain, expand_weight, shrink_weight, merge_gain, merge_weight):
    params = (attend_gain, triple_weight, output_weight, feed_gain, expand_weight, shrink_weight)
    forth = (-(WIN_LEV // 2), -(WIN_LAT // 2), -(WIN_LON // 2))
    back_moves = (WIN_LEV // 2, WIN_LAT // 2, WIN_LON // 2)
    shifted = jnp.roll(fields, forth, axis=(1, 2, 3))
    starts = jnp.arange(LATW, dtype=jnp.int32) * WIN_LAT
    bands = to_bands(shifted)

    def forward_band(band_inputs):
        band, bias_part, start = band_inputs
        return forward(band, start, LAT, bias_part[None], params)[0]
    out_bands = lax.map(forward_band, (bands, bias_table, starts))
    out_field = jnp.roll(from_bands(out_bands), back_moves, axis=(1, 2, 3))

    def add_block(total, block_index):
        start = block_index * C2B
        piece = lax.dynamic_slice_in_dim(merge_cotangent, start, C2B, 4)
        column_part = lax.dynamic_slice_in_dim(merge_weight, start, C2B, 1)
        term = lax.optimization_barrier(backmul(piece, column_part).astype(jnp.bfloat16))
        return (total + term.astype(jnp.float32), None)
    empty = jnp.zeros(merge_cotangent.shape[:4] + (4 * C,), jnp.float32)
    total, _ = lax.scan(add_block, empty, jnp.arange(N_LON, dtype=jnp.int32))
    merge_cot = jnp.transpose(total, (1, 2, 3, 0, 4))
    merged = merge_cells(out_field.astype(jnp.float32))
    grad_merged = norm_back(merged, merge_gain, merge_cot)[0]
    grad_out = split_cells(grad_merged).astype(jnp.bfloat16)
    grad_shift = jnp.roll(grad_out, forth, axis=(1, 2, 3))

    def backward_band(band_inputs):
        band, bias_part, start, upstream_band = band_inputs
        stored = forward(band, start, LAT, bias_part[None], params)[1]
        return backward(upstream_band, stored, params, HEADS)
    grad_bands, weight_grads, table_grads = lax.map(backward_band, (bands, bias_table, starts, to_bands(grad_shift)))
    grad_fields = jnp.roll(from_bands(grad_bands), back_moves, axis=(1, 2, 3))
    grad_table = table_grads.reshape(bias_table.shape)
    return (grad_fields, lax.optimization_barrier(jnp.sum(weight_grads[0], axis=0)), lax.optimization_barrier(jnp.sum(weight_grads[1], axis=0)), lax.optimization_barrier(jnp.sum(weight_grads[2], axis=0)), lax.optimization_barrier(jnp.sum(weight_grads[3], axis=0)), lax.optimization_barrier(jnp.sum(weight_grads[4], axis=0)), lax.optimization_barrier(jnp.sum(weight_grads[5], axis=0)), grad_table)
```

```python
import functools
import math

import jax
import jax.numpy as jnp
import numpy as np
from jax import lax
from jax.experimental import pallas as pl
from jax.experimental.pallas import tpu as pltpu
from jax.sharding import PartitionSpec as P

F32 = jnp.float32
BF16 = jnp.bfloat16
I32 = jnp.int32
MESH = pl.DeviceIdType.MESH

EPS = 1e-05
MASKED = -1000000000.0
NLON = 16
NLAT = 8
C = 192
HEADS = 6
FF = 768
WIN = 144
NWIN = 8
TOK = WIN * NWIN
HALF = TOK // 2
QROWS = 608
POS = 3312
CHUNK = 288
NCHUNK = TOK // CHUNK
FACTOR = 32 ** -0.5


def order_indices():
    natural_to_quad = np.full(640, -1, np.int32)
    quad_to_natural = np.full(640, -1, np.int32)
    quad_to_window = np.full(640, -1, np.int32)
    window_to_quad = np.full(640, -1, np.int32)
    for level in range(4):
        for row in range(6):
            for col in range(24):
                source = (level * 6 + row) * 24 + col
                if col >= 6:
                    place = (0 if row >= 3 else 224) + level * 54 + (row % 3) * 18 + col - 6
                else:
                    place = (448 if row >= 3 else 528) + level * 18 + (row % 3) * 6 + col
                natural_to_quad[source] = place
                quad_to_natural[place] = source
    index = 0
    for lev_win in range(2):
        for lon_win in range(2):
            for s in range(12):
                for p in range(2):
                    for r in range(6):
                        level = (lev_win * 2 + p + 1) % 4
                        col = lon_win * 12 + s
                        if col < 18:
                            place = (0 if r < 3 else 224) + level * 54 + (r % 3) * 18 + col
                        else:
                            place = (448 if r < 3 else 528) + level * 18 + (r % 3) * 6 + col - 18
                        window_to_quad[index] = place
                        quad_to_window[place] = index
                        index += 1
    rows = [natural_to_quad, quad_to_natural, quad_to_window, window_to_quad]
    return np.stack(rows + rows)


def dot_nn(a, b):
    return lax.dot_general(a, b, (((1,), (0,)), ((), ())), preferred_element_type=F32)


def dot_nt(a, b):
    return lax.dot_general(a, b, (((1,), (1,)), ((), ())), preferred_element_type=F32)


def dot_tn(a, b):
    return lax.dot_general(a, b, (((0,), (0,)), ((), ())), preferred_element_type=F32)


def one_hot(rows, targets):
    ids = lax.broadcasted_iota(I32, (rows, targets.shape[1]), 0)
    return jnp.where(ids == targets, 1.0, 0.0).astype(BF16)


def statistics(values):
    centred = values - jnp.mean(values, axis=-1, keepdims=True)
    inverse = lax.rsqrt(jnp.mean(centred * centred, axis=-1, keepdims=True) + EPS)
    return centred * inverse, inverse


def norm_back(normed, inverse, scaled):
    centre = jnp.mean(scaled, axis=-1, keepdims=True)
    projected = jnp.mean(scaled * normed, axis=-1, keepdims=True)
    return inverse * (scaled - centre - normed * projected)


def gelu_parts(values):
    cumulative = 0.5 * (1.0 + lax.erf(values * (1.0 / math.sqrt(2.0))))
    density = jnp.exp(-0.5 * values * values) * (1.0 / math.sqrt(2.0 * math.pi))
    return values * cumulative, cumulative + values * density


def lanes(rows, cols):
    return lax.broadcasted_iota(I32, (rows, cols), 1)


def bias_targets():
    k = lanes(1, WIN)
    s, rest = k // 12, k % 12
    return (rest // 6) * 256 + (rest % 6) * 23 + 11 - s


def spread_matrix(s_i):
    return one_hot(512, bias_targets() + s_i)


def kernel(
    fields, cot, attend_gain, triple_w, bias, output_w, feed_gain, expand_w, shrink_t, merge_gain,
    merge_wt, orders,
    out_fields, out_triple, out_output, out_expand, out_shrink, out_attend, out_feed, out_table,
    sq, rq, gq, hq, x_w, ni_s, q_s, k_s, v_s, wq, wk, wv, p_s, att_s, mid_s, nm_s, act_s, slope_s, vo_s,
    b16, bl_s, bs_s, bx, ds_s,
    cs, cg, ch, wg, qry, qw, st, sx, sup, sdn, tup, tdn, cp_s, go_s, gh_s, gm_s, ga_s, gmh_s,
    dq_s, dk_s, dv_s, gt_s, g1s, g1r, g1l, g1f, g2s, g2r, g2l, g2f, tbs, tbr, tbf, gains,
    halo_ss, halo_rs, cot_ss, cot_rs, w_ss, w_rs, lat_ss, lat_rs, st_ss, st_rs,
    g1_ss, g1_rs, g1l_ss, g1l_rs, g1f_ss, g1f_rs, g2_ss, g2_rs, g2l_ss, g2l_rs, g2f_ss, g2f_rs,
    tb_ss, tb_rs, tbf_ss, tbf_rs, back_ss, back_rs,
):
    e = lax.axis_index("lon")
    d = lax.axis_index("lat")
    e_up, e_dn = lax.rem(e + 1, NLON), lax.rem(e + NLON - 1, NLON)
    d_up, d_dn = lax.rem(d + 1, NLAT), lax.rem(d + NLAT - 1, NLAT)

    def remote(src, dst, ssem, rsem, device):
        return pltpu.make_async_remote_copy(
            src_ref=src, dst_ref=dst, send_sem=ssem, recv_sem=rsem, device_id=device,
            device_id_type=MESH,
        )

    def lon_all(action):
        def body(step, carry):
            action(lax.rem(e + step, NLON))
            return carry

        lax.fori_loop(1, NLON, body, 0)

    def lat_all(action):
        def body(step, carry):
            action(lax.rem(d + step, NLAT))
            return carry

        lax.fori_loop(1, NLAT, body, 0)

    barrier = pltpu.get_barrier_semaphore()
    lon_all(lambda o: pl.semaphore_signal(barrier, inc=1, device_id=(o, d), device_id_type=MESH))
    lat_all(lambda o: pl.semaphore_signal(barrier, inc=1, device_id=(e, o), device_id_type=MESH))
    pl.semaphore_signal(barrier, inc=1, device_id=(e_up, d_up), device_id_type=MESH)
    pl.semaphore_signal(barrier, inc=1, device_id=(e_dn, d_dn), device_id_type=MESH)

    to_quad = one_hot(QROWS, orders[0:1, 0:HALF])
    for b in range(2):
        sq[b] = dot_nn(to_quad, fields[b * HALF:(b + 1) * HALF, :]).astype(BF16)
    pl.semaphore_wait(barrier, NLON - 1 + NLAT - 1 + 2)

    pieces = ((224, 224), (448, 80), (528, 80))

    def halo(src, dst, ssem, rsem, step):
        devices = ((e, step[1]), (step[0], d), (step[0], step[1]))
        return [
            remote(src.at[:, pl.ds(at, size), :], dst.at[:, pl.ds(at, size), :], ssem.at[i], rsem.at[i], dev)
            for i, ((at, size), dev) in enumerate(zip(pieces, devices))
        ]

    halo_copies = halo(sq, rq, halo_ss, halo_rs, (e_dn, d_dn))
    for copy in halo_copies:
        copy.start()

    lane = lanes(1, 256)
    cell_lane = jnp.where(lane % 16 < 12, (12 * (lane // 16) + 3 + lane % 16) % 192, -1)
    cells = dot_nn(cot[...], one_hot(192, cell_lane))
    block_of = lanes(72, 128) // 16
    for o in range(NLON):
        tile, inner = (o // 8) * 128, o % 8
        piece = jnp.zeros((72, 128), F32)
        for bl in range(8):
            part = cells[bl * 72:(bl + 1) * 72, tile:tile + 128]
            shift = (16 * (bl - inner)) % 128
            if shift:
                part = pltpu.roll(part, shift, 1)
            piece = jnp.where(block_of == bl, part, piece)
        for a in range(3):
            padded = jnp.concatenate([piece[a * 24:(a + 1) * 24], jnp.zeros((8, 128), F32)], axis=0)
            cs[o, a] = padded.astype(BF16)
    wg[e] = jnp.concatenate(
        [merge_wt[...].astype(F32), jnp.zeros((8, 768), F32)], axis=0
    ).astype(BF16)
    cg[:, e] = cs[e]

    def cot_copy(o, mine):
        return remote(cs.at[o], cg.at[:, mine], cot_ss.at[o], cot_rs.at[mine], (o, d))

    def w_copy(o, mine):
        return remote(wg.at[mine], wg.at[mine], w_ss.at[o], w_rs.at[mine], (o, d))

    def start_merge(o):
        cot_copy(o, e).start()
        w_copy(o, e).start()

    lon_all(start_merge)

    for h in range(HEADS):
        b16[2 * h:2 * h + 2, :] = bias[h]
    b16[12:16, :] = jnp.zeros((4, POS), F32)
    zero_tail = jnp.zeros((16, 256 - 138), F32)
    for p in range(2):
        for r in range(6):
            parts = []
            for pk in range(2):
                at = (p * 2 + pk) * 828 + r * 138
                parts += [b16[:, at:at + 138], zero_tail]
            row = jnp.concatenate(parts, axis=1)
            high = row.astype(BF16)
            rest = row - high.astype(F32)
            middle = rest.astype(BF16)
            low = (rest - middle.astype(F32)).astype(BF16)
            at = pl.ds((p * 6 + r) * 16, 16)
            bl_s[0, at, :] = high
            bl_s[1, at, :] = middle
            bl_s[2, at, :] = low

    def spread(s_i, carry):
        matrix = spread_matrix(s_i)
        rows = dot_nn(bl_s[0], matrix) + dot_nn(bl_s[1], matrix) + dot_nn(bl_s[2], matrix)
        at = pl.ds(pl.multiple_of(s_i * 192, 192), 192)
        bs_s[0, at, :] = rows[:, 0:128]
        bs_s[1, at, :] = jnp.concatenate([rows[:, 128:144], jnp.zeros((192, 112), F32)], axis=1)
        return carry

    lax.fori_loop(0, 12, spread, 0)

    tok_i = lax.broadcasted_iota(I32, (WIN, WIN), 0) % 12
    tok_k = lax.broadcasted_iota(I32, (WIN, WIN), 1) % 12
    last_band = d == NLAT - 1
    lat_differs = ((tok_i % 6 >= 3) != (tok_k % 6 >= 3)) & last_band
    lev_differs = (tok_i >= 6) != (tok_k >= 6)
    for lw in range(2):
        differs = (lat_differs | lev_differs) if lw else lat_differs
        for h in range(HEADS):
            at = pl.ds(h * 2 + lw, WIN, stride=16)
            full = jnp.concatenate([bs_s.at[0][at, :], bs_s.at[1][at, :]], axis=1)[:, 0:WIN]
            bx[lw, h * WIN:(h + 1) * WIN, :] = jnp.where(differs, MASKED, full)

    wq[...] = triple_w[:, 0:192]
    wk[...] = triple_w[:, 192:384]
    wv[...] = triple_w[:, 384:576]

    head_of = lanes(1, C) // 32
    head_f = [jnp.where(head_of == h, 1.0, 0.0) for h in range(HEADS)]
    head_b = [mask.astype(BF16) for mask in head_f]

    def stacked(values):
        return jnp.concatenate([values * mask for mask in head_b], axis=0)

    def unstacked(values):
        total = values[0:WIN] * head_f[0]
        for h in range(1, HEADS):
            total = total + values[h * WIN:(h + 1) * WIN] * head_f[h]
        return total

    to_window = one_hot(HALF, orders[2:3, 0:QROWS])
    for copy in halo_copies:
        copy.wait()
    rq[:, 0:224, :] = sq[:, 0:224, :]
    for b in range(2):
        x_w[b * HALF:(b + 1) * HALF, :] = dot_nn(to_window, rq[b]).astype(BF16)

    def window_rows(w):
        return pl.ds(pl.multiple_of(w * WIN, WIN), WIN)

    def chunk_rows(i):
        return pl.ds(pl.multiple_of(i * CHUNK, CHUNK), CHUNK)

    def project(i, carry):
        rows = chunk_rows(i)
        normed = statistics(x_w[rows, :].astype(F32))[0]
        normed_in = (normed * attend_gain[...]).astype(BF16)
        ni_s[rows, :] = normed_in
        q_s[rows, :] = dot_nn(normed_in, wq[...]).astype(BF16)
        k_s[rows, :] = dot_nn(normed_in, wk[...]).astype(BF16)
        v_s[rows, :] = dot_nn(normed_in, wv[...]).astype(BF16)
        return carry

    lax.fori_loop(0, NCHUNK, project, 0)

    def attend(w, carry):
        rows = window_rows(w)
        lw = lax.rem(w // 2, 2)
        scores = dot_nt(stacked(q_s[rows, :]), k_s[rows, :]) * FACTOR + bx[lw]
        exponent = jnp.exp(scores - jnp.max(scores, axis=-1, keepdims=True))
        chances = exponent * (1.0 / jnp.sum(exponent, axis=-1, keepdims=True))
        half = chances.astype(BF16)
        p_s[w] = half
        att_s[rows, :] = unstacked(dot_nn(half, v_s[rows, :])).astype(BF16)
        return carry

    lax.fori_loop(0, NWIN, attend, 0)

    lon_all(lambda o: cot_copy(e, o).wait_recv())
    lat_copy = remote(cg.at[pl.ds(0, 2)], ch, lat_ss.at[0], lat_rs.at[0], (e, d_dn))
    lat_copy.start()

    def feed(i, carry):
        rows = chunk_rows(i)
        middle = x_w[rows, :].astype(F32) + dot_nn(att_s[rows, :], output_w[...])
        mid_s[rows, :] = middle
        normed_mid = (statistics(middle)[0] * feed_gain[...]).astype(BF16)
        nm_s[rows, :] = normed_mid
        act, slope = gelu_parts(dot_nn(normed_mid, expand_w[...]))
        act = act.astype(BF16)
        act_s[rows, :] = act
        slope_s[rows, :] = slope
        vo_s[rows, :] = (middle + dot_nt(act, shrink_t[...])).astype(BF16)
        return carry

    lax.fori_loop(0, NCHUNK, feed, 0)

    lat_copy.wait_recv()
    lon_all(lambda o: w_copy(e, o).wait_recv())
    for r in range(6):
        x = (r + 1) % 2
        cell = (0, 1, 1, 2, 2, 3)[r]
        plane = cg[cell + 1] if cell < 2 else ch[cell - 2]
        weight = wg[:, :, x * 384:(x + 1) * 384].reshape(512, 384)
        scaled = dot_tn(plane.reshape(512, 128), weight) * merge_gain[:, x * 384:(x + 1) * 384]
        qry[2 * r] = scaled[:, 0:192].astype(BF16)
        qry[2 * r + 1] = scaled[:, 192:384].astype(BF16)

    st[...] = jnp.zeros_like(st)
    col = lanes(1, 384)
    col_p, col_ry, col_m = col // 192, (col // 16) % 12, col % 16
    stat_lane = lanes(WIN, 128)

    def merge_sums(w, carry):
        rows = window_rows(w)
        b, lw, lon_win = w // 4, lax.rem(w // 2, 2), lax.rem(w, 2)
        parts = []
        for p in range(2):
            level = lax.rem(lw * 2 + p + 1, 4)
            at = pl.ds(pl.multiple_of((b * 4 + level) * 16, 16), 16)
            parts.append(qry[:, at, :].reshape(192, C))
        pair = col_m - lon_win * 6
        token = (2 * pair + col_ry % 2) * 12 + col_p * 6 + col_ry // 2
        token = jnp.where((pair >= 0) & (pair < 6), token, -1)
        q = dot_nn(one_hot(WIN, token), jnp.concatenate(parts, axis=0))
        qw[rows, :] = q.astype(BF16)
        v = vo_s[rows, :].astype(F32)
        mean = jnp.mean(v, axis=-1, keepdims=True)
        centred = v - mean
        squares = jnp.sum(centred * centred, axis=-1, keepdims=True)
        q_sum = jnp.sum(q, axis=-1, keepdims=True)
        qv_sum = jnp.sum(q * centred, axis=-1, keepdims=True)
        total = st[...]
        for j, value in enumerate((mean, squares, q_sum, qv_sum)):
            total = jnp.where(stat_lane == 32 * j + w, value, total)
        st[...] = total
        return carry

    lax.fori_loop(0, NWIN, merge_sums, 0)

    tup[...] = st[pl.ds(5, 24, stride=6), :]
    tdn[...] = st[pl.ds(0, 24, stride=6), :]
    up_copy = remote(tup, sup, st_ss.at[0], st_rs.at[0], (e, d_up))
    dn_copy = remote(tdn, sdn, st_ss.at[1], st_rs.at[1], (e, d_dn))
    up_copy.start()
    dn_copy.start()
    for r, other in ((1, 2), (2, 1), (3, 4), (4, 3)):
        sx[pl.ds(r, 24, stride=6), :] = st[pl.ds(other, 24, stride=6), :]
    up_copy.wait()
    dn_copy.wait()
    sx[pl.ds(0, 24, stride=6), :] = sup[...]
    sx[pl.ds(5, 24, stride=6), :] = sdn[...]

    even = (lax.broadcasted_iota(I32, (WIN, 128), 0) // 12) % 2 == 0

    def pair_of(values):
        return jnp.where(even, pltpu.roll(values, WIN - 12, 0), pltpu.roll(values, 12, 0))

    own, cross = st[...], sx[...]
    group = [own, cross, pair_of(own), pair_of(cross)]
    cell_mean = (group[0] + group[1] + group[2] + group[3]) * 0.25
    variance = jnp.zeros((WIN, 128), F32)
    q_total = jnp.zeros((WIN, 128), F32)
    qv_total = jnp.zeros((WIN, 128), F32)
    for values in group:
        offset = values - cell_mean
        q_sum = pltpu.roll(values, 64, 1)
        variance = variance + pltpu.roll(values, 96, 1) + 192.0 * offset * offset
        q_total = q_total + q_sum
        qv_total = qv_total + pltpu.roll(values, 32, 1) + offset * q_sum
    cell_inverse = lax.rsqrt(jnp.where(stat_lane < 8, variance, 0.0) * (1.0 / 768.0) + EPS)
    cp_s[0] = cell_mean
    cp_s[1] = cell_inverse
    cp_s[2] = q_total * (1.0 / 768.0)
    cp_s[3] = cell_inverse * cell_inverse * qv_total * (1.0 / 768.0)

    def merge_back(w, carry):
        rows = window_rows(w)
        mean, inverse, q_mean, projected = [
            jnp.sum(jnp.where(stat_lane == w, cp_s[j], 0.0), axis=-1, keepdims=True) for j in range(4)
        ]
        v = vo_s[rows, :].astype(F32) - mean
        go_s[rows, :] = (inverse * (qw[rows, :].astype(F32) - q_mean - v * projected)).astype(BF16)
        return carry

    lax.fori_loop(0, NWIN, merge_back, 0)

    def feed_back(i, carry):
        rows = chunk_rows(i)
        go = go_s[rows, :]
        gh = (dot_nn(go, shrink_t[...]) * slope_s[rows, :]).astype(BF16)
        gh_s[rows, :] = gh
        gnm = dot_nt(gh, expand_w[...])
        unit, inverse = statistics(mid_s[rows, :])
        gm = go.astype(F32) + norm_back(unit, inverse, gnm * feed_gain[...])
        gm_s[rows, :] = gm
        half = gm.astype(BF16)
        gmh_s[rows, :] = half
        ga_s[rows, :] = dot_nt(half, output_w[...]).astype(BF16)
        return carry + jnp.sum(gnm * unit, axis=0, keepdims=True)

    feed_sum = lax.fori_loop(0, NCHUNK, feed_back, jnp.zeros((1, C), F32))

    g_expand = dot_tn(nm_s[...], gh_s[...]).astype(BF16)
    g_shrink = dot_tn(go_s[...], act_s[...]).astype(BF16)
    for i in range(4):
        for j in range(2):
            g1s[2 * i + j] = g_expand[i * 48:(i + 1) * 48, j * 384:(j + 1) * 384]
            g1s[8 + 2 * i + j] = g_shrink[i * 48:(i + 1) * 48, j * 384:(j + 1) * 384]
    g1r[e] = g1s[e]

    def g1_copy(o, mine):
        return remote(g1s.at[o], g1r.at[mine], g1_ss.at[o], g1_rs.at[mine], (o, d))

    def g1l_copy(o, mine):
        return remote(g1l.at[mine], g1l.at[mine], g1l_ss.at[o], g1l_rs.at[mine], (e, o))

    def g1f_copy(o, mine):
        return remote(g1f.at[mine], g1f.at[mine], g1f_ss.at[o], g1f_rs.at[mine], (o, d))

    lon_all(lambda o: g1_copy(o, e).start())

    ds_s[...] = jnp.zeros_like(ds_s)

    def attend_back(w, carry):
        rows = window_rows(w)
        lw = lax.rem(w // 2, 2)
        k = k_s[rows, :]
        ga = stacked(ga_s[rows, :])
        half = p_s[w]
        chances = half.astype(F32)
        weighted = dot_nt(ga, v_s[rows, :])
        centre = jnp.sum(chances * weighted, axis=-1, keepdims=True)
        ds = chances * (weighted - centre)
        ds_s[lw] = ds_s[lw] + ds
        ds = ds.astype(BF16)
        dq_s[rows, :] = (unstacked(dot_nn(ds, k)) * FACTOR).astype(BF16)
        dk_s[rows, :] = (dot_tn(ds, stacked(q_s[rows, :])) * FACTOR).astype(BF16)
        dv_s[rows, :] = dot_tn(half, ga).astype(BF16)
        return carry

    lax.fori_loop(0, 5, attend_back, 0)

    lon_all(lambda o: g1_copy(e, o).wait_recv())
    total = g1r[0].astype(F32)
    for o in range(1, NLON):
        total = total + g1r[o].astype(F32)
    g1l[d] = total.astype(BF16)
    lat_all(lambda o: g1l_copy(o, d).start())

    lax.fori_loop(5, NWIN, attend_back, 0)

    lat_all(lambda o: g1l_copy(d, o).wait_recv())
    total = g1l[0].astype(F32)
    for o in range(1, NLAT):
        total = total + g1l[o].astype(F32)
    g1f[e] = total.astype(BF16)
    lon_all(lambda o: g1f_copy(o, e).start())

    def project_back(i, carry):
        rows = chunk_rows(i)
        gni = dot_nt(dq_s[rows, :], wq[...]) + dot_nt(dk_s[rows, :], wk[...]) + dot_nt(dv_s[rows, :], wv[...])
        unit, inverse = statistics(x_w[rows, :].astype(F32))
        gt_s[rows, :] = (gm_s[rows, :] + norm_back(unit, inverse, gni * attend_gain[...])).astype(BF16)
        return carry + jnp.sum(gni * unit, axis=0, keepdims=True)

    attend_sum = lax.fori_loop(0, NCHUNK, project_back, jnp.zeros((1, C), F32))

    from_window = one_hot(QROWS, orders[3:4, 0:HALF])
    for b in range(2):
        gq[b] = dot_nn(from_window, gt_s[b * HALF:(b + 1) * HALF, :]).astype(BF16)
    back_copies = halo(gq, hq, back_ss, back_rs, (e_up, d_up))
    for copy in back_copies:
        copy.start()

    ni = ni_s[...]
    g2s[0:192, 0:192] = dot_tn(ni, dq_s[...]).astype(BF16)
    g2s[0:192, 192:384] = dot_tn(ni, dk_s[...]).astype(BF16)
    g2s[0:192, 384:576] = dot_tn(ni, dv_s[...]).astype(BF16)
    g2s[0:192, 576:768] = dot_tn(att_s[...], gmh_s[...]).astype(BF16)
    row_id = lax.broadcasted_iota(I32, (64, C), 0)
    gain_rows = jnp.where(row_id == 0, attend_sum, jnp.where(row_id == 1, feed_sum, 0.0))
    g2s[192:256, :] = jnp.concatenate([gain_rows, jnp.zeros((64, 768 - C), F32)], axis=1).astype(BF16)

    def g2_rows(o):
        return pl.ds(pl.multiple_of(o * 16, 16), 16)

    g2r[e] = g2s[g2_rows(e), :]

    def g2_copy(o, mine):
        return remote(g2s.at[g2_rows(o), :], g2r.at[mine], g2_ss.at[o], g2_rs.at[mine], (o, d))

    def g2l_copy(o, mine):
        return remote(g2l.at[mine], g2l.at[mine], g2l_ss.at[o], g2l_rs.at[mine], (e, o))

    def g2f_copy(o, mine):
        rows = g2_rows(mine)
        return remote(g2f.at[rows, :], g2f.at[rows, :], g2f_ss.at[o], g2f_rs.at[mine], (o, d))

    lon_all(lambda o: g2_copy(o, e).start())

    for lw in range(2):
        for h in range(HEADS):
            at = pl.ds(h * 2 + lw, WIN, stride=16)
            part = ds_s[lw, h * WIN:(h + 1) * WIN, :]
            bs_s.at[0][at, :] = part[:, 0:128]
            bs_s.at[1][at, :] = jnp.concatenate([part[:, 128:144], jnp.zeros((WIN, 112), F32)], axis=1)

    def fold(s_i, carry):
        at = pl.ds(pl.multiple_of(s_i * 192, 192), 192)
        rows = jnp.concatenate([bs_s[0, at, :], bs_s[1, at, :]], axis=1)[:, 0:WIN].astype(BF16)
        return carry + dot_nt(rows, spread_matrix(s_i))

    folded = lax.fori_loop(0, 12, fold, jnp.zeros((192, 512), F32))
    pieces_t = []
    for p in range(2):
        for pk in range(2):
            for r in range(6):
                at = (p * 6 + r) * 16
                pieces_t.append(folded[at:at + 16, pk * 256:pk * 256 + 138])
    table = jnp.concatenate(pieces_t + [jnp.zeros((16, 4096 - POS), F32)], axis=1).astype(BF16)
    for o in range(NLON):
        tbs[o] = table[:, o * 256:(o + 1) * 256]
    tbr[e] = tbs[e]

    def tb_copy(o, mine):
        return remote(tbs.at[o], tbr.at[mine], tb_ss.at[o], tb_rs.at[mine], (o, d))

    def tbf_copy(o, mine):
        return remote(tbf.at[mine], tbf.at[mine], tbf_ss.at[o], tbf_rs.at[mine], (o, d))

    lon_all(lambda o: tb_copy(o, e).start())

    lon_all(lambda o: g2_copy(e, o).wait_recv())
    total = g2r[0].astype(F32)
    for o in range(1, NLON):
        total = total + g2r[o].astype(F32)
    g2l[d] = total.astype(BF16)
    lat_all(lambda o: g2l_copy(o, d).start())

    lon_all(lambda o: tb_copy(e, o).wait_recv())
    total = tbr[0].astype(F32)
    for o in range(1, NLON):
        total = total + tbr[o].astype(F32)
    tbf[e] = total.astype(BF16)
    lon_all(lambda o: tbf_copy(o, e).start())

    lat_all(lambda o: g2l_copy(d, o).wait_recv())
    total = g2l[0].astype(F32)
    for o in range(1, NLAT):
        total = total + g2l[o].astype(F32)
    g2f[g2_rows(e), :] = total.astype(BF16)
    lon_all(lambda o: g2f_copy(o, e).start())

    to_natural = one_hot(HALF, orders[1:2, 0:QROWS])
    for copy in back_copies:
        copy.wait()
    hq[:, 0:224, :] = gq[:, 0:224, :]
    for b in range(2):
        out_fields[b * HALF:(b + 1) * HALF, :] = dot_nn(to_natural, hq[b]).astype(BF16)

    lon_all(lambda o: g1f_copy(e, o).wait_recv())
    for i in range(4):
        for j in range(2):
            out_expand[i * 48:(i + 1) * 48, j * 384:(j + 1) * 384] = g1f[2 * i + j].astype(F32)
            out_shrink[i * 48:(i + 1) * 48, j * 384:(j + 1) * 384] = g1f[8 + 2 * i + j].astype(F32)

    lon_all(lambda o: tbf_copy(e, o).wait_recv())
    table = jnp.concatenate([tbf[o] for o in range(NLON)], axis=1).astype(F32)
    for h in range(HEADS):
        out_table[h] = table[2 * h:2 * h + 2, 0:POS]

    lon_all(lambda o: g2f_copy(e, o).wait_recv())
    out_triple[...] = g2f[0:192, 0:576].astype(F32)
    out_output[...] = g2f[0:192, 576:768].astype(F32)
    gains[...] = g2f[192:208, 0:256].astype(F32)
    out_attend[...] = gains[0:1, 0:C]
    out_feed[...] = gains[1:2, 0:C]

    def sent(o):
        cot_copy(o, e).wait_send()
        w_copy(o, e).wait_send()
        g1_copy(o, e).wait_send()
        g1f_copy(o, e).wait_send()
        g2_copy(o, e).wait_send()
        g2f_copy(o, e).wait_send()
        tb_copy(o, e).wait_send()
        tbf_copy(o, e).wait_send()

    def sent_lat(o):
        g1l_copy(o, d).wait_send()
        g2l_copy(o, d).wait_send()

    lon_all(sent)
    lat_all(sent_lat)
    lat_copy.wait_send()


def scratch():
    def vmem(*shape, kind=BF16):
        return pltpu.VMEM(shape, kind)

    token = vmem(TOK, C)
    token_f = vmem(TOK, C, kind=F32)
    weight = vmem(C, C)
    quad = vmem(2, QROWS, C)
    stat = vmem(WIN, 128, kind=F32)
    small = vmem(24, 128, kind=F32)
    buffers = [
        quad, quad, quad, quad, token, token, token, token, token, weight, weight, weight,
        vmem(NWIN, HEADS * WIN, WIN), token, token_f, token, vmem(TOK, FF), vmem(TOK, FF, kind=F32), token,
        vmem(16, POS, kind=F32), vmem(3, 192, 512), vmem(2, 2304, 128, kind=F32),
        vmem(2, HEADS * WIN, WIN, kind=F32), vmem(2, HEADS * WIN, WIN, kind=F32),
        vmem(16, 3, 32, 128), vmem(3, 16, 32, 128), vmem(2, 16, 32, 128), vmem(16, 32, 768),
        vmem(12, 128, C), token, stat, stat, small, small, small, small, vmem(4, WIN, 128, kind=F32),
        token, vmem(TOK, FF), token_f, token, token, token, token, token, token,
        vmem(16, 48, 384), vmem(16, 48, 384), vmem(8, 48, 384), vmem(16, 48, 384),
        vmem(256, 768), vmem(16, 16, 768), vmem(8, 16, 768), vmem(256, 768),
        vmem(16, 16, 256), vmem(16, 16, 256), vmem(16, 16, 256), vmem(16, 256, kind=F32),
    ]
    counts = [3, 3, 16, 16, 16, 16, 1, 1, 2, 2]
    counts += [16, 16, 8, 8, 16, 16, 16, 16, 8, 8, 16, 16, 16, 16, 16, 16, 3, 3]
    return buffers + [pltpu.SemaphoreType.DMA((n,)) for n in counts]


def per_device(
    fields, merge_cotangent, attend_gain, triple_weight, bias_table, output_weight, feed_gain,
    expand_weight, shrink_weight, merge_gain, merge_weight,
):
    cot = jnp.transpose(merge_cotangent, (1, 2, 3, 4, 0)).reshape(576, 192)
    bias = jnp.transpose(bias_table[0], (1, 0, 2))
    shapes = [
        ((TOK, C), BF16), ((C, 3 * C), F32), ((C, C), F32), ((C, FF), F32), ((C, FF), F32),
        ((1, C), F32), ((1, C), F32), ((HEADS, 2, POS), F32),
    ]
    results = pl.pallas_call(
        kernel,
        out_shape=[jax.ShapeDtypeStruct(shape, kind) for shape, kind in shapes],
        in_specs=[pl.BlockSpec(memory_space=pltpu.VMEM)] * 12,
        out_specs=[pl.BlockSpec(memory_space=pltpu.VMEM)] * 8,
        scratch_shapes=scratch(),
        compiler_params=pltpu.CompilerParams(
            collective_id=0, has_side_effects=True, vmem_limit_bytes=60 * 1024 * 1024
        ),
    )(
        fields.reshape(TOK, C), cot, attend_gain.reshape(1, C), triple_weight, bias, output_weight,
        feed_gain.reshape(1, C), expand_weight, shrink_weight.T, merge_gain.reshape(1, 4 * C),
        merge_weight.T, jnp.asarray(order_indices()),
    )
    g_fields, g_triple, g_output, g_expand, g_shrink, g_attend, g_feed, g_table = results
    return (
        g_fields.reshape(fields.shape), g_triple, g_output, g_expand, g_shrink.T,
        g_attend.reshape(C), g_feed.reshape(C), jnp.transpose(g_table, (1, 0, 2))[None],
    )


def solution(mesh):
    placed = (
        P(None, None, "lat", "lon", None),
        P(None, None, None, "lat", "lon"),
        P(),
        P(),
        P("lat", None, None, None),
        P(),
        P(),
        P(),
        P(),
        P(),
        P(None, "lon"),
    )
    return jax.shard_map(
        per_device,
        mesh=mesh,
        in_specs=placed,
        out_specs=(
            P(None, None, "lat", "lon", None),
            P(),
            P(),
            P(),
            P(),
            P(),
            P(),
            P("lat", None, None, None),
        ),
        check_vma=False,
    )
```

```python
import functools
import math

import jax
import jax.numpy as jnp
import numpy as np
from jax import lax
from jax.experimental import pallas as pl
from jax.experimental.pallas import tpu as pltpu
from jax.sharding import PartitionSpec as P

F32 = jnp.float32
BF16 = jnp.bfloat16
I32 = jnp.int32
MESH = pl.DeviceIdType.MESH

EPS = 1e-05
MASKED = -1000000000.0
NLON = 16
NLAT = 8
C = 192
HEADS = 6
FF = 768
WIN = 144
NWIN = 8
TOK = WIN * NWIN
HALF = TOK // 2
QROWS = 608
POS = 3312
CHUNK = 288
NCHUNK = TOK // CHUNK
FACTOR = 32 ** -0.5


def order_indices():
    natural_to_quad = np.full(640, -1, np.int32)
    quad_to_natural = np.full(640, -1, np.int32)
    quad_to_window = np.full(640, -1, np.int32)
    window_to_quad = np.full(640, -1, np.int32)
    for level in range(4):
        for row in range(6):
            for col in range(24):
                source = (level * 6 + row) * 24 + col
                if col >= 6:
                    place = (0 if row >= 3 else 224) + level * 54 + (row % 3) * 18 + col - 6
                else:
                    place = (448 if row >= 3 else 528) + level * 18 + (row % 3) * 6 + col
                natural_to_quad[source] = place
                quad_to_natural[place] = source
    index = 0
    for lev_win in range(2):
        for lon_win in range(2):
            for s in range(12):
                for p in range(2):
                    for r in range(6):
                        level = (lev_win * 2 + p + 1) % 4
                        col = lon_win * 12 + s
                        if col < 18:
                            place = (0 if r < 3 else 224) + level * 54 + (r % 3) * 18 + col
                        else:
                            place = (448 if r < 3 else 528) + level * 18 + (r % 3) * 6 + col - 18
                        window_to_quad[index] = place
                        quad_to_window[place] = index
                        index += 1
    rows = [natural_to_quad, quad_to_natural, quad_to_window, window_to_quad]
    return np.stack(rows + rows)


def dot_nn(a, b):
    return lax.dot_general(a, b, (((1,), (0,)), ((), ())), preferred_element_type=F32)


def dot_nt(a, b):
    return lax.dot_general(a, b, (((1,), (1,)), ((), ())), preferred_element_type=F32)


def dot_tn(a, b):
    return lax.dot_general(a, b, (((0,), (0,)), ((), ())), preferred_element_type=F32)


def one_hot(rows, targets):
    ids = lax.broadcasted_iota(I32, (rows, targets.shape[1]), 0)
    return jnp.where(ids == targets, 1.0, 0.0).astype(BF16)


def statistics(values):
    centred = values - jnp.mean(values, axis=-1, keepdims=True)
    inverse = lax.rsqrt(jnp.mean(centred * centred, axis=-1, keepdims=True) + EPS)
    return centred * inverse, inverse


def norm_back(normed, inverse, scaled):
    centre = jnp.mean(scaled, axis=-1, keepdims=True)
    projected = jnp.mean(scaled * normed, axis=-1, keepdims=True)
    return inverse * (scaled - centre - normed * projected)


def gelu_parts(values):
    cumulative = 0.5 * (1.0 + lax.erf(values * (1.0 / math.sqrt(2.0))))
    density = jnp.exp(-0.5 * values * values) * (1.0 / math.sqrt(2.0 * math.pi))
    return values * cumulative, cumulative + values * density


def lanes(rows, cols):
    return lax.broadcasted_iota(I32, (rows, cols), 1)


def bias_targets():
    k = lanes(1, WIN)
    s, rest = k // 12, k % 12
    return (rest // 6) * 256 + (rest % 6) * 23 + 11 - s


def spread_matrix(s_i):
    return one_hot(512, bias_targets() + s_i)


def kernel(
    fields, cot, attend_gain, triple_w, bias, output_w, feed_gain, expand_w, shrink_t, merge_gain,
    merge_wt, orders,
    out_fields, out_g1, out_g2, out_table,
    sq, rq, gq, hq, x_w, ni_s, q_s, k_s, v_s, wq, wk, wv, p_s, att_s, mid_s, nm_s, act_s, slope_s, vo_s,
    b16, bl_s, bs_s, bx, ds_s,
    cs, cg, ch, wg, qry, qw, st, sx, sup, sdn, tup, tdn, cp_s, go_s, gh_s, gm_s, ga_s, gmh_s,
    dq_s, dk_s, dv_s, gt_s, g1s, g1r, g1l, g1f, g2s, g2r, g2l, g2f, tbs, tbr, tbf,
    halo_ss, halo_rs, cot_ss, cot_rs, w_ss, w_rs, lat_ss, lat_rs, st_ss, st_rs,
    g1_ss, g1_rs, g1l_ss, g1l_rs, g1f_ss, g1f_rs, g2_ss, g2_rs, g2l_ss, g2l_rs, g2f_ss, g2f_rs,
    tb_ss, tb_rs, tbf_ss, tbf_rs, back_ss, back_rs,
):
    e = lax.axis_index("lon")
    d = lax.axis_index("lat")
    e_up, e_dn = lax.rem(e + 1, NLON), lax.rem(e + NLON - 1, NLON)
    d_up, d_dn = lax.rem(d + 1, NLAT), lax.rem(d + NLAT - 1, NLAT)

    def remote(src, dst, ssem, rsem, device):
        return pltpu.make_async_remote_copy(
            src_ref=src, dst_ref=dst, send_sem=ssem, recv_sem=rsem, device_id=device,
            device_id_type=MESH,
        )

    def lon_all(action):
        def body(step, carry):
            action(lax.rem(e + step, NLON))
            return carry

        lax.fori_loop(1, NLON, body, 0)

    def lat_all(action):
        def body(step, carry):
            action(lax.rem(d + step, NLAT))
            return carry

        lax.fori_loop(1, NLAT, body, 0)

    barrier = pltpu.get_barrier_semaphore()
    lon_all(lambda o: pl.semaphore_signal(barrier, inc=1, device_id=(o, d), device_id_type=MESH))
    lat_all(lambda o: pl.semaphore_signal(barrier, inc=1, device_id=(e, o), device_id_type=MESH))
    pl.semaphore_signal(barrier, inc=1, device_id=(e_up, d_up), device_id_type=MESH)
    pl.semaphore_signal(barrier, inc=1, device_id=(e_dn, d_dn), device_id_type=MESH)

    to_quad = one_hot(QROWS, orders[0:1, 0:HALF])
    for b in range(2):
        sq[b] = dot_nn(to_quad, fields[b * HALF:(b + 1) * HALF, :]).astype(BF16)
    pl.semaphore_wait(barrier, NLON - 1 + NLAT - 1 + 2)

    pieces = ((224, 224), (448, 80), (528, 80))

    def halo(src, dst, ssem, rsem, step):
        devices = ((e, step[1]), (step[0], d), (step[0], step[1]))
        return [
            remote(src.at[:, pl.ds(at, size), :], dst.at[:, pl.ds(at, size), :], ssem.at[i], rsem.at[i], dev)
            for i, ((at, size), dev) in enumerate(zip(pieces, devices))
        ]

    halo_copies = halo(sq, rq, halo_ss, halo_rs, (e_dn, d_dn))
    for copy in halo_copies:
        copy.start()

    lane = lanes(1, 256)
    cell_lane = jnp.where(lane % 16 < 12, (12 * (lane // 16) + 3 + lane % 16) % 192, -1)
    cells = dot_nn(cot[...], one_hot(192, cell_lane))
    block_of = lanes(72, 128) // 16
    for o in range(NLON):
        tile, inner = (o // 8) * 128, o % 8
        piece = jnp.zeros((72, 128), F32)
        for bl in range(8):
            part = cells[bl * 72:(bl + 1) * 72, tile:tile + 128]
            shift = (16 * (bl - inner)) % 128
            if shift:
                part = pltpu.roll(part, shift, 1)
            piece = jnp.where(block_of == bl, part, piece)
        for a in range(3):
            padded = jnp.concatenate([piece[a * 24:(a + 1) * 24], jnp.zeros((8, 128), F32)], axis=0)
            cs[o, a] = padded.astype(BF16)
    wg[e] = jnp.concatenate(
        [merge_wt[...].astype(F32), jnp.zeros((8, 768), F32)], axis=0
    ).astype(BF16)
    cg[:, e] = cs[e]

    def cot_copy(o, mine):
        return remote(cs.at[o], cg.at[:, mine], cot_ss.at[o], cot_rs.at[mine], (o, d))

    def w_copy(o, mine):
        return remote(wg.at[mine], wg.at[mine], w_ss.at[o], w_rs.at[mine], (o, d))

    def start_merge(o):
        cot_copy(o, e).start()
        w_copy(o, e).start()

    lon_all(start_merge)

    for h in range(HEADS):
        b16[2 * h:2 * h + 2, :] = bias[h]
    b16[12:16, :] = jnp.zeros((4, POS), F32)
    zero_tail = jnp.zeros((16, 256 - 138), F32)
    for p in range(2):
        for r in range(6):
            parts = []
            for pk in range(2):
                at = (p * 2 + pk) * 828 + r * 138
                parts += [b16[:, at:at + 138], zero_tail]
            row = jnp.concatenate(parts, axis=1)
            high = row.astype(BF16)
            rest = row - high.astype(F32)
            middle = rest.astype(BF16)
            low = (rest - middle.astype(F32)).astype(BF16)
            at = pl.ds((p * 6 + r) * 16, 16)
            bl_s[0, at, :] = high
            bl_s[1, at, :] = middle
            bl_s[2, at, :] = low

    def spread(s_i, carry):
        matrix = spread_matrix(s_i)
        rows = dot_nn(bl_s[0], matrix) + dot_nn(bl_s[1], matrix) + dot_nn(bl_s[2], matrix)
        at = pl.ds(pl.multiple_of(s_i * 192, 192), 192)
        bs_s[0, at, :] = rows[:, 0:128]
        bs_s[1, at, :] = jnp.concatenate([rows[:, 128:144], jnp.zeros((192, 112), F32)], axis=1)
        return carry

    lax.fori_loop(0, 12, spread, 0)

    tok_i = lax.broadcasted_iota(I32, (WIN, WIN), 0) % 12
    tok_k = lax.broadcasted_iota(I32, (WIN, WIN), 1) % 12
    last_band = d == NLAT - 1
    lat_differs = ((tok_i % 6 >= 3) != (tok_k % 6 >= 3)) & last_band
    lev_differs = (tok_i >= 6) != (tok_k >= 6)
    for lw in range(2):
        differs = (lat_differs | lev_differs) if lw else lat_differs
        for h in range(HEADS):
            at = pl.ds(h * 2 + lw, WIN, stride=16)
            full = jnp.concatenate([bs_s.at[0][at, :], bs_s.at[1][at, :]], axis=1)[:, 0:WIN]
            bx[lw, h * WIN:(h + 1) * WIN, :] = jnp.where(differs, MASKED, full)

    wq[...] = triple_w[:, 0:192]
    wk[...] = triple_w[:, 192:384]
    wv[...] = triple_w[:, 384:576]

    head_of = lanes(1, C) // 32
    head_f = [jnp.where(head_of == h, 1.0, 0.0) for h in range(HEADS)]
    head_b = [mask.astype(BF16) for mask in head_f]

    def stacked(values):
        return jnp.concatenate([values * mask for mask in head_b], axis=0)

    def unstacked(values):
        total = values[0:WIN] * head_f[0]
        for h in range(1, HEADS):
            total = total + values[h * WIN:(h + 1) * WIN] * head_f[h]
        return total

    to_window = one_hot(HALF, orders[2:3, 0:QROWS])
    for copy in halo_copies:
        copy.wait()
    rq[:, 0:224, :] = sq[:, 0:224, :]
    for b in range(2):
        x_w[b * HALF:(b + 1) * HALF, :] = dot_nn(to_window, rq[b]).astype(BF16)

    def window_rows(w):
        return pl.ds(pl.multiple_of(w * WIN, WIN), WIN)

    def chunk_rows(i):
        return pl.ds(pl.multiple_of(i * CHUNK, CHUNK), CHUNK)

    def project(i, carry):
        rows = chunk_rows(i)
        normed = statistics(x_w[rows, :].astype(F32))[0]
        normed_in = (normed * attend_gain[...]).astype(BF16)
        ni_s[rows, :] = normed_in
        q_s[rows, :] = dot_nn(normed_in, wq[...]).astype(BF16)
        k_s[rows, :] = dot_nn(normed_in, wk[...]).astype(BF16)
        v_s[rows, :] = dot_nn(normed_in, wv[...]).astype(BF16)
        return carry

    lax.fori_loop(0, NCHUNK, project, 0)

    def attend(w, carry):
        rows = window_rows(w)
        lw = lax.rem(w // 2, 2)
        scores = dot_nt(stacked(q_s[rows, :]), k_s[rows, :]) * FACTOR + bx[lw]
        exponent = jnp.exp(scores - jnp.max(scores, axis=-1, keepdims=True))
        chances = exponent * (1.0 / jnp.sum(exponent, axis=-1, keepdims=True))
        half = chances.astype(BF16)
        p_s[w] = half
        att_s[rows, :] = unstacked(dot_nn(half, v_s[rows, :])).astype(BF16)
        return carry

    lax.fori_loop(0, NWIN, attend, 0)

    lon_all(lambda o: cot_copy(e, o).wait_recv())
    lat_copy = remote(cg.at[pl.ds(0, 2)], ch, lat_ss.at[0], lat_rs.at[0], (e, d_dn))
    lat_copy.start()

    def feed(i, carry):
        rows = chunk_rows(i)
        middle = x_w[rows, :].astype(F32) + dot_nn(att_s[rows, :], output_w[...])
        mid_s[rows, :] = middle
        normed_mid = (statistics(middle)[0] * feed_gain[...]).astype(BF16)
        nm_s[rows, :] = normed_mid
        act, slope = gelu_parts(dot_nn(normed_mid, expand_w[...]))
        act = act.astype(BF16)
        act_s[rows, :] = act
        slope_s[rows, :] = slope
        vo_s[rows, :] = (middle + dot_nt(act, shrink_t[...])).astype(BF16)
        return carry

    lax.fori_loop(0, NCHUNK, feed, 0)

    lat_copy.wait_recv()
    lon_all(lambda o: w_copy(e, o).wait_recv())
    gain_row = merge_gain[...].reshape(1, 4 * C)
    for r in range(6):
        x = (r + 1) % 2
        cell = (0, 1, 1, 2, 2, 3)[r]
        plane = cg[cell + 1] if cell < 2 else ch[cell - 2]
        weight = wg[:, :, x * 384:(x + 1) * 384].reshape(512, 384)
        scaled = dot_tn(plane.reshape(512, 128), weight) * gain_row[:, x * 384:(x + 1) * 384]
        qry[2 * r] = scaled[:, 0:192].astype(BF16)
        qry[2 * r + 1] = scaled[:, 192:384].astype(BF16)

    st[...] = jnp.zeros_like(st)
    col = lanes(1, 384)
    col_p, col_ry, col_m = col // 192, (col // 16) % 12, col % 16
    stat_lane = lanes(WIN, 128)

    def merge_sums(w, carry):
        rows = window_rows(w)
        b, lw, lon_win = w // 4, lax.rem(w // 2, 2), lax.rem(w, 2)
        parts = []
        for p in range(2):
            level = lax.rem(lw * 2 + p + 1, 4)
            at = pl.ds(pl.multiple_of((b * 4 + level) * 16, 16), 16)
            parts.append(qry[:, at, :].reshape(192, C))
        pair = col_m - lon_win * 6
        token = (2 * pair + col_ry % 2) * 12 + col_p * 6 + col_ry // 2
        token = jnp.where((pair >= 0) & (pair < 6), token, -1)
        q = dot_nn(one_hot(WIN, token), jnp.concatenate(parts, axis=0))
        qw[rows, :] = q.astype(BF16)
        v = vo_s[rows, :].astype(F32)
        mean = jnp.mean(v, axis=-1, keepdims=True)
        centred = v - mean
        squares = jnp.sum(centred * centred, axis=-1, keepdims=True)
        q_sum = jnp.sum(q, axis=-1, keepdims=True)
        qv_sum = jnp.sum(q * centred, axis=-1, keepdims=True)
        total = st[...]
        for j, value in enumerate((mean, squares, q_sum, qv_sum)):
            total = jnp.where(stat_lane == 32 * j + w, value, total)
        st[...] = total
        return carry

    lax.fori_loop(0, NWIN, merge_sums, 0)

    tup[...] = st[pl.ds(5, 24, stride=6), :]
    tdn[...] = st[pl.ds(0, 24, stride=6), :]
    up_copy = remote(tup, sup, st_ss.at[0], st_rs.at[0], (e, d_up))
    dn_copy = remote(tdn, sdn, st_ss.at[1], st_rs.at[1], (e, d_dn))
    up_copy.start()
    dn_copy.start()
    for r, other in ((1, 2), (2, 1), (3, 4), (4, 3)):
        sx[pl.ds(r, 24, stride=6), :] = st[pl.ds(other, 24, stride=6), :]
    up_copy.wait()
    dn_copy.wait()
    sx[pl.ds(0, 24, stride=6), :] = sup[...]
    sx[pl.ds(5, 24, stride=6), :] = sdn[...]

    even = (lax.broadcasted_iota(I32, (WIN, 128), 0) // 12) % 2 == 0

    def pair_of(values):
        return jnp.where(even, pltpu.roll(values, WIN - 12, 0), pltpu.roll(values, 12, 0))

    own, cross = st[...], sx[...]
    group = [own, cross, pair_of(own), pair_of(cross)]
    cell_mean = (group[0] + group[1] + group[2] + group[3]) * 0.25
    variance = jnp.zeros((WIN, 128), F32)
    q_total = jnp.zeros((WIN, 128), F32)
    qv_total = jnp.zeros((WIN, 128), F32)
    for values in group:
        offset = values - cell_mean
        q_sum = pltpu.roll(values, 64, 1)
        variance = variance + pltpu.roll(values, 96, 1) + 192.0 * offset * offset
        q_total = q_total + q_sum
        qv_total = qv_total + pltpu.roll(values, 32, 1) + offset * q_sum
    cell_inverse = lax.rsqrt(jnp.where(stat_lane < 8, variance, 0.0) * (1.0 / 768.0) + EPS)
    cp_s[0] = cell_mean
    cp_s[1] = cell_inverse
    cp_s[2] = q_total * (1.0 / 768.0)
    cp_s[3] = cell_inverse * cell_inverse * qv_total * (1.0 / 768.0)

    def merge_back(w, carry):
        rows = window_rows(w)
        mean, inverse, q_mean, projected = [
            jnp.sum(jnp.where(stat_lane == w, cp_s[j], 0.0), axis=-1, keepdims=True) for j in range(4)
        ]
        v = vo_s[rows, :].astype(F32) - mean
        go_s[rows, :] = (inverse * (qw[rows, :].astype(F32) - q_mean - v * projected)).astype(BF16)
        return carry

    lax.fori_loop(0, NWIN, merge_back, 0)

    def feed_back(i, carry):
        rows = chunk_rows(i)
        go = go_s[rows, :]
        gh = (dot_nn(go, shrink_t[...]) * slope_s[rows, :]).astype(BF16)
        gh_s[rows, :] = gh
        gnm = dot_nt(gh, expand_w[...])
        unit, inverse = statistics(mid_s[rows, :])
        gm = go.astype(F32) + norm_back(unit, inverse, gnm * feed_gain[...])
        gm_s[rows, :] = gm
        half = gm.astype(BF16)
        gmh_s[rows, :] = half
        ga_s[rows, :] = dot_nt(half, output_w[...]).astype(BF16)
        return carry + jnp.sum(gnm * unit, axis=0, keepdims=True)

    feed_sum = lax.fori_loop(0, NCHUNK, feed_back, jnp.zeros((1, C), F32))

    g_expand = dot_tn(nm_s[...], gh_s[...]).astype(BF16)
    g_shrink = dot_tn(go_s[...], act_s[...]).astype(BF16)
    g_output = dot_tn(att_s[...], gmh_s[...]).astype(BF16)
    for i in range(4):
        for j in range(2):
            g1s[2 * i + j, 0:48] = g_expand[i * 48:(i + 1) * 48, j * 384:(j + 1) * 384]
            g1s[8 + 2 * i + j, 0:48] = g_shrink[i * 48:(i + 1) * 48, j * 384:(j + 1) * 384]
    wide = jnp.concatenate([g_output[0:96], g_output[96:192]], axis=1)
    for i in range(6):
        g1s[i, 48:64] = wide[i * 16:(i + 1) * 16]
    first_row = lax.broadcasted_iota(I32, (16, C), 0) == 0
    g1s[6, 48:64] = jnp.concatenate(
        [jnp.where(first_row, feed_sum, 0.0), jnp.zeros((16, C), F32)], axis=1
    ).astype(BF16)
    for i in range(7, NLON):
        g1s[i, 48:64] = jnp.zeros((16, 384), BF16)
    g1r[e] = g1s[e]

    def g1_copy(o, mine):
        return remote(g1s.at[o], g1r.at[mine], g1_ss.at[o], g1_rs.at[mine], (o, d))

    def g1l_copy(o, mine):
        return remote(g1l.at[mine], g1l.at[mine], g1l_ss.at[o], g1l_rs.at[mine], (e, o))

    def g1f_copy(o, mine):
        return remote(g1f.at[mine], g1f.at[mine], g1f_ss.at[o], g1f_rs.at[mine], (o, d))

    lon_all(lambda o: g1_copy(o, e).start())

    ds_s[...] = jnp.zeros_like(ds_s)

    def attend_back(w, carry):
        rows = window_rows(w)
        lw = lax.rem(w // 2, 2)
        k = k_s[rows, :]
        ga = stacked(ga_s[rows, :])
        half = p_s[w]
        chances = half.astype(F32)
        weighted = dot_nt(ga, v_s[rows, :])
        centre = jnp.sum(chances * weighted, axis=-1, keepdims=True)
        ds = chances * (weighted - centre)
        ds_s[lw] = ds_s[lw] + ds
        ds = ds.astype(BF16)
        dq_s[rows, :] = (unstacked(dot_nn(ds, k)) * FACTOR).astype(BF16)
        dk_s[rows, :] = (dot_tn(ds, stacked(q_s[rows, :])) * FACTOR).astype(BF16)
        dv_s[rows, :] = dot_tn(half, ga).astype(BF16)
        return carry

    lax.fori_loop(0, 5, attend_back, 0)

    lon_all(lambda o: g1_copy(e, o).wait_recv())
    total = g1r[0].astype(F32)
    for o in range(1, NLON):
        total = total + g1r[o].astype(F32)
    g1l[d] = total.astype(BF16)
    lat_all(lambda o: g1l_copy(o, d).start())

    lax.fori_loop(5, NWIN, attend_back, 0)

    lat_all(lambda o: g1l_copy(d, o).wait_recv())
    total = g1l[0].astype(F32)
    for o in range(1, NLAT):
        total = total + g1l[o].astype(F32)
    g1f[e] = total.astype(BF16)
    lon_all(lambda o: g1f_copy(o, e).start())

    ni = ni_s[...]
    g_triple = jnp.concatenate(
        [dot_tn(ni, dq_s[...]), dot_tn(ni, dk_s[...]), dot_tn(ni, dv_s[...]), jnp.zeros((C, 64), F32)], axis=1
    ).astype(BF16)
    for i in range(3):
        for j in range(5):
            g2s[5 * i + j] = g_triple[i * 64:(i + 1) * 64, j * 128:(j + 1) * 128]

    def project_back(i, carry):
        rows = chunk_rows(i)
        gni = dot_nt(dq_s[rows, :], wq[...]) + dot_nt(dk_s[rows, :], wk[...]) + dot_nt(dv_s[rows, :], wv[...])
        unit, inverse = statistics(x_w[rows, :].astype(F32))
        gt_s[rows, :] = (gm_s[rows, :] + norm_back(unit, inverse, gni * attend_gain[...])).astype(BF16)
        return carry + jnp.sum(gni * unit, axis=0, keepdims=True)

    attend_sum = lax.fori_loop(0, NCHUNK, project_back, jnp.zeros((1, C), F32))
    gain_row_id = lax.broadcasted_iota(I32, (64, 128), 0)
    gain_tail = jnp.concatenate([attend_sum[:, 128:C], jnp.zeros((1, 64), F32)], axis=1)
    g2s[15] = jnp.where(
        gain_row_id == 0, attend_sum[:, 0:128], jnp.where(gain_row_id == 1, gain_tail, 0.0)
    ).astype(BF16)
    g2r[e] = g2s[e]

    def g2_copy(o, mine):
        return remote(g2s.at[o], g2r.at[mine], g2_ss.at[o], g2_rs.at[mine], (o, d))

    def g2l_copy(o, mine):
        return remote(g2l.at[mine], g2l.at[mine], g2l_ss.at[o], g2l_rs.at[mine], (e, o))

    def g2f_copy(o, mine):
        return remote(g2f.at[mine], g2f.at[mine], g2f_ss.at[o], g2f_rs.at[mine], (o, d))

    lon_all(lambda o: g2_copy(o, e).start())

    from_window = one_hot(QROWS, orders[3:4, 0:HALF])
    for b in range(2):
        gq[b] = dot_nn(from_window, gt_s[b * HALF:(b + 1) * HALF, :]).astype(BF16)
    back_copies = halo(gq, hq, back_ss, back_rs, (e_up, d_up))
    for copy in back_copies:
        copy.start()

    for lw in range(2):
        for h in range(HEADS):
            at = pl.ds(h * 2 + lw, WIN, stride=16)
            part = ds_s[lw, h * WIN:(h + 1) * WIN, :]
            bs_s.at[0][at, :] = part[:, 0:128]
            bs_s.at[1][at, :] = jnp.concatenate([part[:, 128:144], jnp.zeros((WIN, 112), F32)], axis=1)

    def fold(s_i, carry):
        at = pl.ds(pl.multiple_of(s_i * 192, 192), 192)
        rows = jnp.concatenate([bs_s[0, at, :], bs_s[1, at, :]], axis=1)[:, 0:WIN].astype(BF16)
        return carry + dot_nt(rows, spread_matrix(s_i))

    folded = lax.fori_loop(0, 12, fold, jnp.zeros((192, 512), F32))
    pieces_t = []
    for p in range(2):
        for pk in range(2):
            for r in range(6):
                at = (p * 6 + r) * 16
                pieces_t.append(folded[at:at + 16, pk * 256:pk * 256 + 138])
    table = jnp.concatenate(pieces_t + [jnp.zeros((16, 4096 - POS), F32)], axis=1).astype(BF16)
    for o in range(NLON):
        tbs[o] = table[:, o * 256:(o + 1) * 256]
    tbr[e] = tbs[e]

    def tb_copy(o, mine):
        return remote(tbs.at[o], tbr.at[mine], tb_ss.at[o], tb_rs.at[mine], (o, d))

    def tbf_copy(o, mine):
        return remote(tbf.at[mine], tbf.at[mine], tbf_ss.at[o], tbf_rs.at[mine], (o, d))

    lon_all(lambda o: tb_copy(o, e).start())

    lon_all(lambda o: g2_copy(e, o).wait_recv())
    total = g2r[0].astype(F32)
    for o in range(1, NLON):
        total = total + g2r[o].astype(F32)
    g2l[d] = total.astype(BF16)
    lat_all(lambda o: g2l_copy(o, d).start())

    to_natural = one_hot(HALF, orders[1:2, 0:QROWS])
    for copy in back_copies:
        copy.wait()
    hq[:, 0:224, :] = gq[:, 0:224, :]

    lon_all(lambda o: tb_copy(e, o).wait_recv())
    total = tbr[0].astype(F32)
    for o in range(1, NLON):
        total = total + tbr[o].astype(F32)
    tbf[e] = total.astype(BF16)
    lon_all(lambda o: tbf_copy(o, e).start())

    lat_all(lambda o: g2l_copy(d, o).wait_recv())
    total = g2l[0].astype(F32)
    for o in range(1, NLAT):
        total = total + g2l[o].astype(F32)
    g2f[e] = total.astype(BF16)
    lon_all(lambda o: g2f_copy(o, e).start())

    for b in range(2):
        out_fields[b * HALF:(b + 1) * HALF, :] = dot_nn(to_natural, hq[b]).astype(BF16)
    lon_all(lambda o: g1f_copy(e, o).wait_recv())
    out_g1[...] = g1f[...]
    lon_all(lambda o: tbf_copy(e, o).wait_recv())
    out_table[...] = tbf[...]
    lon_all(lambda o: g2f_copy(e, o).wait_recv())
    out_g2[...] = g2f[...]

    def sent(o):
        cot_copy(o, e).wait_send()
        w_copy(o, e).wait_send()
        g1_copy(o, e).wait_send()
        g1f_copy(o, e).wait_send()
        g2_copy(o, e).wait_send()
        g2f_copy(o, e).wait_send()
        tb_copy(o, e).wait_send()
        tbf_copy(o, e).wait_send()

    def sent_lat(o):
        g1l_copy(o, d).wait_send()
        g2l_copy(o, d).wait_send()

    lon_all(sent)
    lat_all(sent_lat)
    lat_copy.wait_send()


def results_kernel(
    fields, g1, g2, folded,
    out_fields, out_triple, out_output, out_expand, out_shrink, out_attend, out_feed, out_table,
):
    out_fields[...] = fields[...]
    for i in range(4):
        for j in range(2):
            rows, cols = slice(i * 48, (i + 1) * 48), slice(j * 384, (j + 1) * 384)
            out_expand[rows, cols] = g1[2 * i + j, 0:48].astype(F32)
            out_shrink[rows, cols] = g1[8 + 2 * i + j, 0:48].astype(F32)
    for i in range(6):
        wide = g1[i, 48:64].astype(F32)
        out_output[i * 16:(i + 1) * 16, :] = wide[:, 0:C]
        out_output[96 + i * 16:96 + (i + 1) * 16, :] = wide[:, C:2 * C]
    out_feed[...] = g1[6, 48:64].astype(F32)[0:1, 0:C]
    for i in range(3):
        for j in range(5):
            size = 128 if j < 4 else 64
            out_triple[i * 64:(i + 1) * 64, j * 128:j * 128 + size] = g2[5 * i + j].astype(F32)[:, 0:size]
    gain = g2[15].astype(F32)
    out_attend[:, 0:128] = gain[0:1, :]
    out_attend[:, 128:C] = gain[1:2, 0:C - 128]
    table = jnp.concatenate([folded[o] for o in range(NLON)], axis=1).astype(F32)
    for h in range(HEADS):
        out_table[h] = table[2 * h:2 * h + 2, 0:POS]


def scratch():
    def vmem(*shape, kind=BF16):
        return pltpu.VMEM(shape, kind)

    token = vmem(TOK, C)
    token_f = vmem(TOK, C, kind=F32)
    weight = vmem(C, C)
    quad = vmem(2, QROWS, C)
    stat = vmem(WIN, 128, kind=F32)
    small = vmem(24, 128, kind=F32)
    buffers = [
        quad, quad, quad, quad, token, token, token, token, token, weight, weight, weight,
        vmem(NWIN, HEADS * WIN, WIN), token, token_f, token, vmem(TOK, FF), vmem(TOK, FF, kind=F32), token,
        vmem(16, POS, kind=F32), vmem(3, 192, 512), vmem(2, 2304, 128, kind=F32),
        vmem(2, HEADS * WIN, WIN, kind=F32), vmem(2, HEADS * WIN, WIN, kind=F32),
        vmem(16, 3, 32, 128), vmem(3, 16, 32, 128), vmem(2, 16, 32, 128), vmem(16, 32, 768),
        vmem(12, 128, C), token, stat, stat, small, small, small, small, vmem(4, WIN, 128, kind=F32),
        token, vmem(TOK, FF), token_f, token, token, token, token, token, token,
        vmem(16, 64, 384), vmem(16, 64, 384), vmem(8, 64, 384), vmem(16, 64, 384),
        vmem(16, 64, 128), vmem(16, 64, 128), vmem(8, 64, 128), vmem(16, 64, 128),
        vmem(16, 16, 256), vmem(16, 16, 256), vmem(16, 16, 256),
    ]
    counts = [3, 3, 16, 16, 16, 16, 1, 1, 2, 2]
    counts += [16, 16, 8, 8, 16, 16, 16, 16, 8, 8, 16, 16, 16, 16, 16, 16, 3, 3]
    return buffers + [pltpu.SemaphoreType.DMA((n,)) for n in counts]


def per_device(
    fields, merge_cotangent, attend_gain, triple_weight, bias_table, output_weight, feed_gain,
    expand_weight, shrink_weight, merge_gain, merge_weight,
):
    cot = jnp.transpose(merge_cotangent, (1, 2, 3, 4, 0)).reshape(576, 192)
    bias = jnp.transpose(bias_table[0], (1, 0, 2))
    def shaped(shapes):
        return [jax.ShapeDtypeStruct(shape, kind) for shape, kind in shapes]

    vmem_spec = pl.BlockSpec(memory_space=pltpu.VMEM)
    parts = pl.pallas_call(
        kernel,
        out_shape=shaped(
            [((TOK, C), BF16), ((16, 64, 384), BF16), ((16, 64, 128), BF16), ((16, 16, 256), BF16)]
        ),
        in_specs=[vmem_spec] * 12,
        out_specs=[vmem_spec] * 4,
        scratch_shapes=scratch(),
        compiler_params=pltpu.CompilerParams(
            collective_id=0, has_side_effects=True, vmem_limit_bytes=60 * 1024 * 1024
        ),
    )(
        fields.reshape(TOK, C), cot, attend_gain.reshape(1, C), triple_weight, bias, output_weight,
        feed_gain.reshape(1, C), expand_weight, shrink_weight.T, merge_gain,
        merge_weight.T, jnp.asarray(order_indices()),
    )
    g_fields, g_triple, g_output, g_expand, g_shrink, g_attend, g_feed, g_table = pl.pallas_call(
        results_kernel,
        out_shape=shaped(
            [
                ((TOK, C), BF16), ((C, 3 * C), F32), ((C, C), F32), ((C, FF), F32), ((C, FF), F32),
                ((1, C), F32), ((1, C), F32), ((HEADS, 2, POS), F32),
            ]
        ),
        in_specs=[vmem_spec] * 4,
        out_specs=[vmem_spec] * 8,
        compiler_params=pltpu.CompilerParams(vmem_limit_bytes=32 * 1024 * 1024),
    )(*parts)
    return (
        g_fields.reshape(fields.shape), g_triple, g_output, g_expand, g_shrink.T,
        g_attend.reshape(C), g_feed.reshape(C), jnp.transpose(g_table, (1, 0, 2))[None],
    )


def solution(mesh):
    placed = (
        P(None, None, "lat", "lon", None),
        P(None, None, None, "lat", "lon"),
        P(),
        P(),
        P("lat", None, None, None),
        P(),
        P(),
        P(),
        P(),
        P(),
        P(None, "lon"),
    )
    return jax.shard_map(
        per_device,
        mesh=mesh,
        in_specs=placed,
        out_specs=(
            P(None, None, "lat", "lon", None),
            P(),
            P(),
            P(),
            P(),
            P(),
            P(),
            P("lat", None, None, None),
        ),
        check_vma=False,
    )
```

```python
import functools
import math

import jax
import jax.numpy as jnp
import numpy as np
from jax import lax
from jax.experimental import pallas as pl
from jax.experimental.pallas import tpu as pltpu
from jax.sharding import PartitionSpec as P

F32 = jnp.float32
BF16 = jnp.bfloat16
I32 = jnp.int32
MESH = pl.DeviceIdType.MESH

EPS = 1e-05
MASKED = -1000000000.0
NLON = 16
NLAT = 8
C = 192
HEADS = 6
FF = 768
WIN = 144
NWIN = 8
TOK = WIN * NWIN
HALF = TOK // 2
QROWS = 608
POS = 3312
CHUNK = 288
NCHUNK = TOK // CHUNK
TILE = 48
WIDE = 896
FACTOR = 32 ** -0.5


def order_indices():
    natural_to_quad = np.full(640, -1, np.int32)
    quad_to_natural = np.full(640, -1, np.int32)
    quad_to_window = np.full(640, -1, np.int32)
    window_to_quad = np.full(640, -1, np.int32)
    for level in range(4):
        for row in range(6):
            for col in range(24):
                source = (level * 6 + row) * 24 + col
                if col >= 6:
                    place = (0 if row >= 3 else 224) + level * 54 + (row % 3) * 18 + col - 6
                else:
                    place = (448 if row >= 3 else 528) + level * 18 + (row % 3) * 6 + col
                natural_to_quad[source] = place
                quad_to_natural[place] = source
    index = 0
    for lev_win in range(2):
        for lon_win in range(2):
            for s in range(12):
                for p in range(2):
                    for r in range(6):
                        level = (lev_win * 2 + p + 1) % 4
                        col = lon_win * 12 + s
                        if col < 18:
                            place = (0 if r < 3 else 224) + level * 54 + (r % 3) * 18 + col
                        else:
                            place = (448 if r < 3 else 528) + level * 18 + (r % 3) * 6 + col - 18
                        window_to_quad[index] = place
                        quad_to_window[place] = index
                        index += 1
    rows = [natural_to_quad, quad_to_natural, quad_to_window, window_to_quad]
    return np.stack(rows + rows)


def dot_nn(a, b):
    return lax.dot_general(a, b, (((1,), (0,)), ((), ())), preferred_element_type=F32)


def dot_nt(a, b):
    return lax.dot_general(a, b, (((1,), (1,)), ((), ())), preferred_element_type=F32)


def dot_tn(a, b):
    return lax.dot_general(a, b, (((0,), (0,)), ((), ())), preferred_element_type=F32)


def one_hot(rows, targets):
    ids = lax.broadcasted_iota(I32, (rows, targets.shape[1]), 0)
    return jnp.where(ids == targets, 1.0, 0.0).astype(BF16)


def statistics(values):
    centred = values - jnp.mean(values, axis=-1, keepdims=True)
    inverse = lax.rsqrt(jnp.mean(centred * centred, axis=-1, keepdims=True) + EPS)
    return centred * inverse, inverse


def norm_back(normed, inverse, scaled):
    centre = jnp.mean(scaled, axis=-1, keepdims=True)
    projected = jnp.mean(scaled * normed, axis=-1, keepdims=True)
    return inverse * (scaled - centre - normed * projected)


def gelu_parts(values):
    cumulative = 0.5 * (1.0 + lax.erf(values * (1.0 / math.sqrt(2.0))))
    density = jnp.exp(-0.5 * values * values) * (1.0 / math.sqrt(2.0 * math.pi))
    return values * cumulative, cumulative + values * density


def lanes(rows, cols):
    return lax.broadcasted_iota(I32, (rows, cols), 1)


def bias_targets():
    k = lanes(1, WIN)
    s, rest = k // 12, k % 12
    return (rest // 6) * 256 + (rest % 6) * 23 + 11 - s


def spread_matrix(s_i):
    return one_hot(512, bias_targets() + s_i)


def kernel(
    fields, cot, attend_gain, triple_w, bias, output_w, feed_gain, expand_w, shrink_t, merge_gain,
    merge_wt, orders,
    out_fields, out_g1, out_g2, out_table,
    sq, rq, gq, hq, x_w, ni_s, q_s, k_s, v_s, wq, wk, wv, p_s, att_s, mid_s, nm_s, act_s, slope_s, vo_s,
    b16, bl_s, bs_s, bx, ds_s,
    cs, cg, ch, wg, qry, qw, st, sx, sup, sdn, tup, tdn, cp_s, go_s, gh_s, gm_s, ga_s, gmh_s,
    dq_s, dk_s, dv_s, gt_s, raw, dsh, g1s, g1r, g1l, g1f, g2s, g2r, g2l, g2f, tbs, tbr, tbf,
    halo_ss, halo_rs, cot_ss, cot_rs, w_ss, w_rs, lat_ss, lat_rs, st_ss, st_rs,
    g1_ss, g1_rs, g1l_ss, g1l_rs, g1f_ss, g1f_rs, g2_ss, g2_rs, g2l_ss, g2l_rs, g2f_ss, g2f_rs,
    tb_ss, tb_rs, tbf_ss, tbf_rs, back_ss, back_rs,
):
    e = lax.axis_index("lon")
    d = lax.axis_index("lat")
    e_up, e_dn = lax.rem(e + 1, NLON), lax.rem(e + NLON - 1, NLON)
    d_up, d_dn = lax.rem(d + 1, NLAT), lax.rem(d + NLAT - 1, NLAT)

    def remote(src, dst, ssem, rsem, device):
        return pltpu.make_async_remote_copy(
            src_ref=src, dst_ref=dst, send_sem=ssem, recv_sem=rsem, device_id=device,
            device_id_type=MESH,
        )

    def lon_all(action):
        def body(step, carry):
            action(lax.rem(e + step, NLON))
            return carry

        lax.fori_loop(1, NLON, body, 0)

    def lat_all(action):
        def body(step, carry):
            action(lax.rem(d + step, NLAT))
            return carry

        lax.fori_loop(1, NLAT, body, 0)

    barrier = pltpu.get_barrier_semaphore()
    lon_all(lambda o: pl.semaphore_signal(barrier, inc=1, device_id=(o, d), device_id_type=MESH))
    lat_all(lambda o: pl.semaphore_signal(barrier, inc=1, device_id=(e, o), device_id_type=MESH))
    pl.semaphore_signal(barrier, inc=1, device_id=(e_up, d_up), device_id_type=MESH)
    pl.semaphore_signal(barrier, inc=1, device_id=(e_dn, d_dn), device_id_type=MESH)

    to_quad = one_hot(QROWS, orders[0:1, 0:HALF])
    for b in range(2):
        sq[b] = dot_nn(to_quad, fields[b * HALF:(b + 1) * HALF, :]).astype(BF16)
    pl.semaphore_wait(barrier, NLON - 1 + NLAT - 1 + 2)

    pieces = ((224, 224), (448, 80), (528, 80))

    def halo(src, dst, ssem, rsem, step):
        devices = ((e, step[1]), (step[0], d), (step[0], step[1]))
        return [
            remote(src.at[:, pl.ds(at, size), :], dst.at[:, pl.ds(at, size), :], ssem.at[i], rsem.at[i], dev)
            for i, ((at, size), dev) in enumerate(zip(pieces, devices))
        ]

    halo_copies = halo(sq, rq, halo_ss, halo_rs, (e_dn, d_dn))
    for copy in halo_copies:
        copy.start()

    lane = lanes(1, 256)
    cell_lane = jnp.where(lane % 16 < 12, (12 * (lane // 16) + 3 + lane % 16) % 192, -1)
    cells = dot_nn(cot[...], one_hot(192, cell_lane))
    block_of = lanes(72, 128) // 16
    for o in range(NLON):
        tile, inner = (o // 8) * 128, o % 8
        piece = jnp.zeros((72, 128), F32)
        for bl in range(8):
            part = cells[bl * 72:(bl + 1) * 72, tile:tile + 128]
            shift = (16 * (bl - inner)) % 128
            if shift:
                part = pltpu.roll(part, shift, 1)
            piece = jnp.where(block_of == bl, part, piece)
        for a in range(3):
            padded = jnp.concatenate([piece[a * 24:(a + 1) * 24], jnp.zeros((8, 128), F32)], axis=0)
            cs[o, a] = padded.astype(BF16)
    wg[e] = jnp.concatenate(
        [merge_wt[...].astype(F32), jnp.zeros((8, 768), F32)], axis=0
    ).astype(BF16)
    cg[:, e] = cs[e]

    def cot_copy(o, mine):
        return remote(cs.at[o], cg.at[:, mine], cot_ss.at[o], cot_rs.at[mine], (o, d))

    def w_copy(o, mine):
        return remote(wg.at[mine], wg.at[mine], w_ss.at[o], w_rs.at[mine], (o, d))

    def start_merge(o):
        cot_copy(o, e).start()
        w_copy(o, e).start()

    lon_all(start_merge)

    for h in range(HEADS):
        b16[2 * h:2 * h + 2, :] = bias[h]
    b16[12:16, :] = jnp.zeros((4, POS), F32)
    zero_tail = jnp.zeros((16, 256 - 138), F32)
    for p in range(2):
        for r in range(6):
            parts = []
            for pk in range(2):
                at = (p * 2 + pk) * 828 + r * 138
                parts += [b16[:, at:at + 138], zero_tail]
            row = jnp.concatenate(parts, axis=1)
            high = row.astype(BF16)
            rest = row - high.astype(F32)
            middle = rest.astype(BF16)
            low = (rest - middle.astype(F32)).astype(BF16)
            at = pl.ds((p * 6 + r) * 16, 16)
            bl_s[0, at, :] = high
            bl_s[1, at, :] = middle
            bl_s[2, at, :] = low

    def spread(s_i, carry):
        matrix = spread_matrix(s_i)
        rows = dot_nn(bl_s[0], matrix) + dot_nn(bl_s[1], matrix) + dot_nn(bl_s[2], matrix)
        at = pl.ds(pl.multiple_of(s_i * 192, 192), 192)
        bs_s[0, at, :] = rows[:, 0:128]
        bs_s[1, at, :] = jnp.concatenate([rows[:, 128:144], jnp.zeros((192, 112), F32)], axis=1)
        return carry

    lax.fori_loop(0, 12, spread, 0)

    tok_i = lax.broadcasted_iota(I32, (WIN, WIN), 0) % 12
    tok_k = lax.broadcasted_iota(I32, (WIN, WIN), 1) % 12
    last_band = d == NLAT - 1
    lat_differs = ((tok_i % 6 >= 3) != (tok_k % 6 >= 3)) & last_band
    lev_differs = (tok_i >= 6) != (tok_k >= 6)
    bx[:, :, HEADS * WIN:WIDE] = jnp.zeros((2, WIN, WIDE - HEADS * WIN), F32)
    for lw in range(2):
        differs = (lat_differs | lev_differs) if lw else lat_differs
        for h in range(HEADS):
            at = pl.ds(h * 2 + lw, WIN, stride=16)
            full = jnp.concatenate([bs_s.at[0][at, :], bs_s.at[1][at, :]], axis=1)[:, 0:WIN]
            bx[lw, :, h * WIN:(h + 1) * WIN] = jnp.where(differs, MASKED, full).T

    wq[...] = triple_w[:, 0:192]
    wk[...] = triple_w[:, 192:384]
    wv[...] = triple_w[:, 384:576]

    head_of = lanes(1, C) // 32
    head_f = [jnp.where(head_of == h, 1.0, 0.0) for h in range(HEADS)]
    head_b = [mask.astype(BF16) for mask in head_f]

    blank = jnp.zeros((WIDE - HEADS * WIN, C), BF16)

    def stacked(values):
        return jnp.concatenate([values * mask for mask in head_b] + [blank], axis=0)

    def unstacked(values):
        blocks = [values[h * 32:(h + 1) * 32, h * WIN:(h + 1) * WIN] for h in range(HEADS)]
        return jnp.concatenate(blocks, axis=0).T

    to_window = one_hot(HALF, orders[2:3, 0:QROWS])
    for copy in halo_copies:
        copy.wait()
    rq[:, 0:224, :] = sq[:, 0:224, :]
    for b in range(2):
        x_w[b * HALF:(b + 1) * HALF, :] = dot_nn(to_window, rq[b]).astype(BF16)

    def window_rows(w):
        return pl.ds(pl.multiple_of(w * WIN, WIN), WIN)

    def chunk_rows(i):
        return pl.ds(pl.multiple_of(i * CHUNK, CHUNK), CHUNK)

    def tile_rows(i, t):
        return pl.ds(pl.multiple_of(i * CHUNK + t * TILE, 16), TILE)

    def project(i, carry):
        rows = chunk_rows(i)
        for t in range(CHUNK // TILE):
            part = tile_rows(i, t)
            normed = statistics(x_w[part, :].astype(F32))[0]
            ni_s[part, :] = (normed * attend_gain[...]).astype(BF16)
        normed_in = ni_s[rows, :]
        q_s[rows, :] = dot_nn(normed_in, wq[...]).astype(BF16)
        k_s[rows, :] = dot_nn(normed_in, wk[...]).astype(BF16)
        v_s[rows, :] = dot_nn(normed_in, wv[...]).astype(BF16)
        return carry

    lax.fori_loop(0, NCHUNK, project, 0)

    def attend(w, carry):
        rows = window_rows(w)
        lw = lax.rem(w // 2, 2)
        raw[...] = dot_nt(k_s[rows, :], stacked(q_s[rows, :]))
        for t in range(WIDE // 128):
            cols = slice(t * 128, (t + 1) * 128)
            scores = raw[:, cols] * FACTOR + bx[lw, :, cols]
            exponent = jnp.exp(scores - jnp.max(scores, axis=0, keepdims=True))
            chances = exponent * (1.0 / jnp.sum(exponent, axis=0, keepdims=True))
            p_s[w, :, cols] = chances.astype(BF16)
        att_s[rows, :] = unstacked(dot_tn(v_s[rows, :], p_s[w])).astype(BF16)
        return carry

    lax.fori_loop(0, NWIN, attend, 0)

    lon_all(lambda o: cot_copy(e, o).wait_recv())
    lat_copy = remote(cg.at[pl.ds(0, 2)], ch, lat_ss.at[0], lat_rs.at[0], (e, d_dn))
    lat_copy.start()

    def feed(i, carry):
        rows = chunk_rows(i)
        mid_s[rows, :] = x_w[rows, :].astype(F32) + dot_nn(att_s[rows, :], output_w[...])
        for t in range(CHUNK // TILE):
            part = tile_rows(i, t)
            nm_s[part, :] = (statistics(mid_s[part, :])[0] * feed_gain[...]).astype(BF16)
        slope_s[rows, :] = dot_nn(nm_s[rows, :], expand_w[...])
        for t in range(CHUNK // 16):
            part = pl.ds(pl.multiple_of(i * CHUNK + t * 16, 16), 16)
            for j in range(FF // 256):
                cols = slice(j * 256, (j + 1) * 256)
                act, slope = gelu_parts(slope_s[part, cols])
                act_s[part, cols] = act.astype(BF16)
                slope_s[part, cols] = slope
        vo_s[rows, :] = (mid_s[rows, :] + dot_nt(act_s[rows, :], shrink_t[...])).astype(BF16)
        return carry

    lax.fori_loop(0, NCHUNK, feed, 0)

    lat_copy.wait_recv()
    lon_all(lambda o: w_copy(e, o).wait_recv())
    gain_row = merge_gain[...].reshape(1, 4 * C)
    for r in range(6):
        x = (r + 1) % 2
        cell = (0, 1, 1, 2, 2, 3)[r]
        plane = cg[cell + 1] if cell < 2 else ch[cell - 2]
        weight = wg[:, :, x * 384:(x + 1) * 384].reshape(512, 384)
        scaled = dot_tn(plane.reshape(512, 128), weight) * gain_row[:, x * 384:(x + 1) * 384]
        qry[2 * r] = scaled[:, 0:192].astype(BF16)
        qry[2 * r + 1] = scaled[:, 192:384].astype(BF16)

    st[...] = jnp.zeros_like(st)
    col = lanes(1, 384)
    col_p, col_ry, col_m = col // 192, (col // 16) % 12, col % 16
    stat_lane = lanes(WIN, 128)
    tile_lane = lanes(TILE, 128)

    def merge_sums(w, carry):
        rows = window_rows(w)
        b, lw, lon_win = w // 4, lax.rem(w // 2, 2), lax.rem(w, 2)
        parts = []
        for p in range(2):
            level = lax.rem(lw * 2 + p + 1, 4)
            at = pl.ds(pl.multiple_of((b * 4 + level) * 16, 16), 16)
            parts.append(qry[:, at, :].reshape(192, C))
        pair = col_m - lon_win * 6
        token = (2 * pair + col_ry % 2) * 12 + col_p * 6 + col_ry // 2
        token = jnp.where((pair >= 0) & (pair < 6), token, -1)
        qw[rows, :] = dot_nn(one_hot(WIN, token), jnp.concatenate(parts, axis=0)).astype(BF16)
        for t in range(WIN // TILE):
            part = pl.ds(pl.multiple_of(w * WIN + t * TILE, 16), TILE)
            at = slice(t * TILE, (t + 1) * TILE)
            q = qw[part, :].astype(F32)
            v = vo_s[part, :].astype(F32)
            mean = jnp.mean(v, axis=-1, keepdims=True)
            centred = v - mean
            squares = jnp.sum(centred * centred, axis=-1, keepdims=True)
            q_sum = jnp.sum(q, axis=-1, keepdims=True)
            qv_sum = jnp.sum(q * centred, axis=-1, keepdims=True)
            total = st[at, :]
            for j, value in enumerate((mean, squares, q_sum, qv_sum)):
                total = jnp.where(tile_lane == 32 * j + w, value, total)
            st[at, :] = total
        return carry

    lax.fori_loop(0, NWIN, merge_sums, 0)

    tup[...] = st[pl.ds(5, 24, stride=6), :]
    tdn[...] = st[pl.ds(0, 24, stride=6), :]
    up_copy = remote(tup, sup, st_ss.at[0], st_rs.at[0], (e, d_up))
    dn_copy = remote(tdn, sdn, st_ss.at[1], st_rs.at[1], (e, d_dn))
    up_copy.start()
    dn_copy.start()
    for r, other in ((1, 2), (2, 1), (3, 4), (4, 3)):
        sx[pl.ds(r, 24, stride=6), :] = st[pl.ds(other, 24, stride=6), :]
    up_copy.wait()
    dn_copy.wait()
    sx[pl.ds(0, 24, stride=6), :] = sup[...]
    sx[pl.ds(5, 24, stride=6), :] = sdn[...]

    even = (lax.broadcasted_iota(I32, (WIN, 128), 0) // 12) % 2 == 0

    def pair_of(values):
        return jnp.where(even, pltpu.roll(values, WIN - 12, 0), pltpu.roll(values, 12, 0))

    own, cross = st[...], sx[...]
    group = [own, cross, pair_of(own), pair_of(cross)]
    cell_mean = (group[0] + group[1] + group[2] + group[3]) * 0.25
    variance = jnp.zeros((WIN, 128), F32)
    q_total = jnp.zeros((WIN, 128), F32)
    qv_total = jnp.zeros((WIN, 128), F32)
    for values in group:
        offset = values - cell_mean
        q_sum = pltpu.roll(values, 64, 1)
        variance = variance + pltpu.roll(values, 96, 1) + 192.0 * offset * offset
        q_total = q_total + q_sum
        qv_total = qv_total + pltpu.roll(values, 32, 1) + offset * q_sum
    cell_inverse = lax.rsqrt(jnp.where(stat_lane < 8, variance, 0.0) * (1.0 / 768.0) + EPS)
    cp_s[0] = cell_mean
    cp_s[1] = cell_inverse
    cp_s[2] = q_total * (1.0 / 768.0)
    cp_s[3] = cell_inverse * cell_inverse * qv_total * (1.0 / 768.0)

    def merge_back(w, carry):
        for t in range(WIN // TILE):
            part = pl.ds(pl.multiple_of(w * WIN + t * TILE, 16), TILE)
            at = slice(t * TILE, (t + 1) * TILE)
            mean, inverse, q_mean, projected = [
                jnp.sum(jnp.where(tile_lane == w, cp_s[j, at, :], 0.0), axis=-1, keepdims=True) for j in range(4)
            ]
            v = vo_s[part, :].astype(F32) - mean
            go_s[part, :] = (inverse * (qw[part, :].astype(F32) - q_mean - v * projected)).astype(BF16)
        return carry

    lax.fori_loop(0, NWIN, merge_back, 0)

    def feed_back(i, carry):
        rows = chunk_rows(i)
        go = go_s[rows, :]
        gh = (dot_nn(go, shrink_t[...]) * slope_s[rows, :]).astype(BF16)
        gh_s[rows, :] = gh
        gm_s[rows, :] = dot_nt(gh, expand_w[...])
        for t in range(CHUNK // TILE):
            part = tile_rows(i, t)
            gnm = gm_s[part, :]
            unit, inverse = statistics(mid_s[part, :])
            gm = go_s[part, :].astype(F32) + norm_back(unit, inverse, gnm * feed_gain[...])
            gm_s[part, :] = gm
            gmh_s[part, :] = gm.astype(BF16)
            carry = carry + jnp.sum(gnm * unit, axis=0, keepdims=True)
        ga_s[rows, :] = dot_nt(gmh_s[rows, :], output_w[...]).astype(BF16)
        return carry

    feed_sum = lax.fori_loop(0, NCHUNK, feed_back, jnp.zeros((1, C), F32))

    g_expand = dot_tn(nm_s[...], gh_s[...]).astype(BF16)
    g_shrink = dot_tn(go_s[...], act_s[...]).astype(BF16)
    g_output = dot_tn(att_s[...], gmh_s[...]).astype(BF16)
    for i in range(4):
        for j in range(2):
            g1s[2 * i + j, 0:48] = g_expand[i * 48:(i + 1) * 48, j * 384:(j + 1) * 384]
            g1s[8 + 2 * i + j, 0:48] = g_shrink[i * 48:(i + 1) * 48, j * 384:(j + 1) * 384]
    wide = jnp.concatenate([g_output[0:96], g_output[96:192]], axis=1)
    for i in range(6):
        g1s[i, 48:64] = wide[i * 16:(i + 1) * 16]
    first_row = lax.broadcasted_iota(I32, (16, C), 0) == 0
    g1s[6, 48:64] = jnp.concatenate(
        [jnp.where(first_row, feed_sum, 0.0), jnp.zeros((16, C), F32)], axis=1
    ).astype(BF16)
    for i in range(7, NLON):
        g1s[i, 48:64] = jnp.zeros((16, 384), BF16)
    g1r[e] = g1s[e]

    def g1_copy(o, mine):
        return remote(g1s.at[o], g1r.at[mine], g1_ss.at[o], g1_rs.at[mine], (o, d))

    def g1l_copy(o, mine):
        return remote(g1l.at[mine], g1l.at[mine], g1l_ss.at[o], g1l_rs.at[mine], (e, o))

    def g1f_copy(o, mine):
        return remote(g1f.at[mine], g1f.at[mine], g1f_ss.at[o], g1f_rs.at[mine], (o, d))

    lon_all(lambda o: g1_copy(o, e).start())

    ds_s[...] = jnp.zeros_like(ds_s)

    def attend_back(w, carry):
        rows = window_rows(w)
        lw = lax.rem(w // 2, 2)
        k = k_s[rows, :]
        ga = stacked(ga_s[rows, :])
        raw[...] = dot_nt(v_s[rows, :], ga)
        for t in range(WIDE // 128):
            cols = slice(t * 128, (t + 1) * 128)
            chances = p_s[w, :, cols].astype(F32)
            weighted = raw[:, cols]
            centre = jnp.sum(chances * weighted, axis=0, keepdims=True)
            part = chances * (weighted - centre)
            ds_s[lw, :, cols] = ds_s[lw, :, cols] + part
            dsh[:, cols] = part.astype(BF16)
        half, ds = p_s[w], dsh[...]
        dq_s[rows, :] = (unstacked(dot_tn(k, ds)) * FACTOR).astype(BF16)
        dk_s[rows, :] = (dot_nn(ds, stacked(q_s[rows, :])) * FACTOR).astype(BF16)
        dv_s[rows, :] = dot_nn(half, ga).astype(BF16)
        return carry

    lax.fori_loop(0, 5, attend_back, 0)

    lon_all(lambda o: g1_copy(e, o).wait_recv())
    total = g1r[0].astype(F32)
    for o in range(1, NLON):
        total = total + g1r[o].astype(F32)
    g1l[d] = total.astype(BF16)
    lat_all(lambda o: g1l_copy(o, d).start())

    lax.fori_loop(5, NWIN, attend_back, 0)

    lat_all(lambda o: g1l_copy(d, o).wait_recv())
    total = g1l[0].astype(F32)
    for o in range(1, NLAT):
        total = total + g1l[o].astype(F32)
    g1f[e] = total.astype(BF16)
    lon_all(lambda o: g1f_copy(o, e).start())

    ni = ni_s[...]
    g_triple = jnp.concatenate(
        [dot_tn(ni, dq_s[...]), dot_tn(ni, dk_s[...]), dot_tn(ni, dv_s[...]), jnp.zeros((C, 64), F32)], axis=1
    ).astype(BF16)
    for i in range(3):
        for j in range(5):
            g2s[5 * i + j] = g_triple[i * 64:(i + 1) * 64, j * 128:(j + 1) * 128]

    def project_back(i, carry):
        rows = chunk_rows(i)
        mid_s[rows, :] = (
            dot_nt(dq_s[rows, :], wq[...]) + dot_nt(dk_s[rows, :], wk[...]) + dot_nt(dv_s[rows, :], wv[...])
        )
        for t in range(CHUNK // TILE):
            part = tile_rows(i, t)
            gni = mid_s[part, :]
            unit, inverse = statistics(x_w[part, :].astype(F32))
            gt_s[part, :] = (gm_s[part, :] + norm_back(unit, inverse, gni * attend_gain[...])).astype(BF16)
            carry = carry + jnp.sum(gni * unit, axis=0, keepdims=True)
        return carry

    attend_sum = lax.fori_loop(0, NCHUNK, project_back, jnp.zeros((1, C), F32))
    gain_row_id = lax.broadcasted_iota(I32, (64, 128), 0)
    gain_tail = jnp.concatenate([attend_sum[:, 128:C], jnp.zeros((1, 64), F32)], axis=1)
    g2s[15] = jnp.where(
        gain_row_id == 0, attend_sum[:, 0:128], jnp.where(gain_row_id == 1, gain_tail, 0.0)
    ).astype(BF16)
    g2r[e] = g2s[e]

    def g2_copy(o, mine):
        return remote(g2s.at[o], g2r.at[mine], g2_ss.at[o], g2_rs.at[mine], (o, d))

    def g2l_copy(o, mine):
        return remote(g2l.at[mine], g2l.at[mine], g2l_ss.at[o], g2l_rs.at[mine], (e, o))

    def g2f_copy(o, mine):
        return remote(g2f.at[mine], g2f.at[mine], g2f_ss.at[o], g2f_rs.at[mine], (o, d))

    lon_all(lambda o: g2_copy(o, e).start())

    from_window = one_hot(QROWS, orders[3:4, 0:HALF])
    for b in range(2):
        gq[b] = dot_nn(from_window, gt_s[b * HALF:(b + 1) * HALF, :]).astype(BF16)
    back_copies = halo(gq, hq, back_ss, back_rs, (e_up, d_up))
    for copy in back_copies:
        copy.start()

    for lw in range(2):
        for h in range(HEADS):
            at = pl.ds(h * 2 + lw, WIN, stride=16)
            part = ds_s[lw, :, h * WIN:(h + 1) * WIN].T
            bs_s.at[0][at, :] = part[:, 0:128]
            bs_s.at[1][at, :] = jnp.concatenate([part[:, 128:144], jnp.zeros((WIN, 112), F32)], axis=1)

    def fold(s_i, carry):
        at = pl.ds(pl.multiple_of(s_i * 192, 192), 192)
        rows = jnp.concatenate([bs_s[0, at, :], bs_s[1, at, :]], axis=1)[:, 0:WIN].astype(BF16)
        return carry + dot_nt(rows, spread_matrix(s_i))

    folded = lax.fori_loop(0, 12, fold, jnp.zeros((192, 512), F32))
    pieces_t = []
    for p in range(2):
        for pk in range(2):
            for r in range(6):
                at = (p * 6 + r) * 16
                pieces_t.append(folded[at:at + 16, pk * 256:pk * 256 + 138])
    table = jnp.concatenate(pieces_t + [jnp.zeros((16, 4096 - POS), F32)], axis=1).astype(BF16)
    for o in range(NLON):
        tbs[o] = table[:, o * 256:(o + 1) * 256]
    tbr[e] = tbs[e]

    def tb_copy(o, mine):
        return remote(tbs.at[o], tbr.at[mine], tb_ss.at[o], tb_rs.at[mine], (o, d))

    def tbf_copy(o, mine):
        return remote(tbf.at[mine], tbf.at[mine], tbf_ss.at[o], tbf_rs.at[mine], (o, d))

    lon_all(lambda o: tb_copy(o, e).start())

    lon_all(lambda o: g2_copy(e, o).wait_recv())
    total = g2r[0].astype(F32)
    for o in range(1, NLON):
        total = total + g2r[o].astype(F32)
    g2l[d] = total.astype(BF16)
    lat_all(lambda o: g2l_copy(o, d).start())

    to_natural = one_hot(HALF, orders[1:2, 0:QROWS])
    for copy in back_copies:
        copy.wait()
    hq[:, 0:224, :] = gq[:, 0:224, :]

    lon_all(lambda o: tb_copy(e, o).wait_recv())
    total = tbr[0].astype(F32)
    for o in range(1, NLON):
        total = total + tbr[o].astype(F32)
    tbf[e] = total.astype(BF16)
    lon_all(lambda o: tbf_copy(o, e).start())

    lat_all(lambda o: g2l_copy(d, o).wait_recv())
    total = g2l[0].astype(F32)
    for o in range(1, NLAT):
        total = total + g2l[o].astype(F32)
    g2f[e] = total.astype(BF16)
    lon_all(lambda o: g2f_copy(o, e).start())

    for b in range(2):
        out_fields[b * HALF:(b + 1) * HALF, :] = dot_nn(to_natural, hq[b]).astype(BF16)
    lon_all(lambda o: g1f_copy(e, o).wait_recv())
    out_g1[...] = g1f[...]
    lon_all(lambda o: tbf_copy(e, o).wait_recv())
    out_table[...] = tbf[...]
    lon_all(lambda o: g2f_copy(e, o).wait_recv())
    out_g2[...] = g2f[...]

    def sent(o):
        cot_copy(o, e).wait_send()
        w_copy(o, e).wait_send()
        g1_copy(o, e).wait_send()
        g1f_copy(o, e).wait_send()
        g2_copy(o, e).wait_send()
        g2f_copy(o, e).wait_send()
        tb_copy(o, e).wait_send()
        tbf_copy(o, e).wait_send()

    def sent_lat(o):
        g1l_copy(o, d).wait_send()
        g2l_copy(o, d).wait_send()

    lon_all(sent)
    lat_all(sent_lat)
    lat_copy.wait_send()


def results_kernel(
    fields, g1, g2, folded,
    out_fields, out_triple, out_output, out_expand, out_shrink, out_attend, out_feed, out_table,
):
    out_fields[...] = fields[...]
    for i in range(4):
        for j in range(2):
            rows, cols = slice(i * 48, (i + 1) * 48), slice(j * 384, (j + 1) * 384)
            out_expand[rows, cols] = g1[2 * i + j, 0:48].astype(F32)
            out_shrink[rows, cols] = g1[8 + 2 * i + j, 0:48].astype(F32)
    for i in range(6):
        wide = g1[i, 48:64].astype(F32)
        out_output[i * 16:(i + 1) * 16, :] = wide[:, 0:C]
        out_output[96 + i * 16:96 + (i + 1) * 16, :] = wide[:, C:2 * C]
    out_feed[...] = g1[6, 48:64].astype(F32)[0:1, 0:C]
    for i in range(3):
        for j in range(5):
            size = 128 if j < 4 else 64
            out_triple[i * 64:(i + 1) * 64, j * 128:j * 128 + size] = g2[5 * i + j].astype(F32)[:, 0:size]
    gain = g2[15].astype(F32)
    out_attend[:, 0:128] = gain[0:1, :]
    out_attend[:, 128:C] = gain[1:2, 0:C - 128]
    table = jnp.concatenate([folded[o] for o in range(NLON)], axis=1).astype(F32)
    for h in range(HEADS):
        out_table[h] = table[2 * h:2 * h + 2, 0:POS]


def scratch():
    def vmem(*shape, kind=BF16):
        return pltpu.VMEM(shape, kind)

    token = vmem(TOK, C)
    token_f = vmem(TOK, C, kind=F32)
    weight = vmem(C, C)
    quad = vmem(2, QROWS, C)
    stat = vmem(WIN, 128, kind=F32)
    small = vmem(24, 128, kind=F32)
    buffers = [
        quad, quad, quad, quad, token, token, token, token, token, weight, weight, weight,
        vmem(NWIN, WIN, WIDE), token, token_f, token, vmem(TOK, FF), vmem(TOK, FF, kind=F32), token,
        vmem(16, POS, kind=F32), vmem(3, 192, 512), vmem(2, 2304, 128, kind=F32),
        vmem(2, WIN, WIDE, kind=F32), vmem(2, WIN, WIDE, kind=F32),
        vmem(16, 3, 32, 128), vmem(3, 16, 32, 128), vmem(2, 16, 32, 128), vmem(16, 32, 768),
        vmem(12, 128, C), token, stat, stat, small, small, small, small, vmem(4, WIN, 128, kind=F32),
        token, vmem(TOK, FF), token_f, token, token, token, token, token, token,
        vmem(WIN, WIDE, kind=F32), vmem(WIN, WIDE), vmem(16, 64, 384), vmem(16, 64, 384), vmem(8, 64, 384), vmem(16, 64, 384),
        vmem(16, 64, 128), vmem(16, 64, 128), vmem(8, 64, 128), vmem(16, 64, 128),
        vmem(16, 16, 256), vmem(16, 16, 256), vmem(16, 16, 256),
    ]
    counts = [3, 3, 16, 16, 16, 16, 1, 1, 2, 2]
    counts += [16, 16, 8, 8, 16, 16, 16, 16, 8, 8, 16, 16, 16, 16, 16, 16, 3, 3]
    return buffers + [pltpu.SemaphoreType.DMA((n,)) for n in counts]


def per_device(
    fields, merge_cotangent, attend_gain, triple_weight, bias_table, output_weight, feed_gain,
    expand_weight, shrink_weight, merge_gain, merge_weight,
):
    cot = jnp.transpose(merge_cotangent, (1, 2, 3, 4, 0)).reshape(576, 192)
    bias = jnp.transpose(bias_table[0], (1, 0, 2))
    def shaped(shapes):
        return [jax.ShapeDtypeStruct(shape, kind) for shape, kind in shapes]

    vmem_spec = pl.BlockSpec(memory_space=pltpu.VMEM)
    parts = pl.pallas_call(
        kernel,
        out_shape=shaped(
            [((TOK, C), BF16), ((16, 64, 384), BF16), ((16, 64, 128), BF16), ((16, 16, 256), BF16)]
        ),
        in_specs=[vmem_spec] * 12,
        out_specs=[vmem_spec] * 4,
        scratch_shapes=scratch(),
        compiler_params=pltpu.CompilerParams(
            collective_id=0, has_side_effects=True, vmem_limit_bytes=60 * 1024 * 1024
        ),
    )(
        fields.reshape(TOK, C), cot, attend_gain.reshape(1, C), triple_weight, bias, output_weight,
        feed_gain.reshape(1, C), expand_weight, shrink_weight.T, merge_gain,
        merge_weight.T, jnp.asarray(order_indices()),
    )
    g_fields, g_triple, g_output, g_expand, g_shrink, g_attend, g_feed, g_table = pl.pallas_call(
        results_kernel,
        out_shape=shaped(
            [
                ((TOK, C), BF16), ((C, 3 * C), F32), ((C, C), F32), ((C, FF), F32), ((C, FF), F32),
                ((1, C), F32), ((1, C), F32), ((HEADS, 2, POS), F32),
            ]
        ),
        in_specs=[vmem_spec] * 4,
        out_specs=[vmem_spec] * 8,
        compiler_params=pltpu.CompilerParams(vmem_limit_bytes=60 * 1024 * 1024),
    )(*parts)
    return (
        g_fields.reshape(fields.shape), g_triple, g_output, g_expand, g_shrink.T,
        g_attend.reshape(C), g_feed.reshape(C), jnp.transpose(g_table, (1, 0, 2))[None],
    )


def solution(mesh):
    placed = (
        P(None, None, "lat", "lon", None),
        P(None, None, None, "lat", "lon"),
        P(),
        P(),
        P("lat", None, None, None),
        P(),
        P(),
        P(),
        P(),
        P(),
        P(None, "lon"),
    )
    return jax.shard_map(
        per_device,
        mesh=mesh,
        in_specs=placed,
        out_specs=(
            P(None, None, "lat", "lon", None),
            P(),
            P(),
            P(),
            P(),
            P(),
            P(),
            P("lat", None, None, None),
        ),
        check_vma=False,
    )
```

```python
import functools
import math

import jax
import jax.numpy as jnp
import numpy as np
from jax import lax
from jax.experimental import pallas as pl
from jax.experimental.pallas import tpu as pltpu
from jax.sharding import PartitionSpec as P

F32 = jnp.float32
BF16 = jnp.bfloat16
I32 = jnp.int32
MESH = pl.DeviceIdType.MESH

EPS = 1e-05
MASKED = -1000000000.0
NLON = 16
NLAT = 8
NCHIP = 8
C = 192
HEADS = 6
FF = 768
WIN = 144
NWIN = 8
TOK = WIN * NWIN
HALF = TOK // 2
QROWS = 608
POS = 3312
CHUNK = 288
NCHUNK = TOK // CHUNK
TILE = 48
WIDE = 896
FACTOR = 32 ** -0.5


def order_indices():
    natural_to_quad = np.full(640, -1, np.int32)
    quad_to_natural = np.full(640, -1, np.int32)
    quad_to_window = np.full(640, -1, np.int32)
    window_to_quad = np.full(640, -1, np.int32)
    for level in range(4):
        for row in range(6):
            for col in range(24):
                source = (level * 6 + row) * 24 + col
                if col >= 6:
                    place = (0 if row >= 3 else 224) + level * 54 + (row % 3) * 18 + col - 6
                else:
                    place = (448 if row >= 3 else 528) + level * 18 + (row % 3) * 6 + col
                natural_to_quad[source] = place
                quad_to_natural[place] = source
    index = 0
    for lev_win in range(2):
        for lon_win in range(2):
            for s in range(12):
                for p in range(2):
                    for r in range(6):
                        level = (lev_win * 2 + p + 1) % 4
                        col = lon_win * 12 + s
                        if col < 18:
                            place = (0 if r < 3 else 224) + level * 54 + (r % 3) * 18 + col
                        else:
                            place = (448 if r < 3 else 528) + level * 18 + (r % 3) * 6 + col - 18
                        window_to_quad[index] = place
                        quad_to_window[place] = index
                        index += 1
    rows = [natural_to_quad, quad_to_natural, quad_to_window, window_to_quad]
    return np.stack(rows + rows)


def dot_nn(a, b):
    return lax.dot_general(a, b, (((1,), (0,)), ((), ())), preferred_element_type=F32)


def dot_nt(a, b):
    return lax.dot_general(a, b, (((1,), (1,)), ((), ())), preferred_element_type=F32)


def dot_tn(a, b):
    return lax.dot_general(a, b, (((0,), (0,)), ((), ())), preferred_element_type=F32)


def one_hot(rows, targets):
    ids = lax.broadcasted_iota(I32, (rows, targets.shape[1]), 0)
    return jnp.where(ids == targets, 1.0, 0.0).astype(BF16)


def statistics(values):
    centred = values - jnp.mean(values, axis=-1, keepdims=True)
    inverse = lax.rsqrt(jnp.mean(centred * centred, axis=-1, keepdims=True) + EPS)
    return centred * inverse, inverse


def norm_back(normed, inverse, scaled):
    centre = jnp.mean(scaled, axis=-1, keepdims=True)
    projected = jnp.mean(scaled * normed, axis=-1, keepdims=True)
    return inverse * (scaled - centre - normed * projected)


def gelu_parts(values):
    cumulative = 0.5 * (1.0 + lax.erf(values * (1.0 / math.sqrt(2.0))))
    density = jnp.exp(-0.5 * values * values) * (1.0 / math.sqrt(2.0 * math.pi))
    return values * cumulative, cumulative + values * density


def lanes(rows, cols):
    return lax.broadcasted_iota(I32, (rows, cols), 1)


def bias_targets():
    k = lanes(1, WIN)
    s, rest = k // 12, k % 12
    return (rest // 6) * 256 + (rest % 6) * 23 + 11 - s


def spread_matrix(s_i):
    return one_hot(512, bias_targets() + s_i)


def kernel(
    fields, cot, attend_gain, triple_w, bias, output_w, feed_gain, expand_w, shrink_t, merge_gain,
    merge_wt, orders,
    out_fields, out_g1, out_g2,
    sq, rq, gq, hq, x_w, ni_s, q_s, k_s, v_s, wq, wk, wv, p_s, att_s, mid_s, nm_s, act_s, slope_s, vo_s,
    b16, bl_s, bs_s, bx, ds_s,
    cs, cb, cf, ch, wa, wb, qry, qw, st, sx, sup, sdn, tup, tdn, cp_s, go_s, gh_s, gm_s, ga_s, gmh_s,
    dq_s, dk_s, dv_s, gt_s, raw, dsh, g1s, g1p, g1h, g1r, g1l, g1f, g1o, g2s, g2p, g2h, g2r, g2l, g2f, g2o,
    halo_ss, halo_rs, back_ss, back_rs, st_ss, st_rs, sends, recvs,
):
    e = lax.axis_index("lon")
    d = lax.axis_index("lat")
    e_up, e_dn = lax.rem(e + 1, NLON), lax.rem(e + NLON - 1, NLON)
    d_up, d_dn = lax.rem(d + 1, NLAT), lax.rem(d + NLAT - 1, NLAT)

    def remote(src, dst, ssem, rsem, device):
        return pltpu.make_async_remote_copy(
            src_ref=src, dst_ref=dst, send_sem=ssem, recv_sem=rsem, device_id=device,
            device_id_type=MESH,
        )

    core, chip = lax.rem(e, 2), e // 2
    partner = e + 1 - 2 * core

    def chips_all(action):
        def body(step, carry):
            action(lax.rem(chip + step, NCHIP))
            return carry

        lax.fori_loop(1, NCHIP, body, 0)

    def lat_all(action):
        def body(step, carry):
            action(lax.rem(d + step, NLAT))
            return carry

        lax.fori_loop(1, NLAT, body, 0)

    def to_chip(src, dst, phase, o):
        return remote(src, dst, sends.at[phase], recvs.at[phase], (2 * o + core, d))

    def to_band(src, dst, phase, o):
        return remote(src, dst, sends.at[phase], recvs.at[phase], (e, o))

    def to_core(src, dst, phase):
        return remote(src, dst, sends.at[phase], recvs.at[phase], (partner, d))

    def arrived(region, phase):
        remote(region, region, sends.at[phase], recvs.at[phase], (partner, d)).wait_recv()

    def left(region, phase):
        remote(region, region, sends.at[phase], recvs.at[phase], (partner, d)).wait_send()

    barrier = pltpu.get_barrier_semaphore()

    def greet(device):
        pl.semaphore_signal(barrier, inc=1, device_id=device, device_id_type=MESH)

    chips_all(lambda o: greet((2 * o + core, d)))
    lat_all(lambda o: greet((e, o)))
    for device in ((e_up, d), (e_dn, d), (e_up, d_up), (e_dn, d_dn)):
        greet(device)

    to_quad = one_hot(QROWS, orders[0:1, 0:HALF])
    for b in range(2):
        sq[b] = dot_nn(to_quad, fields[b * HALF:(b + 1) * HALF, :]).astype(BF16)
    pl.semaphore_wait(barrier, NCHIP - 1 + NLAT - 1 + 4)

    pieces = ((224, 224), (448, 80), (528, 80))

    def halo(src, dst, ssem, rsem, step):
        devices = ((e, step[1]), (step[0], d), (step[0], step[1]))
        return [
            remote(src.at[:, pl.ds(at, size), :], dst.at[:, pl.ds(at, size), :], ssem.at[i], rsem.at[i], dev)
            for i, ((at, size), dev) in enumerate(zip(pieces, devices))
        ]

    halo_copies = halo(sq, rq, halo_ss, halo_rs, (e_dn, d_dn))
    for copy in halo_copies:
        copy.start()

    lane = lanes(1, 256)
    cell_lane = jnp.where(lane % 16 < 12, (12 * (lane // 16) + 3 + lane % 16) % 192, -1)
    cells = dot_nn(cot[...], one_hot(192, cell_lane))
    block_of = lanes(72, 128) // 16
    for o in range(NLON):
        tile, inner = (o // 8) * 128, o % 8
        piece = jnp.zeros((72, 128), F32)
        for bl in range(8):
            part = cells[bl * 72:(bl + 1) * 72, tile:tile + 128]
            shift = (16 * (bl - inner)) % 128
            if shift:
                part = pltpu.roll(part, shift, 1)
            piece = jnp.where(block_of == bl, part, piece)
        for a in range(3):
            padded = jnp.concatenate([piece[a * 24:(a + 1) * 24], jnp.zeros((8, 128), F32)], axis=0)
            cs[o // 2, o % 2, a] = padded.astype(BF16)
    wa[chip] = jnp.concatenate(
        [merge_wt[...].astype(F32), jnp.zeros((8, 768), F32)], axis=0
    ).astype(BF16)
    cb[:, chip] = cs[chip]
    chips_all(lambda o: to_chip(cs.at[o], cb.at[:, chip], 0, o).start())
    chips_all(lambda o: to_chip(wa.at[chip], wa.at[chip], 1, o).start())

    for h in range(HEADS):
        b16[2 * h:2 * h + 2, :] = bias[h]
    b16[12:16, :] = jnp.zeros((4, POS), F32)
    zero_tail = jnp.zeros((16, 256 - 138), F32)
    for p in range(2):
        for r in range(6):
            parts = []
            for pk in range(2):
                at = (p * 2 + pk) * 828 + r * 138
                parts += [b16[:, at:at + 138], zero_tail]
            row = jnp.concatenate(parts, axis=1)
            high = row.astype(BF16)
            rest = row - high.astype(F32)
            middle = rest.astype(BF16)
            low = (rest - middle.astype(F32)).astype(BF16)
            at = pl.ds((p * 6 + r) * 16, 16)
            bl_s[0, at, :] = high
            bl_s[1, at, :] = middle
            bl_s[2, at, :] = low

    def spread(s_i, carry):
        matrix = spread_matrix(s_i)
        rows = dot_nn(bl_s[0], matrix) + dot_nn(bl_s[1], matrix) + dot_nn(bl_s[2], matrix)
        at = pl.ds(pl.multiple_of(s_i * 192, 192), 192)
        bs_s[0, at, :] = rows[:, 0:128]
        bs_s[1, at, :] = jnp.concatenate([rows[:, 128:144], jnp.zeros((192, 112), F32)], axis=1)
        return carry

    lax.fori_loop(0, 12, spread, 0)

    tok_i = lax.broadcasted_iota(I32, (WIN, WIN), 0) % 12
    tok_k = lax.broadcasted_iota(I32, (WIN, WIN), 1) % 12
    last_band = d == NLAT - 1
    lat_differs = ((tok_i % 6 >= 3) != (tok_k % 6 >= 3)) & last_band
    lev_differs = (tok_i >= 6) != (tok_k >= 6)
    bx[:, :, HEADS * WIN:WIDE] = jnp.zeros((2, WIN, WIDE - HEADS * WIN), F32)
    for lw in range(2):
        differs = (lat_differs | lev_differs) if lw else lat_differs
        for h in range(HEADS):
            at = pl.ds(h * 2 + lw, WIN, stride=16)
            full = jnp.concatenate([bs_s.at[0][at, :], bs_s.at[1][at, :]], axis=1)[:, 0:WIN]
            bx[lw, :, h * WIN:(h + 1) * WIN] = jnp.where(differs, MASKED, full).T

    wq[...] = triple_w[:, 0:192]
    wk[...] = triple_w[:, 192:384]
    wv[...] = triple_w[:, 384:576]

    head_of = lanes(1, C) // 32
    head_f = [jnp.where(head_of == h, 1.0, 0.0) for h in range(HEADS)]
    head_b = [mask.astype(BF16) for mask in head_f]

    blank = jnp.zeros((WIDE - HEADS * WIN, C), BF16)

    def stacked(values):
        return jnp.concatenate([values * mask for mask in head_b] + [blank], axis=0)

    def unstacked(values):
        blocks = [values[h * 32:(h + 1) * 32, h * WIN:(h + 1) * WIN] for h in range(HEADS)]
        return jnp.concatenate(blocks, axis=0).T

    to_window = one_hot(HALF, orders[2:3, 0:QROWS])
    for copy in halo_copies:
        copy.wait()
    rq[:, 0:224, :] = sq[:, 0:224, :]
    for b in range(2):
        x_w[b * HALF:(b + 1) * HALF, :] = dot_nn(to_window, rq[b]).astype(BF16)

    def window_rows(w):
        return pl.ds(pl.multiple_of(w * WIN, WIN), WIN)

    def chunk_rows(i):
        return pl.ds(pl.multiple_of(i * CHUNK, CHUNK), CHUNK)

    def tile_rows(i, t):
        return pl.ds(pl.multiple_of(i * CHUNK + t * TILE, 16), TILE)

    def project(i, carry):
        rows = chunk_rows(i)
        for t in range(CHUNK // TILE):
            part = tile_rows(i, t)
            normed = statistics(x_w[part, :].astype(F32))[0]
            ni_s[part, :] = (normed * attend_gain[...]).astype(BF16)
        normed_in = ni_s[rows, :]
        q_s[rows, :] = dot_nn(normed_in, wq[...]).astype(BF16)
        k_s[rows, :] = dot_nn(normed_in, wk[...]).astype(BF16)
        v_s[rows, :] = dot_nn(normed_in, wv[...]).astype(BF16)
        return carry

    lax.fori_loop(0, NCHUNK, project, 0)

    arrived(cb.at[:, pl.ds(0, NCHIP - 1)], 0)
    to_core(cb.at[1 - core], cf, 2).start()
    arrived(wa.at[pl.ds(0, NCHIP - 1)], 1)
    to_core(wa, wb, 3).start()

    def attend(w, carry):
        rows = window_rows(w)
        lw = lax.rem(w // 2, 2)
        raw[...] = dot_nt(k_s[rows, :], stacked(q_s[rows, :]))
        for t in range(WIDE // 128):
            cols = slice(t * 128, (t + 1) * 128)
            scores = raw[:, cols] * FACTOR + bx[lw, :, cols]
            exponent = jnp.exp(scores - jnp.max(scores, axis=0, keepdims=True))
            chances = exponent * (1.0 / jnp.sum(exponent, axis=0, keepdims=True))
            p_s[w, :, cols] = chances.astype(BF16)
        att_s[rows, :] = unstacked(dot_tn(v_s[rows, :], p_s[w])).astype(BF16)
        return carry

    lax.fori_loop(0, NWIN, attend, 0)

    arrived(cf, 2)
    first_rows = pl.ds(0, 2)
    to_band(cb.at[core, :, first_rows], ch.at[0], 4, d_dn).start()
    to_band(cf.at[:, first_rows], ch.at[1], 4, d_dn).start()

    def feed(i, carry):
        rows = chunk_rows(i)
        mid_s[rows, :] = x_w[rows, :].astype(F32) + dot_nn(att_s[rows, :], output_w[...])
        for t in range(CHUNK // TILE):
            part = tile_rows(i, t)
            nm_s[part, :] = (statistics(mid_s[part, :])[0] * feed_gain[...]).astype(BF16)
        slope_s[rows, :] = dot_nn(nm_s[rows, :], expand_w[...])
        for t in range(CHUNK // 16):
            part = pl.ds(pl.multiple_of(i * CHUNK + t * 16, 16), 16)
            for j in range(FF // 256):
                cols = slice(j * 256, (j + 1) * 256)
                act, slope = gelu_parts(slope_s[part, cols])
                act_s[part, cols] = act.astype(BF16)
                slope_s[part, cols] = slope
        vo_s[rows, :] = (mid_s[rows, :] + dot_nt(act_s[rows, :], shrink_t[...])).astype(BF16)
        return carry

    lax.fori_loop(0, NCHUNK, feed, 0)

    arrived(ch, 4)
    arrived(wb, 3)
    gain_row = merge_gain[...].reshape(1, 4 * C)
    for r in range(6):
        x = (r + 1) % 2
        cell = (0, 1, 1, 2, 2, 3)[r]
        cols = slice(x * 384, (x + 1) * 384)
        if cell < 2:
            planes = cb[core, :, cell + 1], cf[:, cell + 1]
        else:
            planes = ch[0, :, cell - 2], ch[1, :, cell - 2]
        summed = dot_tn(planes[0].reshape(256, 128), wa[:, :, cols].reshape(256, 384))
        summed = summed + dot_tn(planes[1].reshape(256, 128), wb[:, :, cols].reshape(256, 384))
        scaled = summed * gain_row[:, x * 384:(x + 1) * 384]
        qry[2 * r] = scaled[:, 0:192].astype(BF16)
        qry[2 * r + 1] = scaled[:, 192:384].astype(BF16)

    st[...] = jnp.zeros_like(st)
    col = lanes(1, 384)
    col_p, col_ry, col_m = col // 192, (col // 16) % 12, col % 16
    stat_lane = lanes(WIN, 128)
    tile_lane = lanes(TILE, 128)

    def merge_sums(w, carry):
        rows = window_rows(w)
        b, lw, lon_win = w // 4, lax.rem(w // 2, 2), lax.rem(w, 2)
        parts = []
        for p in range(2):
            level = lax.rem(lw * 2 + p + 1, 4)
            at = pl.ds(pl.multiple_of((b * 4 + level) * 16, 16), 16)
            parts.append(qry[:, at, :].reshape(192, C))
        pair = col_m - lon_win * 6
        token = (2 * pair + col_ry % 2) * 12 + col_p * 6 + col_ry // 2
        token = jnp.where((pair >= 0) & (pair < 6), token, -1)
        qw[rows, :] = dot_nn(one_hot(WIN, token), jnp.concatenate(parts, axis=0)).astype(BF16)
        for t in range(WIN // TILE):
            part = pl.ds(pl.multiple_of(w * WIN + t * TILE, 16), TILE)
            at = slice(t * TILE, (t + 1) * TILE)
            q = qw[part, :].astype(F32)
            v = vo_s[part, :].astype(F32)
            mean = jnp.mean(v, axis=-1, keepdims=True)
            centred = v - mean
            squares = jnp.sum(centred * centred, axis=-1, keepdims=True)
            q_sum = jnp.sum(q, axis=-1, keepdims=True)
            qv_sum = jnp.sum(q * centred, axis=-1, keepdims=True)
            total = st[at, :]
            for j, value in enumerate((mean, squares, q_sum, qv_sum)):
                total = jnp.where(tile_lane == 32 * j + w, value, total)
            st[at, :] = total
        return carry

    lax.fori_loop(0, NWIN, merge_sums, 0)

    tup[...] = st[pl.ds(5, 24, stride=6), :]
    tdn[...] = st[pl.ds(0, 24, stride=6), :]
    up_copy = remote(tup, sup, st_ss.at[0], st_rs.at[0], (e, d_up))
    dn_copy = remote(tdn, sdn, st_ss.at[1], st_rs.at[1], (e, d_dn))
    up_copy.start()
    dn_copy.start()
    for r, other in ((1, 2), (2, 1), (3, 4), (4, 3)):
        sx[pl.ds(r, 24, stride=6), :] = st[pl.ds(other, 24, stride=6), :]
    up_copy.wait()
    dn_copy.wait()
    sx[pl.ds(0, 24, stride=6), :] = sup[...]
    sx[pl.ds(5, 24, stride=6), :] = sdn[...]

    even = (lax.broadcasted_iota(I32, (WIN, 128), 0) // 12) % 2 == 0

    def pair_of(values):
        return jnp.where(even, pltpu.roll(values, WIN - 12, 0), pltpu.roll(values, 12, 0))

    own, cross = st[...], sx[...]
    group = [own, cross, pair_of(own), pair_of(cross)]
    cell_mean = (group[0] + group[1] + group[2] + group[3]) * 0.25
    variance = jnp.zeros((WIN, 128), F32)
    q_total = jnp.zeros((WIN, 128), F32)
    qv_total = jnp.zeros((WIN, 128), F32)
    for values in group:
        offset = values - cell_mean
        q_sum = pltpu.roll(values, 64, 1)
        variance = variance + pltpu.roll(values, 96, 1) + 192.0 * offset * offset
        q_total = q_total + q_sum
        qv_total = qv_total + pltpu.roll(values, 32, 1) + offset * q_sum
    cell_inverse = lax.rsqrt(jnp.where(stat_lane < 8, variance, 0.0) * (1.0 / 768.0) + EPS)
    cp_s[0] = cell_mean
    cp_s[1] = cell_inverse
    cp_s[2] = q_total * (1.0 / 768.0)
    cp_s[3] = cell_inverse * cell_inverse * qv_total * (1.0 / 768.0)

    def merge_back(w, carry):
        for t in range(WIN // TILE):
            part = pl.ds(pl.multiple_of(w * WIN + t * TILE, 16), TILE)
            at = slice(t * TILE, (t + 1) * TILE)
            mean, inverse, q_mean, projected = [
                jnp.sum(jnp.where(tile_lane == w, cp_s[j, at, :], 0.0), axis=-1, keepdims=True) for j in range(4)
            ]
            v = vo_s[part, :].astype(F32) - mean
            go_s[part, :] = (inverse * (qw[part, :].astype(F32) - q_mean - v * projected)).astype(BF16)
        return carry

    lax.fori_loop(0, NWIN, merge_back, 0)

    def feed_back(i, carry):
        rows = chunk_rows(i)
        go = go_s[rows, :]
        gh = (dot_nn(go, shrink_t[...]) * slope_s[rows, :]).astype(BF16)
        gh_s[rows, :] = gh
        gm_s[rows, :] = dot_nt(gh, expand_w[...])
        for t in range(CHUNK // TILE):
            part = tile_rows(i, t)
            gnm = gm_s[part, :]
            unit, inverse = statistics(mid_s[part, :])
            gm = go_s[part, :].astype(F32) + norm_back(unit, inverse, gnm * feed_gain[...])
            gm_s[part, :] = gm
            gmh_s[part, :] = gm.astype(BF16)
        ga_s[rows, :] = dot_nt(gmh_s[rows, :], output_w[...]).astype(BF16)
        return carry

    lax.fori_loop(0, NCHUNK, feed_back, 0)

    g_expand = dot_tn(nm_s[...], gh_s[...]).astype(BF16)
    g_shrink = dot_tn(go_s[...], act_s[...]).astype(BF16)
    g_output = dot_tn(att_s[...], gmh_s[...]).astype(BF16)
    for i in range(4):
        for j in range(2):
            g1s[0, 2 * i + j, 0:48] = g_expand[i * 48:(i + 1) * 48, j * 384:(j + 1) * 384]
            g1s[1, 2 * i + j, 0:48] = g_shrink[i * 48:(i + 1) * 48, j * 384:(j + 1) * 384]
    wide = jnp.concatenate([g_output[0:96], g_output[96:192]], axis=1)
    for i in range(NCHIP):
        for j in range(2):
            at = (i * 2 + j) * 16
            g1s[j, i, 48:64] = wide[at:at + 16] if at < 96 else jnp.zeros((16, 384), BF16)

    def sum_of(ref, count, rows):
        total = ref[0, rows].astype(F32)
        for o in range(1, count):
            total = total + ref[o, rows].astype(F32)
        return total.astype(BF16)

    def add_pair(mine, other, out):
        for o in range(NCHIP):
            out[o] = (mine[core, o].astype(F32) + other[o].astype(F32)).astype(BF16)

    others = pl.ds(0, NCHIP - 1)
    to_core(g1s.at[1 - core], g1p, 5).start()

    ds_s[...] = jnp.zeros_like(ds_s)

    def attend_back(w, carry):
        rows = window_rows(w)
        lw = lax.rem(w // 2, 2)
        k = k_s[rows, :]
        ga = stacked(ga_s[rows, :])
        raw[...] = dot_nt(v_s[rows, :], ga)
        for t in range(WIDE // 128):
            cols = slice(t * 128, (t + 1) * 128)
            chances = p_s[w, :, cols].astype(F32)
            weighted = raw[:, cols]
            centre = jnp.sum(chances * weighted, axis=0, keepdims=True)
            part = chances * (weighted - centre)
            ds_s[lw, :, cols] = ds_s[lw, :, cols] + part
            dsh[:, cols] = part.astype(BF16)
        half, ds = p_s[w], dsh[...]
        dq_s[rows, :] = (unstacked(dot_tn(k, ds)) * FACTOR).astype(BF16)
        dk_s[rows, :] = (dot_nn(ds, stacked(q_s[rows, :])) * FACTOR).astype(BF16)
        dv_s[rows, :] = dot_nn(half, ga).astype(BF16)
        return carry

    all_rows = slice(0, 64)
    lax.fori_loop(0, 1, attend_back, 0)
    arrived(g1p, 5)
    add_pair(g1s, g1p, g1h)
    g1r[chip] = g1h[chip]
    chips_all(lambda o: to_chip(g1h.at[o], g1r.at[chip], 6, o).start())
    lax.fori_loop(1, 4, attend_back, 0)
    arrived(g1r.at[others], 6)
    g1l[d] = sum_of(g1r, NCHIP, all_rows)
    lat_all(lambda o: to_band(g1l.at[d], g1l.at[d], 7, o).start())
    lax.fori_loop(4, 6, attend_back, 0)
    arrived(g1l.at[others], 7)
    g1f[chip] = sum_of(g1l, NLAT, all_rows)
    chips_all(lambda o: to_chip(g1f.at[chip], g1f.at[chip], 8, o).start())
    lax.fori_loop(6, NWIN, attend_back, 0)

    ni = ni_s[...]
    g_triple = jnp.concatenate(
        [dot_tn(ni, dq_s[...]), dot_tn(ni, dk_s[...]), dot_tn(ni, dv_s[...]), jnp.zeros((C, 64), F32)], axis=1
    ).astype(BF16)
    for i in range(3):
        for j in range(5):
            at = 5 * i + j
            g2s[at // 8, at % 8, 0:64] = g_triple[i * 64:(i + 1) * 64, j * 128:(j + 1) * 128]
    g2s[1, 7, 0:64] = jnp.zeros((64, 128), BF16)
    for lw in range(2):
        for h in range(HEADS):
            at = pl.ds(h * 2 + lw, WIN, stride=16)
            part = ds_s[lw, :, h * WIN:(h + 1) * WIN].T
            bs_s.at[0][at, :] = part[:, 0:128]
            bs_s.at[1][at, :] = jnp.concatenate([part[:, 128:144], jnp.zeros((WIN, 112), F32)], axis=1)

    def fold(s_i, carry):
        at = pl.ds(pl.multiple_of(s_i * 192, 192), 192)
        rows = jnp.concatenate([bs_s[0, at, :], bs_s[1, at, :]], axis=1)[:, 0:WIN].astype(BF16)
        return carry + dot_nt(rows, spread_matrix(s_i))

    folded = lax.fori_loop(0, 12, fold, jnp.zeros((192, 512), F32))
    pieces_t = []
    for p in range(2):
        for pk in range(2):
            for r in range(6):
                at = (p * 6 + r) * 16
                pieces_t.append(folded[at:at + 16, pk * 256:pk * 256 + 138])
    table = jnp.concatenate(pieces_t + [jnp.zeros((16, 4096 - POS), F32)], axis=1).astype(BF16)
    for o in range(32):
        g2s[o // 16, (o // 2) % 8, 64 + 16 * (o % 2):80 + 16 * (o % 2)] = table[:, o * 128:(o + 1) * 128]
    to_core(g2s.at[1 - core], g2p, 9).start()

    def project_back(i, carry):
        rows = chunk_rows(i)
        mid_s[rows, :] = (
            dot_nt(dq_s[rows, :], wq[...]) + dot_nt(dk_s[rows, :], wk[...]) + dot_nt(dv_s[rows, :], wv[...])
        )
        for t in range(CHUNK // TILE):
            part = tile_rows(i, t)
            unit, inverse = statistics(x_w[part, :].astype(F32))
            back = norm_back(unit, inverse, mid_s[part, :] * attend_gain[...])
            gt_s[part, :] = (gm_s[part, :] + back).astype(BF16)
        return carry

    lax.fori_loop(0, 1, project_back, 0)
    arrived(g2p, 9)
    add_pair(g2s, g2p, g2h)
    g2r[chip] = g2h[chip]
    chips_all(lambda o: to_chip(g2h.at[o], g2r.at[chip], 10, o).start())
    lax.fori_loop(1, NCHUNK, project_back, 0)

    from_window = one_hot(QROWS, orders[3:4, 0:HALF])
    for b in range(2):
        gq[b] = dot_nn(from_window, gt_s[b * HALF:(b + 1) * HALF, :]).astype(BF16)
    back_copies = halo(gq, hq, back_ss, back_rs, (e_up, d_up))
    for copy in back_copies:
        copy.start()

    arrived(g1f.at[others], 8)
    to_core(g1f, g1o, 11).start()

    arrived(g2r.at[others], 10)
    g2l[d] = sum_of(g2r, NCHIP, slice(0, 64))
    lat_all(lambda o: to_band(g2l.at[d], g2l.at[d], 12, o).start())
    g2f[chip, 64:96] = sum_of(g2r, NCHIP, slice(64, 96))

    to_natural = one_hot(HALF, orders[1:2, 0:QROWS])
    for copy in back_copies:
        copy.wait()
    hq[:, 0:224, :] = gq[:, 0:224, :]

    arrived(g2l.at[others], 12)
    g2f[chip, 0:64] = sum_of(g2l, NLAT, slice(0, 64))
    chips_all(lambda o: to_chip(g2f.at[chip], g2f.at[chip], 13, o).start())

    for b in range(2):
        out_fields[b * HALF:(b + 1) * HALF, :] = dot_nn(to_natural, hq[b]).astype(BF16)
    arrived(g1o, 11)
    out_g1[core] = g1f[...]
    out_g1[1 - core] = g1o[...]
    arrived(g2f.at[others], 13)
    to_core(g2f, g2o, 14).start()
    out_g2[core] = g2f[...]
    arrived(g2o, 14)
    out_g2[1 - core] = g2o[...]

    left(cs.at[others], 0)
    left(wa.at[others], 1)
    left(cf, 2)
    left(wb, 3)
    left(ch, 4)
    left(g1p, 5)
    left(g1r.at[others], 6)
    left(g1l.at[others], 7)
    left(g1f.at[others], 8)
    left(g2p, 9)
    left(g2r.at[others], 10)
    left(g1o, 11)
    left(g2l.at[others], 12)
    left(g2f.at[others], 13)
    left(g2o, 14)


def results_kernel(
    fields, g1, g2, attend_gain, triple_w, feed_gain, expand_w,
    out_fields, out_triple, out_output, out_expand, out_shrink, out_attend, out_feed, out_table,
):
    out_fields[...] = fields[...]
    for i in range(4):
        for j in range(2):
            rows, cols = slice(i * 48, (i + 1) * 48), slice(j * 384, (j + 1) * 384)
            out_expand[rows, cols] = g1[0, 2 * i + j, 0:48].astype(F32)
            out_shrink[rows, cols] = g1[1, 2 * i + j, 0:48].astype(F32)
    for i in range(6):
        wide = g1[i % 2, i // 2, 48:64].astype(F32)
        out_output[i * 16:(i + 1) * 16, :] = wide[:, 0:C]
        out_output[96 + i * 16:96 + (i + 1) * 16, :] = wide[:, C:2 * C]
    for i in range(3):
        for j in range(5):
            at, size = 5 * i + j, 128 if j < 4 else 64
            part = g2[at // 8, at % 8, 0:64].astype(F32)
            out_triple[i * 64:(i + 1) * 64, j * 128:j * 128 + size] = part[:, 0:size]
    table = jnp.concatenate(
        [g2[o // 16, (o // 2) % 8, 64 + 16 * (o % 2):80 + 16 * (o % 2)] for o in range(32)], axis=1
    ).astype(F32)
    for h in range(HEADS):
        out_table[h] = table[2 * h:2 * h + 2, 0:POS]

    def gain_gradient(grad, weight, gain):
        product = grad[...] * weight[...].astype(F32)
        ones = jnp.ones((8, product.shape[1]), F32)
        total = lax.dot_general(
            ones, product, (((1,), (1,)), ((), ())), precision=lax.Precision.HIGHEST,
            preferred_element_type=F32,
        )
        return total[0:1] / gain[...]

    out_attend[...] = gain_gradient(out_triple, triple_w, attend_gain)
    out_feed[...] = gain_gradient(out_expand, expand_w, feed_gain)


def scratch():
    def vmem(*shape, kind=BF16):
        return pltpu.VMEM(shape, kind)

    token = vmem(TOK, C)
    token_f = vmem(TOK, C, kind=F32)
    weight = vmem(C, C)
    quad = vmem(2, QROWS, C)
    stat = vmem(WIN, 128, kind=F32)
    small = vmem(24, 128, kind=F32)
    buffers = [
        quad, quad, quad, quad, token, token, token, token, token, weight, weight, weight,
        vmem(NWIN, WIN, WIDE), token, token_f, token, vmem(TOK, FF), vmem(TOK, FF, kind=F32), token,
        vmem(16, POS, kind=F32), vmem(3, 192, 512), vmem(2, 2304, 128, kind=F32),
        vmem(2, WIN, WIDE, kind=F32), vmem(2, WIN, WIDE, kind=F32),
        vmem(8, 2, 3, 32, 128), vmem(2, 8, 3, 32, 128), vmem(8, 3, 32, 128), vmem(2, 8, 2, 32, 128),
        vmem(8, 32, 768), vmem(8, 32, 768),
        vmem(12, 128, C), token, stat, stat, small, small, small, small, vmem(4, WIN, 128, kind=F32),
        token, vmem(TOK, FF), token_f, token, token, token, token, token, token,
        vmem(WIN, WIDE, kind=F32), vmem(WIN, WIDE),
    ]
    for rows, cols in ((64, 384), (96, 128)):
        chunks = vmem(8, rows, cols)
        buffers += [vmem(2, 8, rows, cols), chunks, chunks, chunks, vmem(8, 64, cols), chunks, chunks]
    counts = [3, 3, 3, 3, 2, 2, 15, 15]
    return buffers + [pltpu.SemaphoreType.DMA((n,)) for n in counts]


def per_device(
    fields, merge_cotangent, attend_gain, triple_weight, bias_table, output_weight, feed_gain,
    expand_weight, shrink_weight, merge_gain, merge_weight,
):
    cot = jnp.transpose(merge_cotangent, (1, 2, 3, 4, 0)).reshape(576, 192)
    bias = jnp.transpose(bias_table[0], (1, 0, 2))
    def shaped(shapes):
        return [jax.ShapeDtypeStruct(shape, kind) for shape, kind in shapes]

    vmem_spec = pl.BlockSpec(memory_space=pltpu.VMEM)
    parts = pl.pallas_call(
        kernel,
        out_shape=shaped(
            [((TOK, C), BF16), ((2, 8, 64, 384), BF16), ((2, 8, 96, 128), BF16)]
        ),
        in_specs=[vmem_spec] * 12,
        out_specs=[vmem_spec] * 3,
        scratch_shapes=scratch(),
        compiler_params=pltpu.CompilerParams(
            collective_id=0, has_side_effects=True, vmem_limit_bytes=60 * 1024 * 1024
        ),
    )(
        fields.reshape(TOK, C), cot, attend_gain.reshape(1, C), triple_weight, bias, output_weight,
        feed_gain.reshape(1, C), expand_weight, shrink_weight.T, merge_gain,
        merge_weight.T, jnp.asarray(order_indices()),
    )
    g_fields, g_triple, g_output, g_expand, g_shrink, g_attend, g_feed, g_table = pl.pallas_call(
        results_kernel,
        out_shape=shaped(
            [
                ((TOK, C), BF16), ((C, 3 * C), F32), ((C, C), F32), ((C, FF), F32), ((C, FF), F32),
                ((1, C), F32), ((1, C), F32), ((HEADS, 2, POS), F32),
            ]
        ),
        in_specs=[vmem_spec] * 7,
        out_specs=[vmem_spec] * 8,
        compiler_params=pltpu.CompilerParams(vmem_limit_bytes=60 * 1024 * 1024),
    )(*parts, attend_gain.reshape(1, C), triple_weight, feed_gain.reshape(1, C), expand_weight)
    return (
        g_fields.reshape(fields.shape), g_triple, g_output, g_expand, g_shrink.T,
        g_attend.reshape(C), g_feed.reshape(C), jnp.transpose(g_table, (1, 0, 2))[None],
    )


def solution(mesh):
    placed = (
        P(None, None, "lat", "lon", None),
        P(None, None, None, "lat", "lon"),
        P(),
        P(),
        P("lat", None, None, None),
        P(),
        P(),
        P(),
        P(),
        P(),
        P(None, "lon"),
    )
    return jax.shard_map(
        per_device,
        mesh=mesh,
        in_specs=placed,
        out_specs=(
            P(None, None, "lat", "lon", None),
            P(),
            P(),
            P(),
            P(),
            P(),
            P(),
            P("lat", None, None, None),
        ),
        check_vma=False,
    )
```

```python
import functools
import math

import jax
import jax.numpy as jnp
import numpy as np
from jax import lax
from jax.experimental import pallas as pl
from jax.experimental.pallas import tpu as pltpu
from jax.sharding import PartitionSpec as P

F32 = jnp.float32
BF16 = jnp.bfloat16
I32 = jnp.int32
MESH = pl.DeviceIdType.MESH

EPS = 1e-05
MASKED = -1000000000.0
NLON = 16
NLAT = 8
NCHIP = 8
C = 192
HEADS = 6
FF = 768
WIN = 144
NWIN = 8
TOK = WIN * NWIN
HALF = TOK // 2
QROWS = 608
POS = 3312
CHUNK = 288
NCHUNK = TOK // CHUNK
TILE = 48
WIDE = 896
FACTOR = 32 ** -0.5


def order_indices():
    natural_to_quad = np.full(640, -1, np.int32)
    quad_to_natural = np.full(640, -1, np.int32)
    quad_to_window = np.full(640, -1, np.int32)
    window_to_quad = np.full(640, -1, np.int32)
    for level in range(4):
        for row in range(6):
            for col in range(24):
                source = (level * 6 + row) * 24 + col
                if col >= 6:
                    place = (0 if row >= 3 else 224) + level * 54 + (row % 3) * 18 + col - 6
                else:
                    place = (448 if row >= 3 else 528) + level * 18 + (row % 3) * 6 + col
                natural_to_quad[source] = place
                quad_to_natural[place] = source
    index = 0
    for lev_win in range(2):
        for lon_win in range(2):
            for s in range(12):
                for p in range(2):
                    for r in range(6):
                        level = (lev_win * 2 + p + 1) % 4
                        col = lon_win * 12 + s
                        if col < 18:
                            place = (0 if r < 3 else 224) + level * 54 + (r % 3) * 18 + col
                        else:
                            place = (448 if r < 3 else 528) + level * 18 + (r % 3) * 6 + col - 18
                        window_to_quad[index] = place
                        quad_to_window[place] = index
                        index += 1
    cell_lane = np.full(640, -1, np.int32)
    bias_row = np.full(640, -1, np.int32)
    merged_token = np.full((2, 640), -1, np.int32)
    for lane in range(256):
        if lane % 16 < 12:
            cell_lane[lane] = (12 * (lane // 16) + 3 + lane % 16) % 192
    for k in range(WIN):
        s, p, r = k // 12, (k // 6) % 2, k % 6
        bias_row[k] = p * 256 + r * 23 + 11 - s
    for lon_win in range(2):
        for row in range(384):
            p, r, y, m = row // 192, (row // 32) % 6, (row // 16) % 2, row % 16
            if 0 <= m - lon_win * 6 < 6:
                merged_token[lon_win, row] = (2 * (m - lon_win * 6) + y) * 12 + p * 6 + r
    rows = [natural_to_quad, quad_to_natural, quad_to_window, window_to_quad]
    return np.stack(rows + [cell_lane, bias_row, merged_token[0], merged_token[1]])


def dot_nn(a, b):
    return lax.dot_general(a, b, (((1,), (0,)), ((), ())), preferred_element_type=F32)


def dot_nt(a, b):
    return lax.dot_general(a, b, (((1,), (1,)), ((), ())), preferred_element_type=F32)


def dot_tn(a, b):
    return lax.dot_general(a, b, (((0,), (0,)), ((), ())), preferred_element_type=F32)


def one_hot(rows, targets):
    ids = lax.broadcasted_iota(I32, (rows, targets.shape[1]), 0)
    return jnp.where(ids == targets, 1.0, 0.0).astype(BF16)


def statistics(values):
    centred = values - jnp.mean(values, axis=-1, keepdims=True)
    inverse = lax.rsqrt(jnp.mean(centred * centred, axis=-1, keepdims=True) + EPS)
    return centred * inverse, inverse


def norm_back(normed, inverse, scaled):
    centre = jnp.mean(scaled, axis=-1, keepdims=True)
    projected = jnp.mean(scaled * normed, axis=-1, keepdims=True)
    return inverse * (scaled - centre - normed * projected)


def gelu_parts(values):
    cumulative = 0.5 * (1.0 + lax.erf(values * (1.0 / math.sqrt(2.0))))
    density = jnp.exp(-0.5 * values * values) * (1.0 / math.sqrt(2.0 * math.pi))
    return values * cumulative, cumulative + values * density


def lanes(rows, cols):
    return lax.broadcasted_iota(I32, (rows, cols), 1)


def over_12(ids):
    return (ids * 5462) >> 16


def over_6(ids):
    return (ids * 10923) >> 16


def kernel(
    fields, cot, attend_gain, triple_w, bias, output_w, feed_gain, expand_w, shrink_t, merge_gain,
    merge_wt, orders,
    out_fields, out_g1, out_g2,
    sq, rq, gq, hq, x_w, ni_s, q_s, k_s, v_s, wq, wk, wv, p_s, att_s, mid_s, nm_s, act_s, slope_s, vo_s,
    b16, bl_s, bs_s, bx, ds_s,
    cs, cb, cf, ch, wa, wb, qry, qw, st, sx, sup, sdn, tup, tdn, cp_s, go_s, gh_s, gm_s, ga_s, gmh_s,
    dq_s, dk_s, dv_s, gt_s, raw, dsh, dam, hid, tmp, g1s, g1p, g1h, g1r, g1l, g1f, g1o, g2s, g2p, g2h, g2r, g2l, g2f, g2o,
    halo_ss, halo_rs, back_ss, back_rs, st_ss, st_rs, sends, recvs,
):
    e = lax.axis_index("lon")
    d = lax.axis_index("lat")
    e_up, e_dn = lax.rem(e + 1, NLON), lax.rem(e + NLON - 1, NLON)
    d_up, d_dn = lax.rem(d + 1, NLAT), lax.rem(d + NLAT - 1, NLAT)

    def remote(src, dst, ssem, rsem, device):
        return pltpu.make_async_remote_copy(
            src_ref=src, dst_ref=dst, send_sem=ssem, recv_sem=rsem, device_id=device,
            device_id_type=MESH,
        )

    core, chip = lax.rem(e, 2), e // 2
    partner = e + 1 - 2 * core

    def chips_all(action):
        def body(step, carry):
            action(lax.rem(chip + step, NCHIP))
            return carry

        lax.fori_loop(1, NCHIP, body, 0)

    def lat_all(action):
        def body(step, carry):
            action(lax.rem(d + step, NLAT))
            return carry

        lax.fori_loop(1, NLAT, body, 0)

    def to_chip(src, dst, phase, o):
        return remote(src, dst, sends.at[phase], recvs.at[phase], (2 * o + core, d))

    def to_band(src, dst, phase, o):
        return remote(src, dst, sends.at[phase], recvs.at[phase], (e, o))

    def to_core(src, dst, phase):
        return remote(src, dst, sends.at[phase], recvs.at[phase], (partner, d))

    def arrived(region, phase):
        remote(region, region, sends.at[phase], recvs.at[phase], (partner, d)).wait_recv()

    def left(region, phase):
        remote(region, region, sends.at[phase], recvs.at[phase], (partner, d)).wait_send()

    barrier = pltpu.get_barrier_semaphore()

    def greet(device):
        pl.semaphore_signal(barrier, inc=1, device_id=device, device_id_type=MESH)

    chips_all(lambda o: greet((2 * o + core, d)))
    lat_all(lambda o: greet((e, o)))
    for device in ((e_up, d), (e_dn, d), (e_up, d_up), (e_dn, d_dn)):
        greet(device)

    to_quad = one_hot(QROWS, orders[0:1, 0:HALF])
    for b in range(2):
        sq[b] = dot_nn(to_quad, fields[b * HALF:(b + 1) * HALF, :]).astype(BF16)
    pl.semaphore_wait(barrier, NCHIP - 1 + NLAT - 1 + 4)

    pieces = ((224, 224), (448, 80), (528, 80))

    def halo(src, dst, ssem, rsem, step):
        devices = ((e, step[1]), (step[0], d), (step[0], step[1]))
        return [
            remote(src.at[:, pl.ds(at, size), :], dst.at[:, pl.ds(at, size), :], ssem.at[i], rsem.at[i], dev)
            for i, ((at, size), dev) in enumerate(zip(pieces, devices))
        ]

    halo_copies = halo(sq, rq, halo_ss, halo_rs, (e_dn, d_dn))
    for copy in halo_copies:
        copy.start()

    cells = dot_nn(cot[...], one_hot(192, orders[4:5, 0:256]))
    block_of = lanes(72, 128) >> 4
    for o in range(NLON):
        tile, inner = (o // 8) * 128, o % 8
        piece = jnp.zeros((72, 128), F32)
        for bl in range(8):
            part = cells[bl * 72:(bl + 1) * 72, tile:tile + 128]
            shift = (16 * (bl - inner)) % 128
            if shift:
                part = pltpu.roll(part, shift, 1)
            piece = jnp.where(block_of == bl, part, piece)
        for a in range(3):
            padded = jnp.concatenate([piece[a * 24:(a + 1) * 24], jnp.zeros((8, 128), F32)], axis=0)
            cs[o // 2, o % 2, a] = padded.astype(BF16)
    wa[chip] = jnp.concatenate(
        [merge_wt[...].astype(F32), jnp.zeros((8, 768), F32)], axis=0
    ).astype(BF16)
    cb[:, chip] = cs[chip]
    chips_all(lambda o: to_chip(cs.at[o], cb.at[:, chip], 0, o).start())
    chips_all(lambda o: to_chip(wa.at[chip], wa.at[chip], 1, o).start())

    for h in range(HEADS):
        b16[2 * h:2 * h + 2, :] = bias[h]
    b16[12:16, :] = jnp.zeros((4, POS), F32)
    zero_tail = jnp.zeros((16, 256 - 138), F32)
    for p in range(2):
        for r in range(6):
            parts = []
            for pk in range(2):
                at = (p * 2 + pk) * 828 + r * 138
                parts += [b16[:, at:at + 138], zero_tail]
            row = jnp.concatenate(parts, axis=1)
            high = row.astype(BF16)
            rest = row - high.astype(F32)
            middle = rest.astype(BF16)
            low = (rest - middle.astype(F32)).astype(BF16)
            at = (p * 6 + r) * 16
            bl_s[at:at + 16, :] = high
            bl_s[192 + at:192 + at + 16, :] = middle
            bl_s[384 + at:384 + at + 16, :] = low

    bias_row = orders[5:6, 0:WIN]

    def spread_matrix(s_i):
        return one_hot(512, bias_row + s_i)

    def spread(s_i, carry):
        split = dot_nn(bl_s[...], spread_matrix(s_i))
        rows = split[0:192] + split[192:384] + split[384:576]
        at = pl.ds(pl.multiple_of(s_i * 192, 192), 192)
        bs_s[0, at, :] = rows[:, 0:128]
        bs_s[1, at, :] = jnp.concatenate([rows[:, 128:144], jnp.zeros((192, 112), F32)], axis=1)
        return carry

    lax.fori_loop(0, 12, spread, 0)

    tok_i = lax.broadcasted_iota(I32, (WIN, WIN), 0)
    tok_k = lax.broadcasted_iota(I32, (WIN, WIN), 1)
    half_i, half_k = over_6(tok_i), over_6(tok_k)
    last_band = d == NLAT - 1
    lat_differs = ((tok_i - half_i * 6 >= 3) != (tok_k - half_k * 6 >= 3)) & last_band
    lev_differs = (half_i & 1) != (half_k & 1)
    bx[:, :, HEADS * WIN:WIDE] = jnp.zeros((2, WIN, WIDE - HEADS * WIN), F32)
    for lw in range(2):
        differs = (lat_differs | lev_differs) if lw else lat_differs
        for h in range(HEADS):
            at = pl.ds(h * 2 + lw, WIN, stride=16)
            full = jnp.concatenate([bs_s.at[0][at, :], bs_s.at[1][at, :]], axis=1)[:, 0:WIN]
            bx[lw, :, h * WIN:(h + 1) * WIN] = jnp.where(differs, MASKED, full).T

    wq[...] = triple_w[:, 0:192]
    wk[...] = triple_w[:, 192:384]
    wv[...] = triple_w[:, 384:576]

    head_of = lanes(1, C) >> 5
    head_f = [jnp.where(head_of == h, 1.0, 0.0) for h in range(HEADS)]
    head_b = [mask.astype(BF16) for mask in head_f]

    blank = jnp.zeros((WIDE - HEADS * WIN, C), BF16)

    def stacked(values):
        return jnp.concatenate([values * mask for mask in head_b] + [blank], axis=0)

    def unstacked(values):
        blocks = [values[h * 32:(h + 1) * 32, h * WIN:(h + 1) * WIN] for h in range(HEADS)]
        return jnp.concatenate(blocks, axis=0).T

    to_window = one_hot(HALF, orders[2:3, 0:QROWS])
    for copy in halo_copies:
        copy.wait()
    rq[:, 0:224, :] = sq[:, 0:224, :]
    for b in range(2):
        x_w[b * HALF:(b + 1) * HALF, :] = dot_nn(to_window, rq[b]).astype(BF16)

    def window_rows(w):
        return pl.ds(pl.multiple_of(w * WIN, WIN), WIN)

    def chunk_rows(i):
        return pl.ds(pl.multiple_of(i * CHUNK, CHUNK), CHUNK)

    def tile_rows(i, t):
        return pl.ds(pl.multiple_of(i * CHUNK + t * TILE, 16), TILE)

    def project(i, carry):
        rows = chunk_rows(i)
        for t in range(CHUNK // TILE):
            part = tile_rows(i, t)
            normed = statistics(x_w[part, :].astype(F32))[0]
            ni_s[part, :] = (normed * attend_gain[...]).astype(BF16)
        normed_in = ni_s[rows, :]
        q_s[rows, :] = dot_nn(normed_in, wq[...]).astype(BF16)
        k_s[rows, :] = dot_nn(normed_in, wk[...]).astype(BF16)
        v_s[rows, :] = dot_nn(normed_in, wv[...]).astype(BF16)
        return carry

    lax.fori_loop(0, NCHUNK, project, 0)

    arrived(cb.at[:, pl.ds(0, NCHIP - 1)], 0)
    to_core(cb.at[1 - core], cf, 2).start()
    arrived(wa.at[pl.ds(0, NCHIP - 1)], 1)
    to_core(wa, wb, 3).start()

    def attend(pair, carry):
        lw = lax.rem(pair, 2)
        for i in range(2):
            rows = window_rows(2 * pair + i)
            raw[i] = dot_nt(k_s[rows, :], stacked(q_s[rows, :]))
        for i in range(2):
            for t in range(WIDE // 128):
                cols = slice(t * 128, (t + 1) * 128)
                scores = raw[i, :, cols] * FACTOR + bx[lw, :, cols]
                exponent = jnp.exp(scores - jnp.max(scores, axis=0, keepdims=True))
                chances = exponent * (1.0 / jnp.sum(exponent, axis=0, keepdims=True))
                p_s[2 * pair + i, :, cols] = chances.astype(BF16)
        for i in range(2):
            rows = window_rows(2 * pair + i)
            att_s[rows, :] = unstacked(dot_tn(v_s[rows, :], p_s[2 * pair + i])).astype(BF16)
        return carry

    lax.fori_loop(0, NWIN // 2, attend, 0)

    arrived(cf, 2)
    first_rows = pl.ds(0, 2)
    to_band(cb.at[core, :, first_rows], ch.at[0], 4, d_dn).start()
    to_band(cf.at[:, first_rows], ch.at[1], 4, d_dn).start()

    def feed(i, carry):
        rows = chunk_rows(i)
        tmp[...] = x_w[rows, :].astype(F32) + dot_nn(att_s[rows, :], output_w[...])
        for t in range(CHUNK // TILE):
            part = tile_rows(i, t)
            middle = tmp[t * TILE:(t + 1) * TILE, :]
            mid_s[part, :] = middle
            nm_s[part, :] = (statistics(middle)[0] * feed_gain[...]).astype(BF16)
        hid[...] = dot_nn(nm_s[rows, :], expand_w[...])
        for t in range(CHUNK // 16):
            part = pl.ds(pl.multiple_of(i * CHUNK + t * 16, 16), 16)
            for j in range(FF // 256):
                cols = slice(j * 256, (j + 1) * 256)
                act, slope = gelu_parts(hid[t * 16:(t + 1) * 16, cols])
                act_s[part, cols] = act.astype(BF16)
                slope_s[part, cols] = slope
        vo_s[rows, :] = (tmp[...] + dot_nt(act_s[rows, :], shrink_t[...])).astype(BF16)
        return carry

    lax.fori_loop(0, NCHUNK, feed, 0)

    arrived(ch, 4)
    arrived(wb, 3)
    gain_row = merge_gain[...].reshape(1, 4 * C)
    for r in range(6):
        x = (r + 1) % 2
        cell = (0, 1, 1, 2, 2, 3)[r]
        cols = slice(x * 384, (x + 1) * 384)
        if cell < 2:
            planes = cb[core, :, cell + 1], cf[:, cell + 1]
        else:
            planes = ch[0, :, cell - 2], ch[1, :, cell - 2]
        summed = dot_tn(planes[0].reshape(256, 128), wa[:, :, cols].reshape(256, 384))
        summed = summed + dot_tn(planes[1].reshape(256, 128), wb[:, :, cols].reshape(256, 384))
        scaled = summed * gain_row[:, x * 384:(x + 1) * 384]
        qry[2 * r] = scaled[:, 0:192].astype(BF16)
        qry[2 * r + 1] = scaled[:, 192:384].astype(BF16)

    st[...] = jnp.zeros_like(st)
    stat_lane = lanes(WIN, 128)
    tile_lane = lanes(TILE, 128)

    def merge_sums(w, carry):
        rows = window_rows(w)
        b, lw, lon_win = w // 4, lax.rem(w // 2, 2), lax.rem(w, 2)
        parts = []
        for p in range(2):
            level = lax.rem(lw * 2 + p + 1, 4)
            at = pl.ds(pl.multiple_of((b * 4 + level) * 16, 16), 16)
            parts.append(qry[:, at, :].reshape(192, C))
        token = jnp.where(lon_win == 1, orders[7:8, 0:384], orders[6:7, 0:384])
        qw[rows, :] = dot_nn(one_hot(WIN, token), jnp.concatenate(parts, axis=0)).astype(BF16)
        for t in range(WIN // TILE):
            part = pl.ds(pl.multiple_of(w * WIN + t * TILE, 16), TILE)
            at = slice(t * TILE, (t + 1) * TILE)
            q = qw[part, :].astype(F32)
            v = vo_s[part, :].astype(F32)
            mean = jnp.mean(v, axis=-1, keepdims=True)
            centred = v - mean
            squares = jnp.sum(centred * centred, axis=-1, keepdims=True)
            q_sum = jnp.sum(q, axis=-1, keepdims=True)
            qv_sum = jnp.sum(q * centred, axis=-1, keepdims=True)
            total = st[at, :]
            for j, value in enumerate((mean, squares, q_sum, qv_sum)):
                total = jnp.where(tile_lane == 32 * j + w, value, total)
            st[at, :] = total
        return carry

    lax.fori_loop(0, NWIN, merge_sums, 0)

    tup[...] = st[pl.ds(5, 24, stride=6), :]
    tdn[...] = st[pl.ds(0, 24, stride=6), :]
    up_copy = remote(tup, sup, st_ss.at[0], st_rs.at[0], (e, d_up))
    dn_copy = remote(tdn, sdn, st_ss.at[1], st_rs.at[1], (e, d_dn))
    up_copy.start()
    dn_copy.start()
    for r, other in ((1, 2), (2, 1), (3, 4), (4, 3)):
        sx[pl.ds(r, 24, stride=6), :] = st[pl.ds(other, 24, stride=6), :]
    up_copy.wait()
    dn_copy.wait()
    sx[pl.ds(0, 24, stride=6), :] = sup[...]
    sx[pl.ds(5, 24, stride=6), :] = sdn[...]

    even = (over_12(lax.broadcasted_iota(I32, (WIN, 128), 0)) & 1) == 0

    def pair_of(values):
        return jnp.where(even, pltpu.roll(values, WIN - 12, 0), pltpu.roll(values, 12, 0))

    own, cross = st[...], sx[...]
    group = [own, cross, pair_of(own), pair_of(cross)]
    cell_mean = (group[0] + group[1] + group[2] + group[3]) * 0.25
    variance = jnp.zeros((WIN, 128), F32)
    q_total = jnp.zeros((WIN, 128), F32)
    qv_total = jnp.zeros((WIN, 128), F32)
    for values in group:
        offset = values - cell_mean
        q_sum = pltpu.roll(values, 64, 1)
        variance = variance + pltpu.roll(values, 96, 1) + 192.0 * offset * offset
        q_total = q_total + q_sum
        qv_total = qv_total + pltpu.roll(values, 32, 1) + offset * q_sum
    cell_inverse = lax.rsqrt(jnp.where(stat_lane < 8, variance, 0.0) * (1.0 / 768.0) + EPS)
    cp_s[0] = cell_mean
    cp_s[1] = cell_inverse
    cp_s[2] = q_total * (1.0 / 768.0)
    cp_s[3] = cell_inverse * cell_inverse * qv_total * (1.0 / 768.0)

    def merge_back(w, carry):
        for t in range(WIN // TILE):
            part = pl.ds(pl.multiple_of(w * WIN + t * TILE, 16), TILE)
            at = slice(t * TILE, (t + 1) * TILE)
            mean, inverse, q_mean, projected = [
                jnp.sum(jnp.where(tile_lane == w, cp_s[j, at, :], 0.0), axis=-1, keepdims=True) for j in range(4)
            ]
            v = vo_s[part, :].astype(F32) - mean
            go_s[part, :] = (inverse * (qw[part, :].astype(F32) - q_mean - v * projected)).astype(BF16)
        return carry

    lax.fori_loop(0, NWIN, merge_back, 0)

    def feed_back(i, carry):
        rows = chunk_rows(i)
        go = go_s[rows, :]
        gh = (dot_nn(go, shrink_t[...]) * slope_s[rows, :]).astype(BF16)
        gh_s[rows, :] = gh
        tmp[...] = dot_nt(gh, expand_w[...])
        for t in range(CHUNK // TILE):
            part = tile_rows(i, t)
            gnm = tmp[t * TILE:(t + 1) * TILE, :]
            unit, inverse = statistics(mid_s[part, :])
            gm = go_s[part, :].astype(F32) + norm_back(unit, inverse, gnm * feed_gain[...])
            gm_s[part, :] = gm
            gmh_s[part, :] = gm.astype(BF16)
        ga_s[rows, :] = dot_nt(gmh_s[rows, :], output_w[...]).astype(BF16)
        return carry

    lax.fori_loop(0, NCHUNK, feed_back, 0)

    g_expand = dot_tn(nm_s[...], gh_s[...]).astype(BF16)
    g_shrink = dot_tn(go_s[...], act_s[...]).astype(BF16)
    g_output = dot_tn(att_s[...], gmh_s[...]).astype(BF16)
    for i in range(4):
        for j in range(2):
            g1s[0, 2 * i + j, 0:48] = g_expand[i * 48:(i + 1) * 48, j * 384:(j + 1) * 384]
            g1s[1, 2 * i + j, 0:48] = g_shrink[i * 48:(i + 1) * 48, j * 384:(j + 1) * 384]
    wide = jnp.concatenate([g_output[0:96], g_output[96:192]], axis=1)
    for i in range(NCHIP):
        for j in range(2):
            at = (i * 2 + j) * 16
            g1s[j, i, 48:64] = wide[at:at + 16] if at < 96 else jnp.zeros((16, 384), BF16)

    def sum_of(ref, count, rows):
        total = ref[0, rows].astype(F32)
        for o in range(1, count):
            total = total + ref[o, rows].astype(F32)
        return total.astype(BF16)

    def add_pair(mine, other, out):
        for o in range(NCHIP):
            out[o] = (mine[core, o].astype(F32) + other[o].astype(F32)).astype(BF16)

    others = pl.ds(0, NCHIP - 1)
    to_core(g1s.at[1 - core], g1p, 5).start()

    ds_s[...] = jnp.zeros_like(ds_s)

    def attend_back(pair, carry):
        lw = lax.rem(pair, 2)
        for i in range(2):
            rows = window_rows(2 * pair + i)
            dam[i] = stacked(ga_s[rows, :])
            raw[i] = dot_nt(v_s[rows, :], dam[i])
        for i in range(2):
            for t in range(WIDE // 128):
                cols = slice(t * 128, (t + 1) * 128)
                chances = p_s[2 * pair + i, :, cols].astype(F32)
                weighted = raw[i, :, cols]
                centre = jnp.sum(chances * weighted, axis=0, keepdims=True)
                dsh[i, :, cols] = (chances * (weighted - centre)).astype(BF16)
        for i in range(2):
            rows = window_rows(2 * pair + i)
            dv_s[rows, :] = dot_nn(p_s[2 * pair + i], dam[i]).astype(BF16)
            dq_s[rows, :] = (unstacked(dot_tn(k_s[rows, :], dsh[i])) * FACTOR).astype(BF16)
            dk_s[rows, :] = (dot_nn(dsh[i], stacked(q_s[rows, :])) * FACTOR).astype(BF16)
        ds_s[lw] = ds_s[lw] + (dsh[0].astype(F32) + dsh[1].astype(F32))
        return carry

    all_rows = slice(0, 64)
    lax.fori_loop(0, 1, attend_back, 0)
    arrived(g1p, 5)
    add_pair(g1s, g1p, g1h)
    g1r[chip] = g1h[chip]
    chips_all(lambda o: to_chip(g1h.at[o], g1r.at[chip], 6, o).start())
    lax.fori_loop(1, 3, attend_back, 0)
    arrived(g1r.at[others], 6)
    g1l[d] = sum_of(g1r, NCHIP, all_rows)
    lat_all(lambda o: to_band(g1l.at[d], g1l.at[d], 7, o).start())
    lax.fori_loop(3, 4, attend_back, 0)
    arrived(g1l.at[others], 7)
    g1f[chip] = sum_of(g1l, NLAT, all_rows)
    chips_all(lambda o: to_chip(g1f.at[chip], g1f.at[chip], 8, o).start())

    ni = ni_s[...]
    g_triple = jnp.concatenate(
        [dot_tn(ni, dq_s[...]), dot_tn(ni, dk_s[...]), dot_tn(ni, dv_s[...]), jnp.zeros((C, 64), F32)], axis=1
    ).astype(BF16)
    for i in range(3):
        for j in range(5):
            at = 5 * i + j
            g2s[at // 8, at % 8, 0:64] = g_triple[i * 64:(i + 1) * 64, j * 128:(j + 1) * 128]
    g2s[1, 7, 0:64] = jnp.zeros((64, 128), BF16)
    for lw in range(2):
        for h in range(HEADS):
            at = pl.ds(h * 2 + lw, WIN, stride=16)
            part = ds_s[lw, :, h * WIN:(h + 1) * WIN].T
            bs_s.at[0][at, :] = part[:, 0:128]
            bs_s.at[1][at, :] = jnp.concatenate([part[:, 128:144], jnp.zeros((WIN, 112), F32)], axis=1)

    def fold(s_i, carry):
        at = pl.ds(pl.multiple_of(s_i * 192, 192), 192)
        rows = jnp.concatenate([bs_s[0, at, :], bs_s[1, at, :]], axis=1)[:, 0:WIN].astype(BF16)
        return carry + dot_nt(rows, spread_matrix(s_i))

    folded = lax.fori_loop(0, 12, fold, jnp.zeros((192, 512), F32))
    pieces_t = []
    for p in range(2):
        for pk in range(2):
            for r in range(6):
                at = (p * 6 + r) * 16
                pieces_t.append(folded[at:at + 16, pk * 256:pk * 256 + 138])
    table = jnp.concatenate(pieces_t + [jnp.zeros((16, 4096 - POS), F32)], axis=1).astype(BF16)
    for o in range(32):
        g2s[o // 16, (o // 2) % 8, 64 + 16 * (o % 2):80 + 16 * (o % 2)] = table[:, o * 128:(o + 1) * 128]
    to_core(g2s.at[1 - core], g2p, 9).start()

    def project_back(i, carry):
        rows = chunk_rows(i)
        tmp[...] = (
            dot_nt(dq_s[rows, :], wq[...]) + dot_nt(dk_s[rows, :], wk[...]) + dot_nt(dv_s[rows, :], wv[...])
        )
        for t in range(CHUNK // TILE):
            part = tile_rows(i, t)
            unit, inverse = statistics(x_w[part, :].astype(F32))
            back = norm_back(unit, inverse, tmp[t * TILE:(t + 1) * TILE, :] * attend_gain[...])
            gt_s[part, :] = (gm_s[part, :] + back).astype(BF16)
        return carry

    lax.fori_loop(0, 1, project_back, 0)
    arrived(g2p, 9)
    add_pair(g2s, g2p, g2h)
    g2r[chip] = g2h[chip]
    chips_all(lambda o: to_chip(g2h.at[o], g2r.at[chip], 10, o).start())
    lax.fori_loop(1, NCHUNK, project_back, 0)

    from_window = one_hot(QROWS, orders[3:4, 0:HALF])
    for b in range(2):
        gq[b] = dot_nn(from_window, gt_s[b * HALF:(b + 1) * HALF, :]).astype(BF16)
    back_copies = halo(gq, hq, back_ss, back_rs, (e_up, d_up))
    for copy in back_copies:
        copy.start()

    arrived(g1f.at[others], 8)
    to_core(g1f, g1o, 11).start()

    arrived(g2r.at[others], 10)
    g2l[d] = sum_of(g2r, NCHIP, slice(0, 64))
    lat_all(lambda o: to_band(g2l.at[d], g2l.at[d], 12, o).start())
    g2f[chip, 64:96] = sum_of(g2r, NCHIP, slice(64, 96))

    to_natural = one_hot(HALF, orders[1:2, 0:QROWS])
    for copy in back_copies:
        copy.wait()
    hq[:, 0:224, :] = gq[:, 0:224, :]

    arrived(g2l.at[others], 12)
    g2f[chip, 0:64] = sum_of(g2l, NLAT, slice(0, 64))
    chips_all(lambda o: to_chip(g2f.at[chip], g2f.at[chip], 13, o).start())

    for b in range(2):
        out_fields[b * HALF:(b + 1) * HALF, :] = dot_nn(to_natural, hq[b]).astype(BF16)
    arrived(g1o, 11)
    out_g1[core] = g1f[...]
    out_g1[1 - core] = g1o[...]
    arrived(g2f.at[others], 13)
    to_core(g2f, g2o, 14).start()
    out_g2[core] = g2f[...]
    arrived(g2o, 14)
    out_g2[1 - core] = g2o[...]

    left(cs.at[others], 0)
    left(wa.at[others], 1)
    left(cf, 2)
    left(wb, 3)
    left(ch, 4)
    left(g1p, 5)
    left(g1r.at[others], 6)
    left(g1l.at[others], 7)
    left(g1f.at[others], 8)
    left(g2p, 9)
    left(g2r.at[others], 10)
    left(g1o, 11)
    left(g2l.at[others], 12)
    left(g2f.at[others], 13)
    left(g2o, 14)


def results_kernel(
    fields, g1, g2, attend_gain, triple_w, feed_gain, expand_w,
    out_fields, out_triple, out_output, out_expand, out_shrink, out_attend, out_feed, out_table,
):
    out_fields[...] = fields[...]
    for i in range(4):
        for j in range(2):
            rows, cols = slice(i * 48, (i + 1) * 48), slice(j * 384, (j + 1) * 384)
            out_expand[rows, cols] = g1[0, 2 * i + j, 0:48].astype(F32)
            out_shrink[rows, cols] = g1[1, 2 * i + j, 0:48].astype(F32)
    for i in range(6):
        wide = g1[i % 2, i // 2, 48:64].astype(F32)
        out_output[i * 16:(i + 1) * 16, :] = wide[:, 0:C]
        out_output[96 + i * 16:96 + (i + 1) * 16, :] = wide[:, C:2 * C]
    for i in range(3):
        for j in range(5):
            at, size = 5 * i + j, 128 if j < 4 else 64
            part = g2[at // 8, at % 8, 0:64].astype(F32)
            out_triple[i * 64:(i + 1) * 64, j * 128:j * 128 + size] = part[:, 0:size]
    table = jnp.concatenate(
        [g2[o // 16, (o // 2) % 8, 64 + 16 * (o % 2):80 + 16 * (o % 2)] for o in range(32)], axis=1
    ).astype(F32)
    for h in range(HEADS):
        out_table[h] = table[2 * h:2 * h + 2, 0:POS]

    def gain_gradient(grad, weight, gain):
        product = grad[...] * weight[...].astype(F32)
        ones = jnp.ones((8, product.shape[1]), F32)
        total = lax.dot_general(
            ones, product, (((1,), (1,)), ((), ())), precision=lax.Precision.HIGHEST,
            preferred_element_type=F32,
        )
        return total[0:1] / gain[...]

    out_attend[...] = gain_gradient(out_triple, triple_w, attend_gain)
    out_feed[...] = gain_gradient(out_expand, expand_w, feed_gain)


def scratch():
    def vmem(*shape, kind=BF16):
        return pltpu.VMEM(shape, kind)

    token = vmem(TOK, C)
    token_f = vmem(TOK, C, kind=F32)
    weight = vmem(C, C)
    quad = vmem(2, QROWS, C)
    stat = vmem(WIN, 128, kind=F32)
    small = vmem(24, 128, kind=F32)
    buffers = [
        quad, quad, quad, quad, token, token, token, token, token, weight, weight, weight,
        vmem(NWIN, WIN, WIDE), token, token_f, token, vmem(TOK, FF), vmem(TOK, FF, kind=F32), token,
        vmem(16, POS, kind=F32), vmem(576, 512), vmem(2, 2304, 128, kind=F32),
        vmem(2, WIN, WIDE, kind=F32), vmem(2, WIN, WIDE, kind=F32),
        vmem(8, 2, 3, 32, 128), vmem(2, 8, 3, 32, 128), vmem(8, 3, 32, 128), vmem(2, 8, 2, 32, 128),
        vmem(8, 32, 768), vmem(8, 32, 768),
        vmem(12, 128, C), token, stat, stat, small, small, small, small, vmem(4, WIN, 128, kind=F32),
        token, vmem(TOK, FF), token_f, token, token, token, token, token, token,
        vmem(2, WIN, WIDE, kind=F32), vmem(2, WIN, WIDE), vmem(2, WIDE, C), vmem(CHUNK, FF, kind=F32),
        vmem(CHUNK, C, kind=F32),
    ]
    for rows, cols in ((64, 384), (96, 128)):
        chunks = vmem(8, rows, cols)
        buffers += [vmem(2, 8, rows, cols), chunks, chunks, chunks, vmem(8, 64, cols), chunks, chunks]
    counts = [3, 3, 3, 3, 2, 2, 15, 15]
    return buffers + [pltpu.SemaphoreType.DMA((n,)) for n in counts]


def per_device(
    fields, merge_cotangent, attend_gain, triple_weight, bias_table, output_weight, feed_gain,
    expand_weight, shrink_weight, merge_gain, merge_weight,
):
    cot = jnp.transpose(merge_cotangent, (1, 2, 3, 4, 0)).reshape(576, 192)
    bias = jnp.transpose(bias_table[0], (1, 0, 2))
    def shaped(shapes):
        return [jax.ShapeDtypeStruct(shape, kind) for shape, kind in shapes]

    vmem_spec = pl.BlockSpec(memory_space=pltpu.VMEM)
    parts = pl.pallas_call(
        kernel,
        out_shape=shaped(
            [((TOK, C), BF16), ((2, 8, 64, 384), BF16), ((2, 8, 96, 128), BF16)]
        ),
        in_specs=[vmem_spec] * 12,
        out_specs=[vmem_spec] * 3,
        scratch_shapes=scratch(),
        compiler_params=pltpu.CompilerParams(
            collective_id=0, has_side_effects=True, vmem_limit_bytes=60 * 1024 * 1024
        ),
    )(
        fields.reshape(TOK, C), cot, attend_gain.reshape(1, C), triple_weight, bias, output_weight,
        feed_gain.reshape(1, C), expand_weight, shrink_weight.T, merge_gain,
        merge_weight.T, jnp.asarray(order_indices()),
    )
    g_fields, g_triple, g_output, g_expand, g_shrink, g_attend, g_feed, g_table = pl.pallas_call(
        results_kernel,
        out_shape=shaped(
            [
                ((TOK, C), BF16), ((C, 3 * C), F32), ((C, C), F32), ((C, FF), F32), ((C, FF), F32),
                ((1, C), F32), ((1, C), F32), ((HEADS, 2, POS), F32),
            ]
        ),
        in_specs=[vmem_spec] * 7,
        out_specs=[vmem_spec] * 8,
        compiler_params=pltpu.CompilerParams(vmem_limit_bytes=60 * 1024 * 1024),
    )(*parts, attend_gain.reshape(1, C), triple_weight, feed_gain.reshape(1, C), expand_weight)
    return (
        g_fields.reshape(fields.shape), g_triple, g_output, g_expand, g_shrink.T,
        g_attend.reshape(C), g_feed.reshape(C), jnp.transpose(g_table, (1, 0, 2))[None],
    )


def solution(mesh):
    placed = (
        P(None, None, "lat", "lon", None),
        P(None, None, None, "lat", "lon"),
        P(),
        P(),
        P("lat", None, None, None),
        P(),
        P(),
        P(),
        P(),
        P(),
        P(None, "lon"),
    )
    return jax.shard_map(
        per_device,
        mesh=mesh,
        in_specs=placed,
        out_specs=(
            P(None, None, "lat", "lon", None),
            P(),
            P(),
            P(),
            P(),
            P(),
            P(),
            P("lat", None, None, None),
        ),
        check_vma=False,
    )
```

```python
import functools
import math

import jax
import jax.numpy as jnp
import numpy as np
from jax import lax
from jax.experimental import pallas as pl
from jax.experimental.pallas import tpu as pltpu
from jax.sharding import PartitionSpec as P

F32 = jnp.float32
BF16 = jnp.bfloat16
I32 = jnp.int32
MESH = pl.DeviceIdType.MESH

EPS = 1e-05
MASKED = -1000000000.0
NLON = 16
NLAT = 8
NCHIP = 8
C = 192
HEADS = 6
FF = 768
WIN = 144
NWIN = 8
TOK = WIN * NWIN
HALF = TOK // 2
QROWS = 192
LEVEL = 144
PAIR = 288
POS = 3312
CHUNK = 288
NCHUNK = TOK // CHUNK
TILE = 48
WIDE = 896
FACTOR = 32 ** -0.5


def order_indices():
    natural_to_quad = np.full(640, -1, np.int32)
    quad_to_natural = np.full(640, -1, np.int32)
    quad_to_window = np.full(640, -1, np.int32)
    window_to_quad = np.full(640, -1, np.int32)
    for row in range(6):
        for col in range(24):
            if col >= 6:
                place = (0 if row >= 3 else 64) + (row % 3) * 18 + col - 6
            else:
                place = (128 if row >= 3 else 160) + (row % 3) * 6 + col
            natural_to_quad[row * 24 + col] = place
            quad_to_natural[place] = row * 24 + col
    index = 0
    for lon_win in range(2):
        for s in range(12):
            for p in range(2):
                for r in range(6):
                    col = lon_win * 12 + s
                    if col < 18:
                        place = (0 if r < 3 else 64) + (r % 3) * 18 + col
                    else:
                        place = (128 if r < 3 else 160) + (r % 3) * 6 + col - 18
                    window_to_quad[index] = p * QROWS + place
                    quad_to_window[p * QROWS + place] = index
                    index += 1
    cell_lane = np.full(640, -1, np.int32)
    bias_row = np.full(640, -1, np.int32)
    merged_token = np.full((2, 640), -1, np.int32)
    for lane in range(256):
        if lane % 16 < 12:
            cell_lane[lane] = (12 * (lane // 16) + 3 + lane % 16) % 192
    for k in range(WIN):
        s, p, r = k // 12, (k // 6) % 2, k % 6
        bias_row[k] = p * 256 + r * 23 + 11 - s
    for lon_win in range(2):
        for row in range(384):
            p, r, y, m = row // 192, (row // 32) % 6, (row // 16) % 2, row % 16
            if 0 <= m - lon_win * 6 < 6:
                merged_token[lon_win, row] = (2 * (m - lon_win * 6) + y) * 12 + p * 6 + r
    rows = [natural_to_quad, quad_to_natural, quad_to_window, window_to_quad]
    return np.stack(rows + [cell_lane, bias_row, merged_token[0], merged_token[1]])


def dot_nn(a, b):
    return lax.dot_general(a, b, (((1,), (0,)), ((), ())), preferred_element_type=F32)


def dot_nt(a, b):
    return lax.dot_general(a, b, (((1,), (1,)), ((), ())), preferred_element_type=F32)


def dot_tn(a, b):
    return lax.dot_general(a, b, (((0,), (0,)), ((), ())), preferred_element_type=F32)


def one_hot(rows, targets):
    ids = lax.broadcasted_iota(I32, (rows, targets.shape[1]), 0)
    return jnp.where(ids == targets, 1.0, 0.0).astype(BF16)


def statistics(values):
    centred = values - jnp.mean(values, axis=-1, keepdims=True)
    inverse = lax.rsqrt(jnp.mean(centred * centred, axis=-1, keepdims=True) + EPS)
    return centred * inverse, inverse


def norm_back(normed, inverse, scaled):
    centre = jnp.mean(scaled, axis=-1, keepdims=True)
    projected = jnp.mean(scaled * normed, axis=-1, keepdims=True)
    return inverse * (scaled - centre - normed * projected)


def gelu_parts(values):
    cumulative = 0.5 * (1.0 + lax.erf(values * (1.0 / math.sqrt(2.0))))
    density = jnp.exp(-0.5 * values * values) * (1.0 / math.sqrt(2.0 * math.pi))
    return values * cumulative, cumulative + values * density


def lanes(rows, cols):
    return lax.broadcasted_iota(I32, (rows, cols), 1)


def over_12(ids):
    return (ids * 5462) >> 16


def over_6(ids):
    return (ids * 10923) >> 16


def kernel(
    fields, cot, attend_gain, triple_w, bias, output_w, feed_gain, expand_w, shrink_t, merge_gain,
    merge_wt, orders,
    out_fields, out_g1, out_g2,
    sq, rq, gq, hq, x_w, ni_s, q_s, k_s, v_s, wq, wk, wv, p_s, att_s, mid_s, nm_s, act_s, slope_s, vo_s,
    b16, bl_s, bs_s, bx, ds_s, spread_s, pick_s,
    cs, cb, cf, ch, wa, wb, qry, qw, st, sx, sup, sdn, tup, tdn, cp_s, go_s, gh_s, gm_s, ga_s, gmh_s,
    dq_s, dk_s, dv_s, gt_s, raw, dsh, dam, hid, tmp, g1s, g1p, g1h, g1r, g1l, g1f, g1o, g2s, g2p, g2h, g2r, g2l, g2f, g2o,
    halo_ss, halo_rs, back_ss, back_rs, st_ss, st_rs, sends, recvs,
):
    e = lax.axis_index("lon")
    d = lax.axis_index("lat")
    e_up, e_dn = lax.rem(e + 1, NLON), lax.rem(e + NLON - 1, NLON)
    d_up, d_dn = lax.rem(d + 1, NLAT), lax.rem(d + NLAT - 1, NLAT)

    def remote(src, dst, ssem, rsem, device):
        return pltpu.make_async_remote_copy(
            src_ref=src, dst_ref=dst, send_sem=ssem, recv_sem=rsem, device_id=device,
            device_id_type=MESH,
        )

    core, chip = lax.rem(e, 2), e // 2
    partner = e + 1 - 2 * core

    def chips_all(action):
        def body(step, carry):
            action(lax.rem(chip + step, NCHIP))
            return carry

        lax.fori_loop(1, NCHIP, body, 0)

    def lat_all(action):
        def body(step, carry):
            action(lax.rem(d + step, NLAT))
            return carry

        lax.fori_loop(1, NLAT, body, 0)

    def to_chip(src, dst, phase, o):
        return remote(src, dst, sends.at[phase], recvs.at[phase], (2 * o + core, d))

    def to_band(src, dst, phase, o):
        return remote(src, dst, sends.at[phase], recvs.at[phase], (e, o))

    def to_core(src, dst, phase):
        return remote(src, dst, sends.at[phase], recvs.at[phase], (partner, d))

    def arrived(region, phase):
        remote(region, region, sends.at[phase], recvs.at[phase], (partner, d)).wait_recv()

    def left(region, phase):
        remote(region, region, sends.at[phase], recvs.at[phase], (partner, d)).wait_send()

    barrier = pltpu.get_barrier_semaphore()

    def greet(device):
        pl.semaphore_signal(barrier, inc=1, device_id=device, device_id_type=MESH)

    chips_all(lambda o: greet((2 * o + core, d)))
    lat_all(lambda o: greet((e, o)))
    for device in ((e_up, d), (e_dn, d), (e_up, d_up), (e_dn, d_dn)):
        greet(device)

    to_quad = one_hot(QROWS, orders[0:1, 0:LEVEL])
    for i in range(8):
        quad = dot_nn(to_quad, fields[i * LEVEL:(i + 1) * LEVEL, :])
        sq[(i // 4) * 4 + (i + 3) % 4] = quad.astype(BF16)
    pl.semaphore_wait(barrier, NCHIP - 1 + NLAT - 1 + 4)

    pieces = ((64, 64), (128, 32), (160, 32))

    def halo(src, dst, ssem, rsem, step):
        devices = ((e, step[1]), (step[0], d), (step[0], step[1]))
        return [
            remote(src.at[:, pl.ds(at, size), :], dst.at[:, pl.ds(at, size), :], ssem.at[i], rsem.at[i], dev)
            for i, ((at, size), dev) in enumerate(zip(pieces, devices))
        ]

    halo_copies = halo(sq, rq, halo_ss, halo_rs, (e_dn, d_dn))
    for copy in halo_copies:
        copy.start()

    cells = dot_nn(cot[...], one_hot(192, orders[4:5, 0:256]))
    block_of = lanes(72, 128) >> 4
    for o in range(NLON):
        tile, inner = (o // 8) * 128, o % 8
        piece = jnp.zeros((72, 128), F32)
        for bl in range(8):
            part = cells[bl * 72:(bl + 1) * 72, tile:tile + 128]
            shift = (16 * (bl - inner)) % 128
            if shift:
                part = pltpu.roll(part, shift, 1)
            piece = jnp.where(block_of == bl, part, piece)
        for a in range(3):
            padded = jnp.concatenate([piece[a * 24:(a + 1) * 24], jnp.zeros((8, 128), F32)], axis=0)
            cs[o // 2, o % 2, a] = padded.astype(BF16)
    wa[chip] = jnp.concatenate(
        [merge_wt[...].astype(F32), jnp.zeros((8, 768), F32)], axis=0
    ).astype(BF16)
    cb[:, chip] = cs[chip]
    chips_all(lambda o: to_chip(cs.at[o], cb.at[:, chip], 0, o).start())
    chips_all(lambda o: to_chip(wa.at[chip], wa.at[chip], 1, o).start())

    for h in range(HEADS):
        b16[2 * h:2 * h + 2, :] = bias[h]
    b16[12:16, :] = jnp.zeros((4, POS), F32)
    zero_tail = jnp.zeros((16, 256 - 138), F32)
    for p in range(2):
        for r in range(6):
            parts = []
            for pk in range(2):
                at = (p * 2 + pk) * 828 + r * 138
                parts += [b16[:, at:at + 138], zero_tail]
            row = jnp.concatenate(parts, axis=1)
            high = row.astype(BF16)
            rest = row - high.astype(F32)
            middle = rest.astype(BF16)
            low = (rest - middle.astype(F32)).astype(BF16)
            at = (p * 6 + r) * 16
            bl_s[at:at + 16, :] = high
            bl_s[192 + at:192 + at + 16, :] = middle
            bl_s[384 + at:384 + at + 16, :] = low

    bias_row = orders[5:6, 0:WIN]

    def spread(s_i, carry):
        matrix = one_hot(512, bias_row + s_i)
        spread_s[s_i] = matrix
        split = dot_nn(bl_s[...], matrix)
        rows = split[0:192] + split[192:384] + split[384:576]
        at = pl.ds(pl.multiple_of(s_i * 192, 192), 192)
        bs_s[0, at, :] = rows[:, 0:128]
        bs_s[1, at, :] = jnp.concatenate([rows[:, 128:144], jnp.zeros((192, 112), F32)], axis=1)
        return carry

    lax.fori_loop(0, 12, spread, 0)

    tok_i = lax.broadcasted_iota(I32, (WIN, WIN), 0)
    tok_k = lax.broadcasted_iota(I32, (WIN, WIN), 1)
    half_i, half_k = over_6(tok_i), over_6(tok_k)
    last_band = d == NLAT - 1
    lat_differs = ((tok_i - half_i * 6 >= 3) != (tok_k - half_k * 6 >= 3)) & last_band
    lev_differs = (half_i & 1) != (half_k & 1)
    bx[:, :, HEADS * WIN:WIDE] = jnp.zeros((2, WIN, WIDE - HEADS * WIN), F32)
    for lw in range(2):
        differs = (lat_differs | lev_differs) if lw else lat_differs
        for h in range(HEADS):
            at = pl.ds(h * 2 + lw, WIN, stride=16)
            full = jnp.concatenate([bs_s.at[0][at, :], bs_s.at[1][at, :]], axis=1)[:, 0:WIN]
            bx[lw, :, h * WIN:(h + 1) * WIN] = jnp.where(differs, MASKED, full).T

    wq[...] = triple_w[:, 0:192]
    wk[...] = triple_w[:, 192:384]
    wv[...] = triple_w[:, 384:576]

    head_of = lanes(1, C) >> 5
    head_f = [jnp.where(head_of == h, 1.0, 0.0) for h in range(HEADS)]
    head_b = [mask.astype(BF16) for mask in head_f]

    blank = jnp.zeros((WIDE - HEADS * WIN, C), BF16)

    def stacked(values):
        return jnp.concatenate([values * mask for mask in head_b] + [blank], axis=0)

    def unstacked(values):
        blocks = [values[h * 32:(h + 1) * 32, h * WIN:(h + 1) * WIN] for h in range(HEADS)]
        return jnp.concatenate(blocks, axis=0).T

    to_window = one_hot(PAIR, orders[2:3, 0:2 * QROWS])
    for copy in halo_copies:
        copy.wait()
    rq[:, 0:64, :] = sq[:, 0:64, :]
    for i in range(4):
        quads = rq[2 * i:2 * i + 2].reshape(2 * QROWS, C)
        x_w[i * PAIR:(i + 1) * PAIR, :] = dot_nn(to_window, quads).astype(BF16)

    def window_rows(w):
        return pl.ds(pl.multiple_of(w * WIN, WIN), WIN)

    def chunk_rows(i):
        return pl.ds(pl.multiple_of(i * CHUNK, CHUNK), CHUNK)

    def tile_rows(i, t):
        return pl.ds(pl.multiple_of(i * CHUNK + t * TILE, 16), TILE)

    def project(i, carry):
        rows = chunk_rows(i)
        for t in range(CHUNK // TILE):
            part = tile_rows(i, t)
            normed = statistics(x_w[part, :].astype(F32))[0]
            ni_s[part, :] = (normed * attend_gain[...]).astype(BF16)
        normed_in = ni_s[rows, :]
        q_s[rows, :] = dot_nn(normed_in, wq[...]).astype(BF16)
        k_s[rows, :] = dot_nn(normed_in, wk[...]).astype(BF16)
        v_s[rows, :] = dot_nn(normed_in, wv[...]).astype(BF16)
        return carry

    lax.fori_loop(0, NCHUNK, project, 0)

    arrived(cb.at[:, pl.ds(0, NCHIP - 1)], 0)
    to_core(cb.at[1 - core], cf, 2).start()
    arrived(wa.at[pl.ds(0, NCHIP - 1)], 1)
    to_core(wa, wb, 3).start()

    def attend(pair, carry):
        lw = lax.rem(pair, 2)
        for i in range(2):
            rows = window_rows(2 * pair + i)
            raw[i] = dot_nt(k_s[rows, :], stacked(q_s[rows, :]))
        for i in range(2):
            for t in range(WIDE // 128):
                cols = slice(t * 128, (t + 1) * 128)
                scores = raw[i, :, cols] * FACTOR + bx[lw, :, cols]
                exponent = jnp.exp(scores - jnp.max(scores, axis=0, keepdims=True))
                chances = exponent * (1.0 / jnp.sum(exponent, axis=0, keepdims=True))
                p_s[2 * pair + i, :, cols] = chances.astype(BF16)
        for i in range(2):
            rows = window_rows(2 * pair + i)
            att_s[rows, :] = unstacked(dot_tn(v_s[rows, :], p_s[2 * pair + i])).astype(BF16)
        return carry

    lax.fori_loop(0, NWIN // 2, attend, 0)

    arrived(cf, 2)
    first_rows = pl.ds(0, 2)
    to_band(cb.at[core, :, first_rows], ch.at[0], 4, d_dn).start()
    to_band(cf.at[:, first_rows], ch.at[1], 4, d_dn).start()

    def feed(i, carry):
        rows = chunk_rows(i)
        tmp[...] = x_w[rows, :].astype(F32) + dot_nn(att_s[rows, :], output_w[...])
        for t in range(CHUNK // TILE):
            part = tile_rows(i, t)
            middle = tmp[t * TILE:(t + 1) * TILE, :]
            mid_s[part, :] = middle
            nm_s[part, :] = (statistics(middle)[0] * feed_gain[...]).astype(BF16)
        hid[...] = dot_nn(nm_s[rows, :], expand_w[...])
        for t in range(CHUNK // 16):
            part = pl.ds(pl.multiple_of(i * CHUNK + t * 16, 16), 16)
            for j in range(FF // 256):
                cols = slice(j * 256, (j + 1) * 256)
                act, slope = gelu_parts(hid[t * 16:(t + 1) * 16, cols])
                act_s[part, cols] = act.astype(BF16)
                slope_s[part, cols] = slope
        vo_s[rows, :] = (tmp[...] + dot_nt(act_s[rows, :], shrink_t[...])).astype(BF16)
        return carry

    arrived(ch, 4)
    arrived(wb, 3)
    gain_row = merge_gain[...].reshape(1, 4 * C)
    for r in range(6):
        x = (r + 1) % 2
        cell = (0, 1, 1, 2, 2, 3)[r]
        cols = slice(x * 384, (x + 1) * 384)
        if cell < 2:
            planes = cb[core, :, cell + 1], cf[:, cell + 1]
        else:
            planes = ch[0, :, cell - 2], ch[1, :, cell - 2]
        summed = dot_tn(planes[0].reshape(256, 128), wa[:, :, cols].reshape(256, 384))
        summed = summed + dot_tn(planes[1].reshape(256, 128), wb[:, :, cols].reshape(256, 384))
        scaled = summed * gain_row[:, x * 384:(x + 1) * 384]
        qry[2 * r] = scaled[:, 0:192].astype(BF16)
        qry[2 * r + 1] = scaled[:, 192:384].astype(BF16)

    st[...] = jnp.zeros_like(st)
    for i in range(2):
        pick_s[i] = one_hot(WIN, orders[6 + i:7 + i, 0:384])
    stat_lane = lanes(WIN, 128)
    tile_lane = lanes(TILE, 128)

    def merge_sums(w, carry):
        rows = window_rows(w)
        b, lw, lon_win = w // 4, lax.rem(w // 2, 2), lax.rem(w, 2)
        parts = []
        for p in range(2):
            level = lax.rem(lw * 2 + p + 1, 4)
            at = pl.ds(pl.multiple_of((b * 4 + level) * 16, 16), 16)
            parts.append(qry[:, at, :].reshape(192, C))
        qw[rows, :] = dot_nn(pick_s[lon_win], jnp.concatenate(parts, axis=0)).astype(BF16)
        for t in range(WIN // TILE):
            part = pl.ds(pl.multiple_of(w * WIN + t * TILE, 16), TILE)
            at = slice(t * TILE, (t + 1) * TILE)
            q = qw[part, :].astype(F32)
            v = vo_s[part, :].astype(F32)
            mean = jnp.mean(v, axis=-1, keepdims=True)
            centred = v - mean
            squares = jnp.sum(centred * centred, axis=-1, keepdims=True)
            q_sum = jnp.sum(q, axis=-1, keepdims=True)
            qv_sum = jnp.sum(q * centred, axis=-1, keepdims=True)
            total = st[b, at, :]
            for j, value in enumerate((mean, squares, q_sum, qv_sum)):
                total = jnp.where(tile_lane == 32 * j + w, value, total)
            st[b, at, :] = total
        return carry

    def exchange(b):
        tup[b] = st.at[b][pl.ds(5, 24, stride=6), :]
        tdn[b] = st.at[b][pl.ds(0, 24, stride=6), :]
        copies = (
            remote(tup.at[b], sup.at[b], st_ss.at[2 * b], st_rs.at[2 * b], (e, d_up)),
            remote(tdn.at[b], sdn.at[b], st_ss.at[2 * b + 1], st_rs.at[2 * b + 1], (e, d_dn)),
        )
        for copy in copies:
            copy.start()
        return copies

    even = (over_12(lax.broadcasted_iota(I32, (WIN, 128), 0)) & 1) == 0

    def pair_of(values):
        return jnp.where(even, pltpu.roll(values, WIN - 12, 0), pltpu.roll(values, 12, 0))

    def cell_norm(b, copies):
        for r, other in ((1, 2), (2, 1), (3, 4), (4, 3)):
            sx[pl.ds(r, 24, stride=6), :] = st.at[b][pl.ds(other, 24, stride=6), :]
        for copy in copies:
            copy.wait()
        sx[pl.ds(0, 24, stride=6), :] = sup[b]
        sx[pl.ds(5, 24, stride=6), :] = sdn[b]
        own, cross = st[b], sx[...]
        group = [own, cross, pair_of(own), pair_of(cross)]
        cell_mean = (group[0] + group[1] + group[2] + group[3]) * 0.25
        variance = jnp.zeros((WIN, 128), F32)
        q_total = jnp.zeros((WIN, 128), F32)
        qv_total = jnp.zeros((WIN, 128), F32)
        for values in group:
            offset = values - cell_mean
            q_sum = pltpu.roll(values, 64, 1)
            variance = variance + pltpu.roll(values, 96, 1) + 192.0 * offset * offset
            q_total = q_total + q_sum
            qv_total = qv_total + pltpu.roll(values, 32, 1) + offset * q_sum
        cell_inverse = lax.rsqrt(jnp.where(stat_lane < 8, variance, 0.0) * (1.0 / 768.0) + EPS)
        cp_s[0] = cell_mean
        cp_s[1] = cell_inverse
        cp_s[2] = q_total * (1.0 / 768.0)
        cp_s[3] = cell_inverse * cell_inverse * qv_total * (1.0 / 768.0)

    def merge_back(w, carry):
        for t in range(WIN // TILE):
            part = pl.ds(pl.multiple_of(w * WIN + t * TILE, 16), TILE)
            at = slice(t * TILE, (t + 1) * TILE)
            mean, inverse, q_mean, projected = [
                jnp.sum(jnp.where(tile_lane == w, cp_s[j, at, :], 0.0), axis=-1, keepdims=True) for j in range(4)
            ]
            v = vo_s[part, :].astype(F32) - mean
            go_s[part, :] = (inverse * (qw[part, :].astype(F32) - q_mean - v * projected)).astype(BF16)
        return carry

    def feed_back(i, carry):
        rows = chunk_rows(i)
        go = go_s[rows, :]
        gh = (dot_nn(go, shrink_t[...]) * slope_s[rows, :]).astype(BF16)
        gh_s[rows, :] = gh
        tmp[...] = dot_nt(gh, expand_w[...])
        for t in range(CHUNK // TILE):
            part = tile_rows(i, t)
            gnm = tmp[t * TILE:(t + 1) * TILE, :]
            unit, inverse = statistics(mid_s[part, :])
            gm = go_s[part, :].astype(F32) + norm_back(unit, inverse, gnm * feed_gain[...])
            gm_s[part, :] = gm
            gmh_s[part, :] = gm.astype(BF16)
        ga_s[rows, :] = dot_nt(gmh_s[rows, :], output_w[...]).astype(BF16)
        return carry

    sums = []
    for b in range(2):
        lax.fori_loop(2 * b, 2 * b + 2, feed, 0)
        lax.fori_loop(4 * b, 4 * b + 4, merge_sums, 0)
        sums.append(exchange(b))
    for b in range(2):
        cell_norm(b, sums[b])
        lax.fori_loop(4 * b, 4 * b + 4, merge_back, 0)
        lax.fori_loop(2 * b, 2 * b + 2, feed_back, 0)

    g_expand = dot_tn(nm_s[...], gh_s[...]).astype(BF16)
    g_shrink = dot_tn(go_s[...], act_s[...]).astype(BF16)
    g_output = dot_tn(att_s[...], gmh_s[...]).astype(BF16)
    for i in range(4):
        for j in range(2):
            g1s[0, 2 * i + j, 0:48] = g_expand[i * 48:(i + 1) * 48, j * 384:(j + 1) * 384]
            g1s[1, 2 * i + j, 0:48] = g_shrink[i * 48:(i + 1) * 48, j * 384:(j + 1) * 384]
    wide = jnp.concatenate([g_output[0:96], g_output[96:192]], axis=1)
    for i in range(NCHIP):
        for j in range(2):
            at = (i * 2 + j) * 16
            g1s[j, i, 48:64] = wide[at:at + 16] if at < 96 else jnp.zeros((16, 384), BF16)

    def sum_of(ref, count, rows):
        total = ref[0, rows].astype(F32)
        for o in range(1, count):
            total = total + ref[o, rows].astype(F32)
        return total.astype(BF16)

    def add_pair(mine, other, out):
        for o in range(NCHIP):
            out[o] = (mine[core, o].astype(F32) + other[o].astype(F32)).astype(BF16)

    others = pl.ds(0, NCHIP - 1)
    to_core(g1s.at[1 - core], g1p, 5).start()

    ds_s[...] = jnp.zeros_like(ds_s)

    def attend_back(pair, carry):
        lw = lax.rem(pair, 2)
        for i in range(2):
            rows = window_rows(2 * pair + i)
            dam[i] = stacked(ga_s[rows, :])
            raw[i] = dot_nt(v_s[rows, :], dam[i])
        for i in range(2):
            for t in range(WIDE // 128):
                cols = slice(t * 128, (t + 1) * 128)
                chances = p_s[2 * pair + i, :, cols].astype(F32)
                weighted = raw[i, :, cols]
                centre = jnp.sum(chances * weighted, axis=0, keepdims=True)
                dsh[i, :, cols] = (chances * (weighted - centre)).astype(BF16)
        for i in range(2):
            rows = window_rows(2 * pair + i)
            dv_s[rows, :] = dot_nn(p_s[2 * pair + i], dam[i]).astype(BF16)
            dq_s[rows, :] = (unstacked(dot_tn(k_s[rows, :], dsh[i])) * FACTOR).astype(BF16)
            dk_s[rows, :] = (dot_nn(dsh[i], stacked(q_s[rows, :])) * FACTOR).astype(BF16)
        ds_s[lw] = ds_s[lw] + (dsh[0].astype(F32) + dsh[1].astype(F32))
        return carry

    all_rows = slice(0, 64)
    lax.fori_loop(0, 1, attend_back, 0)
    arrived(g1p, 5)
    add_pair(g1s, g1p, g1h)
    g1r[chip] = g1h[chip]
    chips_all(lambda o: to_chip(g1h.at[o], g1r.at[chip], 6, o).start())
    lax.fori_loop(1, 3, attend_back, 0)
    arrived(g1r.at[others], 6)
    g1l[d] = sum_of(g1r, NCHIP, all_rows)
    lat_all(lambda o: to_band(g1l.at[d], g1l.at[d], 7, o).start())
    lax.fori_loop(3, 4, attend_back, 0)
    arrived(g1l.at[others], 7)
    g1f[chip] = sum_of(g1l, NLAT, all_rows)
    chips_all(lambda o: to_chip(g1f.at[chip], g1f.at[chip], 8, o).start())

    ni = ni_s[...]
    g_triple = jnp.concatenate(
        [dot_tn(ni, dq_s[...]), dot_tn(ni, dk_s[...]), dot_tn(ni, dv_s[...]), jnp.zeros((C, 64), F32)], axis=1
    ).astype(BF16)
    for i in range(3):
        for j in range(5):
            at = 5 * i + j
            g2s[at // 8, at % 8, 0:64] = g_triple[i * 64:(i + 1) * 64, j * 128:(j + 1) * 128]
    g2s[1, 7, 0:64] = jnp.zeros((64, 128), BF16)
    for lw in range(2):
        for h in range(HEADS):
            at = pl.ds(h * 2 + lw, WIN, stride=16)
            part = ds_s[lw, :, h * WIN:(h + 1) * WIN].T
            bs_s.at[0][at, :] = part[:, 0:128]
            bs_s.at[1][at, :] = jnp.concatenate([part[:, 128:144], jnp.zeros((WIN, 112), F32)], axis=1)

    def fold(s_i, carry):
        at = pl.ds(pl.multiple_of(s_i * 192, 192), 192)
        rows = jnp.concatenate([bs_s[0, at, :], bs_s[1, at, :]], axis=1)[:, 0:WIN].astype(BF16)
        return carry + dot_nt(rows, spread_s[s_i])

    folded = lax.fori_loop(0, 12, fold, jnp.zeros((192, 512), F32))
    pieces_t = []
    for p in range(2):
        for pk in range(2):
            for r in range(6):
                at = (p * 6 + r) * 16
                pieces_t.append(folded[at:at + 16, pk * 256:pk * 256 + 138])
    table = jnp.concatenate(pieces_t + [jnp.zeros((16, 4096 - POS), F32)], axis=1).astype(BF16)
    for o in range(32):
        g2s[o // 16, (o // 2) % 8, 64 + 16 * (o % 2):80 + 16 * (o % 2)] = table[:, o * 128:(o + 1) * 128]
    to_core(g2s.at[1 - core], g2p, 9).start()

    def project_back(i, carry):
        rows = chunk_rows(i)
        tmp[...] = (
            dot_nt(dq_s[rows, :], wq[...]) + dot_nt(dk_s[rows, :], wk[...]) + dot_nt(dv_s[rows, :], wv[...])
        )
        for t in range(CHUNK // TILE):
            part = tile_rows(i, t)
            unit, inverse = statistics(x_w[part, :].astype(F32))
            back = norm_back(unit, inverse, tmp[t * TILE:(t + 1) * TILE, :] * attend_gain[...])
            gt_s[part, :] = (gm_s[part, :] + back).astype(BF16)
        return carry

    lax.fori_loop(0, 1, project_back, 0)
    arrived(g2p, 9)
    add_pair(g2s, g2p, g2h)
    g2r[chip] = g2h[chip]
    chips_all(lambda o: to_chip(g2h.at[o], g2r.at[chip], 10, o).start())
    lax.fori_loop(1, NCHUNK, project_back, 0)

    from_window = one_hot(2 * QROWS, orders[3:4, 0:PAIR])
    for i in range(4):
        quads = dot_nn(from_window, gt_s[i * PAIR:(i + 1) * PAIR, :]).astype(BF16)
        gq[2 * i:2 * i + 2] = quads.reshape(2, QROWS, C)
    back_copies = halo(gq, hq, back_ss, back_rs, (e_up, d_up))
    for copy in back_copies:
        copy.start()

    arrived(g1f.at[others], 8)
    to_core(g1f, g1o, 11).start()

    arrived(g2r.at[others], 10)
    g2l[d] = sum_of(g2r, NCHIP, slice(0, 64))
    lat_all(lambda o: to_band(g2l.at[d], g2l.at[d], 12, o).start())
    g2f[chip, 64:96] = sum_of(g2r, NCHIP, slice(64, 96))

    to_natural = one_hot(LEVEL, orders[1:2, 0:QROWS])
    for copy in back_copies:
        copy.wait()
    hq[:, 0:64, :] = gq[:, 0:64, :]

    arrived(g2l.at[others], 12)
    g2f[chip, 0:64] = sum_of(g2l, NLAT, slice(0, 64))
    chips_all(lambda o: to_chip(g2f.at[chip], g2f.at[chip], 13, o).start())

    for i in range(8):
        natural = dot_nn(to_natural, hq[(i // 4) * 4 + (i + 3) % 4])
        out_fields[i * LEVEL:(i + 1) * LEVEL, :] = natural.astype(BF16)
    arrived(g1o, 11)
    out_g1[core] = g1f[...]
    out_g1[1 - core] = g1o[...]
    arrived(g2f.at[others], 13)
    to_core(g2f, g2o, 14).start()
    out_g2[core] = g2f[...]
    arrived(g2o, 14)
    out_g2[1 - core] = g2o[...]

    left(cs.at[others], 0)
    left(wa.at[others], 1)
    left(cf, 2)
    left(wb, 3)
    left(ch, 4)
    left(g1p, 5)
    left(g1r.at[others], 6)
    left(g1l.at[others], 7)
    left(g1f.at[others], 8)
    left(g2p, 9)
    left(g2r.at[others], 10)
    left(g1o, 11)
    left(g2l.at[others], 12)
    left(g2f.at[others], 13)
    left(g2o, 14)


def results_kernel(
    fields, g1, g2, attend_gain, triple_w, feed_gain, expand_w,
    out_fields, out_triple, out_output, out_expand, out_shrink, out_attend, out_feed, out_table,
):
    out_fields[...] = fields[...]
    for i in range(4):
        for j in range(2):
            rows, cols = slice(i * 48, (i + 1) * 48), slice(j * 384, (j + 1) * 384)
            out_expand[rows, cols] = g1[0, 2 * i + j, 0:48].astype(F32)
            out_shrink[rows, cols] = g1[1, 2 * i + j, 0:48].astype(F32)
    for i in range(6):
        wide = g1[i % 2, i // 2, 48:64].astype(F32)
        out_output[i * 16:(i + 1) * 16, :] = wide[:, 0:C]
        out_output[96 + i * 16:96 + (i + 1) * 16, :] = wide[:, C:2 * C]
    for i in range(3):
        for j in range(5):
            at, size = 5 * i + j, 128 if j < 4 else 64
            part = g2[at // 8, at % 8, 0:64].astype(F32)
            out_triple[i * 64:(i + 1) * 64, j * 128:j * 128 + size] = part[:, 0:size]
    table = jnp.concatenate(
        [g2[o // 16, (o // 2) % 8, 64 + 16 * (o % 2):80 + 16 * (o % 2)] for o in range(32)], axis=1
    ).astype(F32)
    for h in range(HEADS):
        out_table[h] = table[2 * h:2 * h + 2, 0:POS]

    def gain_gradient(grad, weight, gain):
        product = (grad[...] * weight[...].astype(F32)).astype(BF16)
        total = dot_nt(jnp.ones((16, product.shape[1]), BF16), product)
        return total[0:1] / gain[...]

    out_attend[...] = gain_gradient(out_triple, triple_w, attend_gain)
    out_feed[...] = gain_gradient(out_expand, expand_w, feed_gain)


def scratch():
    def vmem(*shape, kind=BF16):
        return pltpu.VMEM(shape, kind)

    token = vmem(TOK, C)
    token_f = vmem(TOK, C, kind=F32)
    weight = vmem(C, C)
    quad = vmem(8, QROWS, C)
    stat = vmem(WIN, 128, kind=F32)
    small = vmem(2, 24, 128, kind=F32)
    buffers = [
        quad, quad, quad, quad, token, token, token, token, token, weight, weight, weight,
        vmem(NWIN, WIN, WIDE), token, token_f, token, vmem(TOK, FF), vmem(TOK, FF, kind=F32), token,
        vmem(16, POS, kind=F32), vmem(576, 512), vmem(2, 2304, 128, kind=F32),
        vmem(2, WIN, WIDE, kind=F32), vmem(2, WIN, WIDE, kind=F32),
        vmem(12, 512, WIN), vmem(2, WIN, 384),
        vmem(8, 2, 3, 32, 128), vmem(2, 8, 3, 32, 128), vmem(8, 3, 32, 128), vmem(2, 8, 2, 32, 128),
        vmem(8, 32, 768), vmem(8, 32, 768),
        vmem(12, 128, C), token, vmem(2, WIN, 128, kind=F32), stat, small, small, small, small, vmem(4, WIN, 128, kind=F32),
        token, vmem(TOK, FF), token_f, token, token, token, token, token, token,
        vmem(2, WIN, WIDE, kind=F32), vmem(2, WIN, WIDE), vmem(2, WIDE, C), vmem(CHUNK, FF, kind=F32),
        vmem(CHUNK, C, kind=F32),
    ]
    for rows, cols in ((64, 384), (96, 128)):
        chunks = vmem(8, rows, cols)
        buffers += [vmem(2, 8, rows, cols), chunks, chunks, chunks, vmem(8, 64, cols), chunks, chunks]
    counts = [3, 3, 3, 3, 4, 4, 15, 15]
    return buffers + [pltpu.SemaphoreType.DMA((n,)) for n in counts]


def per_device(
    fields, merge_cotangent, attend_gain, triple_weight, bias_table, output_weight, feed_gain,
    expand_weight, shrink_weight, merge_gain, merge_weight,
):
    cot = jnp.transpose(merge_cotangent, (1, 2, 3, 4, 0)).reshape(576, 192)
    bias = jnp.transpose(bias_table[0], (1, 0, 2))
    def shaped(shapes):
        return [jax.ShapeDtypeStruct(shape, kind) for shape, kind in shapes]

    vmem_spec = pl.BlockSpec(memory_space=pltpu.VMEM)
    parts = pl.pallas_call(
        kernel,
        out_shape=shaped(
            [((TOK, C), BF16), ((2, 8, 64, 384), BF16), ((2, 8, 96, 128), BF16)]
        ),
        in_specs=[vmem_spec] * 12,
        out_specs=[vmem_spec] * 3,
        scratch_shapes=scratch(),
        compiler_params=pltpu.CompilerParams(
            collective_id=0, has_side_effects=True, vmem_limit_bytes=60 * 1024 * 1024
        ),
    )(
        fields.reshape(TOK, C), cot, attend_gain.reshape(1, C), triple_weight, bias, output_weight,
        feed_gain.reshape(1, C), expand_weight, shrink_weight.T, merge_gain,
        merge_weight.T, jnp.asarray(order_indices()),
    )
    g_fields, g_triple, g_output, g_expand, g_shrink, g_attend, g_feed, g_table = pl.pallas_call(
        results_kernel,
        out_shape=shaped(
            [
                ((TOK, C), BF16), ((C, 3 * C), F32), ((C, C), F32), ((C, FF), F32), ((C, FF), F32),
                ((1, C), F32), ((1, C), F32), ((HEADS, 2, POS), F32),
            ]
        ),
        in_specs=[vmem_spec] * 7,
        out_specs=[vmem_spec] * 8,
        compiler_params=pltpu.CompilerParams(vmem_limit_bytes=60 * 1024 * 1024),
    )(*parts, attend_gain.reshape(1, C), triple_weight, feed_gain.reshape(1, C), expand_weight)
    return (
        g_fields.reshape(fields.shape), g_triple, g_output, g_expand, g_shrink.T,
        g_attend.reshape(C), g_feed.reshape(C), jnp.transpose(g_table, (1, 0, 2))[None],
    )


def solution(mesh):
    placed = (
        P(None, None, "lat", "lon", None),
        P(None, None, None, "lat", "lon"),
        P(),
        P(),
        P("lat", None, None, None),
        P(),
        P(),
        P(),
        P(),
        P(),
        P(None, "lon"),
    )
    return jax.shard_map(
        per_device,
        mesh=mesh,
        in_specs=placed,
        out_specs=(
            P(None, None, "lat", "lon", None),
            P(),
            P(),
            P(),
            P(),
            P(),
            P(),
            P("lat", None, None, None),
        ),
        check_vma=False,
    )
```

```python
import functools
import math

import jax
import jax.numpy as jnp
import numpy as np
from jax import lax
from jax.experimental import pallas as pl
from jax.experimental.pallas import tpu as pltpu
from jax.sharding import PartitionSpec as P

F32 = jnp.float32
BF16 = jnp.bfloat16
I32 = jnp.int32
MESH = pl.DeviceIdType.MESH

EPS = 1e-05
MASKED = -1000000000.0
NLON = 16
NLAT = 8
NCHIP = 8
C = 192
HEADS = 6
FF = 768
WIN = 144
NWIN = 8
TOK = WIN * NWIN
HALF = TOK // 2
QROWS = 192
LEVEL = 144
PAIR = 288
POS = 3312
CHUNK = 288
NCHUNK = TOK // CHUNK
TILE = 48
WIDE = 896
FACTOR = 32 ** -0.5


def order_indices():
    natural_to_quad = np.full(640, -1, np.int32)
    quad_to_natural = np.full(640, -1, np.int32)
    quad_to_window = np.full(640, -1, np.int32)
    window_to_quad = np.full(640, -1, np.int32)
    for row in range(6):
        for col in range(24):
            if col >= 6:
                place = (0 if row >= 3 else 64) + (row % 3) * 18 + col - 6
            else:
                place = (128 if row >= 3 else 160) + (row % 3) * 6 + col
            natural_to_quad[row * 24 + col] = place
            quad_to_natural[place] = row * 24 + col
    index = 0
    for lon_win in range(2):
        for s in range(12):
            for p in range(2):
                for r in range(6):
                    col = lon_win * 12 + s
                    if col < 18:
                        place = (0 if r < 3 else 64) + (r % 3) * 18 + col
                    else:
                        place = (128 if r < 3 else 160) + (r % 3) * 6 + col - 18
                    window_to_quad[index] = p * QROWS + place
                    quad_to_window[p * QROWS + place] = index
                    index += 1
    cell_lane = np.full(640, -1, np.int32)
    bias_row = np.full(640, -1, np.int32)
    merged_token = np.full((2, 640), -1, np.int32)
    for lane in range(256):
        if lane % 16 < 12:
            cell_lane[lane] = (12 * (lane // 16) + 3 + lane % 16) % 192
    for k in range(WIN):
        s, p, r = k // 12, (k // 6) % 2, k % 6
        bias_row[k] = p * 256 + r * 23 + 11 - s
    for lon_win in range(2):
        for row in range(384):
            p, r, y, m = row // 192, (row // 32) % 6, (row // 16) % 2, row % 16
            if 0 <= m - lon_win * 6 < 6:
                merged_token[lon_win, row] = (2 * (m - lon_win * 6) + y) * 12 + p * 6 + r
    rows = [natural_to_quad, quad_to_natural, quad_to_window, window_to_quad]
    return np.stack(rows + [cell_lane, bias_row, merged_token[0], merged_token[1]])


def dot_nn(a, b):
    return lax.dot_general(a, b, (((1,), (0,)), ((), ())), preferred_element_type=F32)


def dot_nt(a, b):
    return lax.dot_general(a, b, (((1,), (1,)), ((), ())), preferred_element_type=F32)


def dot_tn(a, b):
    return lax.dot_general(a, b, (((0,), (0,)), ((), ())), preferred_element_type=F32)


def one_hot(rows, targets):
    ids = lax.broadcasted_iota(I32, (rows, targets.shape[1]), 0)
    return jnp.where(ids == targets, 1.0, 0.0).astype(BF16)


def statistics(values):
    centred = values - jnp.mean(values, axis=-1, keepdims=True)
    inverse = lax.rsqrt(jnp.mean(centred * centred, axis=-1, keepdims=True) + EPS)
    return centred * inverse, inverse


def norm_back(normed, inverse, scaled):
    centre = jnp.mean(scaled, axis=-1, keepdims=True)
    projected = jnp.mean(scaled * normed, axis=-1, keepdims=True)
    return inverse * (scaled - centre - normed * projected)


def gelu_parts(values):
    cumulative = 0.5 * (1.0 + lax.erf(values * (1.0 / math.sqrt(2.0))))
    density = jnp.exp(-0.5 * values * values) * (1.0 / math.sqrt(2.0 * math.pi))
    return values * cumulative, cumulative + values * density


def lanes(rows, cols):
    return lax.broadcasted_iota(I32, (rows, cols), 1)


def over_12(ids):
    return (ids * 5462) >> 16


def over_6(ids):
    return (ids * 10923) >> 16


def kernel(
    fields, cot, attend_gain, triple_w, bias, output_w, feed_gain, expand_w, shrink_t, merge_gain,
    merge_wt, orders,
    out_fields, out_g1, out_g2,
    sq, rq, gq, hq, x_w, ni_s, q_s, k_s, v_s, wq, wk, wv, p_s, att_s, mid_s, nm_s, act_s, slope_s, vo_s,
    b16, bl_s, bs_s, bx, ds_s, spread_s, pick_s,
    cells, cs, cb, cf, ch, wa, wb, qry, qw, st, sx, sup, sdn, tup, tdn, cp_s, go_s, gh_s, gm_s, ga_s, gmh_s,
    dq_s, dk_s, dv_s, gt_s, raw, dsh, dam, hid, tmp, g1s, g1p, g1h, g1r, g1l, g1f, g1o, g2s, g2p, g2h, g2r, g2l, g2f, g2o,
    halo_ss, halo_rs, back_ss, back_rs, st_ss, st_rs, sends, recvs,
):
    e = lax.axis_index("lon")
    d = lax.axis_index("lat")
    e_up, e_dn = lax.rem(e + 1, NLON), lax.rem(e + NLON - 1, NLON)
    d_up, d_dn = lax.rem(d + 1, NLAT), lax.rem(d + NLAT - 1, NLAT)

    def remote(src, dst, ssem, rsem, device):
        return pltpu.make_async_remote_copy(
            src_ref=src, dst_ref=dst, send_sem=ssem, recv_sem=rsem, device_id=device,
            device_id_type=MESH,
        )

    core, chip = lax.rem(e, 2), e // 2
    partner = e + 1 - 2 * core

    def chips_all(action):
        def body(step, carry):
            action(lax.rem(chip + step, NCHIP))
            return carry

        lax.fori_loop(1, NCHIP, body, 0)

    def lat_all(action):
        def body(step, carry):
            action(lax.rem(d + step, NLAT))
            return carry

        lax.fori_loop(1, NLAT, body, 0)

    def to_chip(src, dst, phase, o):
        return remote(src, dst, sends.at[phase], recvs.at[phase], (2 * o + core, d))

    def to_band(src, dst, phase, o):
        return remote(src, dst, sends.at[phase], recvs.at[phase], (e, o))

    def to_core(src, dst, phase):
        return remote(src, dst, sends.at[phase], recvs.at[phase], (partner, d))

    def arrived(region, phase):
        remote(region, region, sends.at[phase], recvs.at[phase], (partner, d)).wait_recv()

    def left(region, phase):
        remote(region, region, sends.at[phase], recvs.at[phase], (partner, d)).wait_send()

    barrier = pltpu.get_barrier_semaphore()

    def greet(device):
        pl.semaphore_signal(barrier, inc=1, device_id=device, device_id_type=MESH)

    chips_all(lambda o: greet((2 * o + core, d)))
    lat_all(lambda o: greet((e, o)))
    for device in ((e_up, d), (e_dn, d), (e_up, d_up), (e_dn, d_dn)):
        greet(device)

    to_quad = one_hot(QROWS, orders[0:1, 0:LEVEL])

    def sample_rows(i, size):
        return pl.ds(pl.multiple_of(i * size, size), size)

    def shifted_level(i):
        return (i // 4) * 4 + lax.rem(i + 3, 4)

    def sort_level(i, carry):
        sq[shifted_level(i)] = dot_nn(to_quad, fields[sample_rows(i, LEVEL), :]).astype(BF16)
        return carry

    lax.fori_loop(0, 8, sort_level, 0)
    pl.semaphore_wait(barrier, NCHIP - 1 + NLAT - 1 + 4)

    pieces = ((64, 64), (128, 32), (160, 32))

    def halo(src, dst, ssem, rsem, step):
        devices = ((e, step[1]), (step[0], d), (step[0], step[1]))
        return [
            remote(src.at[:, pl.ds(at, size), :], dst.at[:, pl.ds(at, size), :], ssem.at[i], rsem.at[i], dev)
            for i, ((at, size), dev) in enumerate(zip(pieces, devices))
        ]

    halo_copies = halo(sq, rq, halo_ss, halo_rs, (e_dn, d_dn))
    for copy in halo_copies:
        copy.start()

    cells[...] = dot_nn(cot[...], one_hot(192, orders[4:5, 0:256]))
    block_of = lanes(72, 128) >> 4

    def gather_cells(o, carry):
        tile = pl.ds(pl.multiple_of((o // 8) * 128, 128), 128)
        inner = lax.rem(o, 8)
        piece = jnp.zeros((72, 128), F32)
        for bl in range(8):
            part = pltpu.roll(cells[bl * 72:(bl + 1) * 72, tile], lax.rem(16 * (bl - inner) + 128, 128), 1)
            piece = jnp.where(block_of == bl, part, piece)
        for a in range(3):
            padded = jnp.concatenate([piece[a * 24:(a + 1) * 24], jnp.zeros((8, 128), F32)], axis=0)
            cs[o // 2, lax.rem(o, 2), a] = padded.astype(BF16)
        return carry

    lax.fori_loop(0, NLON, gather_cells, 0)
    wa[chip] = jnp.concatenate(
        [merge_wt[...].astype(F32), jnp.zeros((8, 768), F32)], axis=0
    ).astype(BF16)
    cb[:, chip] = cs[chip]
    chips_all(lambda o: to_chip(cs.at[o], cb.at[:, chip], 0, o).start())
    chips_all(lambda o: to_chip(wa.at[chip], wa.at[chip], 1, o).start())

    for h in range(HEADS):
        b16[2 * h:2 * h + 2, :] = bias[h]
    b16[12:16, :] = jnp.zeros((4, POS), F32)
    zero_tail = jnp.zeros((16, 256 - 138), F32)
    for p in range(2):
        for r in range(6):
            parts = []
            for pk in range(2):
                at = (p * 2 + pk) * 828 + r * 138
                parts += [b16[:, at:at + 138], zero_tail]
            row = jnp.concatenate(parts, axis=1)
            high = row.astype(BF16)
            rest = row - high.astype(F32)
            middle = rest.astype(BF16)
            low = (rest - middle.astype(F32)).astype(BF16)
            at = (p * 6 + r) * 16
            bl_s[at:at + 16, :] = high
            bl_s[192 + at:192 + at + 16, :] = middle
            bl_s[384 + at:384 + at + 16, :] = low

    bias_row = orders[5:6, 0:WIN]

    def spread(s_i, carry):
        matrix = one_hot(512, bias_row + s_i)
        spread_s[s_i] = matrix
        split = dot_nn(bl_s[...], matrix)
        rows = split[0:192] + split[192:384] + split[384:576]
        at = pl.ds(pl.multiple_of(s_i * 192, 192), 192)
        bs_s[0, at, :] = rows[:, 0:128]
        bs_s[1, at, :] = jnp.concatenate([rows[:, 128:144], jnp.zeros((192, 112), F32)], axis=1)
        return carry

    lax.fori_loop(0, 12, spread, 0)

    tok_i = lax.broadcasted_iota(I32, (WIN, WIN), 0)
    tok_k = lax.broadcasted_iota(I32, (WIN, WIN), 1)
    half_i, half_k = over_6(tok_i), over_6(tok_k)
    last_band = d == NLAT - 1
    lat_differs = ((tok_i - half_i * 6 >= 3) != (tok_k - half_k * 6 >= 3)) & last_band
    lev_differs = (half_i & 1) != (half_k & 1)
    bx[:, :, HEADS * WIN:WIDE] = jnp.zeros((2, WIN, WIDE - HEADS * WIN), F32)
    for lw in range(2):
        differs = (lat_differs | lev_differs) if lw else lat_differs
        for h in range(HEADS):
            at = pl.ds(h * 2 + lw, WIN, stride=16)
            full = jnp.concatenate([bs_s.at[0][at, :], bs_s.at[1][at, :]], axis=1)[:, 0:WIN]
            bx[lw, :, h * WIN:(h + 1) * WIN] = jnp.where(differs, MASKED, full).T

    wq[...] = triple_w[:, 0:192]
    wk[...] = triple_w[:, 192:384]
    wv[...] = triple_w[:, 384:576]

    head_of = lanes(1, C) >> 5
    head_f = [jnp.where(head_of == h, 1.0, 0.0) for h in range(HEADS)]
    head_b = [mask.astype(BF16) for mask in head_f]

    blank = jnp.zeros((WIDE - HEADS * WIN, C), BF16)

    def stacked(values):
        return jnp.concatenate([values * mask for mask in head_b] + [blank], axis=0)

    def unstacked(values):
        blocks = [values[h * 32:(h + 1) * 32, h * WIN:(h + 1) * WIN] for h in range(HEADS)]
        return jnp.concatenate(blocks, axis=0).T

    to_window = one_hot(PAIR, orders[2:3, 0:2 * QROWS])
    for copy in halo_copies:
        copy.wait()
    rq[:, 0:64, :] = sq[:, 0:64, :]

    def sort_window(i, carry):
        quads = rq[pl.ds(2 * i, 2)].reshape(2 * QROWS, C)
        x_w[sample_rows(i, PAIR), :] = dot_nn(to_window, quads).astype(BF16)
        return carry

    lax.fori_loop(0, 4, sort_window, 0)

    def window_rows(w):
        return pl.ds(pl.multiple_of(w * WIN, WIN), WIN)

    def chunk_rows(i):
        return pl.ds(pl.multiple_of(i * CHUNK, CHUNK), CHUNK)

    def tile_rows(i, t):
        return pl.ds(pl.multiple_of(i * CHUNK + t * TILE, 16), TILE)

    def project(i, carry):
        rows = chunk_rows(i)
        for t in range(CHUNK // TILE):
            part = tile_rows(i, t)
            normed = statistics(x_w[part, :].astype(F32))[0]
            ni_s[part, :] = (normed * attend_gain[...]).astype(BF16)
        normed_in = ni_s[rows, :]
        q_s[rows, :] = dot_nn(normed_in, wq[...]).astype(BF16)
        k_s[rows, :] = dot_nn(normed_in, wk[...]).astype(BF16)
        v_s[rows, :] = dot_nn(normed_in, wv[...]).astype(BF16)
        return carry

    lax.fori_loop(0, NCHUNK, project, 0)

    arrived(cb.at[:, pl.ds(0, NCHIP - 1)], 0)
    to_core(cb.at[1 - core], cf, 2).start()
    arrived(wa.at[pl.ds(0, NCHIP - 1)], 1)
    to_core(wa, wb, 3).start()

    def attend(pair, carry):
        lw = lax.rem(pair, 2)
        for i in range(2):
            rows = window_rows(2 * pair + i)
            raw[i] = dot_nt(k_s[rows, :], stacked(q_s[rows, :]))
        for i in range(2):
            for t in range(WIDE // 128):
                cols = slice(t * 128, (t + 1) * 128)
                scores = raw[i, :, cols] * FACTOR + bx[lw, :, cols]
                exponent = jnp.exp(scores - jnp.max(scores, axis=0, keepdims=True))
                chances = exponent * (1.0 / jnp.sum(exponent, axis=0, keepdims=True))
                p_s[2 * pair + i, :, cols] = chances.astype(BF16)
        for i in range(2):
            rows = window_rows(2 * pair + i)
            att_s[rows, :] = unstacked(dot_tn(v_s[rows, :], p_s[2 * pair + i])).astype(BF16)
        return carry

    lax.fori_loop(0, NWIN // 2, attend, 0)

    arrived(cf, 2)
    first_rows = pl.ds(0, 2)
    to_band(cb.at[core, :, first_rows], ch.at[0], 4, d_dn).start()
    to_band(cf.at[:, first_rows], ch.at[1], 4, d_dn).start()

    def feed(i, carry):
        rows = chunk_rows(i)
        tmp[...] = x_w[rows, :].astype(F32) + dot_nn(att_s[rows, :], output_w[...])
        for t in range(CHUNK // TILE):
            part = tile_rows(i, t)
            middle = tmp[t * TILE:(t + 1) * TILE, :]
            mid_s[part, :] = middle
            nm_s[part, :] = (statistics(middle)[0] * feed_gain[...]).astype(BF16)
        hid[...] = dot_nn(nm_s[rows, :], expand_w[...])
        for t in range(CHUNK // 16):
            part = pl.ds(pl.multiple_of(i * CHUNK + t * 16, 16), 16)
            for j in range(FF // 256):
                cols = slice(j * 256, (j + 1) * 256)
                act, slope = gelu_parts(hid[t * 16:(t + 1) * 16, cols])
                act_s[part, cols] = act.astype(BF16)
                slope_s[part, cols] = slope
        vo_s[rows, :] = (tmp[...] + dot_nt(act_s[rows, :], shrink_t[...])).astype(BF16)
        return carry

    arrived(ch, 4)
    arrived(wb, 3)
    gain_row = merge_gain[...].reshape(1, 4 * C)
    for r in range(6):
        x = (r + 1) % 2
        cell = (0, 1, 1, 2, 2, 3)[r]
        cols = slice(x * 384, (x + 1) * 384)
        if cell < 2:
            planes = cb[core, :, cell + 1], cf[:, cell + 1]
        else:
            planes = ch[0, :, cell - 2], ch[1, :, cell - 2]
        summed = dot_tn(planes[0].reshape(256, 128), wa[:, :, cols].reshape(256, 384))
        summed = summed + dot_tn(planes[1].reshape(256, 128), wb[:, :, cols].reshape(256, 384))
        scaled = summed * gain_row[:, x * 384:(x + 1) * 384]
        qry[2 * r] = scaled[:, 0:192].astype(BF16)
        qry[2 * r + 1] = scaled[:, 192:384].astype(BF16)

    st[...] = jnp.zeros_like(st)
    for i in range(2):
        pick_s[i] = one_hot(WIN, orders[6 + i:7 + i, 0:384])
    stat_lane = lanes(WIN, 128)
    tile_lane = lanes(TILE, 128)

    def merge_sums(w, carry):
        rows = window_rows(w)
        b, lw, lon_win = w // 4, lax.rem(w // 2, 2), lax.rem(w, 2)
        parts = []
        for p in range(2):
            level = lax.rem(lw * 2 + p + 1, 4)
            at = pl.ds(pl.multiple_of((b * 4 + level) * 16, 16), 16)
            parts.append(qry[:, at, :].reshape(192, C))
        qw[rows, :] = dot_nn(pick_s[lon_win], jnp.concatenate(parts, axis=0)).astype(BF16)
        for t in range(WIN // TILE):
            part = pl.ds(pl.multiple_of(w * WIN + t * TILE, 16), TILE)
            at = slice(t * TILE, (t + 1) * TILE)
            q = qw[part, :].astype(F32)
            v = vo_s[part, :].astype(F32)
            mean = jnp.mean(v, axis=-1, keepdims=True)
            centred = v - mean
            squares = jnp.sum(centred * centred, axis=-1, keepdims=True)
            q_sum = jnp.sum(q, axis=-1, keepdims=True)
            qv_sum = jnp.sum(q * centred, axis=-1, keepdims=True)
            total = st[b, at, :]
            for j, value in enumerate((mean, squares, q_sum, qv_sum)):
                total = jnp.where(tile_lane == 32 * j + w, value, total)
            st[b, at, :] = total
        return carry

    def sums_copies(b):
        return (
            remote(tup.at[b], sup.at[b], st_ss.at[2 * b], st_rs.at[2 * b], (e, d_up)),
            remote(tdn.at[b], sdn.at[b], st_ss.at[2 * b + 1], st_rs.at[2 * b + 1], (e, d_dn)),
        )

    def exchange(b):
        tup[b] = st.at[b][pl.ds(5, 24, stride=6), :]
        tdn[b] = st.at[b][pl.ds(0, 24, stride=6), :]
        for copy in sums_copies(b):
            copy.start()

    even = (over_12(lax.broadcasted_iota(I32, (WIN, 128), 0)) & 1) == 0

    def pair_of(values):
        return jnp.where(even, pltpu.roll(values, WIN - 12, 0), pltpu.roll(values, 12, 0))

    def cell_norm(b):
        for r, other in ((1, 2), (2, 1), (3, 4), (4, 3)):
            sx[pl.ds(r, 24, stride=6), :] = st.at[b][pl.ds(other, 24, stride=6), :]
        for copy in sums_copies(b):
            copy.wait()
        sx[pl.ds(0, 24, stride=6), :] = sup[b]
        sx[pl.ds(5, 24, stride=6), :] = sdn[b]
        own, cross = st[b], sx[...]
        group = [own, cross, pair_of(own), pair_of(cross)]
        cell_mean = (group[0] + group[1] + group[2] + group[3]) * 0.25
        variance = jnp.zeros((WIN, 128), F32)
        q_total = jnp.zeros((WIN, 128), F32)
        qv_total = jnp.zeros((WIN, 128), F32)
        for values in group:
            offset = values - cell_mean
            q_sum = pltpu.roll(values, 64, 1)
            variance = variance + pltpu.roll(values, 96, 1) + 192.0 * offset * offset
            q_total = q_total + q_sum
            qv_total = qv_total + pltpu.roll(values, 32, 1) + offset * q_sum
        cell_inverse = lax.rsqrt(jnp.where(stat_lane < 8, variance, 0.0) * (1.0 / 768.0) + EPS)
        cp_s[0] = cell_mean
        cp_s[1] = cell_inverse
        cp_s[2] = q_total * (1.0 / 768.0)
        cp_s[3] = cell_inverse * cell_inverse * qv_total * (1.0 / 768.0)

    def merge_back(w, carry):
        for t in range(WIN // TILE):
            part = pl.ds(pl.multiple_of(w * WIN + t * TILE, 16), TILE)
            at = slice(t * TILE, (t + 1) * TILE)
            mean, inverse, q_mean, projected = [
                jnp.sum(jnp.where(tile_lane == w, cp_s[j, at, :], 0.0), axis=-1, keepdims=True) for j in range(4)
            ]
            v = vo_s[part, :].astype(F32) - mean
            go_s[part, :] = (inverse * (qw[part, :].astype(F32) - q_mean - v * projected)).astype(BF16)
        return carry

    def feed_back(i, carry):
        rows = chunk_rows(i)
        go = go_s[rows, :]
        gh = (dot_nn(go, shrink_t[...]) * slope_s[rows, :]).astype(BF16)
        gh_s[rows, :] = gh
        tmp[...] = dot_nt(gh, expand_w[...])
        for t in range(CHUNK // TILE):
            part = tile_rows(i, t)
            gnm = tmp[t * TILE:(t + 1) * TILE, :]
            unit, inverse = statistics(mid_s[part, :])
            gm = go_s[part, :].astype(F32) + norm_back(unit, inverse, gnm * feed_gain[...])
            gm_s[part, :] = gm
            gmh_s[part, :] = gm.astype(BF16)
        ga_s[rows, :] = dot_nt(gmh_s[rows, :], output_w[...]).astype(BF16)
        return carry

    def forward_sample(b, carry):
        lax.fori_loop(2 * b, 2 * b + 2, feed, 0)
        lax.fori_loop(4 * b, 4 * b + 4, merge_sums, 0)
        exchange(b)
        return carry

    def backward_sample(b, carry):
        cell_norm(b)
        lax.fori_loop(4 * b, 4 * b + 4, merge_back, 0)
        lax.fori_loop(2 * b, 2 * b + 2, feed_back, 0)
        return carry

    lax.fori_loop(0, 2, forward_sample, 0)
    lax.fori_loop(0, 2, backward_sample, 0)

    g_expand = dot_tn(nm_s[...], gh_s[...]).astype(BF16)
    g_shrink = dot_tn(go_s[...], act_s[...]).astype(BF16)
    g_output = dot_tn(att_s[...], gmh_s[...]).astype(BF16)
    for i in range(4):
        for j in range(2):
            g1s[0, 2 * i + j, 0:48] = g_expand[i * 48:(i + 1) * 48, j * 384:(j + 1) * 384]
            g1s[1, 2 * i + j, 0:48] = g_shrink[i * 48:(i + 1) * 48, j * 384:(j + 1) * 384]
    wide = jnp.concatenate([g_output[0:96], g_output[96:192]], axis=1)
    for i in range(NCHIP):
        for j in range(2):
            at = (i * 2 + j) * 16
            g1s[j, i, 48:64] = wide[at:at + 16] if at < 96 else jnp.zeros((16, 384), BF16)

    def sum_of(ref, count, rows):
        total = ref[0, rows].astype(F32)
        for o in range(1, count):
            total = total + ref[o, rows].astype(F32)
        return total.astype(BF16)

    def add_pair(mine, other, out):
        def body(o, carry):
            out[o] = (mine[core, o].astype(F32) + other[o].astype(F32)).astype(BF16)
            return carry

        lax.fori_loop(0, NCHIP, body, 0)

    others = pl.ds(0, NCHIP - 1)
    to_core(g1s.at[1 - core], g1p, 5).start()

    ds_s[...] = jnp.zeros_like(ds_s)

    def attend_back(pair, carry):
        lw = lax.rem(pair, 2)
        for i in range(2):
            rows = window_rows(2 * pair + i)
            dam[i] = stacked(ga_s[rows, :])
            raw[i] = dot_nt(v_s[rows, :], dam[i])
        for i in range(2):
            for t in range(WIDE // 128):
                cols = slice(t * 128, (t + 1) * 128)
                chances = p_s[2 * pair + i, :, cols].astype(F32)
                weighted = raw[i, :, cols]
                centre = jnp.sum(chances * weighted, axis=0, keepdims=True)
                dsh[i, :, cols] = (chances * (weighted - centre)).astype(BF16)
        for i in range(2):
            rows = window_rows(2 * pair + i)
            dv_s[rows, :] = dot_nn(p_s[2 * pair + i], dam[i]).astype(BF16)
            dq_s[rows, :] = (unstacked(dot_tn(k_s[rows, :], dsh[i])) * FACTOR).astype(BF16)
            dk_s[rows, :] = (dot_nn(dsh[i], stacked(q_s[rows, :])) * FACTOR).astype(BF16)
        ds_s[lw] = ds_s[lw] + (dsh[0].astype(F32) + dsh[1].astype(F32))
        return carry

    all_rows = slice(0, 64)
    def windows_back(pair, carry):
        attend_back(pair, carry)

        @pl.when(pair == 0)
        def _():
            arrived(g1p, 5)
            add_pair(g1s, g1p, g1h)
            g1r[chip] = g1h[chip]
            chips_all(lambda o: to_chip(g1h.at[o], g1r.at[chip], 6, o).start())

        @pl.when(pair == 2)
        def _():
            arrived(g1r.at[others], 6)
            g1l[d] = sum_of(g1r, NCHIP, all_rows)
            lat_all(lambda o: to_band(g1l.at[d], g1l.at[d], 7, o).start())

        return carry

    lax.fori_loop(0, NWIN // 2, windows_back, 0)
    arrived(g1l.at[others], 7)
    g1f[chip] = sum_of(g1l, NLAT, all_rows)
    chips_all(lambda o: to_chip(g1f.at[chip], g1f.at[chip], 8, o).start())

    ni = ni_s[...]
    g_triple = jnp.concatenate(
        [dot_tn(ni, dq_s[...]), dot_tn(ni, dk_s[...]), dot_tn(ni, dv_s[...]), jnp.zeros((C, 64), F32)], axis=1
    ).astype(BF16)
    for i in range(3):
        for j in range(5):
            at = 5 * i + j
            g2s[at // 8, at % 8, 0:64] = g_triple[i * 64:(i + 1) * 64, j * 128:(j + 1) * 128]
    g2s[1, 7, 0:64] = jnp.zeros((64, 128), BF16)
    for lw in range(2):
        for h in range(HEADS):
            at = pl.ds(h * 2 + lw, WIN, stride=16)
            part = ds_s[lw, :, h * WIN:(h + 1) * WIN].T
            bs_s.at[0][at, :] = part[:, 0:128]
            bs_s.at[1][at, :] = jnp.concatenate([part[:, 128:144], jnp.zeros((WIN, 112), F32)], axis=1)

    def fold(s_i, carry):
        at = pl.ds(pl.multiple_of(s_i * 192, 192), 192)
        rows = jnp.concatenate([bs_s[0, at, :], bs_s[1, at, :]], axis=1)[:, 0:WIN].astype(BF16)
        return carry + dot_nt(rows, spread_s[s_i])

    folded = lax.fori_loop(0, 12, fold, jnp.zeros((192, 512), F32))
    pieces_t = []
    for p in range(2):
        for pk in range(2):
            for r in range(6):
                at = (p * 6 + r) * 16
                pieces_t.append(folded[at:at + 16, pk * 256:pk * 256 + 138])
    table = jnp.concatenate(pieces_t + [jnp.zeros((16, 4096 - POS), F32)], axis=1).astype(BF16)
    for o in range(32):
        g2s[o // 16, (o // 2) % 8, 64 + 16 * (o % 2):80 + 16 * (o % 2)] = table[:, o * 128:(o + 1) * 128]
    to_core(g2s.at[1 - core], g2p, 9).start()

    def project_back(i, carry):
        rows = chunk_rows(i)
        tmp[...] = (
            dot_nt(dq_s[rows, :], wq[...]) + dot_nt(dk_s[rows, :], wk[...]) + dot_nt(dv_s[rows, :], wv[...])
        )
        for t in range(CHUNK // TILE):
            part = tile_rows(i, t)
            unit, inverse = statistics(x_w[part, :].astype(F32))
            back = norm_back(unit, inverse, tmp[t * TILE:(t + 1) * TILE, :] * attend_gain[...])
            gt_s[part, :] = (gm_s[part, :] + back).astype(BF16)
        return carry

    def chunks_back(i, carry):
        project_back(i, carry)

        @pl.when(i == 0)
        def _():
            arrived(g2p, 9)
            add_pair(g2s, g2p, g2h)
            g2r[chip] = g2h[chip]
            chips_all(lambda o: to_chip(g2h.at[o], g2r.at[chip], 10, o).start())

        return carry

    lax.fori_loop(0, NCHUNK, chunks_back, 0)

    from_window = one_hot(2 * QROWS, orders[3:4, 0:PAIR])

    def unsort_window(i, carry):
        quads = dot_nn(from_window, gt_s[sample_rows(i, PAIR), :]).astype(BF16)
        gq[pl.ds(2 * i, 2)] = quads.reshape(2, QROWS, C)
        return carry

    lax.fori_loop(0, 4, unsort_window, 0)
    back_copies = halo(gq, hq, back_ss, back_rs, (e_up, d_up))
    for copy in back_copies:
        copy.start()

    arrived(g1f.at[others], 8)
    to_core(g1f, g1o, 11).start()

    arrived(g2r.at[others], 10)
    g2l[d] = sum_of(g2r, NCHIP, slice(0, 64))
    lat_all(lambda o: to_band(g2l.at[d], g2l.at[d], 12, o).start())
    g2f[chip, 64:96] = sum_of(g2r, NCHIP, slice(64, 96))

    to_natural = one_hot(LEVEL, orders[1:2, 0:QROWS])
    for copy in back_copies:
        copy.wait()
    hq[:, 0:64, :] = gq[:, 0:64, :]

    arrived(g2l.at[others], 12)
    g2f[chip, 0:64] = sum_of(g2l, NLAT, slice(0, 64))
    chips_all(lambda o: to_chip(g2f.at[chip], g2f.at[chip], 13, o).start())


    def unsort_level(i, carry):
        out_fields[sample_rows(i, LEVEL), :] = dot_nn(to_natural, hq[shifted_level(i)]).astype(BF16)
        return carry

    lax.fori_loop(0, 8, unsort_level, 0)
    arrived(g1o, 11)
    out_g1[core] = g1f[...]
    out_g1[1 - core] = g1o[...]
    arrived(g2f.at[others], 13)
    to_core(g2f, g2o, 14).start()
    out_g2[core] = g2f[...]
    arrived(g2o, 14)
    out_g2[1 - core] = g2o[...]

    left(cs.at[others], 0)
    left(wa.at[others], 1)
    left(cf, 2)
    left(wb, 3)
    left(ch, 4)
    left(g1p, 5)
    left(g1r.at[others], 6)
    left(g1l.at[others], 7)
    left(g1f.at[others], 8)
    left(g2p, 9)
    left(g2r.at[others], 10)
    left(g1o, 11)
    left(g2l.at[others], 12)
    left(g2f.at[others], 13)
    left(g2o, 14)


def results_kernel(
    fields, g1, g2, attend_gain, triple_w, feed_gain, expand_w,
    out_fields, out_triple, out_output, out_expand, out_shrink, out_attend, out_feed, out_table,
):
    out_fields[...] = fields[...]
    for i in range(4):
        for j in range(2):
            rows, cols = slice(i * 48, (i + 1) * 48), slice(j * 384, (j + 1) * 384)
            out_expand[rows, cols] = g1[0, 2 * i + j, 0:48].astype(F32)
            out_shrink[rows, cols] = g1[1, 2 * i + j, 0:48].astype(F32)
    for i in range(6):
        wide = g1[i % 2, i // 2, 48:64].astype(F32)
        out_output[i * 16:(i + 1) * 16, :] = wide[:, 0:C]
        out_output[96 + i * 16:96 + (i + 1) * 16, :] = wide[:, C:2 * C]
    for i in range(3):
        for j in range(5):
            at, size = 5 * i + j, 128 if j < 4 else 64
            part = g2[at // 8, at % 8, 0:64].astype(F32)
            out_triple[i * 64:(i + 1) * 64, j * 128:j * 128 + size] = part[:, 0:size]
    table = jnp.concatenate(
        [g2[o // 16, (o // 2) % 8, 64 + 16 * (o % 2):80 + 16 * (o % 2)] for o in range(32)], axis=1
    ).astype(F32)
    for h in range(HEADS):
        out_table[h] = table[2 * h:2 * h + 2, 0:POS]

    def gain_gradient(grad, weight, gain):
        product = (grad[...] * weight[...].astype(F32)).astype(BF16)
        total = dot_nt(jnp.ones((16, product.shape[1]), BF16), product)
        return total[0:1] / gain[...]

    out_attend[...] = gain_gradient(out_triple, triple_w, attend_gain)
    out_feed[...] = gain_gradient(out_expand, expand_w, feed_gain)


def scratch():
    def vmem(*shape, kind=BF16):
        return pltpu.VMEM(shape, kind)

    token = vmem(TOK, C)
    token_f = vmem(TOK, C, kind=F32)
    weight = vmem(C, C)
    quad = vmem(8, QROWS, C)
    stat = vmem(WIN, 128, kind=F32)
    small = vmem(2, 24, 128, kind=F32)
    buffers = [
        quad, quad, quad, quad, token, token, token, token, token, weight, weight, weight,
        vmem(NWIN, WIN, WIDE), token, token_f, token, vmem(TOK, FF), vmem(TOK, FF, kind=F32), token,
        vmem(16, POS, kind=F32), vmem(576, 512), vmem(2, 2304, 128, kind=F32),
        vmem(2, WIN, WIDE, kind=F32), vmem(2, WIN, WIDE, kind=F32),
        vmem(12, 512, WIN), vmem(2, WIN, 384),
        vmem(576, 256, kind=F32), vmem(8, 2, 3, 32, 128), vmem(2, 8, 3, 32, 128), vmem(8, 3, 32, 128), vmem(2, 8, 2, 32, 128),
        vmem(8, 32, 768), vmem(8, 32, 768),
        vmem(12, 128, C), token, vmem(2, WIN, 128, kind=F32), stat, small, small, small, small, vmem(4, WIN, 128, kind=F32),
        token, vmem(TOK, FF), token_f, token, token, token, token, token, token,
        vmem(2, WIN, WIDE, kind=F32), vmem(2, WIN, WIDE), vmem(2, WIDE, C), vmem(CHUNK, FF, kind=F32),
        vmem(CHUNK, C, kind=F32),
    ]
    for rows, cols in ((64, 384), (96, 128)):
        chunks = vmem(8, rows, cols)
        buffers += [vmem(2, 8, rows, cols), chunks, chunks, chunks, vmem(8, 64, cols), chunks, chunks]
    counts = [3, 3, 3, 3, 4, 4, 15, 15]
    return buffers + [pltpu.SemaphoreType.DMA((n,)) for n in counts]


def per_device(
    fields, merge_cotangent, attend_gain, triple_weight, bias_table, output_weight, feed_gain,
    expand_weight, shrink_weight, merge_gain, merge_weight,
):
    cot = jnp.transpose(merge_cotangent, (1, 2, 3, 4, 0)).reshape(576, 192)
    bias = jnp.transpose(bias_table[0], (1, 0, 2))
    def shaped(shapes):
        return [jax.ShapeDtypeStruct(shape, kind) for shape, kind in shapes]

    vmem_spec = pl.BlockSpec(memory_space=pltpu.VMEM)
    parts = pl.pallas_call(
        kernel,
        out_shape=shaped(
            [((TOK, C), BF16), ((2, 8, 64, 384), BF16), ((2, 8, 96, 128), BF16)]
        ),
        in_specs=[vmem_spec] * 12,
        out_specs=[vmem_spec] * 3,
        scratch_shapes=scratch(),
        compiler_params=pltpu.CompilerParams(
            collective_id=0, has_side_effects=True, vmem_limit_bytes=60 * 1024 * 1024
        ),
    )(
        fields.reshape(TOK, C), cot, attend_gain.reshape(1, C), triple_weight, bias, output_weight,
        feed_gain.reshape(1, C), expand_weight, shrink_weight.T, merge_gain,
        merge_weight.T, jnp.asarray(order_indices()),
    )
    g_fields, g_triple, g_output, g_expand, g_shrink, g_attend, g_feed, g_table = pl.pallas_call(
        results_kernel,
        out_shape=shaped(
            [
                ((TOK, C), BF16), ((C, 3 * C), F32), ((C, C), F32), ((C, FF), F32), ((C, FF), F32),
                ((1, C), F32), ((1, C), F32), ((HEADS, 2, POS), F32),
            ]
        ),
        in_specs=[vmem_spec] * 7,
        out_specs=[vmem_spec] * 8,
        compiler_params=pltpu.CompilerParams(vmem_limit_bytes=60 * 1024 * 1024),
    )(*parts, attend_gain.reshape(1, C), triple_weight, feed_gain.reshape(1, C), expand_weight)
    return (
        g_fields.reshape(fields.shape), g_triple, g_output, g_expand, g_shrink.T,
        g_attend.reshape(C), g_feed.reshape(C), jnp.transpose(g_table, (1, 0, 2))[None],
    )


def solution(mesh):
    placed = (
        P(None, None, "lat", "lon", None),
        P(None, None, None, "lat", "lon"),
        P(),
        P(),
        P("lat", None, None, None),
        P(),
        P(),
        P(),
        P(),
        P(),
        P(None, "lon"),
    )
    return jax.shard_map(
        per_device,
        mesh=mesh,
        in_specs=placed,
        out_specs=(
            P(None, None, "lat", "lon", None),
            P(),
            P(),
            P(),
            P(),
            P(),
            P(),
            P("lat", None, None, None),
        ),
        check_vma=False,
    )
```

```python
import functools
import math

import jax
import jax.numpy as jnp
import numpy as np
from jax import lax
from jax.experimental import pallas as pl
from jax.experimental.pallas import tpu as pltpu
from jax.sharding import PartitionSpec as P

F32 = jnp.float32
BF16 = jnp.bfloat16
I32 = jnp.int32
MESH = pl.DeviceIdType.MESH

EPS = 1e-05
MASKED = -1000000000.0
NLON = 16
NLAT = 8
NCHIP = 8
C = 192
HEADS = 6
FF = 768
WIN = 144
NWIN = 8
TOK = WIN * NWIN
HALF = TOK // 2
SIZES = (216, 72, 72)
POS = 3312
CHUNK = 288
NCHUNK = TOK // CHUNK
TILE = 48
WIDE = 896
FACTOR = 32 ** -0.5


def order_indices():
    natural_to_quad = np.full(640, -1, np.int32)
    quad_to_natural = np.full(640, -1, np.int32)
    quad_to_window = np.full(640, -1, np.int32)
    window_to_quad = np.full(640, -1, np.int32)
    for level in range(4):
        for row in range(6):
            for col in range(24):
                source = (level * 6 + row) * 24 + col
                if col >= 6:
                    place = (0 if row >= 3 else 216) + level * 54 + (row % 3) * 18 + col - 6
                else:
                    place = (432 if row >= 3 else 504) + level * 18 + (row % 3) * 6 + col
                natural_to_quad[source] = place
                quad_to_natural[place] = source
    index = 0
    for lev_win in range(2):
        for lon_win in range(2):
            for s in range(12):
                for p in range(2):
                    for r in range(6):
                        level = (lev_win * 2 + p + 1) % 4
                        col = lon_win * 12 + s
                        if col < 18:
                            place = (0 if r < 3 else 216) + level * 54 + (r % 3) * 18 + col
                        else:
                            place = (432 if r < 3 else 504) + level * 18 + (r % 3) * 6 + col - 18
                        window_to_quad[index] = place
                        quad_to_window[place] = index
                        index += 1
    cell_lane = np.full(640, -1, np.int32)
    bias_row = np.full(640, -1, np.int32)
    merged_token = np.full((2, 640), -1, np.int32)
    for lane in range(256):
        if lane % 16 < 12:
            cell_lane[lane] = (12 * (lane // 16) + 3 + lane % 16) % 192
    for k in range(WIN):
        s, p, r = k // 12, (k // 6) % 2, k % 6
        bias_row[k] = p * 256 + r * 23 + 11 - s
    for lon_win in range(2):
        for row in range(384):
            p, r, y, m = row // 192, (row // 32) % 6, (row // 16) % 2, row % 16
            if 0 <= m - lon_win * 6 < 6:
                merged_token[lon_win, row] = (2 * (m - lon_win * 6) + y) * 12 + p * 6 + r
    rows = [natural_to_quad, quad_to_natural, quad_to_window, window_to_quad]
    return np.stack(rows + [cell_lane, bias_row, merged_token[0], merged_token[1]])


def dot_nn(a, b):
    return lax.dot_general(a, b, (((1,), (0,)), ((), ())), preferred_element_type=F32)


def dot_nt(a, b):
    return lax.dot_general(a, b, (((1,), (1,)), ((), ())), preferred_element_type=F32)


def dot_tn(a, b):
    return lax.dot_general(a, b, (((0,), (0,)), ((), ())), preferred_element_type=F32)


def one_hot(rows, targets):
    ids = lax.broadcasted_iota(I32, (rows, targets.shape[1]), 0)
    return jnp.where(ids == targets, 1.0, 0.0).astype(BF16)


def statistics(values):
    centred = values - jnp.mean(values, axis=-1, keepdims=True)
    inverse = lax.rsqrt(jnp.mean(centred * centred, axis=-1, keepdims=True) + EPS)
    return centred * inverse, inverse


def norm_back(normed, inverse, scaled):
    centre = jnp.mean(scaled, axis=-1, keepdims=True)
    projected = jnp.mean(scaled * normed, axis=-1, keepdims=True)
    return inverse * (scaled - centre - normed * projected)


def gelu_parts(values):
    cumulative = 0.5 * (1.0 + lax.erf(values * (1.0 / math.sqrt(2.0))))
    density = jnp.exp(-0.5 * values * values) * (1.0 / math.sqrt(2.0 * math.pi))
    return values * cumulative, cumulative + values * density


def lanes(rows, cols):
    return lax.broadcasted_iota(I32, (rows, cols), 1)


def over_12(ids):
    return (ids * 5462) >> 16


def over_6(ids):
    return (ids * 10923) >> 16


def kernel(
    fields, cot, attend_gain, triple_w, bias, output_w, feed_gain, expand_w, shrink_t, merge_gain,
    merge_wt, orders,
    out_fields, out_g1, out_g2,
    sq, gq, a10, a01, a11, b10, b01, b11, c10, c01, c11, d10, d01, d11, x_w, ni_s, q_s, k_s, v_s, wq, wk, wv, p_s, att_s, mid_s, nm_s, act_s, slope_s, vo_s,
    b16, bl_s, bs_s, bx, ds_s, spread_s, pick_s,
    cells, cs, cb, cf, ch, wa, wb, qry, qw, st, sx, sup, sdn, tup, tdn, cp_s, go_s, gh_s, gm_s, ga_s, gmh_s,
    dq_s, dk_s, dv_s, gt_s, raw, dsh, dam, hid, tmp, g1s, g1p, g1h, g1r, g1l, g1f, g1o, g2s, g2p, g2h, g2r, g2l, g2f, g2o,
    halo_ss, halo_rs, back_ss, back_rs, st_ss, st_rs, sends, recvs,
):
    e = lax.axis_index("lon")
    d = lax.axis_index("lat")
    e_up, e_dn = lax.rem(e + 1, NLON), lax.rem(e + NLON - 1, NLON)
    d_up, d_dn = lax.rem(d + 1, NLAT), lax.rem(d + NLAT - 1, NLAT)

    def remote(src, dst, ssem, rsem, device):
        return pltpu.make_async_remote_copy(
            src_ref=src, dst_ref=dst, send_sem=ssem, recv_sem=rsem, device_id=device,
            device_id_type=MESH,
        )

    core, chip = lax.rem(e, 2), e // 2
    partner = e + 1 - 2 * core

    def chips_all(action):
        def body(step, carry):
            action(lax.rem(chip + step, NCHIP))
            return carry

        lax.fori_loop(1, NCHIP, body, 0)

    def lat_all(action):
        def body(step, carry):
            action(lax.rem(d + step, NLAT))
            return carry

        lax.fori_loop(1, NLAT, body, 0)

    def to_chip(src, dst, phase, o):
        return remote(src, dst, sends.at[phase], recvs.at[phase], (2 * o + core, d))

    def to_band(src, dst, phase, o):
        return remote(src, dst, sends.at[phase], recvs.at[phase], (e, o))

    def to_core(src, dst, phase):
        return remote(src, dst, sends.at[phase], recvs.at[phase], (partner, d))

    def arrived(region, phase):
        remote(region, region, sends.at[phase], recvs.at[phase], (partner, d)).wait_recv()

    def left(region, phase):
        remote(region, region, sends.at[phase], recvs.at[phase], (partner, d)).wait_send()

    barrier = pltpu.get_barrier_semaphore()

    def greet(device):
        pl.semaphore_signal(barrier, inc=1, device_id=device, device_id_type=MESH)

    chips_all(lambda o: greet((2 * o + core, d)))
    lat_all(lambda o: greet((e, o)))
    for device in ((e_up, d), (e_dn, d), (e_up, d_up), (e_dn, d_dn)):
        greet(device)

    def half_rows(b):
        return pl.ds(pl.multiple_of(b * HALF, HALF), HALF)

    def pack(quads, out):
        at = 216
        for size, message in zip(SIZES, out):
            first, second = quads[0, at:at + size, :], quads[1, at:at + size, :]
            tails = jnp.concatenate([first[:, 128:C], second[:, 128:C]], axis=1)
            parts = [first[:, 0:128], second[:, 0:128], tails, jnp.zeros((8, 128), F32)]
            message[...] = jnp.concatenate(parts, axis=0).astype(BF16)
            at += size

    def unpack(quads, messages):
        at = 216
        for size, message in zip(SIZES, messages):
            rows = message[...].astype(F32)
            tails = rows[2 * size:3 * size]
            quads[0, at:at + size, :] = jnp.concatenate([rows[0:size], tails[:, 0:64]], axis=1)
            quads[1, at:at + size, :] = jnp.concatenate([rows[size:2 * size], tails[:, 64:128]], axis=1)
            at += size

    to_quad = one_hot(HALF, orders[0:1, 0:HALF])

    def sort_sample(b, carry):
        sq[b] = dot_nn(to_quad, fields[half_rows(b), :])
        return carry

    lax.fori_loop(0, 2, sort_sample, 0)
    pack(sq, (a10, a01, a11))
    pl.semaphore_wait(barrier, NCHIP - 1 + NLAT - 1 + 4)

    def halo(sources, targets, ssem, rsem, step):
        devices = ((e, step[1]), (step[0], d), (step[0], step[1]))
        return [
            remote(src, dst, ssem.at[i], rsem.at[i], dev)
            for i, (src, dst, dev) in enumerate(zip(sources, targets, devices))
        ]

    halo_copies = halo((a10, a01, a11), (b10, b01, b11), halo_ss, halo_rs, (e_dn, d_dn))
    for copy in halo_copies:
        copy.start()

    cells[...] = dot_nn(cot[...], one_hot(192, orders[4:5, 0:256]))
    block_of = lanes(72, 128) >> 4

    def gather_cells(o, carry):
        tile = pl.ds(pl.multiple_of((o // 8) * 128, 128), 128)
        inner = lax.rem(o, 8)
        piece = jnp.zeros((72, 128), F32)
        for bl in range(8):
            part = pltpu.roll(cells[bl * 72:(bl + 1) * 72, tile], lax.rem(16 * (bl - inner) + 128, 128), 1)
            piece = jnp.where(block_of == bl, part, piece)
        for a in range(3):
            padded = jnp.concatenate([piece[a * 24:(a + 1) * 24], jnp.zeros((8, 128), F32)], axis=0)
            cs[o // 2, lax.rem(o, 2), a] = padded.astype(BF16)
        return carry

    lax.fori_loop(0, NLON, gather_cells, 0)
    wa[chip] = jnp.concatenate(
        [merge_wt[...].astype(F32), jnp.zeros((8, 768), F32)], axis=0
    ).astype(BF16)
    cb[:, chip] = cs[chip]
    for h in range(HEADS):
        b16[2 * h:2 * h + 2, :] = bias[h]
    b16[12:16, :] = jnp.zeros((4, POS), F32)
    zero_tail = jnp.zeros((16, 256 - 138), F32)
    for p in range(2):
        for r in range(6):
            parts = []
            for pk in range(2):
                at = (p * 2 + pk) * 828 + r * 138
                parts += [b16[:, at:at + 138], zero_tail]
            row = jnp.concatenate(parts, axis=1)
            high = row.astype(BF16)
            rest = row - high.astype(F32)
            middle = rest.astype(BF16)
            low = (rest - middle.astype(F32)).astype(BF16)
            at = (p * 6 + r) * 16
            bl_s[at:at + 16, :] = high
            bl_s[192 + at:192 + at + 16, :] = middle
            bl_s[384 + at:384 + at + 16, :] = low

    bias_row = orders[5:6, 0:WIN]

    def spread(s_i, carry):
        matrix = one_hot(512, bias_row + s_i)
        spread_s[s_i] = matrix
        split = dot_nn(bl_s[...], matrix)
        rows = split[0:192] + split[192:384] + split[384:576]
        at = pl.ds(pl.multiple_of(s_i * 192, 192), 192)
        bs_s[0, at, :] = rows[:, 0:128]
        bs_s[1, at, :] = jnp.concatenate([rows[:, 128:144], jnp.zeros((192, 112), F32)], axis=1)
        return carry

    lax.fori_loop(0, 12, spread, 0)

    tok_i = lax.broadcasted_iota(I32, (WIN, WIN), 0)
    tok_k = lax.broadcasted_iota(I32, (WIN, WIN), 1)
    half_i, half_k = over_6(tok_i), over_6(tok_k)
    last_band = d == NLAT - 1
    lat_differs = ((tok_i - half_i * 6 >= 3) != (tok_k - half_k * 6 >= 3)) & last_band
    lev_differs = (half_i & 1) != (half_k & 1)
    bx[:, :, HEADS * WIN:WIDE] = jnp.zeros((2, WIN, WIDE - HEADS * WIN), F32)
    for lw in range(2):
        differs = (lat_differs | lev_differs) if lw else lat_differs
        for h in range(HEADS):
            at = pl.ds(h * 2 + lw, WIN, stride=16)
            full = jnp.concatenate([bs_s.at[0][at, :], bs_s.at[1][at, :]], axis=1)[:, 0:WIN]
            bx[lw, :, h * WIN:(h + 1) * WIN] = jnp.where(differs, MASKED, full).T

    wq[...] = triple_w[:, 0:192]
    wk[...] = triple_w[:, 192:384]
    wv[...] = triple_w[:, 384:576]

    head_of = lanes(1, C) >> 5
    head_f = [jnp.where(head_of == h, 1.0, 0.0) for h in range(HEADS)]
    head_b = [mask.astype(BF16) for mask in head_f]

    blank = jnp.zeros((WIDE - HEADS * WIN, C), BF16)

    def stacked(values):
        return jnp.concatenate([values * mask for mask in head_b] + [blank], axis=0)

    def unstacked(values):
        blocks = [values[h * 32:(h + 1) * 32, h * WIN:(h + 1) * WIN] for h in range(HEADS)]
        return jnp.concatenate(blocks, axis=0).T

    to_window = one_hot(HALF, orders[2:3, 0:HALF])
    for copy in halo_copies:
        copy.wait()
    chips_all(lambda o: to_chip(cs.at[o], cb.at[:, chip], 0, o).start())
    chips_all(lambda o: to_chip(wa.at[chip], wa.at[chip], 1, o).start())
    unpack(sq, (b10, b01, b11))

    def sort_window(b, carry):
        x_w[half_rows(b), :] = dot_nn(to_window, sq[b].astype(BF16)).astype(BF16)
        return carry

    lax.fori_loop(0, 2, sort_window, 0)

    def window_rows(w):
        return pl.ds(pl.multiple_of(w * WIN, WIN), WIN)

    def chunk_rows(i):
        return pl.ds(pl.multiple_of(i * CHUNK, CHUNK), CHUNK)

    def tile_rows(i, t):
        return pl.ds(pl.multiple_of(i * CHUNK + t * TILE, 16), TILE)

    def project(i, carry):
        rows = chunk_rows(i)
        for t in range(CHUNK // TILE):
            part = tile_rows(i, t)
            normed = statistics(x_w[part, :].astype(F32))[0]
            ni_s[part, :] = (normed * attend_gain[...]).astype(BF16)
        normed_in = ni_s[rows, :]
        q_s[rows, :] = dot_nn(normed_in, wq[...]).astype(BF16)
        k_s[rows, :] = dot_nn(normed_in, wk[...]).astype(BF16)
        v_s[rows, :] = dot_nn(normed_in, wv[...]).astype(BF16)
        return carry

    lax.fori_loop(0, NCHUNK, project, 0)

    arrived(cb.at[:, pl.ds(0, NCHIP - 1)], 0)
    to_core(cb.at[1 - core], cf, 2).start()
    arrived(wa.at[pl.ds(0, NCHIP - 1)], 1)
    to_core(wa, wb, 3).start()

    def attend(pair, carry):
        lw = lax.rem(pair, 2)
        for i in range(2):
            rows = window_rows(2 * pair + i)
            raw[i] = dot_nt(k_s[rows, :], stacked(q_s[rows, :]))
        for i in range(2):
            for t in range(WIDE // 128):
                cols = slice(t * 128, (t + 1) * 128)
                scores = raw[i, :, cols] * FACTOR + bx[lw, :, cols]
                exponent = jnp.exp(scores - jnp.max(scores, axis=0, keepdims=True))
                chances = exponent * (1.0 / jnp.sum(exponent, axis=0, keepdims=True))
                p_s[2 * pair + i, :, cols] = chances.astype(BF16)
        for i in range(2):
            rows = window_rows(2 * pair + i)
            att_s[rows, :] = unstacked(dot_tn(v_s[rows, :], p_s[2 * pair + i])).astype(BF16)
        return carry

    lax.fori_loop(0, NWIN // 2, attend, 0)

    arrived(cf, 2)
    first_rows = pl.ds(0, 2)
    to_band(cb.at[core, :, first_rows], ch.at[0], 4, d_dn).start()
    to_band(cf.at[:, first_rows], ch.at[1], 4, d_dn).start()

    def feed(i, carry):
        rows = chunk_rows(i)
        tmp[...] = x_w[rows, :].astype(F32) + dot_nn(att_s[rows, :], output_w[...])
        for t in range(CHUNK // TILE):
            part = tile_rows(i, t)
            middle = tmp[t * TILE:(t + 1) * TILE, :]
            mid_s[part, :] = middle
            nm_s[part, :] = (statistics(middle)[0] * feed_gain[...]).astype(BF16)
        hid[...] = dot_nn(nm_s[rows, :], expand_w[...])
        for t in range(CHUNK // 16):
            part = pl.ds(pl.multiple_of(i * CHUNK + t * 16, 16), 16)
            for j in range(FF // 256):
                cols = slice(j * 256, (j + 1) * 256)
                act, slope = gelu_parts(hid[t * 16:(t + 1) * 16, cols])
                act_s[part, cols] = act.astype(BF16)
                slope_s[part, cols] = slope
        vo_s[rows, :] = (tmp[...] + dot_nt(act_s[rows, :], shrink_t[...])).astype(BF16)
        return carry

    arrived(ch, 4)
    arrived(wb, 3)
    gain_row = merge_gain[...].reshape(1, 4 * C)
    for r in range(6):
        x = (r + 1) % 2
        cell = (0, 1, 1, 2, 2, 3)[r]
        cols = slice(x * 384, (x + 1) * 384)
        if cell < 2:
            planes = cb[core, :, cell + 1], cf[:, cell + 1]
        else:
            planes = ch[0, :, cell - 2], ch[1, :, cell - 2]
        summed = dot_tn(planes[0].reshape(256, 128), wa[:, :, cols].reshape(256, 384))
        summed = summed + dot_tn(planes[1].reshape(256, 128), wb[:, :, cols].reshape(256, 384))
        scaled = summed * gain_row[:, x * 384:(x + 1) * 384]
        qry[2 * r] = scaled[:, 0:192].astype(BF16)
        qry[2 * r + 1] = scaled[:, 192:384].astype(BF16)

    st[...] = jnp.zeros_like(st)
    for i in range(2):
        pick_s[i] = one_hot(WIN, orders[6 + i:7 + i, 0:384])
    stat_lane = lanes(WIN, 128)
    tile_lane = lanes(TILE, 128)

    def merge_sums(w, carry):
        rows = window_rows(w)
        b, lw, lon_win = w // 4, lax.rem(w // 2, 2), lax.rem(w, 2)
        parts = []
        for p in range(2):
            level = lax.rem(lw * 2 + p + 1, 4)
            at = pl.ds(pl.multiple_of((b * 4 + level) * 16, 16), 16)
            parts.append(qry[:, at, :].reshape(192, C))
        qw[rows, :] = dot_nn(pick_s[lon_win], jnp.concatenate(parts, axis=0)).astype(BF16)
        for t in range(WIN // TILE):
            part = pl.ds(pl.multiple_of(w * WIN + t * TILE, 16), TILE)
            at = slice(t * TILE, (t + 1) * TILE)
            q = qw[part, :].astype(F32)
            v = vo_s[part, :].astype(F32)
            mean = jnp.mean(v, axis=-1, keepdims=True)
            centred = v - mean
            squares = jnp.sum(centred * centred, axis=-1, keepdims=True)
            q_sum = jnp.sum(q, axis=-1, keepdims=True)
            qv_sum = jnp.sum(q * centred, axis=-1, keepdims=True)
            total = st[b, at, :]
            for j, value in enumerate((mean, squares, q_sum, qv_sum)):
                total = jnp.where(tile_lane == 32 * j + w, value, total)
            st[b, at, :] = total
        return carry

    def sums_copies(b):
        return (
            remote(tup.at[b], sup.at[b], st_ss.at[2 * b], st_rs.at[2 * b], (e, d_up)),
            remote(tdn.at[b], sdn.at[b], st_ss.at[2 * b + 1], st_rs.at[2 * b + 1], (e, d_dn)),
        )

    def exchange(b):
        tup[b] = st.at[b][pl.ds(5, 24, stride=6), :]
        tdn[b] = st.at[b][pl.ds(0, 24, stride=6), :]
        for copy in sums_copies(b):
            copy.start()

    even = (over_12(lax.broadcasted_iota(I32, (WIN, 128), 0)) & 1) == 0

    def pair_of(values):
        return jnp.where(even, pltpu.roll(values, WIN - 12, 0), pltpu.roll(values, 12, 0))

    def cell_norm(b):
        for r, other in ((1, 2), (2, 1), (3, 4), (4, 3)):
            sx[pl.ds(r, 24, stride=6), :] = st.at[b][pl.ds(other, 24, stride=6), :]
        for copy in sums_copies(b):
            copy.wait()
        sx[pl.ds(0, 24, stride=6), :] = sup[b]
        sx[pl.ds(5, 24, stride=6), :] = sdn[b]
        own, cross = st[b], sx[...]
        group = [own, cross, pair_of(own), pair_of(cross)]
        cell_mean = (group[0] + group[1] + group[2] + group[3]) * 0.25
        variance = jnp.zeros((WIN, 128), F32)
        q_total = jnp.zeros((WIN, 128), F32)
        qv_total = jnp.zeros((WIN, 128), F32)
        for values in group:
            offset = values - cell_mean
            q_sum = pltpu.roll(values, 64, 1)
            variance = variance + pltpu.roll(values, 96, 1) + 192.0 * offset * offset
            q_total = q_total + q_sum
            qv_total = qv_total + pltpu.roll(values, 32, 1) + offset * q_sum
        cell_inverse = lax.rsqrt(jnp.where(stat_lane < 8, variance, 0.0) * (1.0 / 768.0) + EPS)
        cp_s[0] = cell_mean
        cp_s[1] = cell_inverse
        cp_s[2] = q_total * (1.0 / 768.0)
        cp_s[3] = cell_inverse * cell_inverse * qv_total * (1.0 / 768.0)

    def merge_back(w, carry):
        for t in range(WIN // TILE):
            part = pl.ds(pl.multiple_of(w * WIN + t * TILE, 16), TILE)
            at = slice(t * TILE, (t + 1) * TILE)
            mean, inverse, q_mean, projected = [
                jnp.sum(jnp.where(tile_lane == w, cp_s[j, at, :], 0.0), axis=-1, keepdims=True) for j in range(4)
            ]
            v = vo_s[part, :].astype(F32) - mean
            go_s[part, :] = (inverse * (qw[part, :].astype(F32) - q_mean - v * projected)).astype(BF16)
        return carry

    def feed_back(i, carry):
        rows = chunk_rows(i)
        go = go_s[rows, :]
        gh = (dot_nn(go, shrink_t[...]) * slope_s[rows, :]).astype(BF16)
        gh_s[rows, :] = gh
        tmp[...] = dot_nt(gh, expand_w[...])
        for t in range(CHUNK // TILE):
            part = tile_rows(i, t)
            gnm = tmp[t * TILE:(t + 1) * TILE, :]
            unit, inverse = statistics(mid_s[part, :])
            gm = go_s[part, :].astype(F32) + norm_back(unit, inverse, gnm * feed_gain[...])
            gm_s[part, :] = gm
            gmh_s[part, :] = gm.astype(BF16)
        ga_s[rows, :] = dot_nt(gmh_s[rows, :], output_w[...]).astype(BF16)
        return carry

    def forward_sample(b, carry):
        lax.fori_loop(2 * b, 2 * b + 2, feed, 0)
        lax.fori_loop(4 * b, 4 * b + 4, merge_sums, 0)
        exchange(b)
        return carry

    def backward_sample(b, carry):
        cell_norm(b)
        lax.fori_loop(4 * b, 4 * b + 4, merge_back, 0)
        lax.fori_loop(2 * b, 2 * b + 2, feed_back, 0)
        return carry

    lax.fori_loop(0, 2, forward_sample, 0)
    lax.fori_loop(0, 2, backward_sample, 0)

    g_expand = dot_tn(nm_s[...], gh_s[...]).astype(BF16)
    g_shrink = dot_tn(go_s[...], act_s[...]).astype(BF16)
    g_output = dot_tn(att_s[...], gmh_s[...]).astype(BF16)
    for i in range(4):
        for j in range(2):
            g1s[0, 2 * i + j, 0:48] = g_expand[i * 48:(i + 1) * 48, j * 384:(j + 1) * 384]
            g1s[1, 2 * i + j, 0:48] = g_shrink[i * 48:(i + 1) * 48, j * 384:(j + 1) * 384]
    wide = jnp.concatenate([g_output[0:96], g_output[96:192]], axis=1)
    for i in range(NCHIP):
        for j in range(2):
            at = (i * 2 + j) * 16
            g1s[j, i, 48:64] = wide[at:at + 16] if at < 96 else jnp.zeros((16, 384), BF16)

    def sum_of(ref, count, rows):
        total = ref[0, rows].astype(F32)
        for o in range(1, count):
            total = total + ref[o, rows].astype(F32)
        return total.astype(BF16)

    def add_pair(mine, other, out):
        def body(o, carry):
            out[o] = (mine[core, o].astype(F32) + other[o].astype(F32)).astype(BF16)
            return carry

        lax.fori_loop(0, NCHIP, body, 0)

    others = pl.ds(0, NCHIP - 1)
    to_core(g1s.at[1 - core], g1p, 5).start()

    ds_s[...] = jnp.zeros_like(ds_s)

    def attend_back(pair, carry):
        lw = lax.rem(pair, 2)
        for i in range(2):
            rows = window_rows(2 * pair + i)
            dam[i] = stacked(ga_s[rows, :])
            raw[i] = dot_nt(v_s[rows, :], dam[i])
        for i in range(2):
            for t in range(WIDE // 128):
                cols = slice(t * 128, (t + 1) * 128)
                chances = p_s[2 * pair + i, :, cols].astype(F32)
                weighted = raw[i, :, cols]
                centre = jnp.sum(chances * weighted, axis=0, keepdims=True)
                dsh[i, :, cols] = (chances * (weighted - centre)).astype(BF16)
        for i in range(2):
            rows = window_rows(2 * pair + i)
            dv_s[rows, :] = dot_nn(p_s[2 * pair + i], dam[i]).astype(BF16)
            dq_s[rows, :] = (unstacked(dot_tn(k_s[rows, :], dsh[i])) * FACTOR).astype(BF16)
            dk_s[rows, :] = (dot_nn(dsh[i], stacked(q_s[rows, :])) * FACTOR).astype(BF16)
        ds_s[lw] = ds_s[lw] + (dsh[0].astype(F32) + dsh[1].astype(F32))
        return carry

    all_rows = slice(0, 64)
    def windows_back(pair, carry):
        attend_back(pair, carry)

        @pl.when(pair == 0)
        def _():
            arrived(g1p, 5)
            add_pair(g1s, g1p, g1h)
            g1r[chip] = g1h[chip]
            chips_all(lambda o: to_chip(g1h.at[o], g1r.at[chip], 6, o).start())

        @pl.when(pair == 2)
        def _():
            arrived(g1r.at[others], 6)
            g1l[d] = sum_of(g1r, NCHIP, all_rows)
            lat_all(lambda o: to_band(g1l.at[d], g1l.at[d], 7, o).start())

        return carry

    lax.fori_loop(0, NWIN // 2, windows_back, 0)
    arrived(g1l.at[others], 7)
    g1f[chip] = sum_of(g1l, NLAT, all_rows)
    chips_all(lambda o: to_chip(g1f.at[chip], g1f.at[chip], 8, o).start())

    ni = ni_s[...]
    g_triple = jnp.concatenate(
        [dot_tn(ni, dq_s[...]), dot_tn(ni, dk_s[...]), dot_tn(ni, dv_s[...]), jnp.zeros((C, 64), F32)], axis=1
    ).astype(BF16)
    for i in range(3):
        for j in range(5):
            at = 5 * i + j
            g2s[at // 8, at % 8, 0:64] = g_triple[i * 64:(i + 1) * 64, j * 128:(j + 1) * 128]
    g2s[1, 7, 0:64] = jnp.zeros((64, 128), BF16)
    for lw in range(2):
        for h in range(HEADS):
            at = pl.ds(h * 2 + lw, WIN, stride=16)
            part = ds_s[lw, :, h * WIN:(h + 1) * WIN].T
            bs_s.at[0][at, :] = part[:, 0:128]
            bs_s.at[1][at, :] = jnp.concatenate([part[:, 128:144], jnp.zeros((WIN, 112), F32)], axis=1)

    def fold(s_i, carry):
        at = pl.ds(pl.multiple_of(s_i * 192, 192), 192)
        rows = jnp.concatenate([bs_s[0, at, :], bs_s[1, at, :]], axis=1)[:, 0:WIN].astype(BF16)
        return carry + dot_nt(rows, spread_s[s_i])

    folded = lax.fori_loop(0, 12, fold, jnp.zeros((192, 512), F32))
    pieces_t = []
    for p in range(2):
        for pk in range(2):
            for r in range(6):
                at = (p * 6 + r) * 16
                pieces_t.append(folded[at:at + 16, pk * 256:pk * 256 + 138])
    table = jnp.concatenate(pieces_t + [jnp.zeros((16, 4096 - POS), F32)], axis=1).astype(BF16)
    for o in range(32):
        g2s[o // 16, (o // 2) % 8, 64 + 16 * (o % 2):80 + 16 * (o % 2)] = table[:, o * 128:(o + 1) * 128]
    to_core(g2s.at[1 - core], g2p, 9).start()

    def project_back(i, carry):
        rows = chunk_rows(i)
        tmp[...] = (
            dot_nt(dq_s[rows, :], wq[...]) + dot_nt(dk_s[rows, :], wk[...]) + dot_nt(dv_s[rows, :], wv[...])
        )
        for t in range(CHUNK // TILE):
            part = tile_rows(i, t)
            unit, inverse = statistics(x_w[part, :].astype(F32))
            back = norm_back(unit, inverse, tmp[t * TILE:(t + 1) * TILE, :] * attend_gain[...])
            gt_s[part, :] = (gm_s[part, :] + back).astype(BF16)
        return carry

    def chunks_back(i, carry):
        project_back(i, carry)

        @pl.when(i == 0)
        def _():
            arrived(g2p, 9)
            add_pair(g2s, g2p, g2h)
            g2r[chip] = g2h[chip]
            chips_all(lambda o: to_chip(g2h.at[o], g2r.at[chip], 10, o).start())

        return carry

    lax.fori_loop(0, NCHUNK, chunks_back, 0)

    from_window = one_hot(HALF, orders[3:4, 0:HALF])

    def unsort_window(b, carry):
        gq[b] = dot_nn(from_window, gt_s[half_rows(b), :])
        return carry

    lax.fori_loop(0, 2, unsort_window, 0)
    pack(gq, (c10, c01, c11))
    back_copies = halo((c10, c01, c11), (d10, d01, d11), back_ss, back_rs, (e_up, d_up))
    for copy in back_copies:
        copy.start()

    arrived(g1f.at[others], 8)
    to_core(g1f, g1o, 11).start()

    arrived(g2r.at[others], 10)
    g2l[d] = sum_of(g2r, NCHIP, slice(0, 64))
    lat_all(lambda o: to_band(g2l.at[d], g2l.at[d], 12, o).start())
    g2f[chip, 64:96] = sum_of(g2r, NCHIP, slice(64, 96))

    to_natural = one_hot(HALF, orders[1:2, 0:HALF])
    for copy in back_copies:
        copy.wait()
    unpack(gq, (d10, d01, d11))

    arrived(g2l.at[others], 12)
    g2f[chip, 0:64] = sum_of(g2l, NLAT, slice(0, 64))
    chips_all(lambda o: to_chip(g2f.at[chip], g2f.at[chip], 13, o).start())


    def unsort_sample(b, carry):
        out_fields[half_rows(b), :] = dot_nn(to_natural, gq[b].astype(BF16)).astype(BF16)
        return carry

    lax.fori_loop(0, 2, unsort_sample, 0)
    arrived(g1o, 11)
    out_g1[core] = g1f[...]
    out_g1[1 - core] = g1o[...]
    arrived(g2f.at[others], 13)
    to_core(g2f, g2o, 14).start()
    out_g2[core] = g2f[...]
    arrived(g2o, 14)
    out_g2[1 - core] = g2o[...]

    left(cs.at[others], 0)
    left(wa.at[others], 1)
    left(cf, 2)
    left(wb, 3)
    left(ch, 4)
    left(g1p, 5)
    left(g1r.at[others], 6)
    left(g1l.at[others], 7)
    left(g1f.at[others], 8)
    left(g2p, 9)
    left(g2r.at[others], 10)
    left(g1o, 11)
    left(g2l.at[others], 12)
    left(g2f.at[others], 13)
    left(g2o, 14)


def results_kernel(
    fields, g1, g2, attend_gain, triple_w, feed_gain, expand_w,
    out_fields, out_triple, out_output, out_expand, out_shrink, out_attend, out_feed, out_table,
):
    out_fields[...] = fields[...]
    for i in range(4):
        for j in range(2):
            rows, cols = slice(i * 48, (i + 1) * 48), slice(j * 384, (j + 1) * 384)
            out_expand[rows, cols] = g1[0, 2 * i + j, 0:48].astype(F32)
            out_shrink[rows, cols] = g1[1, 2 * i + j, 0:48].astype(F32)
    for i in range(6):
        wide = g1[i % 2, i // 2, 48:64].astype(F32)
        out_output[i * 16:(i + 1) * 16, :] = wide[:, 0:C]
        out_output[96 + i * 16:96 + (i + 1) * 16, :] = wide[:, C:2 * C]
    for i in range(3):
        for j in range(5):
            at, size = 5 * i + j, 128 if j < 4 else 64
            part = g2[at // 8, at % 8, 0:64].astype(F32)
            out_triple[i * 64:(i + 1) * 64, j * 128:j * 128 + size] = part[:, 0:size]
    table = jnp.concatenate(
        [g2[o // 16, (o // 2) % 8, 64 + 16 * (o % 2):80 + 16 * (o % 2)] for o in range(32)], axis=1
    ).astype(F32)
    for h in range(HEADS):
        out_table[h] = table[2 * h:2 * h + 2, 0:POS]

    def gain_gradient(grad, weight, gain):
        product = (grad[...] * weight[...].astype(F32)).astype(BF16)
        total = dot_nt(jnp.ones((16, product.shape[1]), BF16), product)
        return total[0:1] / gain[...]

    out_attend[...] = gain_gradient(out_triple, triple_w, attend_gain)
    out_feed[...] = gain_gradient(out_expand, expand_w, feed_gain)


def scratch():
    def vmem(*shape, kind=BF16):
        return pltpu.VMEM(shape, kind)

    token = vmem(TOK, C)
    token_f = vmem(TOK, C, kind=F32)
    weight = vmem(C, C)
    quad = vmem(2, HALF, C, kind=F32)
    halves = [vmem(656, 128), vmem(224, 128), vmem(224, 128)]
    stat = vmem(WIN, 128, kind=F32)
    small = vmem(2, 24, 128, kind=F32)
    buffers = [
        quad, quad, *halves, *halves, *halves, *halves, token, token, token, token, token, weight, weight, weight,
        vmem(NWIN, WIN, WIDE), token, token_f, token, vmem(TOK, FF), vmem(TOK, FF, kind=F32), token,
        vmem(16, POS, kind=F32), vmem(576, 512), vmem(2, 2304, 128, kind=F32),
        vmem(2, WIN, WIDE, kind=F32), vmem(2, WIN, WIDE, kind=F32),
        vmem(12, 512, WIN), vmem(2, WIN, 384),
        vmem(576, 256, kind=F32), vmem(8, 2, 3, 32, 128), vmem(2, 8, 3, 32, 128), vmem(8, 3, 32, 128), vmem(2, 8, 2, 32, 128),
        vmem(8, 32, 768), vmem(8, 32, 768),
        vmem(12, 128, C), token, vmem(2, WIN, 128, kind=F32), stat, small, small, small, small, vmem(4, WIN, 128, kind=F32),
        token, vmem(TOK, FF), token_f, token, token, token, token, token, token,
        vmem(2, WIN, WIDE, kind=F32), vmem(2, WIN, WIDE), vmem(2, WIDE, C), vmem(CHUNK, FF, kind=F32),
        vmem(CHUNK, C, kind=F32),
    ]
    for rows, cols in ((64, 384), (96, 128)):
        chunks = vmem(8, rows, cols)
        buffers += [vmem(2, 8, rows, cols), chunks, chunks, chunks, vmem(8, 64, cols), chunks, chunks]
    counts = [3, 3, 3, 3, 4, 4, 15, 15]
    return buffers + [pltpu.SemaphoreType.DMA((n,)) for n in counts]


def per_device(
    fields, merge_cotangent, attend_gain, triple_weight, bias_table, output_weight, feed_gain,
    expand_weight, shrink_weight, merge_gain, merge_weight,
):
    cot = jnp.transpose(merge_cotangent, (1, 2, 3, 4, 0)).reshape(576, 192)
    bias = jnp.transpose(bias_table[0], (1, 0, 2))
    def shaped(shapes):
        return [jax.ShapeDtypeStruct(shape, kind) for shape, kind in shapes]

    vmem_spec = pl.BlockSpec(memory_space=pltpu.VMEM)
    parts = pl.pallas_call(
        kernel,
        out_shape=shaped(
            [((TOK, C), BF16), ((2, 8, 64, 384), BF16), ((2, 8, 96, 128), BF16)]
        ),
        in_specs=[vmem_spec] * 12,
        out_specs=[vmem_spec] * 3,
        scratch_shapes=scratch(),
        compiler_params=pltpu.CompilerParams(
            collective_id=0, has_side_effects=True, vmem_limit_bytes=60 * 1024 * 1024
        ),
    )(
        fields.reshape(TOK, C), cot, attend_gain.reshape(1, C), triple_weight, bias, output_weight,
        feed_gain.reshape(1, C), expand_weight, shrink_weight.T, merge_gain,
        merge_weight.T, jnp.asarray(order_indices()),
    )
    g_fields, g_triple, g_output, g_expand, g_shrink, g_attend, g_feed, g_table = pl.pallas_call(
        results_kernel,
        out_shape=shaped(
            [
                ((TOK, C), BF16), ((C, 3 * C), F32), ((C, C), F32), ((C, FF), F32), ((C, FF), F32),
                ((1, C), F32), ((1, C), F32), ((HEADS, 2, POS), F32),
            ]
        ),
        in_specs=[vmem_spec] * 7,
        out_specs=[vmem_spec] * 8,
        compiler_params=pltpu.CompilerParams(vmem_limit_bytes=60 * 1024 * 1024),
    )(*parts, attend_gain.reshape(1, C), triple_weight, feed_gain.reshape(1, C), expand_weight)
    return (
        g_fields.reshape(fields.shape), g_triple, g_output, g_expand, g_shrink.T,
        g_attend.reshape(C), g_feed.reshape(C), jnp.transpose(g_table, (1, 0, 2))[None],
    )


def solution(mesh):
    placed = (
        P(None, None, "lat", "lon", None),
        P(None, None, None, "lat", "lon"),
        P(),
        P(),
        P("lat", None, None, None),
        P(),
        P(),
        P(),
        P(),
        P(),
        P(None, "lon"),
    )
    return jax.shard_map(
        per_device,
        mesh=mesh,
        in_specs=placed,
        out_specs=(
            P(None, None, "lat", "lon", None),
            P(),
            P(),
            P(),
            P(),
            P(),
            P(),
            P("lat", None, None, None),
        ),
        check_vma=False,
    )
```

```python
import functools
import math

import jax
import jax.numpy as jnp
import numpy as np
from jax import lax
from jax.experimental import pallas as pl
from jax.experimental.pallas import tpu as pltpu
from jax.sharding import PartitionSpec as P

F32 = jnp.float32
BF16 = jnp.bfloat16
I32 = jnp.int32
MESH = pl.DeviceIdType.MESH

EPS = 1e-05
MASKED = -1000000000.0
NLON = 16
NLAT = 8
NCHIP = 8
C = 192
HEADS = 6
FF = 768
WIN = 144
NWIN = 8
TOK = WIN * NWIN
HALF = TOK // 2
SIZES = (216, 72, 72)
POS = 3312
CHUNK = 288
NCHUNK = TOK // CHUNK
TILE = 48
WIDE = 896
FACTOR = 32 ** -0.5


def order_indices():
    natural_to_quad = np.full(640, -1, np.int32)
    quad_to_natural = np.full(640, -1, np.int32)
    quad_to_window = np.full(640, -1, np.int32)
    window_to_quad = np.full(640, -1, np.int32)
    for level in range(4):
        for row in range(6):
            for col in range(24):
                source = (level * 6 + row) * 24 + col
                if col >= 6:
                    place = (0 if row >= 3 else 216) + level * 54 + (row % 3) * 18 + col - 6
                else:
                    place = (432 if row >= 3 else 504) + level * 18 + (row % 3) * 6 + col
                natural_to_quad[source] = place
                quad_to_natural[place] = source
    index = 0
    for lev_win in range(2):
        for lon_win in range(2):
            for s in range(12):
                for p in range(2):
                    for r in range(6):
                        level = (lev_win * 2 + p + 1) % 4
                        col = lon_win * 12 + s
                        if col < 18:
                            place = (0 if r < 3 else 216) + level * 54 + (r % 3) * 18 + col
                        else:
                            place = (432 if r < 3 else 504) + level * 18 + (r % 3) * 6 + col - 18
                        window_to_quad[index] = place
                        quad_to_window[place] = index
                        index += 1
    cell_lane = np.full(640, -1, np.int32)
    bias_row = np.full(640, -1, np.int32)
    merged_token = np.full((2, 640), -1, np.int32)
    for lane in range(256):
        if lane % 16 < 12:
            cell_lane[lane] = (12 * (lane // 16) + 3 + lane % 16) % 192
    for k in range(WIN):
        s, p, r = k // 12, (k // 6) % 2, k % 6
        bias_row[k] = p * 256 + r * 23 + 11 - s
    for lon_win in range(2):
        for row in range(384):
            p, r, y, m = row // 192, (row // 32) % 6, (row // 16) % 2, row % 16
            if 0 <= m - lon_win * 6 < 6:
                merged_token[lon_win, row] = (2 * (m - lon_win * 6) + y) * 12 + p * 6 + r
    rows = [natural_to_quad, quad_to_natural, quad_to_window, window_to_quad]
    return np.stack(rows + [cell_lane, bias_row, merged_token[0], merged_token[1]])


def dot_nn(a, b):
    return lax.dot_general(a, b, (((1,), (0,)), ((), ())), preferred_element_type=F32)


def dot_nt(a, b):
    return lax.dot_general(a, b, (((1,), (1,)), ((), ())), preferred_element_type=F32)


def dot_tn(a, b):
    return lax.dot_general(a, b, (((0,), (0,)), ((), ())), preferred_element_type=F32)


def one_hot(rows, targets):
    ids = lax.broadcasted_iota(I32, (rows, targets.shape[1]), 0)
    return jnp.where(ids == targets, 1.0, 0.0).astype(BF16)


def statistics(values):
    centred = values - jnp.mean(values, axis=-1, keepdims=True)
    inverse = lax.rsqrt(jnp.mean(centred * centred, axis=-1, keepdims=True) + EPS)
    return centred * inverse, inverse


def norm_back(normed, inverse, scaled):
    centre = jnp.mean(scaled, axis=-1, keepdims=True)
    projected = jnp.mean(scaled * normed, axis=-1, keepdims=True)
    return inverse * (scaled - centre - normed * projected)


def gelu_parts(values):
    cumulative = 0.5 * (1.0 + lax.erf(values * (1.0 / math.sqrt(2.0))))
    density = jnp.exp(-0.5 * values * values) * (1.0 / math.sqrt(2.0 * math.pi))
    return values * cumulative, cumulative + values * density


def lanes(rows, cols):
    return lax.broadcasted_iota(I32, (rows, cols), 1)


def over_12(ids):
    return (ids * 5462) >> 16


def over_6(ids):
    return (ids * 10923) >> 16


def kernel(
    fields, cot, attend_gain, triple_w, bias, output_w, feed_gain, expand_w, shrink_t, merge_gain,
    merge_wt, orders,
    out_fields, out_g1, out_g2,
    sq, gq, a10, a01, a11, b10, b01, b11, c10, c01, c11, d10, d01, d11, x_w, ni_s, q_s, k_s, v_s, wq, wk, wv, p_s, att_s, mid_s, nm_s, act_s, slope_s, vo_s,
    b16, bl_s, bs_s, bx, ds_s, spread_s, pick_s,
    cells, cs, cb, cf, ch, wa, wb, qry, qw, st, sx, sup, sdn, tup, tdn, cp_s, go_s, gh_s, gm_s, ga_s, gmh_s,
    dq_s, dk_s, dv_s, gt_s, raw, dsh, dam, hid, tmp, g1s, g1p, g1h, g1r, g1l, g1f, g1o, g2s, g2p, g2h, g2r, g2l, g2f, g2o,
    halo_ss, halo_rs, back_ss, back_rs, st_ss, st_rs, sends, recvs,
):
    e = lax.axis_index("lon")
    d = lax.axis_index("lat")
    e_up, e_dn = lax.rem(e + 1, NLON), lax.rem(e + NLON - 1, NLON)
    d_up, d_dn = lax.rem(d + 1, NLAT), lax.rem(d + NLAT - 1, NLAT)

    def remote(src, dst, ssem, rsem, device):
        return pltpu.make_async_remote_copy(
            src_ref=src, dst_ref=dst, send_sem=ssem, recv_sem=rsem, device_id=device,
            device_id_type=MESH,
        )

    core, chip = lax.rem(e, 2), e // 2
    partner = e + 1 - 2 * core

    def chips_all(action):
        def body(step, carry):
            action(lax.rem(chip + step, NCHIP))
            return carry

        lax.fori_loop(1, NCHIP, body, 0)

    def lat_all(action):
        def body(step, carry):
            action(lax.rem(d + step, NLAT))
            return carry

        lax.fori_loop(1, NLAT, body, 0)

    def to_chip(src, dst, phase, o):
        return remote(src, dst, sends.at[phase], recvs.at[phase], (2 * o + core, d))

    def to_band(src, dst, phase, o):
        return remote(src, dst, sends.at[phase], recvs.at[phase], (e, o))

    def to_core(src, dst, phase):
        return remote(src, dst, sends.at[phase], recvs.at[phase], (partner, d))

    def arrived(region, phase):
        remote(region, region, sends.at[phase], recvs.at[phase], (partner, d)).wait_recv()

    def left(region, phase):
        remote(region, region, sends.at[phase], recvs.at[phase], (partner, d)).wait_send()

    barrier = pltpu.get_barrier_semaphore()

    def greet(device):
        pl.semaphore_signal(barrier, inc=1, device_id=device, device_id_type=MESH)

    chips_all(lambda o: greet((2 * o + core, d)))
    lat_all(lambda o: greet((e, o)))
    for device in ((e_up, d), (e_dn, d), (e_up, d_up), (e_dn, d_dn)):
        greet(device)

    def half_rows(b):
        return pl.ds(pl.multiple_of(b * HALF, HALF), HALF)

    def pack(quads, out):
        at = 216
        for size, message in zip(SIZES, out):
            first, second = quads[0, at:at + size, :], quads[1, at:at + size, :]
            tails = jnp.concatenate([first[:, 128:C], second[:, 128:C]], axis=1)
            parts = [first[:, 0:128], second[:, 0:128], tails, jnp.zeros((8, 128), F32)]
            message[...] = jnp.concatenate(parts, axis=0).astype(BF16)
            at += size

    def unpack(quads, messages):
        at = 216
        for size, message in zip(SIZES, messages):
            rows = message[...].astype(F32)
            tails = rows[2 * size:3 * size]
            quads[0, at:at + size, :] = jnp.concatenate([rows[0:size], tails[:, 0:64]], axis=1)
            quads[1, at:at + size, :] = jnp.concatenate([rows[size:2 * size], tails[:, 64:128]], axis=1)
            at += size

    to_quad = one_hot(HALF, orders[0:1, 0:HALF])

    def sort_sample(b, carry):
        sq[b] = dot_nn(to_quad, fields[half_rows(b), :])
        return carry

    lax.fori_loop(0, 2, sort_sample, 0)
    pack(sq, (a10, a01, a11))
    pl.semaphore_wait(barrier, NCHIP - 1 + NLAT - 1 + 4)

    def halo(sources, targets, ssem, rsem, step):
        devices = ((e, step[1]), (step[0], d), (step[0], step[1]))
        return [
            remote(src, dst, ssem.at[i], rsem.at[i], dev)
            for i, (src, dst, dev) in enumerate(zip(sources, targets, devices))
        ]

    halo_copies = halo((a10, a01, a11), (b10, b01, b11), halo_ss, halo_rs, (e_dn, d_dn))
    for copy in halo_copies:
        copy.start()

    cells[...] = dot_nn(cot[...], one_hot(192, orders[4:5, 0:256]))
    block_of = lanes(72, 128) >> 4

    def gather_cells(o, carry):
        tile = pl.ds(pl.multiple_of((o // 8) * 128, 128), 128)
        inner = lax.rem(o, 8)
        piece = jnp.zeros((72, 128), F32)
        for bl in range(8):
            part = pltpu.roll(cells[bl * 72:(bl + 1) * 72, tile], lax.rem(16 * (bl - inner) + 128, 128), 1)
            piece = jnp.where(block_of == bl, part, piece)
        for a in range(3):
            padded = jnp.concatenate([piece[a * 24:(a + 1) * 24], jnp.zeros((8, 128), F32)], axis=0)
            cs[o // 2, lax.rem(o, 2), a] = padded.astype(BF16)
        return carry

    lax.fori_loop(0, NLON, gather_cells, 0)
    wa[chip] = jnp.concatenate(
        [merge_wt[...].astype(F32), jnp.zeros((8, 768), F32)], axis=0
    ).astype(BF16)
    cb[:, chip] = cs[chip]
    for h in range(HEADS):
        b16[2 * h:2 * h + 2, :] = bias[h]
    b16[12:16, :] = jnp.zeros((4, POS), F32)
    zero_tail = jnp.zeros((16, 256 - 138), F32)
    for p in range(2):
        for r in range(6):
            parts = []
            for pk in range(2):
                at = (p * 2 + pk) * 828 + r * 138
                parts += [b16[:, at:at + 138], zero_tail]
            row = jnp.concatenate(parts, axis=1)
            high = row.astype(BF16)
            rest = row - high.astype(F32)
            middle = rest.astype(BF16)
            low = (rest - middle.astype(F32)).astype(BF16)
            at = (p * 6 + r) * 16
            bl_s[at:at + 16, :] = high
            bl_s[192 + at:192 + at + 16, :] = middle
            bl_s[384 + at:384 + at + 16, :] = low

    bias_row = orders[5:6, 0:WIN]

    def spread(s_i, carry):
        matrix = one_hot(512, bias_row + s_i)
        spread_s[s_i] = matrix
        split = dot_nn(bl_s[...], matrix)
        rows = split[0:192] + split[192:384] + split[384:576]
        at = pl.ds(pl.multiple_of(s_i * 192, 192), 192)
        bs_s[0, at, :] = rows[:, 0:128]
        bs_s[1, at, :] = jnp.concatenate([rows[:, 128:144], jnp.zeros((192, 112), F32)], axis=1)
        return carry

    lax.fori_loop(0, 12, spread, 0)

    tok_i = lax.broadcasted_iota(I32, (WIN, WIN), 0)
    tok_k = lax.broadcasted_iota(I32, (WIN, WIN), 1)
    half_i, half_k = over_6(tok_i), over_6(tok_k)
    last_band = d == NLAT - 1
    lat_differs = ((tok_i - half_i * 6 >= 3) != (tok_k - half_k * 6 >= 3)) & last_band
    lev_differs = (half_i & 1) != (half_k & 1)
    bx[:, :, HEADS * WIN:WIDE] = jnp.zeros((2, WIN, WIDE - HEADS * WIN), F32)
    for lw in range(2):
        differs = (lat_differs | lev_differs) if lw else lat_differs
        for h in range(HEADS):
            at = pl.ds(h * 2 + lw, WIN, stride=16)
            full = jnp.concatenate([bs_s.at[0][at, :], bs_s.at[1][at, :]], axis=1)[:, 0:WIN]
            bx[lw, :, h * WIN:(h + 1) * WIN] = jnp.where(differs, MASKED, full).T

    wq[...] = triple_w[:, 0:192]
    wk[...] = triple_w[:, 192:384]
    wv[...] = triple_w[:, 384:576]

    head_of = lanes(1, C) >> 5
    head_f = [jnp.where(head_of == h, 1.0, 0.0) for h in range(HEADS)]
    head_b = [mask.astype(BF16) for mask in head_f]

    blank = jnp.zeros((WIDE - HEADS * WIN, C), BF16)

    def stacked(values):
        return jnp.concatenate([values * mask for mask in head_b] + [blank], axis=0)

    def unstacked(values):
        blocks = [values[h * 32:(h + 1) * 32, h * WIN:(h + 1) * WIN] for h in range(HEADS)]
        return jnp.concatenate(blocks, axis=0).T

    to_window = one_hot(HALF, orders[2:3, 0:HALF])
    for copy in halo_copies:
        copy.wait()
    chips_all(lambda o: to_chip(cs.at[o], cb.at[:, chip], 0, o).start())
    chips_all(lambda o: to_chip(wa.at[chip], wa.at[chip], 1, o).start())
    unpack(sq, (b10, b01, b11))

    def sort_window(b, carry):
        x_w[half_rows(b), :] = dot_nn(to_window, sq[b].astype(BF16)).astype(BF16)
        return carry

    lax.fori_loop(0, 2, sort_window, 0)

    def window_rows(w):
        return pl.ds(pl.multiple_of(w * WIN, WIN), WIN)

    def chunk_rows(i):
        return pl.ds(pl.multiple_of(i * CHUNK, CHUNK), CHUNK)

    def tile_rows(i, t):
        return pl.ds(pl.multiple_of(i * CHUNK + t * TILE, 16), TILE)

    def project(i, carry):
        rows = chunk_rows(i)
        for t in range(CHUNK // TILE):
            part = tile_rows(i, t)
            normed = statistics(x_w[part, :].astype(F32))[0]
            ni_s[part, :] = (normed * attend_gain[...]).astype(BF16)
        normed_in = ni_s[rows, :]
        q_s[rows, :] = dot_nn(normed_in, wq[...]).astype(BF16)
        k_s[rows, :] = dot_nn(normed_in, wk[...]).astype(BF16)
        v_s[rows, :] = dot_nn(normed_in, wv[...]).astype(BF16)
        return carry

    lax.fori_loop(0, NCHUNK, project, 0)

    def attend(pair, carry):
        lw = lax.rem(pair, 2)
        for i in range(2):
            rows = window_rows(2 * pair + i)
            raw[i] = dot_nt(k_s[rows, :], stacked(q_s[rows, :]))
        for i in range(2):
            for t in range(WIDE // 128):
                cols = slice(t * 128, (t + 1) * 128)
                scores = raw[i, :, cols] * FACTOR + bx[lw, :, cols]
                exponent = jnp.exp(scores - jnp.max(scores, axis=0, keepdims=True))
                chances = exponent * (1.0 / jnp.sum(exponent, axis=0, keepdims=True))
                p_s[2 * pair + i, :, cols] = chances.astype(BF16)
        for i in range(2):
            rows = window_rows(2 * pair + i)
            att_s[rows, :] = unstacked(dot_tn(v_s[rows, :], p_s[2 * pair + i])).astype(BF16)
        return carry

    def attend_and_pass(pair, carry):
        attend(pair, carry)

        @pl.when(pair == 0)
        def _():
            arrived(cb.at[:, pl.ds(0, NCHIP - 1)], 0)
            to_core(cb.at[1 - core], cf, 2).start()

        @pl.when(pair == 1)
        def _():
            arrived(cf, 2)
            first_rows = pl.ds(0, 2)
            to_band(cb.at[core, :, first_rows], ch.at[0], 4, d_dn).start()
            to_band(cf.at[:, first_rows], ch.at[1], 4, d_dn).start()
            arrived(wa.at[pl.ds(0, NCHIP - 1)], 1)
            to_core(wa, wb, 3).start()

        return carry

    lax.fori_loop(0, NWIN // 2, attend_and_pass, 0)

    def feed(i, carry):
        rows = chunk_rows(i)
        tmp[...] = x_w[rows, :].astype(F32) + dot_nn(att_s[rows, :], output_w[...])
        for t in range(CHUNK // TILE):
            part = tile_rows(i, t)
            middle = tmp[t * TILE:(t + 1) * TILE, :]
            mid_s[part, :] = middle
            nm_s[part, :] = (statistics(middle)[0] * feed_gain[...]).astype(BF16)
        hid[...] = dot_nn(nm_s[rows, :], expand_w[...])
        for t in range(CHUNK // 16):
            part = pl.ds(pl.multiple_of(i * CHUNK + t * 16, 16), 16)
            for j in range(FF // 256):
                cols = slice(j * 256, (j + 1) * 256)
                act, slope = gelu_parts(hid[t * 16:(t + 1) * 16, cols])
                act_s[part, cols] = act.astype(BF16)
                slope_s[part, cols] = slope
        vo_s[rows, :] = (tmp[...] + dot_nt(act_s[rows, :], shrink_t[...])).astype(BF16)
        return carry

    lax.fori_loop(0, NCHUNK, feed, 0)

    arrived(ch, 4)
    arrived(wb, 3)
    gain_row = merge_gain[...].reshape(1, 4 * C)
    for r in range(6):
        x = (r + 1) % 2
        cell = (0, 1, 1, 2, 2, 3)[r]
        cols = slice(x * 384, (x + 1) * 384)
        if cell < 2:
            planes = cb[core, :, cell + 1], cf[:, cell + 1]
        else:
            planes = ch[0, :, cell - 2], ch[1, :, cell - 2]
        summed = dot_tn(planes[0].reshape(256, 128), wa[:, :, cols].reshape(256, 384))
        summed = summed + dot_tn(planes[1].reshape(256, 128), wb[:, :, cols].reshape(256, 384))
        scaled = summed * gain_row[:, x * 384:(x + 1) * 384]
        qry[2 * r] = scaled[:, 0:192].astype(BF16)
        qry[2 * r + 1] = scaled[:, 192:384].astype(BF16)

    st[...] = jnp.zeros_like(st)
    for i in range(2):
        pick_s[i] = one_hot(WIN, orders[6 + i:7 + i, 0:384])
    stat_lane = lanes(WIN, 128)
    tile_lane = lanes(TILE, 128)

    def merge_sums(w, carry):
        rows = window_rows(w)
        b, lw, lon_win = w // 4, lax.rem(w // 2, 2), lax.rem(w, 2)
        parts = []
        for p in range(2):
            level = lax.rem(lw * 2 + p + 1, 4)
            at = pl.ds(pl.multiple_of((b * 4 + level) * 16, 16), 16)
            parts.append(qry[:, at, :].reshape(192, C))
        qw[rows, :] = dot_nn(pick_s[lon_win], jnp.concatenate(parts, axis=0)).astype(BF16)
        for t in range(WIN // TILE):
            part = pl.ds(pl.multiple_of(w * WIN + t * TILE, 16), TILE)
            at = slice(t * TILE, (t + 1) * TILE)
            q = qw[part, :].astype(F32)
            v = vo_s[part, :].astype(F32)
            mean = jnp.mean(v, axis=-1, keepdims=True)
            centred = v - mean
            squares = jnp.sum(centred * centred, axis=-1, keepdims=True)
            q_sum = jnp.sum(q, axis=-1, keepdims=True)
            qv_sum = jnp.sum(q * centred, axis=-1, keepdims=True)
            total = st[b, at, :]
            for j, value in enumerate((mean, squares, q_sum, qv_sum)):
                total = jnp.where(tile_lane == 32 * j + w, value, total)
            st[b, at, :] = total
        return carry

    def sums_copies(b):
        return (
            remote(tup.at[b], sup.at[b], st_ss.at[2 * b], st_rs.at[2 * b], (e, d_up)),
            remote(tdn.at[b], sdn.at[b], st_ss.at[2 * b + 1], st_rs.at[2 * b + 1], (e, d_dn)),
        )

    def exchange(b):
        tup[b] = st.at[b][pl.ds(5, 24, stride=6), :]
        tdn[b] = st.at[b][pl.ds(0, 24, stride=6), :]
        for copy in sums_copies(b):
            copy.start()

    even = (over_12(lax.broadcasted_iota(I32, (WIN, 128), 0)) & 1) == 0

    def pair_of(values):
        return jnp.where(even, pltpu.roll(values, WIN - 12, 0), pltpu.roll(values, 12, 0))

    def cell_norm(b):
        for r, other in ((1, 2), (2, 1), (3, 4), (4, 3)):
            sx[pl.ds(r, 24, stride=6), :] = st.at[b][pl.ds(other, 24, stride=6), :]
        for copy in sums_copies(b):
            copy.wait()
        sx[pl.ds(0, 24, stride=6), :] = sup[b]
        sx[pl.ds(5, 24, stride=6), :] = sdn[b]
        own, cross = st[b], sx[...]
        group = [own, cross, pair_of(own), pair_of(cross)]
        cell_mean = (group[0] + group[1] + group[2] + group[3]) * 0.25
        variance = jnp.zeros((WIN, 128), F32)
        q_total = jnp.zeros((WIN, 128), F32)
        qv_total = jnp.zeros((WIN, 128), F32)
        for values in group:
            offset = values - cell_mean
            q_sum = pltpu.roll(values, 64, 1)
            variance = variance + pltpu.roll(values, 96, 1) + 192.0 * offset * offset
            q_total = q_total + q_sum
            qv_total = qv_total + pltpu.roll(values, 32, 1) + offset * q_sum
        cell_inverse = lax.rsqrt(jnp.where(stat_lane < 8, variance, 0.0) * (1.0 / 768.0) + EPS)
        cp_s[0] = cell_mean
        cp_s[1] = cell_inverse
        cp_s[2] = q_total * (1.0 / 768.0)
        cp_s[3] = cell_inverse * cell_inverse * qv_total * (1.0 / 768.0)

    def merge_back(w, carry):
        for t in range(WIN // TILE):
            part = pl.ds(pl.multiple_of(w * WIN + t * TILE, 16), TILE)
            at = slice(t * TILE, (t + 1) * TILE)
            mean, inverse, q_mean, projected = [
                jnp.sum(jnp.where(tile_lane == w, cp_s[j, at, :], 0.0), axis=-1, keepdims=True) for j in range(4)
            ]
            v = vo_s[part, :].astype(F32) - mean
            go_s[part, :] = (inverse * (qw[part, :].astype(F32) - q_mean - v * projected)).astype(BF16)
        return carry

    def feed_back(i, carry):
        rows = chunk_rows(i)
        go = go_s[rows, :]
        gh = (dot_nn(go, shrink_t[...]) * slope_s[rows, :]).astype(BF16)
        gh_s[rows, :] = gh
        tmp[...] = dot_nt(gh, expand_w[...])
        for t in range(CHUNK // TILE):
            part = tile_rows(i, t)
            gnm = tmp[t * TILE:(t + 1) * TILE, :]
            unit, inverse = statistics(mid_s[part, :])
            gm = go_s[part, :].astype(F32) + norm_back(unit, inverse, gnm * feed_gain[...])
            gm_s[part, :] = gm
            gmh_s[part, :] = gm.astype(BF16)
        ga_s[rows, :] = dot_nt(gmh_s[rows, :], output_w[...]).astype(BF16)
        return carry

    def forward_sample(b, carry):
        lax.fori_loop(4 * b, 4 * b + 4, merge_sums, 0)
        exchange(b)
        return carry

    def backward_sample(b, carry):
        cell_norm(b)
        lax.fori_loop(4 * b, 4 * b + 4, merge_back, 0)
        lax.fori_loop(2 * b, 2 * b + 2, feed_back, 0)
        return carry

    lax.fori_loop(0, 2, forward_sample, 0)
    lax.fori_loop(0, 2, backward_sample, 0)

    g_expand = dot_tn(nm_s[...], gh_s[...]).astype(BF16)
    g_shrink = dot_tn(go_s[...], act_s[...]).astype(BF16)
    g_output = dot_tn(att_s[...], gmh_s[...]).astype(BF16)
    for i in range(4):
        for j in range(2):
            g1s[0, 2 * i + j, 0:48] = g_expand[i * 48:(i + 1) * 48, j * 384:(j + 1) * 384]
            g1s[1, 2 * i + j, 0:48] = g_shrink[i * 48:(i + 1) * 48, j * 384:(j + 1) * 384]
    wide = jnp.concatenate([g_output[0:96], g_output[96:192]], axis=1)
    for i in range(NCHIP):
        for j in range(2):
            at = (i * 2 + j) * 16
            g1s[j, i, 48:64] = wide[at:at + 16] if at < 96 else jnp.zeros((16, 384), BF16)

    def sum_of(ref, count, rows):
        total = ref[0, rows].astype(F32)
        for o in range(1, count):
            total = total + ref[o, rows].astype(F32)
        return total.astype(BF16)

    def add_pair(mine, other, out):
        def body(o, carry):
            out[o] = (mine[core, o].astype(F32) + other[o].astype(F32)).astype(BF16)
            return carry

        lax.fori_loop(0, NCHIP, body, 0)

    others = pl.ds(0, NCHIP - 1)
    to_core(g1s.at[1 - core], g1p, 5).start()

    ds_s[...] = jnp.zeros_like(ds_s)

    def attend_back(pair, carry):
        lw = lax.rem(pair, 2)
        for i in range(2):
            rows = window_rows(2 * pair + i)
            dam[i] = stacked(ga_s[rows, :])
            raw[i] = dot_nt(v_s[rows, :], dam[i])
        for i in range(2):
            for t in range(WIDE // 128):
                cols = slice(t * 128, (t + 1) * 128)
                chances = p_s[2 * pair + i, :, cols].astype(F32)
                weighted = raw[i, :, cols]
                centre = jnp.sum(chances * weighted, axis=0, keepdims=True)
                dsh[i, :, cols] = (chances * (weighted - centre)).astype(BF16)
        for i in range(2):
            rows = window_rows(2 * pair + i)
            dv_s[rows, :] = dot_nn(p_s[2 * pair + i], dam[i]).astype(BF16)
            dq_s[rows, :] = (unstacked(dot_tn(k_s[rows, :], dsh[i])) * FACTOR).astype(BF16)
            dk_s[rows, :] = (dot_nn(dsh[i], stacked(q_s[rows, :])) * FACTOR).astype(BF16)
        ds_s[lw] = ds_s[lw] + (dsh[0].astype(F32) + dsh[1].astype(F32))
        return carry

    all_rows = slice(0, 64)
    def windows_back(pair, carry):
        attend_back(pair, carry)

        @pl.when(pair == 0)
        def _():
            arrived(g1p, 5)
            add_pair(g1s, g1p, g1h)
            g1r[chip] = g1h[chip]
            chips_all(lambda o: to_chip(g1h.at[o], g1r.at[chip], 6, o).start())

        @pl.when(pair == 2)
        def _():
            arrived(g1r.at[others], 6)
            g1l[d] = sum_of(g1r, NCHIP, all_rows)
            lat_all(lambda o: to_band(g1l.at[d], g1l.at[d], 7, o).start())

        return carry

    lax.fori_loop(0, NWIN // 2, windows_back, 0)
    arrived(g1l.at[others], 7)
    g1f[chip] = sum_of(g1l, NLAT, all_rows)
    chips_all(lambda o: to_chip(g1f.at[chip], g1f.at[chip], 8, o).start())

    ni = ni_s[...]
    g_triple = jnp.concatenate(
        [dot_tn(ni, dq_s[...]), dot_tn(ni, dk_s[...]), dot_tn(ni, dv_s[...]), jnp.zeros((C, 64), F32)], axis=1
    ).astype(BF16)
    for i in range(3):
        for j in range(5):
            at = 5 * i + j
            g2s[at // 8, at % 8, 0:64] = g_triple[i * 64:(i + 1) * 64, j * 128:(j + 1) * 128]
    g2s[1, 7, 0:64] = jnp.zeros((64, 128), BF16)
    for lw in range(2):
        for h in range(HEADS):
            at = pl.ds(h * 2 + lw, WIN, stride=16)
            part = ds_s[lw, :, h * WIN:(h + 1) * WIN].T
            bs_s.at[0][at, :] = part[:, 0:128]
            bs_s.at[1][at, :] = jnp.concatenate([part[:, 128:144], jnp.zeros((WIN, 112), F32)], axis=1)

    def fold(s_i, carry):
        at = pl.ds(pl.multiple_of(s_i * 192, 192), 192)
        rows = jnp.concatenate([bs_s[0, at, :], bs_s[1, at, :]], axis=1)[:, 0:WIN].astype(BF16)
        return carry + dot_nt(rows, spread_s[s_i])

    folded = lax.fori_loop(0, 12, fold, jnp.zeros((192, 512), F32))
    pieces_t = []
    for p in range(2):
        for pk in range(2):
            for r in range(6):
                at = (p * 6 + r) * 16
                pieces_t.append(folded[at:at + 16, pk * 256:pk * 256 + 138])
    table = jnp.concatenate(pieces_t + [jnp.zeros((16, 4096 - POS), F32)], axis=1).astype(BF16)
    for o in range(32):
        g2s[o // 16, (o // 2) % 8, 64 + 16 * (o % 2):80 + 16 * (o % 2)] = table[:, o * 128:(o + 1) * 128]
    to_core(g2s.at[1 - core], g2p, 9).start()

    def project_back(i, carry):
        rows = chunk_rows(i)
        tmp[...] = (
            dot_nt(dq_s[rows, :], wq[...]) + dot_nt(dk_s[rows, :], wk[...]) + dot_nt(dv_s[rows, :], wv[...])
        )
        for t in range(CHUNK // TILE):
            part = tile_rows(i, t)
            unit, inverse = statistics(x_w[part, :].astype(F32))
            back = norm_back(unit, inverse, tmp[t * TILE:(t + 1) * TILE, :] * attend_gain[...])
            gt_s[part, :] = (gm_s[part, :] + back).astype(BF16)
        return carry

    def chunks_back(i, carry):
        project_back(i, carry)

        @pl.when(i == 0)
        def _():
            arrived(g2p, 9)
            add_pair(g2s, g2p, g2h)
            g2r[chip] = g2h[chip]
            chips_all(lambda o: to_chip(g2h.at[o], g2r.at[chip], 10, o).start())

        return carry

    lax.fori_loop(0, NCHUNK, chunks_back, 0)

    from_window = one_hot(HALF, orders[3:4, 0:HALF])

    def unsort_window(b, carry):
        gq[b] = dot_nn(from_window, gt_s[half_rows(b), :])
        return carry

    lax.fori_loop(0, 2, unsort_window, 0)
    pack(gq, (c10, c01, c11))
    back_copies = halo((c10, c01, c11), (d10, d01, d11), back_ss, back_rs, (e_up, d_up))
    for copy in back_copies:
        copy.start()

    arrived(g1f.at[others], 8)
    to_core(g1f, g1o, 11).start()

    arrived(g2r.at[others], 10)
    g2l[d] = sum_of(g2r, NCHIP, slice(0, 64))
    lat_all(lambda o: to_band(g2l.at[d], g2l.at[d], 12, o).start())
    g2f[chip, 64:96] = sum_of(g2r, NCHIP, slice(64, 96))

    to_natural = one_hot(HALF, orders[1:2, 0:HALF])
    for copy in back_copies:
        copy.wait()
    unpack(gq, (d10, d01, d11))

    arrived(g2l.at[others], 12)
    g2f[chip, 0:64] = sum_of(g2l, NLAT, slice(0, 64))
    chips_all(lambda o: to_chip(g2f.at[chip], g2f.at[chip], 13, o).start())


    def unsort_sample(b, carry):
        out_fields[half_rows(b), :] = dot_nn(to_natural, gq[b].astype(BF16)).astype(BF16)
        return carry

    lax.fori_loop(0, 2, unsort_sample, 0)
    arrived(g1o, 11)
    out_g1[core] = g1f[...]
    out_g1[1 - core] = g1o[...]
    arrived(g2f.at[others], 13)
    to_core(g2f, g2o, 14).start()
    out_g2[core] = g2f[...]
    arrived(g2o, 14)
    out_g2[1 - core] = g2o[...]

    left(cs.at[others], 0)
    left(wa.at[others], 1)
    left(cf, 2)
    left(wb, 3)
    left(ch, 4)
    left(g1p, 5)
    left(g1r.at[others], 6)
    left(g1l.at[others], 7)
    left(g1f.at[others], 8)
    left(g2p, 9)
    left(g2r.at[others], 10)
    left(g1o, 11)
    left(g2l.at[others], 12)
    left(g2f.at[others], 13)
    left(g2o, 14)


def results_kernel(
    fields, g1, g2, attend_gain, triple_w, feed_gain, expand_w,
    out_fields, out_triple, out_output, out_expand, out_shrink, out_attend, out_feed, out_table,
):
    out_fields[...] = fields[...]
    for i in range(4):
        for j in range(2):
            rows, cols = slice(i * 48, (i + 1) * 48), slice(j * 384, (j + 1) * 384)
            out_expand[rows, cols] = g1[0, 2 * i + j, 0:48].astype(F32)
            out_shrink[rows, cols] = g1[1, 2 * i + j, 0:48].astype(F32)
    for i in range(6):
        wide = g1[i % 2, i // 2, 48:64].astype(F32)
        out_output[i * 16:(i + 1) * 16, :] = wide[:, 0:C]
        out_output[96 + i * 16:96 + (i + 1) * 16, :] = wide[:, C:2 * C]
    for i in range(3):
        for j in range(5):
            at, size = 5 * i + j, 128 if j < 4 else 64
            part = g2[at // 8, at % 8, 0:64].astype(F32)
            out_triple[i * 64:(i + 1) * 64, j * 128:j * 128 + size] = part[:, 0:size]
    table = jnp.concatenate(
        [g2[o // 16, (o // 2) % 8, 64 + 16 * (o % 2):80 + 16 * (o % 2)] for o in range(32)], axis=1
    ).astype(F32)
    for h in range(HEADS):
        out_table[h] = table[2 * h:2 * h + 2, 0:POS]

    def gain_gradient(grad, weight, gain):
        product = (grad[...] * weight[...].astype(F32)).astype(BF16)
        total = dot_nt(jnp.ones((16, product.shape[1]), BF16), product)
        return total[0:1] / gain[...]

    out_attend[...] = gain_gradient(out_triple, triple_w, attend_gain)
    out_feed[...] = gain_gradient(out_expand, expand_w, feed_gain)


def scratch():
    def vmem(*shape, kind=BF16):
        return pltpu.VMEM(shape, kind)

    token = vmem(TOK, C)
    token_f = vmem(TOK, C, kind=F32)
    weight = vmem(C, C)
    quad = vmem(2, HALF, C, kind=F32)
    halves = [vmem(656, 128), vmem(224, 128), vmem(224, 128)]
    stat = vmem(WIN, 128, kind=F32)
    small = vmem(2, 24, 128, kind=F32)
    buffers = [
        quad, quad, *halves, *halves, *halves, *halves, token, token, token, token, token, weight, weight, weight,
        vmem(NWIN, WIN, WIDE), token, token_f, token, vmem(TOK, FF), vmem(TOK, FF, kind=F32), token,
        vmem(16, POS, kind=F32), vmem(576, 512), vmem(2, 2304, 128, kind=F32),
        vmem(2, WIN, WIDE, kind=F32), vmem(2, WIN, WIDE, kind=F32),
        vmem(12, 512, WIN), vmem(2, WIN, 384),
        vmem(576, 256, kind=F32), vmem(8, 2, 3, 32, 128), vmem(2, 8, 3, 32, 128), vmem(8, 3, 32, 128), vmem(2, 8, 2, 32, 128),
        vmem(8, 32, 768), vmem(8, 32, 768),
        vmem(12, 128, C), token, vmem(2, WIN, 128, kind=F32), stat, small, small, small, small, vmem(4, WIN, 128, kind=F32),
        token, vmem(TOK, FF), token_f, token, token, token, token, token, token,
        vmem(2, WIN, WIDE, kind=F32), vmem(2, WIN, WIDE), vmem(2, WIDE, C), vmem(CHUNK, FF, kind=F32),
        vmem(CHUNK, C, kind=F32),
    ]
    for rows, cols in ((64, 384), (96, 128)):
        chunks = vmem(8, rows, cols)
        buffers += [vmem(2, 8, rows, cols), chunks, chunks, chunks, vmem(8, 64, cols), chunks, chunks]
    counts = [3, 3, 3, 3, 4, 4, 15, 15]
    return buffers + [pltpu.SemaphoreType.DMA((n,)) for n in counts]


def per_device(
    fields, merge_cotangent, attend_gain, triple_weight, bias_table, output_weight, feed_gain,
    expand_weight, shrink_weight, merge_gain, merge_weight,
):
    cot = jnp.transpose(merge_cotangent, (1, 2, 3, 4, 0)).reshape(576, 192)
    bias = jnp.transpose(bias_table[0], (1, 0, 2))
    def shaped(shapes):
        return [jax.ShapeDtypeStruct(shape, kind) for shape, kind in shapes]

    vmem_spec = pl.BlockSpec(memory_space=pltpu.VMEM)
    parts = pl.pallas_call(
        kernel,
        out_shape=shaped(
            [((TOK, C), BF16), ((2, 8, 64, 384), BF16), ((2, 8, 96, 128), BF16)]
        ),
        in_specs=[vmem_spec] * 12,
        out_specs=[vmem_spec] * 3,
        scratch_shapes=scratch(),
        compiler_params=pltpu.CompilerParams(
            collective_id=0, has_side_effects=True, vmem_limit_bytes=60 * 1024 * 1024
        ),
    )(
        fields.reshape(TOK, C), cot, attend_gain.reshape(1, C), triple_weight, bias, output_weight,
        feed_gain.reshape(1, C), expand_weight, shrink_weight.T, merge_gain,
        merge_weight.T, jnp.asarray(order_indices()),
    )
    g_fields, g_triple, g_output, g_expand, g_shrink, g_attend, g_feed, g_table = pl.pallas_call(
        results_kernel,
        out_shape=shaped(
            [
                ((TOK, C), BF16), ((C, 3 * C), F32), ((C, C), F32), ((C, FF), F32), ((C, FF), F32),
                ((1, C), F32), ((1, C), F32), ((HEADS, 2, POS), F32),
            ]
        ),
        in_specs=[vmem_spec] * 7,
        out_specs=[vmem_spec] * 8,
        compiler_params=pltpu.CompilerParams(vmem_limit_bytes=60 * 1024 * 1024),
    )(*parts, attend_gain.reshape(1, C), triple_weight, feed_gain.reshape(1, C), expand_weight)
    return (
        g_fields.reshape(fields.shape), g_triple, g_output, g_expand, g_shrink.T,
        g_attend.reshape(C), g_feed.reshape(C), jnp.transpose(g_table, (1, 0, 2))[None],
    )


def solution(mesh):
    placed = (
        P(None, None, "lat", "lon", None),
        P(None, None, None, "lat", "lon"),
        P(),
        P(),
        P("lat", None, None, None),
        P(),
        P(),
        P(),
        P(),
        P(),
        P(None, "lon"),
    )
    return jax.shard_map(
        per_device,
        mesh=mesh,
        in_specs=placed,
        out_specs=(
            P(None, None, "lat", "lon", None),
            P(),
            P(),
            P(),
            P(),
            P(),
            P(),
            P("lat", None, None, None),
        ),
        check_vma=False,
    )
```

```python
import functools
import math

import jax
import jax.numpy as jnp
import numpy as np
from jax import lax
from jax.experimental import pallas as pl
from jax.experimental.pallas import tpu as pltpu
from jax.sharding import PartitionSpec as P

F32 = jnp.float32
BF16 = jnp.bfloat16
I32 = jnp.int32
MESH = pl.DeviceIdType.MESH

EPS = 1e-05
MASKED = -1000000000.0
NLON = 16
NLAT = 8
NCHIP = 8
C = 192
HEADS = 6
FF = 768
WIN = 144
NWIN = 8
TOK = WIN * NWIN
HALF = TOK // 2
SIZES = ((216, 112), (72, 40), (72, 40))
POS = 3312
CHUNK = 288
NCHUNK = TOK // CHUNK
TILE = 48
WIDE = 896
FACTOR = 32 ** -0.5


def order_indices():
    natural_to_quad = np.full(640, -1, np.int32)
    quad_to_natural = np.full(640, -1, np.int32)
    quad_to_window = np.full(640, -1, np.int32)
    window_to_quad = np.full(640, -1, np.int32)
    for level in range(4):
        for row in range(6):
            for col in range(24):
                source = (level * 6 + row) * 24 + col
                if col >= 6:
                    place = (0 if row >= 3 else 216) + level * 54 + (row % 3) * 18 + col - 6
                else:
                    place = (432 if row >= 3 else 504) + level * 18 + (row % 3) * 6 + col
                natural_to_quad[source] = place
                quad_to_natural[place] = source
    index = 0
    for lev_win in range(2):
        for lon_win in range(2):
            for s in range(12):
                for p in range(2):
                    for r in range(6):
                        level = (lev_win * 2 + p + 1) % 4
                        col = lon_win * 12 + s
                        if col < 18:
                            place = (0 if r < 3 else 216) + level * 54 + (r % 3) * 18 + col
                        else:
                            place = (432 if r < 3 else 504) + level * 18 + (r % 3) * 6 + col - 18
                        window_to_quad[index] = place
                        quad_to_window[place] = index
                        index += 1
    cell_lane = np.full(640, -1, np.int32)
    bias_row = np.full(640, -1, np.int32)
    merged_token = np.full((2, 640), -1, np.int32)
    for lane in range(256):
        if lane % 16 < 12:
            cell_lane[lane] = (12 * (lane // 16) + 3 + lane % 16) % 192
    for k in range(WIN):
        s, p, r = k // 12, (k // 6) % 2, k % 6
        bias_row[k] = p * 256 + r * 23 + 11 - s
    for lon_win in range(2):
        for row in range(384):
            p, r, y, m = row // 192, (row // 32) % 6, (row // 16) % 2, row % 16
            if 0 <= m - lon_win * 6 < 6:
                merged_token[lon_win, row] = (2 * (m - lon_win * 6) + y) * 12 + p * 6 + r
    rows = [natural_to_quad, quad_to_natural, quad_to_window, window_to_quad]
    return np.stack(rows + [cell_lane, bias_row, merged_token[0], merged_token[1]])


def dot_nn(a, b):
    return lax.dot_general(a, b, (((1,), (0,)), ((), ())), preferred_element_type=F32)


def dot_nt(a, b):
    return lax.dot_general(a, b, (((1,), (1,)), ((), ())), preferred_element_type=F32)


def dot_tn(a, b):
    return lax.dot_general(a, b, (((0,), (0,)), ((), ())), preferred_element_type=F32)


def one_hot(rows, targets):
    ids = lax.broadcasted_iota(I32, (rows, targets.shape[1]), 0)
    return jnp.where(ids == targets, 1.0, 0.0).astype(BF16)


def statistics(values):
    centred = values - jnp.mean(values, axis=-1, keepdims=True)
    inverse = lax.rsqrt(jnp.mean(centred * centred, axis=-1, keepdims=True) + EPS)
    return centred * inverse, inverse


def norm_back(normed, inverse, scaled):
    centre = jnp.mean(scaled, axis=-1, keepdims=True)
    projected = jnp.mean(scaled * normed, axis=-1, keepdims=True)
    return inverse * (scaled - centre - normed * projected)


def gelu_parts(values):
    cumulative = 0.5 * (1.0 + lax.erf(values * (1.0 / math.sqrt(2.0))))
    density = jnp.exp(-0.5 * values * values) * (1.0 / math.sqrt(2.0 * math.pi))
    return values * cumulative, cumulative + values * density


def lanes(rows, cols):
    return lax.broadcasted_iota(I32, (rows, cols), 1)


def over_12(ids):
    return (ids * 5462) >> 16


def over_6(ids):
    return (ids * 10923) >> 16


def kernel(
    fields, cot, attend_gain, triple_w, bias, output_w, feed_gain, expand_w, shrink_t, merge_gain,
    merge_wt, orders,
    out_fields, out_g1, out_g2,
    sq, gq, a10, a01, a11, b10, b01, b11, c10, c01, c11, d10, d01, d11, x_w, ni_s, q_s, k_s, v_s, wq, wk, wv, p_s, att_s, mid_s, nm_s, act_s, slope_s, vo_s,
    b16, bl_s, bs_s, bx, ds_s, spread_s, pick_s,
    cells, cs, cb, cf, ch, wa, wb, qry, qw, st, sx, sup, sdn, tup, tdn, cp_s, go_s, gh_s, gm_s, ga_s, gmh_s,
    dq_s, dk_s, dv_s, gt_s, raw, dsh, dam, hid, tmp, g1s, g1p, g1h, g1r, g1l, g1f, g1o, g2s, g2p, g2h, g2r, g2l, g2f, g2o,
    halo_ss, halo_rs, back_ss, back_rs, st_ss, st_rs, sends, recvs,
):
    e = lax.axis_index("lon")
    d = lax.axis_index("lat")
    e_up, e_dn = lax.rem(e + 1, NLON), lax.rem(e + NLON - 1, NLON)
    d_up, d_dn = lax.rem(d + 1, NLAT), lax.rem(d + NLAT - 1, NLAT)

    def remote(src, dst, ssem, rsem, device):
        return pltpu.make_async_remote_copy(
            src_ref=src, dst_ref=dst, send_sem=ssem, recv_sem=rsem, device_id=device,
            device_id_type=MESH,
        )

    core, chip = lax.rem(e, 2), e // 2
    partner = e + 1 - 2 * core

    def chips_all(action):
        def body(step, carry):
            action(lax.rem(chip + step, NCHIP))
            return carry

        lax.fori_loop(1, NCHIP, body, 0)

    def lat_all(action):
        def body(step, carry):
            action(lax.rem(d + step, NLAT))
            return carry

        lax.fori_loop(1, NLAT, body, 0)

    def to_chip(src, dst, phase, o):
        return remote(src, dst, sends.at[phase], recvs.at[phase], (2 * o + core, d))

    def to_band(src, dst, phase, o):
        return remote(src, dst, sends.at[phase], recvs.at[phase], (e, o))

    def to_core(src, dst, phase):
        return remote(src, dst, sends.at[phase], recvs.at[phase], (partner, d))

    def arrived(region, phase):
        remote(region, region, sends.at[phase], recvs.at[phase], (partner, d)).wait_recv()

    def left(region, phase):
        remote(region, region, sends.at[phase], recvs.at[phase], (partner, d)).wait_send()

    barrier = pltpu.get_barrier_semaphore()

    def greet(device):
        pl.semaphore_signal(barrier, inc=1, device_id=device, device_id_type=MESH)

    chips_all(lambda o: greet((2 * o + core, d)))
    lat_all(lambda o: greet((e, o)))
    for device in ((e_up, d), (e_dn, d), (e_up, d_up), (e_dn, d_dn)):
        greet(device)

    def half_rows(b):
        return pl.ds(pl.multiple_of(b * HALF, HALF), HALF)

    def pack(quads, b, out):
        at = 216
        for (size, cut), message in zip(SIZES, out):
            rows = quads[at:at + size]
            rest = jnp.concatenate([rows[cut:, 128:C], jnp.zeros((2 * cut - size, 64), F32)], axis=0)
            parts = [rows[:, 0:128], jnp.concatenate([rows[:cut, 128:C], rest], axis=1)]
            if (size + cut) % 16:
                parts.append(jnp.zeros((8, 128), F32))
            message[b] = jnp.concatenate(parts, axis=0).astype(BF16)
            at += size

    def unpack(quads, b, messages):
        at = 216
        for (size, cut), message in zip(SIZES, messages):
            rows = message[b].astype(F32)
            tails = rows[size:size + cut]
            tail = jnp.concatenate([tails[:, 0:64], tails[0:size - cut, 64:128]], axis=0)
            quads[b, at:at + size, :] = jnp.concatenate([rows[0:size], tail], axis=1)
            at += size

    def halo(sources, targets, ssem, rsem, step, b):
        devices = ((e, step[1]), (step[0], d), (step[0], step[1]))
        return [
            remote(src.at[b], dst.at[b], ssem.at[3 * b + i], rsem.at[3 * b + i], dev)
            for i, (src, dst, dev) in enumerate(zip(sources, targets, devices))
        ]

    def rows_ahead(b):
        return halo((a10, a01, a11), (b10, b01, b11), halo_ss, halo_rs, (e_dn, d_dn), b)

    def rows_behind(b):
        return halo((c10, c01, c11), (d10, d01, d11), back_ss, back_rs, (e_up, d_up), b)

    to_quad = one_hot(HALF, orders[0:1, 0:HALF])

    def sort_sample(b, carry):
        quads = dot_nn(to_quad, fields[half_rows(b), :])
        sq[b] = quads
        pack(quads, b, (a10, a01, a11))
        return carry

    lax.fori_loop(0, 2, sort_sample, 0)
    pl.semaphore_wait(barrier, NCHIP - 1 + NLAT - 1 + 4)
    for b in range(2):
        for copy in rows_ahead(b):
            copy.start()

    cells[...] = dot_nn(cot[...], one_hot(192, orders[4:5, 0:256]))
    block_of = lanes(72, 128) >> 4

    def gather_cells(o, carry):
        tile = pl.ds(pl.multiple_of((o // 8) * 128, 128), 128)
        inner = lax.rem(o, 8)
        piece = jnp.zeros((72, 128), F32)
        for bl in range(8):
            part = pltpu.roll(cells[bl * 72:(bl + 1) * 72, tile], lax.rem(16 * (bl - inner) + 128, 128), 1)
            piece = jnp.where(block_of == bl, part, piece)
        for a in range(3):
            padded = jnp.concatenate([piece[a * 24:(a + 1) * 24], jnp.zeros((8, 128), F32)], axis=0)
            cs[o // 2, lax.rem(o, 2), a] = padded.astype(BF16)
        return carry

    lax.fori_loop(0, NLON, gather_cells, 0)
    wa[chip] = jnp.concatenate(
        [merge_wt[...].astype(F32), jnp.zeros((8, 768), F32)], axis=0
    ).astype(BF16)
    cb[:, chip] = cs[chip]
    for h in range(HEADS):
        b16[2 * h:2 * h + 2, :] = bias[h]
    b16[12:16, :] = jnp.zeros((4, POS), F32)
    zero_tail = jnp.zeros((16, 256 - 138), F32)
    for p in range(2):
        for r in range(6):
            parts = []
            for pk in range(2):
                at = (p * 2 + pk) * 828 + r * 138
                parts += [b16[:, at:at + 138], zero_tail]
            row = jnp.concatenate(parts, axis=1)
            high = row.astype(BF16)
            rest = row - high.astype(F32)
            middle = rest.astype(BF16)
            low = (rest - middle.astype(F32)).astype(BF16)
            at = (p * 6 + r) * 16
            bl_s[at:at + 16, :] = high
            bl_s[192 + at:192 + at + 16, :] = middle
            bl_s[384 + at:384 + at + 16, :] = low

    bias_row = orders[5:6, 0:WIN]

    def spread(s_i, carry):
        matrix = one_hot(512, bias_row + s_i)
        spread_s[s_i] = matrix
        split = dot_nn(bl_s[...], matrix)
        rows = split[0:192] + split[192:384] + split[384:576]
        at = pl.ds(pl.multiple_of(s_i * 192, 192), 192)
        bs_s[0, at, :] = rows[:, 0:128]
        bs_s[1, at, :] = jnp.concatenate([rows[:, 128:144], jnp.zeros((192, 112), F32)], axis=1)
        return carry

    lax.fori_loop(0, 12, spread, 0)

    tok_i = lax.broadcasted_iota(I32, (WIN, WIN), 0)
    tok_k = lax.broadcasted_iota(I32, (WIN, WIN), 1)
    half_i, half_k = over_6(tok_i), over_6(tok_k)
    last_band = d == NLAT - 1
    lat_differs = ((tok_i - half_i * 6 >= 3) != (tok_k - half_k * 6 >= 3)) & last_band
    lev_differs = (half_i & 1) != (half_k & 1)
    bx[:, :, HEADS * WIN:WIDE] = jnp.zeros((2, WIN, WIDE - HEADS * WIN), F32)
    for lw in range(2):
        differs = (lat_differs | lev_differs) if lw else lat_differs
        for h in range(HEADS):
            at = pl.ds(h * 2 + lw, WIN, stride=16)
            full = jnp.concatenate([bs_s.at[0][at, :], bs_s.at[1][at, :]], axis=1)[:, 0:WIN]
            bx[lw, :, h * WIN:(h + 1) * WIN] = jnp.where(differs, MASKED, full).T

    wq[...] = triple_w[:, 0:192]
    wk[...] = triple_w[:, 192:384]
    wv[...] = triple_w[:, 384:576]

    head_of = lanes(1, C) >> 5
    head_f = [jnp.where(head_of == h, 1.0, 0.0) for h in range(HEADS)]
    head_b = [mask.astype(BF16) for mask in head_f]

    blank = jnp.zeros((WIDE - HEADS * WIN, C), BF16)

    def stacked(values):
        return jnp.concatenate([values * mask for mask in head_b] + [blank], axis=0)

    def unstacked(values):
        blocks = [values[h * 32:(h + 1) * 32, h * WIN:(h + 1) * WIN] for h in range(HEADS)]
        return jnp.concatenate(blocks, axis=0).T

    to_window = one_hot(HALF, orders[2:3, 0:HALF])

    def window_rows(w):
        return pl.ds(pl.multiple_of(w * WIN, WIN), WIN)

    def chunk_rows(i):
        return pl.ds(pl.multiple_of(i * CHUNK, CHUNK), CHUNK)

    def tile_rows(i, t):
        return pl.ds(pl.multiple_of(i * CHUNK + t * TILE, 16), TILE)

    def project(i, carry):
        rows = chunk_rows(i)
        for t in range(CHUNK // TILE):
            part = tile_rows(i, t)
            normed = statistics(x_w[part, :].astype(F32))[0]
            ni_s[part, :] = (normed * attend_gain[...]).astype(BF16)
        normed_in = ni_s[rows, :]
        q_s[rows, :] = dot_nn(normed_in, wq[...]).astype(BF16)
        k_s[rows, :] = dot_nn(normed_in, wk[...]).astype(BF16)
        v_s[rows, :] = dot_nn(normed_in, wv[...]).astype(BF16)
        return carry


    def attend(pair, carry):
        lw = lax.rem(pair, 2)
        for i in range(2):
            rows = window_rows(2 * pair + i)
            raw[i] = dot_nt(k_s[rows, :], stacked(q_s[rows, :]))
        for i in range(2):
            for t in range(WIDE // 128):
                cols = slice(t * 128, (t + 1) * 128)
                scores = raw[i, :, cols] * FACTOR + bx[lw, :, cols]
                exponent = jnp.exp(scores - jnp.max(scores, axis=0, keepdims=True))
                chances = exponent * (1.0 / jnp.sum(exponent, axis=0, keepdims=True))
                p_s[2 * pair + i, :, cols] = chances.astype(BF16)
        for i in range(2):
            rows = window_rows(2 * pair + i)
            att_s[rows, :] = unstacked(dot_tn(v_s[rows, :], p_s[2 * pair + i])).astype(BF16)
        return carry

    def forward_windows(b, carry):
        for copy in rows_ahead(b):
            copy.wait()

        @pl.when(b == 0)
        def _():
            chips_all(lambda o: to_chip(cs.at[o], cb.at[:, chip], 0, o).start())
            chips_all(lambda o: to_chip(wa.at[chip], wa.at[chip], 1, o).start())

        unpack(sq, b, (b10, b01, b11))
        x_w[half_rows(b), :] = dot_nn(to_window, sq[b].astype(BF16)).astype(BF16)
        lax.fori_loop(2 * b, 2 * b + 2, project, 0)

        @pl.when(b == 1)
        def _():
            arrived(cf, 2)
            first_rows = pl.ds(0, 2)
            to_band(cb.at[core, :, first_rows], ch.at[0], 4, d_dn).start()
            to_band(cf.at[:, first_rows], ch.at[1], 4, d_dn).start()

        lax.fori_loop(2 * b, 2 * b + 2, attend, 0)

        @pl.when(b == 0)
        def _():
            arrived(cb.at[:, pl.ds(0, NCHIP - 1)], 0)
            to_core(cb.at[1 - core], cf, 2).start()

        return carry

    lax.fori_loop(0, 2, forward_windows, 0)
    arrived(wa.at[pl.ds(0, NCHIP - 1)], 1)
    to_core(wa, wb, 3).start()

    def feed(i, carry):
        rows = chunk_rows(i)
        tmp[...] = x_w[rows, :].astype(F32) + dot_nn(att_s[rows, :], output_w[...])
        for t in range(CHUNK // TILE):
            part = tile_rows(i, t)
            middle = tmp[t * TILE:(t + 1) * TILE, :]
            mid_s[part, :] = middle
            nm_s[part, :] = (statistics(middle)[0] * feed_gain[...]).astype(BF16)
        hid[...] = dot_nn(nm_s[rows, :], expand_w[...])
        for t in range(CHUNK // 16):
            part = pl.ds(pl.multiple_of(i * CHUNK + t * 16, 16), 16)
            for j in range(FF // 256):
                cols = slice(j * 256, (j + 1) * 256)
                act, slope = gelu_parts(hid[t * 16:(t + 1) * 16, cols])
                act_s[part, cols] = act.astype(BF16)
                slope_s[part, cols] = slope
        vo_s[rows, :] = (tmp[...] + dot_nt(act_s[rows, :], shrink_t[...])).astype(BF16)
        return carry

    lax.fori_loop(0, NCHUNK, feed, 0)

    arrived(ch, 4)
    arrived(wb, 3)
    gain_row = merge_gain[...].reshape(1, 4 * C)
    for r in range(6):
        x = (r + 1) % 2
        cell = (0, 1, 1, 2, 2, 3)[r]
        cols = slice(x * 384, (x + 1) * 384)
        if cell < 2:
            planes = cb[core, :, cell + 1], cf[:, cell + 1]
        else:
            planes = ch[0, :, cell - 2], ch[1, :, cell - 2]
        summed = dot_tn(planes[0].reshape(256, 128), wa[:, :, cols].reshape(256, 384))
        summed = summed + dot_tn(planes[1].reshape(256, 128), wb[:, :, cols].reshape(256, 384))
        scaled = summed * gain_row[:, x * 384:(x + 1) * 384]
        qry[2 * r] = scaled[:, 0:192].astype(BF16)
        qry[2 * r + 1] = scaled[:, 192:384].astype(BF16)

    st[...] = jnp.zeros_like(st)
    for i in range(2):
        pick_s[i] = one_hot(WIN, orders[6 + i:7 + i, 0:384])
    stat_lane = lanes(WIN, 128)
    tile_lane = lanes(TILE, 128)

    def merge_sums(w, carry):
        rows = window_rows(w)
        b, lw, lon_win = w // 4, lax.rem(w // 2, 2), lax.rem(w, 2)
        parts = []
        for p in range(2):
            level = lax.rem(lw * 2 + p + 1, 4)
            at = pl.ds(pl.multiple_of((b * 4 + level) * 16, 16), 16)
            parts.append(qry[:, at, :].reshape(192, C))
        qw[rows, :] = dot_nn(pick_s[lon_win], jnp.concatenate(parts, axis=0)).astype(BF16)
        for t in range(WIN // TILE):
            part = pl.ds(pl.multiple_of(w * WIN + t * TILE, 16), TILE)
            at = slice(t * TILE, (t + 1) * TILE)
            q = qw[part, :].astype(F32)
            v = vo_s[part, :].astype(F32)
            mean = jnp.mean(v, axis=-1, keepdims=True)
            centred = v - mean
            squares = jnp.sum(centred * centred, axis=-1, keepdims=True)
            q_sum = jnp.sum(q, axis=-1, keepdims=True)
            qv_sum = jnp.sum(q * centred, axis=-1, keepdims=True)
            total = st[b, at, :]
            for j, value in enumerate((mean, squares, q_sum, qv_sum)):
                total = jnp.where(tile_lane == 32 * j + w, value, total)
            st[b, at, :] = total
        return carry

    def sums_copies(b):
        return (
            remote(tup.at[b], sup.at[b], st_ss.at[2 * b], st_rs.at[2 * b], (e, d_up)),
            remote(tdn.at[b], sdn.at[b], st_ss.at[2 * b + 1], st_rs.at[2 * b + 1], (e, d_dn)),
        )

    def exchange(b):
        tup[b] = st.at[b][pl.ds(5, 24, stride=6), :]
        tdn[b] = st.at[b][pl.ds(0, 24, stride=6), :]
        for copy in sums_copies(b):
            copy.start()

    even = (over_12(lax.broadcasted_iota(I32, (WIN, 128), 0)) & 1) == 0

    def pair_of(values):
        return jnp.where(even, pltpu.roll(values, WIN - 12, 0), pltpu.roll(values, 12, 0))

    def cell_norm(b):
        for r, other in ((1, 2), (2, 1), (3, 4), (4, 3)):
            sx[pl.ds(r, 24, stride=6), :] = st.at[b][pl.ds(other, 24, stride=6), :]
        for copy in sums_copies(b):
            copy.wait()
        sx[pl.ds(0, 24, stride=6), :] = sup[b]
        sx[pl.ds(5, 24, stride=6), :] = sdn[b]
        own, cross = st[b], sx[...]
        group = [own, cross, pair_of(own), pair_of(cross)]
        cell_mean = (group[0] + group[1] + group[2] + group[3]) * 0.25
        variance = jnp.zeros((WIN, 128), F32)
        q_total = jnp.zeros((WIN, 128), F32)
        qv_total = jnp.zeros((WIN, 128), F32)
        for values in group:
            offset = values - cell_mean
            q_sum = pltpu.roll(values, 64, 1)
            variance = variance + pltpu.roll(values, 96, 1) + 192.0 * offset * offset
            q_total = q_total + q_sum
            qv_total = qv_total + pltpu.roll(values, 32, 1) + offset * q_sum
        cell_inverse = lax.rsqrt(jnp.where(stat_lane < 8, variance, 0.0) * (1.0 / 768.0) + EPS)
        cp_s[0] = cell_mean
        cp_s[1] = cell_inverse
        cp_s[2] = q_total * (1.0 / 768.0)
        cp_s[3] = cell_inverse * cell_inverse * qv_total * (1.0 / 768.0)

    def merge_back(w, carry):
        for t in range(WIN // TILE):
            part = pl.ds(pl.multiple_of(w * WIN + t * TILE, 16), TILE)
            at = slice(t * TILE, (t + 1) * TILE)
            mean, inverse, q_mean, projected = [
                jnp.sum(jnp.where(tile_lane == w, cp_s[j, at, :], 0.0), axis=-1, keepdims=True) for j in range(4)
            ]
            v = vo_s[part, :].astype(F32) - mean
            go_s[part, :] = (inverse * (qw[part, :].astype(F32) - q_mean - v * projected)).astype(BF16)
        return carry

    def feed_back(i, carry):
        rows = chunk_rows(i)
        go = go_s[rows, :]
        gh = (dot_nn(go, shrink_t[...]) * slope_s[rows, :]).astype(BF16)
        gh_s[rows, :] = gh
        tmp[...] = dot_nt(gh, expand_w[...])
        for t in range(CHUNK // TILE):
            part = tile_rows(i, t)
            gnm = tmp[t * TILE:(t + 1) * TILE, :]
            unit, inverse = statistics(mid_s[part, :])
            gm = go_s[part, :].astype(F32) + norm_back(unit, inverse, gnm * feed_gain[...])
            gm_s[part, :] = gm
            gmh_s[part, :] = gm.astype(BF16)
        ga_s[rows, :] = dot_nt(gmh_s[rows, :], output_w[...]).astype(BF16)
        return carry

    def forward_sample(b, carry):
        lax.fori_loop(4 * b, 4 * b + 4, merge_sums, 0)
        exchange(b)
        return carry

    def backward_sample(b, carry):
        cell_norm(b)
        lax.fori_loop(4 * b, 4 * b + 4, merge_back, 0)
        lax.fori_loop(2 * b, 2 * b + 2, feed_back, 0)
        return carry

    lax.fori_loop(0, 2, forward_sample, 0)
    lax.fori_loop(0, 2, backward_sample, 0)

    g_expand = dot_tn(nm_s[...], gh_s[...]).astype(BF16)
    g_shrink = dot_tn(go_s[...], act_s[...]).astype(BF16)
    g_output = dot_tn(att_s[...], gmh_s[...]).astype(BF16)
    for i in range(4):
        for j in range(2):
            g1s[0, 2 * i + j, 0:48] = g_expand[i * 48:(i + 1) * 48, j * 384:(j + 1) * 384]
            g1s[1, 2 * i + j, 0:48] = g_shrink[i * 48:(i + 1) * 48, j * 384:(j + 1) * 384]
    wide = jnp.concatenate([g_output[0:96], g_output[96:192]], axis=1)
    for i in range(NCHIP):
        for j in range(2):
            at = (i * 2 + j) * 16
            g1s[j, i, 48:64] = wide[at:at + 16] if at < 96 else jnp.zeros((16, 384), BF16)

    def sum_of(ref, count, rows):
        total = ref[0, rows].astype(F32)
        for o in range(1, count):
            total = total + ref[o, rows].astype(F32)
        return total.astype(BF16)

    def add_pair(mine, other, out):
        def body(o, carry):
            out[o] = (mine[core, o].astype(F32) + other[o].astype(F32)).astype(BF16)
            return carry

        lax.fori_loop(0, NCHIP, body, 0)

    others = pl.ds(0, NCHIP - 1)
    to_core(g1s.at[1 - core], g1p, 5).start()

    ds_s[...] = jnp.zeros_like(ds_s)

    def attend_back(pair, carry):
        lw = lax.rem(pair, 2)
        for i in range(2):
            rows = window_rows(2 * pair + i)
            dam[i] = stacked(ga_s[rows, :])
            raw[i] = dot_nt(v_s[rows, :], dam[i])
        for i in range(2):
            for t in range(WIDE // 128):
                cols = slice(t * 128, (t + 1) * 128)
                chances = p_s[2 * pair + i, :, cols].astype(F32)
                weighted = raw[i, :, cols]
                centre = jnp.sum(chances * weighted, axis=0, keepdims=True)
                dsh[i, :, cols] = (chances * (weighted - centre)).astype(BF16)
        for i in range(2):
            rows = window_rows(2 * pair + i)
            dv_s[rows, :] = dot_nn(p_s[2 * pair + i], dam[i]).astype(BF16)
            dq_s[rows, :] = (unstacked(dot_tn(k_s[rows, :], dsh[i])) * FACTOR).astype(BF16)
            dk_s[rows, :] = (dot_nn(dsh[i], stacked(q_s[rows, :])) * FACTOR).astype(BF16)
        ds_s[lw] = ds_s[lw] + (dsh[0].astype(F32) + dsh[1].astype(F32))
        return carry

    all_rows = slice(0, 64)
    def windows_back(pair, carry):
        attend_back(pair, carry)

        @pl.when(pair == 0)
        def _():
            arrived(g1p, 5)
            add_pair(g1s, g1p, g1h)
            g1r[chip] = g1h[chip]
            chips_all(lambda o: to_chip(g1h.at[o], g1r.at[chip], 6, o).start())

        return carry

    def second_gradients():
        ni = ni_s[...]
        g_triple = jnp.concatenate(
            [dot_tn(ni, dq_s[...]), dot_tn(ni, dk_s[...]), dot_tn(ni, dv_s[...]), jnp.zeros((C, 64), F32)], axis=1
        ).astype(BF16)
        for i in range(3):
            for j in range(5):
                at = 5 * i + j
                g2s[at // 8, at % 8, 0:64] = g_triple[i * 64:(i + 1) * 64, j * 128:(j + 1) * 128]
        g2s[1, 7, 0:64] = jnp.zeros((64, 128), BF16)
        for lw in range(2):
            for h in range(HEADS):
                at = pl.ds(h * 2 + lw, WIN, stride=16)
                part = ds_s[lw, :, h * WIN:(h + 1) * WIN].T
                bs_s.at[0][at, :] = part[:, 0:128]
                bs_s.at[1][at, :] = jnp.concatenate([part[:, 128:144], jnp.zeros((WIN, 112), F32)], axis=1)

        def fold(s_i, carry):
            at = pl.ds(pl.multiple_of(s_i * 192, 192), 192)
            rows = jnp.concatenate([bs_s[0, at, :], bs_s[1, at, :]], axis=1)[:, 0:WIN].astype(BF16)
            return carry + dot_nt(rows, spread_s[s_i])

        folded = lax.fori_loop(0, 12, fold, jnp.zeros((192, 512), F32))
        pieces_t = []
        for p in range(2):
            for pk in range(2):
                for r in range(6):
                    at = (p * 6 + r) * 16
                    pieces_t.append(folded[at:at + 16, pk * 256:pk * 256 + 138])
        table = jnp.concatenate(pieces_t + [jnp.zeros((16, 4096 - POS), F32)], axis=1).astype(BF16)
        for o in range(32):
            g2s[o // 16, (o // 2) % 8, 64 + 16 * (o % 2):80 + 16 * (o % 2)] = table[:, o * 128:(o + 1) * 128]
        to_core(g2s.at[1 - core], g2p, 9).start()

    def project_back(i, carry):
        rows = chunk_rows(i)
        tmp[...] = (
            dot_nt(dq_s[rows, :], wq[...]) + dot_nt(dk_s[rows, :], wk[...]) + dot_nt(dv_s[rows, :], wv[...])
        )
        for t in range(CHUNK // TILE):
            part = tile_rows(i, t)
            unit, inverse = statistics(x_w[part, :].astype(F32))
            back = norm_back(unit, inverse, tmp[t * TILE:(t + 1) * TILE, :] * attend_gain[...])
            gt_s[part, :] = (gm_s[part, :] + back).astype(BF16)
        return carry

    from_window = one_hot(HALF, orders[3:4, 0:HALF])

    def backward_windows(b, carry):
        lax.fori_loop(2 * b, 2 * b + 2, windows_back, 0)

        @pl.when(b == 1)
        def _():
            arrived(g1l.at[others], 7)
            g1f[chip] = sum_of(g1l, NLAT, all_rows)
            chips_all(lambda o: to_chip(g1f.at[chip], g1f.at[chip], 8, o).start())
            second_gradients()

        lax.fori_loop(2 * b, 2 * b + 2, project_back, 0)

        @pl.when(b == 0)
        def _():
            arrived(g1r.at[others], 6)
            g1l[d] = sum_of(g1r, NCHIP, all_rows)
            lat_all(lambda o: to_band(g1l.at[d], g1l.at[d], 7, o).start())

        @pl.when(b == 1)
        def _():
            arrived(g2p, 9)
            add_pair(g2s, g2p, g2h)
            g2r[chip] = g2h[chip]
            chips_all(lambda o: to_chip(g2h.at[o], g2r.at[chip], 10, o).start())

        quads = dot_nn(from_window, gt_s[half_rows(b), :])
        gq[b] = quads
        pack(quads, b, (c10, c01, c11))
        for copy in rows_behind(b):
            copy.start()
        return carry

    lax.fori_loop(0, 2, backward_windows, 0)

    arrived(g1f.at[others], 8)
    to_core(g1f, g1o, 11).start()

    arrived(g2r.at[others], 10)
    g2l[d] = sum_of(g2r, NCHIP, slice(0, 64))
    lat_all(lambda o: to_band(g2l.at[d], g2l.at[d], 12, o).start())
    g2f[chip, 64:96] = sum_of(g2r, NCHIP, slice(64, 96))

    to_natural = one_hot(HALF, orders[1:2, 0:HALF])

    def unsort_sample(b, carry):
        for copy in rows_behind(b):
            copy.wait()
        unpack(gq, b, (d10, d01, d11))
        out_fields[half_rows(b), :] = dot_nn(to_natural, gq[b].astype(BF16)).astype(BF16)
        return carry

    lax.fori_loop(0, 1, unsort_sample, 0)
    arrived(g2l.at[others], 12)
    g2f[chip, 0:64] = sum_of(g2l, NLAT, slice(0, 64))
    chips_all(lambda o: to_chip(g2f.at[chip], g2f.at[chip], 13, o).start())


    lax.fori_loop(1, 2, unsort_sample, 0)
    arrived(g1o, 11)
    out_g1[core] = g1f[...]
    out_g1[1 - core] = g1o[...]
    arrived(g2f.at[others], 13)
    to_core(g2f, g2o, 14).start()
    out_g2[core] = g2f[...]
    arrived(g2o, 14)
    out_g2[1 - core] = g2o[...]

    left(cs.at[others], 0)
    left(wa.at[others], 1)
    left(cf, 2)
    left(wb, 3)
    left(ch, 4)
    left(g1p, 5)
    left(g1r.at[others], 6)
    left(g1l.at[others], 7)
    left(g1f.at[others], 8)
    left(g2p, 9)
    left(g2r.at[others], 10)
    left(g1o, 11)
    left(g2l.at[others], 12)
    left(g2f.at[others], 13)
    left(g2o, 14)


def results_kernel(
    fields, g1, g2, attend_gain, triple_w, feed_gain, expand_w,
    out_fields, out_triple, out_output, out_expand, out_shrink, out_attend, out_feed, out_table,
):
    out_fields[...] = fields[...]
    for i in range(4):
        for j in range(2):
            rows, cols = slice(i * 48, (i + 1) * 48), slice(j * 384, (j + 1) * 384)
            out_expand[rows, cols] = g1[0, 2 * i + j, 0:48].astype(F32)
            out_shrink[rows, cols] = g1[1, 2 * i + j, 0:48].astype(F32)
    for i in range(6):
        wide = g1[i % 2, i // 2, 48:64].astype(F32)
        out_output[i * 16:(i + 1) * 16, :] = wide[:, 0:C]
        out_output[96 + i * 16:96 + (i + 1) * 16, :] = wide[:, C:2 * C]
    for i in range(3):
        for j in range(5):
            at, size = 5 * i + j, 128 if j < 4 else 64
            part = g2[at // 8, at % 8, 0:64].astype(F32)
            out_triple[i * 64:(i + 1) * 64, j * 128:j * 128 + size] = part[:, 0:size]
    table = jnp.concatenate(
        [g2[o // 16, (o // 2) % 8, 64 + 16 * (o % 2):80 + 16 * (o % 2)] for o in range(32)], axis=1
    ).astype(F32)
    for h in range(HEADS):
        out_table[h] = table[2 * h:2 * h + 2, 0:POS]

    def gain_gradient(grad, weight, gain):
        product = (grad[...] * weight[...].astype(F32)).astype(BF16)
        total = dot_nt(jnp.ones((16, product.shape[1]), BF16), product)
        return total[0:1] / gain[...]

    out_attend[...] = gain_gradient(out_triple, triple_w, attend_gain)
    out_feed[...] = gain_gradient(out_expand, expand_w, feed_gain)


def scratch():
    def vmem(*shape, kind=BF16):
        return pltpu.VMEM(shape, kind)

    token = vmem(TOK, C)
    token_f = vmem(TOK, C, kind=F32)
    weight = vmem(C, C)
    quad = vmem(2, HALF, C, kind=F32)
    halves = [vmem(2, 336, 128), vmem(2, 112, 128), vmem(2, 112, 128)]
    stat = vmem(WIN, 128, kind=F32)
    small = vmem(2, 24, 128, kind=F32)
    buffers = [
        quad, quad, *halves, *halves, *halves, *halves, token, token, token, token, token, weight, weight, weight,
        vmem(NWIN, WIN, WIDE), token, token_f, token, vmem(TOK, FF), vmem(TOK, FF, kind=F32), token,
        vmem(16, POS, kind=F32), vmem(576, 512), vmem(2, 2304, 128, kind=F32),
        vmem(2, WIN, WIDE, kind=F32), vmem(2, WIN, WIDE, kind=F32),
        vmem(12, 512, WIN), vmem(2, WIN, 384),
        vmem(576, 256, kind=F32), vmem(8, 2, 3, 32, 128), vmem(2, 8, 3, 32, 128), vmem(8, 3, 32, 128), vmem(2, 8, 2, 32, 128),
        vmem(8, 32, 768), vmem(8, 32, 768),
        vmem(12, 128, C), token, vmem(2, WIN, 128, kind=F32), stat, small, small, small, small, vmem(4, WIN, 128, kind=F32),
        token, vmem(TOK, FF), token_f, token, token, token, token, token, token,
        vmem(2, WIN, WIDE, kind=F32), vmem(2, WIN, WIDE), vmem(2, WIDE, C), vmem(CHUNK, FF, kind=F32),
        vmem(CHUNK, C, kind=F32),
    ]
    for rows, cols in ((64, 384), (96, 128)):
        chunks = vmem(8, rows, cols)
        buffers += [vmem(2, 8, rows, cols), chunks, chunks, chunks, vmem(8, 64, cols), chunks, chunks]
    counts = [6, 6, 6, 6, 4, 4, 15, 15]
    return buffers + [pltpu.SemaphoreType.DMA((n,)) for n in counts]


def per_device(
    fields, merge_cotangent, attend_gain, triple_weight, bias_table, output_weight, feed_gain,
    expand_weight, shrink_weight, merge_gain, merge_weight,
):
    cot = jnp.transpose(merge_cotangent, (1, 2, 3, 4, 0)).reshape(576, 192)
    bias = jnp.transpose(bias_table[0], (1, 0, 2))
    def shaped(shapes):
        return [jax.ShapeDtypeStruct(shape, kind) for shape, kind in shapes]

    vmem_spec = pl.BlockSpec(memory_space=pltpu.VMEM)
    parts = pl.pallas_call(
        kernel,
        out_shape=shaped(
            [((TOK, C), BF16), ((2, 8, 64, 384), BF16), ((2, 8, 96, 128), BF16)]
        ),
        in_specs=[vmem_spec] * 12,
        out_specs=[vmem_spec] * 3,
        scratch_shapes=scratch(),
        compiler_params=pltpu.CompilerParams(
            collective_id=0, has_side_effects=True, vmem_limit_bytes=60 * 1024 * 1024
        ),
    )(
        fields.reshape(TOK, C), cot, attend_gain.reshape(1, C), triple_weight, bias, output_weight,
        feed_gain.reshape(1, C), expand_weight, shrink_weight.T, merge_gain,
        merge_weight.T, jnp.asarray(order_indices()),
    )
    g_fields, g_triple, g_output, g_expand, g_shrink, g_attend, g_feed, g_table = pl.pallas_call(
        results_kernel,
        out_shape=shaped(
            [
                ((TOK, C), BF16), ((C, 3 * C), F32), ((C, C), F32), ((C, FF), F32), ((C, FF), F32),
                ((1, C), F32), ((1, C), F32), ((HEADS, 2, POS), F32),
            ]
        ),
        in_specs=[vmem_spec] * 7,
        out_specs=[vmem_spec] * 8,
        compiler_params=pltpu.CompilerParams(vmem_limit_bytes=60 * 1024 * 1024),
    )(*parts, attend_gain.reshape(1, C), triple_weight, feed_gain.reshape(1, C), expand_weight)
    return (
        g_fields.reshape(fields.shape), g_triple, g_output, g_expand, g_shrink.T,
        g_attend.reshape(C), g_feed.reshape(C), jnp.transpose(g_table, (1, 0, 2))[None],
    )


def solution(mesh):
    placed = (
        P(None, None, "lat", "lon", None),
        P(None, None, None, "lat", "lon"),
        P(),
        P(),
        P("lat", None, None, None),
        P(),
        P(),
        P(),
        P(),
        P(),
        P(None, "lon"),
    )
    return jax.shard_map(
        per_device,
        mesh=mesh,
        in_specs=placed,
        out_specs=(
            P(None, None, "lat", "lon", None),
            P(),
            P(),
            P(),
            P(),
            P(),
            P(),
            P("lat", None, None, None),
        ),
        check_vma=False,
    )
```

```python
import functools
import math

import jax
import jax.numpy as jnp
import numpy as np
from jax import lax
from jax.experimental import pallas as pl
from jax.experimental.pallas import tpu as pltpu
from jax.sharding import PartitionSpec as P

F32 = jnp.float32
BF16 = jnp.bfloat16
I32 = jnp.int32
MESH = pl.DeviceIdType.MESH

EPS = 1e-05
MASKED = -1000000000.0
NLON = 16
NLAT = 8
NCHIP = 8
C = 192
HEADS = 6
FF = 768
WIN = 144
NWIN = 8
TOK = WIN * NWIN
HALF = TOK // 2
SIZES = ((216, 112), (72, 40), (72, 40))
POS = 3312
CHUNK = 288
NCHUNK = TOK // CHUNK
TILE = 48
WIDE = 896
FACTOR = 32 ** -0.5


def order_indices():
    natural_to_quad = np.full(640, -1, np.int32)
    quad_to_natural = np.full(640, -1, np.int32)
    quad_to_window = np.full(640, -1, np.int32)
    window_to_quad = np.full(640, -1, np.int32)
    for level in range(4):
        for row in range(6):
            for col in range(24):
                source = (level * 6 + row) * 24 + col
                if col >= 6:
                    place = (0 if row >= 3 else 216) + level * 54 + (row % 3) * 18 + col - 6
                else:
                    place = (432 if row >= 3 else 504) + level * 18 + (row % 3) * 6 + col
                natural_to_quad[source] = place
                quad_to_natural[place] = source
    index = 0
    for lev_win in range(2):
        for lon_win in range(2):
            for s in range(12):
                for p in range(2):
                    for r in range(6):
                        level = (lev_win * 2 + p + 1) % 4
                        col = lon_win * 12 + s
                        if col < 18:
                            place = (0 if r < 3 else 216) + level * 54 + (r % 3) * 18 + col
                        else:
                            place = (432 if r < 3 else 504) + level * 18 + (r % 3) * 6 + col - 18
                        window_to_quad[index] = place
                        quad_to_window[place] = index
                        index += 1
    cell_lane = np.full(640, -1, np.int32)
    bias_row = np.full(640, -1, np.int32)
    merged_token = np.full((2, 640), -1, np.int32)
    for lane in range(256):
        if lane % 16 < 12:
            cell_lane[lane] = (12 * (lane // 16) + 3 + lane % 16) % 192
    for k in range(WIN):
        s, p, r = k // 12, (k // 6) % 2, k % 6
        bias_row[k] = p * 256 + r * 23 + 11 - s
    for lon_win in range(2):
        for row in range(384):
            p, r, y, m = row // 192, (row // 32) % 6, (row // 16) % 2, row % 16
            if 0 <= m - lon_win * 6 < 6:
                merged_token[lon_win, row] = (2 * (m - lon_win * 6) + y) * 12 + p * 6 + r
    rows = [natural_to_quad, quad_to_natural, quad_to_window, window_to_quad]
    return np.stack(rows + [cell_lane, bias_row, merged_token[0], merged_token[1]])


def dot_nn(a, b):
    return lax.dot_general(a, b, (((1,), (0,)), ((), ())), preferred_element_type=F32)


def dot_nt(a, b):
    return lax.dot_general(a, b, (((1,), (1,)), ((), ())), preferred_element_type=F32)


def dot_tn(a, b):
    return lax.dot_general(a, b, (((0,), (0,)), ((), ())), preferred_element_type=F32)


def one_hot(rows, targets):
    ids = lax.broadcasted_iota(I32, (rows, targets.shape[1]), 0)
    return jnp.where(ids == targets, 1.0, 0.0).astype(BF16)


def statistics(values):
    centred = values - jnp.mean(values, axis=-1, keepdims=True)
    inverse = lax.rsqrt(jnp.mean(centred * centred, axis=-1, keepdims=True) + EPS)
    return centred * inverse, inverse


def norm_back(normed, inverse, scaled):
    centre = jnp.mean(scaled, axis=-1, keepdims=True)
    projected = jnp.mean(scaled * normed, axis=-1, keepdims=True)
    return inverse * (scaled - centre - normed * projected)


def gelu_parts(values):
    cumulative = 0.5 * (1.0 + lax.erf(values * (1.0 / math.sqrt(2.0))))
    density = jnp.exp(-0.5 * values * values) * (1.0 / math.sqrt(2.0 * math.pi))
    return values * cumulative, cumulative + values * density


def lanes(rows, cols):
    return lax.broadcasted_iota(I32, (rows, cols), 1)


def over_12(ids):
    return (ids * 5462) >> 16


def over_6(ids):
    return (ids * 10923) >> 16


def kernel(
    fields, cot, attend_gain, triple_w, bias, output_w, feed_gain, expand_w, shrink_t, merge_gain,
    merge_wt, orders,
    out_fields, out_g1, out_g2,
    sq, gq, a10, a01, a11, b10, b01, b11, c10, c01, c11, d10, d01, d11, x_w, ni_s, q_s, k_s, v_s, wq, wk, wv, p_s, att_s, mid_s, nm_s, act_s, slope_s, vo_s,
    b16, bl_s, bs_s, bx, ds_s, spread_s, pick_s,
    cells, cs, cb, cf, ch, wa, wb, qry, qw, st, sx, sup, sdn, tup, tdn, cp_s, go_s, gh_s, gm_s, ga_s, gmh_s,
    dt_s, gt_s, raw, dsh, dam, hid, tmp, g1s, g1p, g1h, g1r, g1l, g1f, g1o, g2s, g2p, g2h, g2r, g2l, g2f, g2o,
    halo_ss, halo_rs, back_ss, back_rs, st_ss, st_rs, sends, recvs,
):
    e = lax.axis_index("lon")
    d = lax.axis_index("lat")
    e_up, e_dn = lax.rem(e + 1, NLON), lax.rem(e + NLON - 1, NLON)
    d_up, d_dn = lax.rem(d + 1, NLAT), lax.rem(d + NLAT - 1, NLAT)

    def remote(src, dst, ssem, rsem, device):
        return pltpu.make_async_remote_copy(
            src_ref=src, dst_ref=dst, send_sem=ssem, recv_sem=rsem, device_id=device,
            device_id_type=MESH,
        )

    core, chip = lax.rem(e, 2), e // 2
    partner = e + 1 - 2 * core

    def chips_all(action):
        def body(step, carry):
            action(lax.rem(chip + step, NCHIP))
            return carry

        lax.fori_loop(1, NCHIP, body, 0)

    def lat_all(action):
        def body(step, carry):
            action(lax.rem(d + step, NLAT))
            return carry

        lax.fori_loop(1, NLAT, body, 0)

    def to_chip(src, dst, phase, o):
        return remote(src, dst, sends.at[phase], recvs.at[phase], (2 * o + core, d))

    def to_band(src, dst, phase, o):
        return remote(src, dst, sends.at[phase], recvs.at[phase], (e, o))

    def to_core(src, dst, phase):
        return remote(src, dst, sends.at[phase], recvs.at[phase], (partner, d))

    def arrived(region, phase):
        remote(region, region, sends.at[phase], recvs.at[phase], (partner, d)).wait_recv()

    def left(region, phase):
        remote(region, region, sends.at[phase], recvs.at[phase], (partner, d)).wait_send()

    barrier = pltpu.get_barrier_semaphore()

    def greet(device):
        pl.semaphore_signal(barrier, inc=1, device_id=device, device_id_type=MESH)

    chips_all(lambda o: greet((2 * o + core, d)))
    lat_all(lambda o: greet((e, o)))
    for device in ((e_up, d), (e_dn, d), (e_up, d_up), (e_dn, d_dn)):
        greet(device)

    def half_rows(b):
        return pl.ds(pl.multiple_of(b * HALF, HALF), HALF)

    def pack(quads, b, out):
        at = 216
        for (size, cut), message in zip(SIZES, out):
            rows = quads[at:at + size]
            rest = jnp.concatenate([rows[cut:, 128:C], jnp.zeros((2 * cut - size, 64), F32)], axis=0)
            parts = [rows[:, 0:128], jnp.concatenate([rows[:cut, 128:C], rest], axis=1)]
            if (size + cut) % 16:
                parts.append(jnp.zeros((8, 128), F32))
            message[b] = jnp.concatenate(parts, axis=0).astype(BF16)
            at += size

    def unpack(quads, b, messages):
        at = 216
        for (size, cut), message in zip(SIZES, messages):
            rows = message[b].astype(F32)
            tails = rows[size:size + cut]
            tail = jnp.concatenate([tails[:, 0:64], tails[0:size - cut, 64:128]], axis=0)
            quads[b, at:at + size, :] = jnp.concatenate([rows[0:size], tail], axis=1)
            at += size

    def halo(sources, targets, ssem, rsem, step, b):
        devices = ((e, step[1]), (step[0], d), (step[0], step[1]))
        return [
            remote(src.at[b], dst.at[b], ssem.at[3 * b + i], rsem.at[3 * b + i], dev)
            for i, (src, dst, dev) in enumerate(zip(sources, targets, devices))
        ]

    def rows_ahead(b):
        return halo((a10, a01, a11), (b10, b01, b11), halo_ss, halo_rs, (e_dn, d_dn), b)

    def rows_behind(b):
        return halo((c10, c01, c11), (d10, d01, d11), back_ss, back_rs, (e_up, d_up), b)

    to_quad = one_hot(HALF, orders[0:1, 0:HALF])

    def sort_sample(b, carry):
        quads = dot_nn(to_quad, fields[half_rows(b), :])
        sq[b] = quads
        pack(quads, b, (a10, a01, a11))
        return carry

    lax.fori_loop(0, 2, sort_sample, 0)
    pl.semaphore_wait(barrier, NCHIP - 1 + NLAT - 1 + 4)
    for b in range(2):
        for copy in rows_ahead(b):
            copy.start()

    cells[...] = dot_nn(cot[...], one_hot(192, orders[4:5, 0:256]))
    block_of = lanes(72, 128) >> 4

    def gather_cells(o, carry):
        tile = pl.ds(pl.multiple_of((o // 8) * 128, 128), 128)
        inner = lax.rem(o, 8)
        piece = jnp.zeros((72, 128), F32)
        for bl in range(8):
            part = pltpu.roll(cells[bl * 72:(bl + 1) * 72, tile], lax.rem(16 * (bl - inner) + 128, 128), 1)
            piece = jnp.where(block_of == bl, part, piece)
        for a in range(3):
            padded = jnp.concatenate([piece[a * 24:(a + 1) * 24], jnp.zeros((8, 128), F32)], axis=0)
            cs[o // 2, lax.rem(o, 2), a] = padded.astype(BF16)
        return carry

    lax.fori_loop(0, NLON, gather_cells, 0)
    wa[chip] = jnp.concatenate(
        [merge_wt[...].astype(F32), jnp.zeros((8, 768), F32)], axis=0
    ).astype(BF16)
    cb[:, chip] = cs[chip]
    for h in range(HEADS):
        b16[2 * h:2 * h + 2, :] = bias[h]
    b16[12:16, :] = jnp.zeros((4, POS), F32)
    zero_tail = jnp.zeros((16, 256 - 138), F32)
    for p in range(2):
        for r in range(6):
            parts = []
            for pk in range(2):
                at = (p * 2 + pk) * 828 + r * 138
                parts += [b16[:, at:at + 138], zero_tail]
            row = jnp.concatenate(parts, axis=1)
            high = row.astype(BF16)
            rest = row - high.astype(F32)
            middle = rest.astype(BF16)
            low = (rest - middle.astype(F32)).astype(BF16)
            at = (p * 6 + r) * 16
            bl_s[at:at + 16, :] = high
            bl_s[192 + at:192 + at + 16, :] = middle
            bl_s[384 + at:384 + at + 16, :] = low

    bias_row = orders[5:6, 0:WIN]

    def spread(s_i, carry):
        matrix = one_hot(512, bias_row + s_i)
        spread_s[s_i] = matrix
        split = dot_nn(bl_s[...], matrix)
        rows = split[0:192] + split[192:384] + split[384:576]
        at = pl.ds(pl.multiple_of(s_i * 192, 192), 192)
        bs_s[0, at, :] = rows[:, 0:128]
        bs_s[1, at, :] = jnp.concatenate([rows[:, 128:144], jnp.zeros((192, 112), F32)], axis=1)
        return carry

    lax.fori_loop(0, 12, spread, 0)

    tok_i = lax.broadcasted_iota(I32, (WIN, WIN), 0)
    tok_k = lax.broadcasted_iota(I32, (WIN, WIN), 1)
    half_i, half_k = over_6(tok_i), over_6(tok_k)
    last_band = d == NLAT - 1
    lat_differs = ((tok_i - half_i * 6 >= 3) != (tok_k - half_k * 6 >= 3)) & last_band
    lev_differs = (half_i & 1) != (half_k & 1)
    bx[:, :, HEADS * WIN:WIDE] = jnp.zeros((2, WIN, WIDE - HEADS * WIN), F32)
    for lw in range(2):
        differs = (lat_differs | lev_differs) if lw else lat_differs
        for h in range(HEADS):
            at = pl.ds(h * 2 + lw, WIN, stride=16)
            full = jnp.concatenate([bs_s.at[0][at, :], bs_s.at[1][at, :]], axis=1)[:, 0:WIN]
            spread_bias = jnp.where(differs, MASKED, full).T
            bx[lw, :, h * 128:(h + 1) * 128] = spread_bias[:, 0:128]
            bx[lw, :, 768 + h * 16:784 + h * 16] = spread_bias[:, 128:WIN]

    wq[...] = triple_w[:, 0:192]
    wk[...] = triple_w[:, 192:384]
    wv[...] = triple_w[:, 384:576]

    head_of = lanes(1, C) >> 5
    head_f = [jnp.where(head_of == h, 1.0, 0.0) for h in range(HEADS)]
    head_b = [mask.astype(BF16) for mask in head_f]

    blank = jnp.zeros((WIDE - HEADS * WIN, C), BF16)

    def stacked(values):
        first, rest = values[0:128], values[128:WIN]
        parts = [first * mask for mask in head_b] + [rest * mask for mask in head_b]
        return jnp.concatenate(parts + [blank], axis=0)

    def per_head(left, right):
        turned = left.T
        wide = [dot_nn(turned[64 * i:64 * i + 64], right[:, 256 * i:256 * i + 256]) for i in range(3)]
        tail = dot_nn(turned, right[:, 768:WIDE])
        blocks = []
        for h in range(HEADS):
            at, row = 128 * (h % 2), 32 * (h % 2)
            blocks.append(
                jnp.concatenate(
                    [wide[h // 2][row:row + 32, at:at + 128], tail[32 * h:32 * h + 32, 16 * h:16 * h + 16]], axis=1
                )
            )
        return jnp.concatenate(blocks, axis=0).T

    to_window = one_hot(HALF, orders[2:3, 0:HALF])

    def window_rows(w):
        return pl.ds(pl.multiple_of(w * WIN, WIN), WIN)

    def chunk_rows(i):
        return pl.ds(pl.multiple_of(i * CHUNK, CHUNK), CHUNK)

    def tile_rows(i, t):
        return pl.ds(pl.multiple_of(i * CHUNK + t * TILE, 16), TILE)

    def project(i, carry):
        rows = chunk_rows(i)
        for t in range(CHUNK // TILE):
            part = tile_rows(i, t)
            normed = statistics(x_w[part, :].astype(F32))[0]
            ni_s[part, :] = (normed * attend_gain[...]).astype(BF16)
        normed_in = ni_s[rows, :]
        q_s[rows, :] = dot_nn(normed_in, wq[...]).astype(BF16)
        k_s[rows, :] = dot_nn(normed_in, wk[...]).astype(BF16)
        v_s[rows, :] = dot_nn(normed_in, wv[...]).astype(BF16)
        return carry


    def attend(pair, carry):
        lw = lax.rem(pair, 2)
        for i in range(2):
            rows = window_rows(2 * pair + i)
            raw[i] = dot_nt(k_s[rows, :], stacked(q_s[rows, :]))
        for i in range(2):
            for t in range(WIDE // 128):
                cols = slice(t * 128, (t + 1) * 128)
                scores = raw[i, :, cols] * FACTOR + bx[lw, :, cols]
                exponent = jnp.exp(scores - jnp.max(scores, axis=0, keepdims=True))
                chances = exponent * (1.0 / jnp.sum(exponent, axis=0, keepdims=True))
                p_s[2 * pair + i, :, cols] = chances.astype(BF16)
        for i in range(2):
            rows = window_rows(2 * pair + i)
            att_s[rows, :] = per_head(v_s[rows, :], p_s[2 * pair + i]).astype(BF16)
        return carry

    def forward_windows(b, carry):
        for copy in rows_ahead(b):
            copy.wait()

        @pl.when(b == 0)
        def _():
            chips_all(lambda o: to_chip(cs.at[o], cb.at[:, chip], 0, o).start())
            chips_all(lambda o: to_chip(wa.at[chip], wa.at[chip], 1, o).start())

        unpack(sq, b, (b10, b01, b11))
        x_w[half_rows(b), :] = dot_nn(to_window, sq[b].astype(BF16)).astype(BF16)
        lax.fori_loop(2 * b, 2 * b + 2, project, 0)

        @pl.when(b == 1)
        def _():
            arrived(cf, 2)
            first_rows = pl.ds(0, 2)
            to_band(cb.at[core, :, first_rows], ch.at[0], 4, d_dn).start()
            to_band(cf.at[:, first_rows], ch.at[1], 4, d_dn).start()

        lax.fori_loop(2 * b, 2 * b + 2, attend, 0)

        @pl.when(b == 0)
        def _():
            arrived(cb.at[:, pl.ds(0, NCHIP - 1)], 0)
            to_core(cb.at[1 - core], cf, 2).start()

        return carry

    lax.fori_loop(0, 2, forward_windows, 0)
    arrived(wa.at[pl.ds(0, NCHIP - 1)], 1)
    to_core(wa, wb, 3).start()

    def feed(i, carry):
        rows = chunk_rows(i)
        tmp[...] = x_w[rows, :].astype(F32) + dot_nn(att_s[rows, :], output_w[...])
        for t in range(CHUNK // TILE):
            part = tile_rows(i, t)
            middle = tmp[t * TILE:(t + 1) * TILE, :]
            mid_s[part, :] = middle
            nm_s[part, :] = (statistics(middle)[0] * feed_gain[...]).astype(BF16)
        hid[...] = dot_nn(nm_s[rows, :], expand_w[...])
        for t in range(CHUNK // 16):
            part = pl.ds(pl.multiple_of(i * CHUNK + t * 16, 16), 16)
            for j in range(FF // 256):
                cols = slice(j * 256, (j + 1) * 256)
                act, slope = gelu_parts(hid[t * 16:(t + 1) * 16, cols])
                act_s[part, cols] = act.astype(BF16)
                slope_s[part, cols] = slope
        vo_s[rows, :] = (tmp[...] + dot_nt(act_s[rows, :], shrink_t[...])).astype(BF16)
        return carry

    lax.fori_loop(0, NCHUNK, feed, 0)

    arrived(ch, 4)
    arrived(wb, 3)
    gain_row = merge_gain[...].reshape(1, 4 * C)
    for r in range(6):
        x = (r + 1) % 2
        cell = (0, 1, 1, 2, 2, 3)[r]
        cols = slice(x * 384, (x + 1) * 384)
        if cell < 2:
            planes = cb[core, :, cell + 1], cf[:, cell + 1]
        else:
            planes = ch[0, :, cell - 2], ch[1, :, cell - 2]
        summed = dot_tn(planes[0].reshape(256, 128), wa[:, :, cols].reshape(256, 384))
        summed = summed + dot_tn(planes[1].reshape(256, 128), wb[:, :, cols].reshape(256, 384))
        scaled = summed * gain_row[:, x * 384:(x + 1) * 384]
        qry[2 * r] = scaled[:, 0:192].astype(BF16)
        qry[2 * r + 1] = scaled[:, 192:384].astype(BF16)

    st[...] = jnp.zeros_like(st)
    for i in range(2):
        pick_s[i] = one_hot(WIN, orders[6 + i:7 + i, 0:384])
    stat_lane = lanes(WIN, 128)
    tile_lane = lanes(TILE, 128)

    def merge_sums(w, carry):
        rows = window_rows(w)
        b, lw, lon_win = w // 4, lax.rem(w // 2, 2), lax.rem(w, 2)
        parts = []
        for p in range(2):
            level = lax.rem(lw * 2 + p + 1, 4)
            at = pl.ds(pl.multiple_of((b * 4 + level) * 16, 16), 16)
            parts.append(qry[:, at, :].reshape(192, C))
        qw[rows, :] = dot_nn(pick_s[lon_win], jnp.concatenate(parts, axis=0)).astype(BF16)
        for t in range(WIN // TILE):
            part = pl.ds(pl.multiple_of(w * WIN + t * TILE, 16), TILE)
            at = slice(t * TILE, (t + 1) * TILE)
            q = qw[part, :].astype(F32)
            v = vo_s[part, :].astype(F32)
            mean = jnp.mean(v, axis=-1, keepdims=True)
            centred = v - mean
            squares = jnp.sum(centred * centred, axis=-1, keepdims=True)
            q_sum = jnp.sum(q, axis=-1, keepdims=True)
            qv_sum = jnp.sum(q * centred, axis=-1, keepdims=True)
            total = st[b, at, :]
            for j, value in enumerate((mean, squares, q_sum, qv_sum)):
                total = jnp.where(tile_lane == 32 * j + w, value, total)
            st[b, at, :] = total
        return carry

    def sums_copies(b):
        return (
            remote(tup.at[b], sup.at[b], st_ss.at[2 * b], st_rs.at[2 * b], (e, d_up)),
            remote(tdn.at[b], sdn.at[b], st_ss.at[2 * b + 1], st_rs.at[2 * b + 1], (e, d_dn)),
        )

    def exchange(b):
        tup[b] = st.at[b][pl.ds(5, 24, stride=6), :]
        tdn[b] = st.at[b][pl.ds(0, 24, stride=6), :]
        for copy in sums_copies(b):
            copy.start()

    even = (over_12(lax.broadcasted_iota(I32, (WIN, 128), 0)) & 1) == 0

    def pair_of(values):
        return jnp.where(even, pltpu.roll(values, WIN - 12, 0), pltpu.roll(values, 12, 0))

    def cell_norm(b):
        for r, other in ((1, 2), (2, 1), (3, 4), (4, 3)):
            sx[pl.ds(r, 24, stride=6), :] = st.at[b][pl.ds(other, 24, stride=6), :]
        for copy in sums_copies(b):
            copy.wait()
        sx[pl.ds(0, 24, stride=6), :] = sup[b]
        sx[pl.ds(5, 24, stride=6), :] = sdn[b]
        own, cross = st[b], sx[...]
        group = [own, cross, pair_of(own), pair_of(cross)]
        cell_mean = (group[0] + group[1] + group[2] + group[3]) * 0.25
        variance = jnp.zeros((WIN, 128), F32)
        q_total = jnp.zeros((WIN, 128), F32)
        qv_total = jnp.zeros((WIN, 128), F32)
        for values in group:
            offset = values - cell_mean
            q_sum = pltpu.roll(values, 64, 1)
            variance = variance + pltpu.roll(values, 96, 1) + 192.0 * offset * offset
            q_total = q_total + q_sum
            qv_total = qv_total + pltpu.roll(values, 32, 1) + offset * q_sum
        cell_inverse = lax.rsqrt(jnp.where(stat_lane < 8, variance, 0.0) * (1.0 / 768.0) + EPS)
        cp_s[0] = cell_mean
        cp_s[1] = cell_inverse
        cp_s[2] = q_total * (1.0 / 768.0)
        cp_s[3] = cell_inverse * cell_inverse * qv_total * (1.0 / 768.0)

    def merge_back(w, carry):
        for t in range(WIN // TILE):
            part = pl.ds(pl.multiple_of(w * WIN + t * TILE, 16), TILE)
            at = slice(t * TILE, (t + 1) * TILE)
            mean, inverse, q_mean, projected = [
                jnp.sum(jnp.where(tile_lane == w, cp_s[j, at, :], 0.0), axis=-1, keepdims=True) for j in range(4)
            ]
            v = vo_s[part, :].astype(F32) - mean
            go_s[part, :] = (inverse * (qw[part, :].astype(F32) - q_mean - v * projected)).astype(BF16)
        return carry

    def feed_back(i, carry):
        rows = chunk_rows(i)
        go = go_s[rows, :]
        gh = (dot_nn(go, shrink_t[...]) * slope_s[rows, :]).astype(BF16)
        gh_s[rows, :] = gh
        tmp[...] = dot_nt(gh, expand_w[...])
        for t in range(CHUNK // TILE):
            part = tile_rows(i, t)
            gnm = tmp[t * TILE:(t + 1) * TILE, :]
            unit, inverse = statistics(mid_s[part, :])
            gm = go_s[part, :].astype(F32) + norm_back(unit, inverse, gnm * feed_gain[...])
            gm_s[part, :] = gm
            gmh_s[part, :] = gm.astype(BF16)
        ga_s[rows, :] = dot_nt(gmh_s[rows, :], output_w[...]).astype(BF16)
        return carry

    def forward_sample(b, carry):
        lax.fori_loop(4 * b, 4 * b + 4, merge_sums, 0)
        exchange(b)
        return carry

    def backward_sample(b, carry):
        cell_norm(b)
        lax.fori_loop(4 * b, 4 * b + 4, merge_back, 0)
        lax.fori_loop(2 * b, 2 * b + 2, feed_back, 0)
        return carry

    lax.fori_loop(0, 2, forward_sample, 0)
    lax.fori_loop(0, 2, backward_sample, 0)

    g_expand = dot_tn(nm_s[...], gh_s[...]).astype(BF16)
    g_shrink = dot_tn(go_s[...], act_s[...]).astype(BF16)
    g_output = dot_tn(att_s[...], gmh_s[...]).astype(BF16)
    for i in range(4):
        for j in range(2):
            g1s[0, 2 * i + j, 0:48] = g_expand[i * 48:(i + 1) * 48, j * 384:(j + 1) * 384]
            g1s[1, 2 * i + j, 0:48] = g_shrink[i * 48:(i + 1) * 48, j * 384:(j + 1) * 384]
    wide = jnp.concatenate([g_output[0:96], g_output[96:192]], axis=1)
    for i in range(NCHIP):
        for j in range(2):
            at = (i * 2 + j) * 16
            g1s[j, i, 48:64] = wide[at:at + 16] if at < 96 else jnp.zeros((16, 384), BF16)

    def sum_of(ref, count, rows):
        total = ref[0, rows].astype(F32)
        for o in range(1, count):
            total = total + ref[o, rows].astype(F32)
        return total.astype(BF16)

    def add_pair(mine, other, out):
        def body(o, carry):
            out[o] = (mine[core, o].astype(F32) + other[o].astype(F32)).astype(BF16)
            return carry

        lax.fori_loop(0, NCHIP, body, 0)

    others = pl.ds(0, NCHIP - 1)
    to_core(g1s.at[1 - core], g1p, 5).start()

    ds_s[...] = jnp.zeros_like(ds_s)
    dt_s[...] = jnp.zeros_like(dt_s)

    def attend_back(pair, carry):
        lw = lax.rem(pair, 2)
        for i in range(2):
            rows = window_rows(2 * pair + i)
            dam[i] = stacked(ga_s[rows, :])
            raw[i] = dot_nt(v_s[rows, :], dam[i])
        for i in range(2):
            for t in range(WIDE // 128):
                cols = slice(t * 128, (t + 1) * 128)
                chances = p_s[2 * pair + i, :, cols].astype(F32)
                weighted = raw[i, :, cols]
                centre = jnp.sum(chances * weighted, axis=0, keepdims=True)
                dsh[i, :, cols] = (chances * (weighted - centre)).astype(BF16)
        for i in range(2):
            rows = window_rows(2 * pair + i)
            dt_s[rows, 512:704] = dot_nn(p_s[2 * pair + i], dam[i]).astype(BF16)
            dt_s[rows, 0:C] = (per_head(k_s[rows, :], dsh[i]) * FACTOR).astype(BF16)
            dt_s[rows, 256:448] = (dot_nn(dsh[i], stacked(q_s[rows, :])) * FACTOR).astype(BF16)
        ds_s[lw] = ds_s[lw] + (dsh[0].astype(F32) + dsh[1].astype(F32))
        return carry

    all_rows = slice(0, 64)
    def windows_back(pair, carry):
        attend_back(pair, carry)

        @pl.when(pair == 0)
        def _():
            arrived(g1p, 5)
            add_pair(g1s, g1p, g1h)
            g1r[chip] = g1h[chip]
            chips_all(lambda o: to_chip(g1h.at[o], g1r.at[chip], 6, o).start())

        return carry

    def second_gradients():
        summed = dot_tn(ni_s[...], dt_s[...])
        sections = [summed[:, 0:C], summed[:, 256:448], summed[:, 512:704], jnp.zeros((C, 64), F32)]
        g_triple = jnp.concatenate(sections, axis=1).astype(BF16)
        for i in range(3):
            for j in range(5):
                at = 5 * i + j
                g2s[at // 8, at % 8, 0:64] = g_triple[i * 64:(i + 1) * 64, j * 128:(j + 1) * 128]
        g2s[1, 7, 0:64] = jnp.zeros((64, 128), BF16)
        for lw in range(2):
            for h in range(HEADS):
                at = pl.ds(h * 2 + lw, WIN, stride=16)
                part = jnp.concatenate(
                [ds_s[lw, :, h * 128:(h + 1) * 128], ds_s[lw, :, 768 + h * 16:784 + h * 16]], axis=1
            ).T
                bs_s.at[0][at, :] = part[:, 0:128]
                bs_s.at[1][at, :] = jnp.concatenate([part[:, 128:144], jnp.zeros((WIN, 112), F32)], axis=1)

        def fold(s_i, carry):
            at = pl.ds(pl.multiple_of(s_i * 192, 192), 192)
            rows = jnp.concatenate([bs_s[0, at, :], bs_s[1, at, :]], axis=1)[:, 0:WIN].astype(BF16)
            return carry + dot_nt(rows, spread_s[s_i])

        folded = lax.fori_loop(0, 12, fold, jnp.zeros((192, 512), F32))
        pieces_t = []
        for p in range(2):
            for pk in range(2):
                for r in range(6):
                    at = (p * 6 + r) * 16
                    pieces_t.append(folded[at:at + 16, pk * 256:pk * 256 + 138])
        table = jnp.concatenate(pieces_t + [jnp.zeros((16, 4096 - POS), F32)], axis=1).astype(BF16)
        for o in range(32):
            g2s[o // 16, (o // 2) % 8, 64 + 16 * (o % 2):80 + 16 * (o % 2)] = table[:, o * 128:(o + 1) * 128]
        to_core(g2s.at[1 - core], g2p, 9).start()

    def project_back(i, carry):
        rows = chunk_rows(i)
        tmp[...] = (
            dot_nt(dt_s[rows, 0:C], wq[...])
            + dot_nt(dt_s[rows, 256:448], wk[...])
            + dot_nt(dt_s[rows, 512:704], wv[...])
        )
        for t in range(CHUNK // TILE):
            part = tile_rows(i, t)
            unit, inverse = statistics(x_w[part, :].astype(F32))
            back = norm_back(unit, inverse, tmp[t * TILE:(t + 1) * TILE, :] * attend_gain[...])
            gt_s[part, :] = (gm_s[part, :] + back).astype(BF16)
        return carry

    from_window = one_hot(HALF, orders[3:4, 0:HALF])

    def backward_windows(b, carry):
        lax.fori_loop(2 * b, 2 * b + 2, windows_back, 0)

        @pl.when(b == 1)
        def _():
            arrived(g1l.at[others], 7)
            g1f[chip] = sum_of(g1l, NLAT, all_rows)
            chips_all(lambda o: to_chip(g1f.at[chip], g1f.at[chip], 8, o).start())
            second_gradients()

        lax.fori_loop(2 * b, 2 * b + 2, project_back, 0)

        @pl.when(b == 0)
        def _():
            arrived(g1r.at[others], 6)
            g1l[d] = sum_of(g1r, NCHIP, all_rows)
            lat_all(lambda o: to_band(g1l.at[d], g1l.at[d], 7, o).start())

        @pl.when(b == 1)
        def _():
            arrived(g2p, 9)
            add_pair(g2s, g2p, g2h)
            g2r[chip] = g2h[chip]
            chips_all(lambda o: to_chip(g2h.at[o], g2r.at[chip], 10, o).start())

        quads = dot_nn(from_window, gt_s[half_rows(b), :])
        gq[b] = quads
        pack(quads, b, (c10, c01, c11))
        for copy in rows_behind(b):
            copy.start()
        return carry

    lax.fori_loop(0, 2, backward_windows, 0)

    arrived(g1f.at[others], 8)
    to_core(g1f, g1o, 11).start()

    arrived(g2r.at[others], 10)
    g2l[d] = sum_of(g2r, NCHIP, slice(0, 64))
    lat_all(lambda o: to_band(g2l.at[d], g2l.at[d], 12, o).start())
    g2f[chip, 64:96] = sum_of(g2r, NCHIP, slice(64, 96))

    to_natural = one_hot(HALF, orders[1:2, 0:HALF])

    def unsort_sample(b, carry):
        for copy in rows_behind(b):
            copy.wait()
        unpack(gq, b, (d10, d01, d11))
        out_fields[half_rows(b), :] = dot_nn(to_natural, gq[b].astype(BF16)).astype(BF16)
        return carry

    lax.fori_loop(0, 1, unsort_sample, 0)
    arrived(g2l.at[others], 12)
    g2f[chip, 0:64] = sum_of(g2l, NLAT, slice(0, 64))
    chips_all(lambda o: to_chip(g2f.at[chip], g2f.at[chip], 13, o).start())


    lax.fori_loop(1, 2, unsort_sample, 0)
    arrived(g1o, 11)
    out_g1[core] = g1f[...]
    out_g1[1 - core] = g1o[...]
    arrived(g2f.at[others], 13)
    to_core(g2f, g2o, 14).start()
    out_g2[core] = g2f[...]
    arrived(g2o, 14)
    out_g2[1 - core] = g2o[...]

    left(cs.at[others], 0)
    left(wa.at[others], 1)
    left(cf, 2)
    left(wb, 3)
    left(ch, 4)
    left(g1p, 5)
    left(g1r.at[others], 6)
    left(g1l.at[others], 7)
    left(g1f.at[others], 8)
    left(g2p, 9)
    left(g2r.at[others], 10)
    left(g1o, 11)
    left(g2l.at[others], 12)
    left(g2f.at[others], 13)
    left(g2o, 14)


def results_kernel(
    fields, g1, g2, attend_gain, triple_w, feed_gain, expand_w,
    out_fields, out_triple, out_output, out_expand, out_shrink, out_attend, out_feed, out_table,
):
    out_fields[...] = fields[...]
    for i in range(4):
        for j in range(2):
            rows, cols = slice(i * 48, (i + 1) * 48), slice(j * 384, (j + 1) * 384)
            out_expand[rows, cols] = g1[0, 2 * i + j, 0:48].astype(F32)
            out_shrink[rows, cols] = g1[1, 2 * i + j, 0:48].astype(F32)
    for i in range(6):
        wide = g1[i % 2, i // 2, 48:64].astype(F32)
        out_output[i * 16:(i + 1) * 16, :] = wide[:, 0:C]
        out_output[96 + i * 16:96 + (i + 1) * 16, :] = wide[:, C:2 * C]
    for i in range(3):
        for j in range(5):
            at, size = 5 * i + j, 128 if j < 4 else 64
            part = g2[at // 8, at % 8, 0:64].astype(F32)
            out_triple[i * 64:(i + 1) * 64, j * 128:j * 128 + size] = part[:, 0:size]
    table = jnp.concatenate(
        [g2[o // 16, (o // 2) % 8, 64 + 16 * (o % 2):80 + 16 * (o % 2)] for o in range(32)], axis=1
    ).astype(F32)
    for h in range(HEADS):
        out_table[h] = table[2 * h:2 * h + 2, 0:POS]

    def gain_gradient(grad, weight, gain):
        product = (grad[...] * weight[...].astype(F32)).astype(BF16)
        total = dot_nt(jnp.ones((16, product.shape[1]), BF16), product)
        return total[0:1] / gain[...]

    out_attend[...] = gain_gradient(out_triple, triple_w, attend_gain)
    out_feed[...] = gain_gradient(out_expand, expand_w, feed_gain)


def scratch():
    def vmem(*shape, kind=BF16):
        return pltpu.VMEM(shape, kind)

    token = vmem(TOK, C)
    token_f = vmem(TOK, C, kind=F32)
    weight = vmem(C, C)
    quad = vmem(2, HALF, C, kind=F32)
    halves = [vmem(2, 336, 128), vmem(2, 112, 128), vmem(2, 112, 128)]
    stat = vmem(WIN, 128, kind=F32)
    small = vmem(2, 24, 128, kind=F32)
    buffers = [
        quad, quad, *halves, *halves, *halves, *halves, token, token, token, token, token, weight, weight, weight,
        vmem(NWIN, WIN, WIDE), token, token_f, token, vmem(TOK, FF), vmem(TOK, FF, kind=F32), token,
        vmem(16, POS, kind=F32), vmem(576, 512), vmem(2, 2304, 128, kind=F32),
        vmem(2, WIN, WIDE, kind=F32), vmem(2, WIN, WIDE, kind=F32),
        vmem(12, 512, WIN), vmem(2, WIN, 384),
        vmem(576, 256, kind=F32), vmem(8, 2, 3, 32, 128), vmem(2, 8, 3, 32, 128), vmem(8, 3, 32, 128), vmem(2, 8, 2, 32, 128),
        vmem(8, 32, 768), vmem(8, 32, 768),
        vmem(12, 128, C), token, vmem(2, WIN, 128, kind=F32), stat, small, small, small, small, vmem(4, WIN, 128, kind=F32),
        token, vmem(TOK, FF), token_f, token, token, vmem(TOK, 768), token,
        vmem(2, WIN, WIDE, kind=F32), vmem(2, WIN, WIDE), vmem(2, WIDE, C), vmem(CHUNK, FF, kind=F32),
        vmem(CHUNK, C, kind=F32),
    ]
    for rows, cols in ((64, 384), (96, 128)):
        chunks = vmem(8, rows, cols)
        buffers += [vmem(2, 8, rows, cols), chunks, chunks, chunks, vmem(8, 64, cols), chunks, chunks]
    counts = [6, 6, 6, 6, 4, 4, 15, 15]
    return buffers + [pltpu.SemaphoreType.DMA((n,)) for n in counts]


def per_device(
    fields, merge_cotangent, attend_gain, triple_weight, bias_table, output_weight, feed_gain,
    expand_weight, shrink_weight, merge_gain, merge_weight,
):
    cot = jnp.transpose(merge_cotangent, (1, 2, 3, 4, 0)).reshape(576, 192)
    bias = jnp.transpose(bias_table[0], (1, 0, 2))
    def shaped(shapes):
        return [jax.ShapeDtypeStruct(shape, kind) for shape, kind in shapes]

    vmem_spec = pl.BlockSpec(memory_space=pltpu.VMEM)
    parts = pl.pallas_call(
        kernel,
        out_shape=shaped(
            [((TOK, C), BF16), ((2, 8, 64, 384), BF16), ((2, 8, 96, 128), BF16)]
        ),
        in_specs=[vmem_spec] * 12,
        out_specs=[vmem_spec] * 3,
        scratch_shapes=scratch(),
        compiler_params=pltpu.CompilerParams(
            collective_id=0, has_side_effects=True, vmem_limit_bytes=60 * 1024 * 1024
        ),
    )(
        fields.reshape(TOK, C), cot, attend_gain.reshape(1, C), triple_weight, bias, output_weight,
        feed_gain.reshape(1, C), expand_weight, shrink_weight.T, merge_gain,
        merge_weight.T, jnp.asarray(order_indices()),
    )
    g_fields, g_triple, g_output, g_expand, g_shrink, g_attend, g_feed, g_table = pl.pallas_call(
        results_kernel,
        out_shape=shaped(
            [
                ((TOK, C), BF16), ((C, 3 * C), F32), ((C, C), F32), ((C, FF), F32), ((C, FF), F32),
                ((1, C), F32), ((1, C), F32), ((HEADS, 2, POS), F32),
            ]
        ),
        in_specs=[vmem_spec] * 7,
        out_specs=[vmem_spec] * 8,
        compiler_params=pltpu.CompilerParams(vmem_limit_bytes=60 * 1024 * 1024),
    )(*parts, attend_gain.reshape(1, C), triple_weight, feed_gain.reshape(1, C), expand_weight)
    return (
        g_fields.reshape(fields.shape), g_triple, g_output, g_expand, g_shrink.T,
        g_attend.reshape(C), g_feed.reshape(C), jnp.transpose(g_table, (1, 0, 2))[None],
    )


def solution(mesh):
    placed = (
        P(None, None, "lat", "lon", None),
        P(None, None, None, "lat", "lon"),
        P(),
        P(),
        P("lat", None, None, None),
        P(),
        P(),
        P(),
        P(),
        P(),
        P(None, "lon"),
    )
    return jax.shard_map(
        per_device,
        mesh=mesh,
        in_specs=placed,
        out_specs=(
            P(None, None, "lat", "lon", None),
            P(),
            P(),
            P(),
            P(),
            P(),
            P(),
            P("lat", None, None, None),
        ),
        check_vma=False,
    )
```

```python
import functools
import math

import jax
import jax.numpy as jnp
import numpy as np
from jax import lax
from jax.experimental import pallas as pl
from jax.experimental.pallas import tpu as pltpu
from jax.sharding import PartitionSpec as P

F32 = jnp.float32
BF16 = jnp.bfloat16
I32 = jnp.int32
MESH = pl.DeviceIdType.MESH

EPS = 1e-05
MASKED = -1000000000.0
NLON = 16
NLAT = 8
NCHIP = 8
C = 192
HEADS = 6
FF = 768
WIN = 144
NWIN = 8
TOK = WIN * NWIN
HALF = TOK // 2
SIZES = ((216, 112), (72, 40), (72, 40))
POS = 3312
CHUNK = 288
NCHUNK = TOK // CHUNK
TILE = 48
WIDE = 896
FACTOR = 32 ** -0.5


def order_indices():
    natural_to_quad = np.full(640, -1, np.int32)
    quad_to_natural = np.full(640, -1, np.int32)
    quad_to_window = np.full(640, -1, np.int32)
    window_to_quad = np.full(640, -1, np.int32)
    for level in range(4):
        for row in range(6):
            for col in range(24):
                source = (level * 6 + row) * 24 + col
                if col >= 6:
                    place = (0 if row >= 3 else 216) + level * 54 + (row % 3) * 18 + col - 6
                else:
                    place = (432 if row >= 3 else 504) + level * 18 + (row % 3) * 6 + col
                natural_to_quad[source] = place
                quad_to_natural[place] = source
    index = 0
    for lev_win in range(2):
        for lon_win in range(2):
            for s in range(12):
                for p in range(2):
                    for r in range(6):
                        level = (lev_win * 2 + p + 1) % 4
                        col = lon_win * 12 + s
                        if col < 18:
                            place = (0 if r < 3 else 216) + level * 54 + (r % 3) * 18 + col
                        else:
                            place = (432 if r < 3 else 504) + level * 18 + (r % 3) * 6 + col - 18
                        window_to_quad[index] = place
                        quad_to_window[place] = index
                        index += 1
    cell_lane = np.full(640, -1, np.int32)
    bias_row = np.full(640, -1, np.int32)
    merged_token = np.full((2, 640), -1, np.int32)
    for lane in range(256):
        if lane % 16 < 12:
            cell_lane[lane] = (12 * (lane // 16) + 3 + lane % 16) % 192
    for k in range(WIN):
        s, p, r = k // 12, (k // 6) % 2, k % 6
        bias_row[k] = p * 256 + r * 23 + 11 - s
    for lon_win in range(2):
        for row in range(384):
            p, r, y, m = row // 192, (row // 32) % 6, (row // 16) % 2, row % 16
            if 0 <= m - lon_win * 6 < 6:
                merged_token[lon_win, row] = (2 * (m - lon_win * 6) + y) * 12 + p * 6 + r
    rows = [natural_to_quad, quad_to_natural, quad_to_window, window_to_quad]
    return np.stack(rows + [cell_lane, bias_row, merged_token[0], merged_token[1]])


def dot_nn(a, b):
    return lax.dot_general(a, b, (((1,), (0,)), ((), ())), preferred_element_type=F32)


def dot_nt(a, b):
    return lax.dot_general(a, b, (((1,), (1,)), ((), ())), preferred_element_type=F32)


def dot_tn(a, b):
    return lax.dot_general(a, b, (((0,), (0,)), ((), ())), preferred_element_type=F32)


def one_hot(rows, targets):
    ids = lax.broadcasted_iota(I32, (rows, targets.shape[1]), 0)
    return jnp.where(ids == targets, 1.0, 0.0).astype(BF16)


def statistics(values):
    centred = values - jnp.mean(values, axis=-1, keepdims=True)
    inverse = lax.rsqrt(jnp.mean(centred * centred, axis=-1, keepdims=True) + EPS)
    return centred * inverse, inverse


def norm_back(normed, inverse, scaled):
    centre = jnp.mean(scaled, axis=-1, keepdims=True)
    projected = jnp.mean(scaled * normed, axis=-1, keepdims=True)
    return inverse * (scaled - centre - normed * projected)


def gelu_parts(values):
    cumulative = 0.5 * (1.0 + lax.erf(values * (1.0 / math.sqrt(2.0))))
    density = jnp.exp(-0.5 * values * values) * (1.0 / math.sqrt(2.0 * math.pi))
    return values * cumulative, cumulative + values * density


def lanes(rows, cols):
    return lax.broadcasted_iota(I32, (rows, cols), 1)


def over_12(ids):
    return (ids * 5462) >> 16


def over_6(ids):
    return (ids * 10923) >> 16


def kernel(
    fields, cot, attend_gain, triple_w, bias, output_w, feed_gain, expand_w, shrink_t, merge_gain,
    merge_wt, orders,
    out_fields, out_g1, out_g2,
    sq, gq, a10, a01, a11, b10, b01, b11, c10, c01, c11, d10, d01, d11, x_w, ni_s, q_s, k_s, v_s, wq, wk, wv, p_s, att_s, mid_s, nm_s, act_s, slope_s, vo_s,
    b16, bl_s, bs_s, bx, ds_s, spread_s, pick_s,
    cells, cs, cb, cf, ch, planes, wa, wb, w_all, qry, qw, st, sx, sup, sdn, tup, tdn, cp_s, go_s, gh_s, gm_s, ga_s, gmh_s,
    dt_s, gt_s, raw, dsh, dam, hid, tmp, g1s, g1p, g1h, g1r, g1l, g1f, g1o, g2s, g2p, g2h, g2r, g2l, g2f, g2o,
    halo_ss, halo_rs, back_ss, back_rs, st_ss, st_rs, sends, recvs,
):
    e = lax.axis_index("lon")
    d = lax.axis_index("lat")
    e_up, e_dn = lax.rem(e + 1, NLON), lax.rem(e + NLON - 1, NLON)
    d_up, d_dn = lax.rem(d + 1, NLAT), lax.rem(d + NLAT - 1, NLAT)

    def remote(src, dst, ssem, rsem, device):
        return pltpu.make_async_remote_copy(
            src_ref=src, dst_ref=dst, send_sem=ssem, recv_sem=rsem, device_id=device,
            device_id_type=MESH,
        )

    core, chip = lax.rem(e, 2), e // 2
    partner = e + 1 - 2 * core
    d_pair = d + 1 - 2 * lax.rem(d, 2)

    def chips_all(action):
        def body(step, carry):
            action(lax.rem(chip + step, NCHIP))
            return carry

        lax.fori_loop(1, NCHIP, body, 0)

    def lat_all(action):
        def body(step, carry):
            action(lax.rem(d + step, NLAT))
            return carry

        lax.fori_loop(1, NLAT, body, 0)

    def to_chip(src, dst, phase, o):
        return remote(src, dst, sends.at[phase], recvs.at[phase], (2 * o + core, d))

    def to_band(src, dst, phase, o):
        return remote(src, dst, sends.at[phase], recvs.at[phase], (e, o))

    def to_core(src, dst, phase):
        return remote(src, dst, sends.at[phase], recvs.at[phase], (partner, d))

    def arrived(region, phase):
        remote(region, region, sends.at[phase], recvs.at[phase], (partner, d)).wait_recv()

    def left(region, phase):
        remote(region, region, sends.at[phase], recvs.at[phase], (partner, d)).wait_send()

    barrier = pltpu.get_barrier_semaphore()

    def greet(device):
        pl.semaphore_signal(barrier, inc=1, device_id=device, device_id_type=MESH)

    chips_all(lambda o: greet((2 * o + core, d)))
    lat_all(lambda o: greet((e, o)))
    for device in ((e_up, d), (e_dn, d), (e_up, d_up), (e_dn, d_dn)):
        greet(device)

    def half_rows(b):
        return pl.ds(pl.multiple_of(b * HALF, HALF), HALF)

    def pack(quads, b, out):
        at = 216
        for (size, cut), message in zip(SIZES, out):
            rows = quads[at:at + size]
            rest = jnp.concatenate([rows[cut:, 128:C], jnp.zeros((2 * cut - size, 64), F32)], axis=0)
            parts = [rows[:, 0:128], jnp.concatenate([rows[:cut, 128:C], rest], axis=1)]
            if (size + cut) % 16:
                parts.append(jnp.zeros((8, 128), F32))
            message[b] = jnp.concatenate(parts, axis=0).astype(BF16)
            at += size

    def unpack(quads, b, messages):
        at = 216
        for (size, cut), message in zip(SIZES, messages):
            rows = message[b].astype(F32)
            tails = rows[size:size + cut]
            tail = jnp.concatenate([tails[:, 0:64], tails[0:size - cut, 64:128]], axis=0)
            quads[b, at:at + size, :] = jnp.concatenate([rows[0:size], tail], axis=1)
            at += size

    def halo(sources, targets, ssem, rsem, step, b):
        devices = ((e, step[1]), (step[0], d), (step[0], step[1]))
        return [
            remote(src.at[b], dst.at[b], ssem.at[3 * b + i], rsem.at[3 * b + i], dev)
            for i, (src, dst, dev) in enumerate(zip(sources, targets, devices))
        ]

    def rows_ahead(b):
        return halo((a10, a01, a11), (b10, b01, b11), halo_ss, halo_rs, (e_dn, d_dn), b)

    def rows_behind(b):
        return halo((c10, c01, c11), (d10, d01, d11), back_ss, back_rs, (e_up, d_up), b)

    to_quad = one_hot(HALF, orders[0:1, 0:HALF])

    def sort_sample(b, carry):
        quads = dot_nn(to_quad, fields[half_rows(b), :])
        sq[b] = quads
        pack(quads, b, (a10, a01, a11))
        return carry

    lax.fori_loop(0, 2, sort_sample, 0)
    pl.semaphore_wait(barrier, NCHIP - 1 + NLAT - 1 + 4)
    for b in range(2):
        for copy in rows_ahead(b):
            copy.start()

    cells[...] = dot_nn(cot[...], one_hot(192, orders[4:5, 0:256]))
    block_of = lanes(72, 128) >> 4

    def gather_cells(o, carry):
        tile = pl.ds(pl.multiple_of((o // 8) * 128, 128), 128)
        inner = lax.rem(o, 8)
        piece = jnp.zeros((72, 128), F32)
        for bl in range(8):
            part = pltpu.roll(cells[bl * 72:(bl + 1) * 72, tile], lax.rem(16 * (bl - inner) + 128, 128), 1)
            piece = jnp.where(block_of == bl, part, piece)
        for a in range(3):
            padded = jnp.concatenate([piece[a * 24:(a + 1) * 24], jnp.zeros((8, 128), F32)], axis=0)
            cs[o // 2, lax.rem(o, 2), a] = padded.astype(BF16)
        return carry

    lax.fori_loop(0, NLON, gather_cells, 0)
    wa[chip] = jnp.concatenate(
        [merge_wt[...].astype(F32), jnp.zeros((8, 768), F32)], axis=0
    ).astype(BF16)
    cb[:, chip] = cs[chip]
    for h in range(HEADS):
        b16[2 * h:2 * h + 2, :] = bias[h]
    b16[12:16, :] = jnp.zeros((4, POS), F32)
    zero_tail = jnp.zeros((16, 256 - 138), F32)
    for p in range(2):
        for r in range(6):
            parts = []
            for pk in range(2):
                at = (p * 2 + pk) * 828 + r * 138
                parts += [b16[:, at:at + 138], zero_tail]
            row = jnp.concatenate(parts, axis=1)
            high = row.astype(BF16)
            rest = row - high.astype(F32)
            middle = rest.astype(BF16)
            low = (rest - middle.astype(F32)).astype(BF16)
            at = (p * 6 + r) * 16
            bl_s[at:at + 16, :] = high
            bl_s[192 + at:192 + at + 16, :] = middle
            bl_s[384 + at:384 + at + 16, :] = low

    bias_row = orders[5:6, 0:WIN]

    def spread(s_i, carry):
        matrix = one_hot(512, bias_row + s_i)
        spread_s[s_i] = matrix
        split = dot_nn(bl_s[...], matrix)
        rows = split[0:192] + split[192:384] + split[384:576]
        at = pl.ds(pl.multiple_of(s_i * 192, 192), 192)
        bs_s[0, at, :] = rows[:, 0:128]
        bs_s[1, at, :] = jnp.concatenate([rows[:, 128:144], jnp.zeros((192, 112), F32)], axis=1)
        return carry

    lax.fori_loop(0, 12, spread, 0)

    tok_i = lax.broadcasted_iota(I32, (WIN, WIN), 0)
    tok_k = lax.broadcasted_iota(I32, (WIN, WIN), 1)
    half_i, half_k = over_6(tok_i), over_6(tok_k)
    last_band = d == NLAT - 1
    lat_differs = ((tok_i - half_i * 6 >= 3) != (tok_k - half_k * 6 >= 3)) & last_band
    lev_differs = (half_i & 1) != (half_k & 1)
    bx[:, :, HEADS * WIN:WIDE] = jnp.zeros((2, WIN, WIDE - HEADS * WIN), F32)
    for lw in range(2):
        differs = (lat_differs | lev_differs) if lw else lat_differs
        for h in range(HEADS):
            at = pl.ds(h * 2 + lw, WIN, stride=16)
            full = jnp.concatenate([bs_s.at[0][at, :], bs_s.at[1][at, :]], axis=1)[:, 0:WIN]
            spread_bias = jnp.where(differs, MASKED, full).T
            bx[lw, :, h * 128:(h + 1) * 128] = spread_bias[:, 0:128]
            bx[lw, :, 768 + h * 16:784 + h * 16] = spread_bias[:, 128:WIN]

    wq[...] = triple_w[:, 0:192]
    wk[...] = triple_w[:, 192:384]
    wv[...] = triple_w[:, 384:576]

    head_of = lanes(1, C) >> 5
    head_f = [jnp.where(head_of == h, 1.0, 0.0) for h in range(HEADS)]
    head_b = [mask.astype(BF16) for mask in head_f]

    blank = jnp.zeros((WIDE - HEADS * WIN, C), BF16)

    def stacked(values):
        first, rest = values[0:128], values[128:WIN]
        parts = [first * mask for mask in head_b] + [rest * mask for mask in head_b]
        return jnp.concatenate(parts + [blank], axis=0)

    def per_head(left, right):
        turned = left.T
        wide = [dot_nn(turned[64 * i:64 * i + 64], right[:, 256 * i:256 * i + 256]) for i in range(3)]
        tail = dot_nn(turned, right[:, 768:WIDE])
        blocks = []
        for h in range(HEADS):
            at, row = 128 * (h % 2), 32 * (h % 2)
            blocks.append(
                jnp.concatenate(
                    [wide[h // 2][row:row + 32, at:at + 128], tail[32 * h:32 * h + 32, 16 * h:16 * h + 16]], axis=1
                )
            )
        return jnp.concatenate(blocks, axis=0).T

    to_window = one_hot(HALF, orders[2:3, 0:HALF])

    def window_rows(w):
        return pl.ds(pl.multiple_of(w * WIN, WIN), WIN)

    def chunk_rows(i):
        return pl.ds(pl.multiple_of(i * CHUNK, CHUNK), CHUNK)

    def tile_rows(i, t):
        return pl.ds(pl.multiple_of(i * CHUNK + t * TILE, 16), TILE)

    def project(i, carry):
        rows = chunk_rows(i)
        for t in range(CHUNK // TILE):
            part = tile_rows(i, t)
            normed = statistics(x_w[part, :].astype(F32))[0]
            ni_s[part, :] = (normed * attend_gain[...]).astype(BF16)
        normed_in = ni_s[rows, :]
        q_s[rows, :] = dot_nn(normed_in, wq[...]).astype(BF16)
        k_s[rows, :] = dot_nn(normed_in, wk[...]).astype(BF16)
        v_s[rows, :] = dot_nn(normed_in, wv[...]).astype(BF16)
        return carry


    def attend(pair, carry):
        lw = lax.rem(pair, 2)
        for i in range(2):
            rows = window_rows(2 * pair + i)
            raw[i] = dot_nt(k_s[rows, :], stacked(q_s[rows, :]))
        for i in range(2):
            for t in range(WIDE // 128):
                cols = slice(t * 128, (t + 1) * 128)
                scores = raw[i, :, cols] * FACTOR + bx[lw, :, cols]
                exponent = jnp.exp(scores - jnp.max(scores, axis=0, keepdims=True))
                chances = exponent * (1.0 / jnp.sum(exponent, axis=0, keepdims=True))
                p_s[2 * pair + i, :, cols] = chances.astype(BF16)
        for i in range(2):
            rows = window_rows(2 * pair + i)
            att_s[rows, :] = per_head(v_s[rows, :], p_s[2 * pair + i]).astype(BF16)
        return carry

    def dense(first, second):
        return jnp.concatenate([first.astype(F32)[0:24], second.astype(F32)[0:24]], axis=0).astype(BF16)

    def forward_windows(b, carry):
        for copy in rows_ahead(b):
            copy.wait()

        @pl.when(b == 0)
        def _():
            chips_all(lambda o: to_chip(cs.at[o], cb.at[:, chip], 0, o).start())
            chips_all(lambda o: to_chip(wa.at[chip], wa.at[chip], 1, o).start())

        unpack(sq, b, (b10, b01, b11))
        x_w[half_rows(b), :] = dot_nn(to_window, sq[b].astype(BF16)).astype(BF16)
        lax.fori_loop(2 * b, 2 * b + 2, project, 0)

        @pl.when(b == 1)
        def _():
            arrived(cf, 2)
            for a in range(3):
                for i in range(NCHIP // 2):
                    planes[a, 48 * i:48 * i + 48] = dense(cb[core, 2 * i, a], cb[core, 2 * i + 1, a])
                    planes[a, 192 + 48 * i:240 + 48 * i] = dense(cf[2 * i, a], cf[2 * i + 1, a])
            to_band(planes.at[pl.ds(0, 2)], ch, 4, d_dn).start()

        lax.fori_loop(2 * b, 2 * b + 2, attend, 0)

        @pl.when(b == 0)
        def _():
            arrived(cb.at[:, pl.ds(0, NCHIP - 1)], 0)
            to_core(cb.at[1 - core], cf, 2).start()

        return carry

    lax.fori_loop(0, 2, forward_windows, 0)
    arrived(wa.at[pl.ds(0, NCHIP - 1)], 1)
    to_core(wa, wb, 3).start()

    def feed(i, carry):
        rows = chunk_rows(i)
        tmp[...] = x_w[rows, :].astype(F32) + dot_nn(att_s[rows, :], output_w[...])
        for t in range(CHUNK // TILE):
            part = tile_rows(i, t)
            middle = tmp[t * TILE:(t + 1) * TILE, :]
            mid_s[part, :] = middle
            nm_s[part, :] = (statistics(middle)[0] * feed_gain[...]).astype(BF16)
        hid[...] = dot_nn(nm_s[rows, :], expand_w[...])
        for t in range(CHUNK // 16):
            part = pl.ds(pl.multiple_of(i * CHUNK + t * 16, 16), 16)
            for j in range(FF // 256):
                cols = slice(j * 256, (j + 1) * 256)
                act, slope = gelu_parts(hid[t * 16:(t + 1) * 16, cols])
                act_s[part, cols] = act.astype(BF16)
                slope_s[part, cols] = slope
        vo_s[rows, :] = (tmp[...] + dot_nt(act_s[rows, :], shrink_t[...])).astype(BF16)
        return carry

    lax.fori_loop(0, NCHUNK, feed, 0)

    arrived(wb, 3)
    for i in range(NCHIP // 2):
        w_all[48 * i:48 * i + 48] = dense(wa[2 * i], wa[2 * i + 1])
        w_all[192 + 48 * i:240 + 48 * i] = dense(wb[2 * i], wb[2 * i + 1])
    gain_row = merge_gain[...].reshape(1, 4 * C)
    for r in range(6):
        x = (r + 1) % 2
        cell = (0, 1, 1, 2, 2, 3)[r]
        cols = slice(x * 384, (x + 1) * 384)
        if r == 3:
            arrived(ch, 4)
        plane = planes[cell + 1] if cell < 2 else ch[cell - 2]
        summed = dot_tn(plane, w_all[:, cols])
        scaled = summed * gain_row[:, x * 384:(x + 1) * 384]
        qry[2 * r] = scaled[:, 0:192].astype(BF16)
        qry[2 * r + 1] = scaled[:, 192:384].astype(BF16)

    st[...] = jnp.zeros_like(st)
    for i in range(2):
        pick_s[i] = one_hot(WIN, orders[6 + i:7 + i, 0:384])
    stat_lane = lanes(WIN, 128)
    tile_lane = lanes(TILE, 128)

    def merge_sums(w, carry):
        rows = window_rows(w)
        b, lw, lon_win = w // 4, lax.rem(w // 2, 2), lax.rem(w, 2)
        parts = []
        for p in range(2):
            level = lax.rem(lw * 2 + p + 1, 4)
            at = pl.ds(pl.multiple_of((b * 4 + level) * 16, 16), 16)
            parts.append(qry[:, at, :].reshape(192, C))
        qw[rows, :] = dot_nn(pick_s[lon_win], jnp.concatenate(parts, axis=0)).astype(BF16)
        for t in range(WIN // TILE):
            part = pl.ds(pl.multiple_of(w * WIN + t * TILE, 16), TILE)
            at = slice(t * TILE, (t + 1) * TILE)
            q = qw[part, :].astype(F32)
            v = vo_s[part, :].astype(F32)
            mean = jnp.mean(v, axis=-1, keepdims=True)
            centred = v - mean
            squares = jnp.sum(centred * centred, axis=-1, keepdims=True)
            q_sum = jnp.sum(q, axis=-1, keepdims=True)
            qv_sum = jnp.sum(q * centred, axis=-1, keepdims=True)
            total = st[b, at, :]
            for j, value in enumerate((mean, squares, q_sum, qv_sum)):
                total = jnp.where(tile_lane == 32 * j + w, value, total)
            st[b, at, :] = total
        return carry

    def sums_copies(b):
        return (
            remote(tup.at[b], sup.at[b], st_ss.at[2 * b], st_rs.at[2 * b], (e, d_up)),
            remote(tdn.at[b], sdn.at[b], st_ss.at[2 * b + 1], st_rs.at[2 * b + 1], (e, d_dn)),
        )

    def exchange(b):
        tup[b] = st.at[b][pl.ds(5, 24, stride=6), :]
        tdn[b] = st.at[b][pl.ds(0, 24, stride=6), :]
        for copy in sums_copies(b):
            copy.start()

    even = (over_12(lax.broadcasted_iota(I32, (WIN, 128), 0)) & 1) == 0

    def pair_of(values):
        return jnp.where(even, pltpu.roll(values, WIN - 12, 0), pltpu.roll(values, 12, 0))

    def cell_norm(b):
        for r, other in ((1, 2), (2, 1), (3, 4), (4, 3)):
            sx[pl.ds(r, 24, stride=6), :] = st.at[b][pl.ds(other, 24, stride=6), :]
        for copy in sums_copies(b):
            copy.wait()
        sx[pl.ds(0, 24, stride=6), :] = sup[b]
        sx[pl.ds(5, 24, stride=6), :] = sdn[b]
        own, cross = st[b], sx[...]
        group = [own, cross, pair_of(own), pair_of(cross)]
        cell_mean = (group[0] + group[1] + group[2] + group[3]) * 0.25
        variance = jnp.zeros((WIN, 128), F32)
        q_total = jnp.zeros((WIN, 128), F32)
        qv_total = jnp.zeros((WIN, 128), F32)
        for values in group:
            offset = values - cell_mean
            q_sum = pltpu.roll(values, 64, 1)
            variance = variance + pltpu.roll(values, 96, 1) + 192.0 * offset * offset
            q_total = q_total + q_sum
            qv_total = qv_total + pltpu.roll(values, 32, 1) + offset * q_sum
        cell_inverse = lax.rsqrt(jnp.where(stat_lane < 8, variance, 0.0) * (1.0 / 768.0) + EPS)
        cp_s[0] = cell_mean
        cp_s[1] = cell_inverse
        cp_s[2] = q_total * (1.0 / 768.0)
        cp_s[3] = cell_inverse * cell_inverse * qv_total * (1.0 / 768.0)

    def merge_back(w, carry):
        for t in range(WIN // TILE):
            part = pl.ds(pl.multiple_of(w * WIN + t * TILE, 16), TILE)
            at = slice(t * TILE, (t + 1) * TILE)
            mean, inverse, q_mean, projected = [
                jnp.sum(jnp.where(tile_lane == w, cp_s[j, at, :], 0.0), axis=-1, keepdims=True) for j in range(4)
            ]
            v = vo_s[part, :].astype(F32) - mean
            go_s[part, :] = (inverse * (qw[part, :].astype(F32) - q_mean - v * projected)).astype(BF16)
        return carry

    def feed_back(i, carry):
        rows = chunk_rows(i)
        go = go_s[rows, :]
        gh = (dot_nn(go, shrink_t[...]) * slope_s[rows, :]).astype(BF16)
        gh_s[rows, :] = gh
        tmp[...] = dot_nt(gh, expand_w[...])
        for t in range(CHUNK // TILE):
            part = tile_rows(i, t)
            gnm = tmp[t * TILE:(t + 1) * TILE, :]
            unit, inverse = statistics(mid_s[part, :])
            gm = go_s[part, :].astype(F32) + norm_back(unit, inverse, gnm * feed_gain[...])
            gm_s[part, :] = gm
            gmh_s[part, :] = gm.astype(BF16)
        ga_s[rows, :] = dot_nt(gmh_s[rows, :], output_w[...]).astype(BF16)
        return carry

    def forward_sample(b, carry):
        lax.fori_loop(4 * b, 4 * b + 4, merge_sums, 0)
        exchange(b)
        return carry

    def backward_sample(b, carry):
        cell_norm(b)
        lax.fori_loop(4 * b, 4 * b + 4, merge_back, 0)
        lax.fori_loop(2 * b, 2 * b + 2, feed_back, 0)
        return carry

    lax.fori_loop(0, 2, forward_sample, 0)
    lax.fori_loop(0, 2, backward_sample, 0)

    g_expand = dot_tn(nm_s[...], gh_s[...]).astype(BF16)
    g_shrink = dot_tn(go_s[...], act_s[...]).astype(BF16)
    g_output = dot_tn(att_s[...], gmh_s[...]).astype(BF16)
    for i in range(4):
        for j in range(2):
            g1s[0, 2 * i + j, 0:48] = g_expand[i * 48:(i + 1) * 48, j * 384:(j + 1) * 384]
            g1s[1, 2 * i + j, 0:48] = g_shrink[i * 48:(i + 1) * 48, j * 384:(j + 1) * 384]
    wide = jnp.concatenate([g_output[0:96], g_output[96:192]], axis=1)
    for i in range(NCHIP):
        for j in range(2):
            at = (i * 2 + j) * 16
            g1s[j, i, 48:64] = wide[at:at + 16] if at < 96 else jnp.zeros((16, 384), BF16)

    def sum_of(ref, count, rows):
        total = ref[0, rows].astype(F32)
        for o in range(1, count):
            total = total + ref[o, rows].astype(F32)
        return total.astype(BF16)

    def add_pair(mine, other, out):
        def body(o, carry):
            out[o] = (mine[core, o].astype(F32) + other[o].astype(F32)).astype(BF16)
            return carry

        lax.fori_loop(0, NCHIP, body, 0)

    others = pl.ds(0, NCHIP - 1)
    to_core(g1s.at[1 - core], g1p, 5).start()

    ds_s[...] = jnp.zeros_like(ds_s)
    dt_s[...] = jnp.zeros_like(dt_s)

    def attend_back(pair, carry):
        lw = lax.rem(pair, 2)
        for i in range(2):
            rows = window_rows(2 * pair + i)
            dam[i] = stacked(ga_s[rows, :])
            raw[i] = dot_nt(v_s[rows, :], dam[i])
        for i in range(2):
            for t in range(WIDE // 128):
                cols = slice(t * 128, (t + 1) * 128)
                chances = p_s[2 * pair + i, :, cols].astype(F32)
                weighted = raw[i, :, cols]
                centre = jnp.sum(chances * weighted, axis=0, keepdims=True)
                dsh[i, :, cols] = (chances * (weighted - centre)).astype(BF16)
        for i in range(2):
            rows = window_rows(2 * pair + i)
            dt_s[rows, 512:704] = dot_nn(p_s[2 * pair + i], dam[i]).astype(BF16)
            dt_s[rows, 0:C] = (per_head(k_s[rows, :], dsh[i]) * FACTOR).astype(BF16)
            dt_s[rows, 256:448] = (dot_nn(dsh[i], stacked(q_s[rows, :])) * FACTOR).astype(BF16)
        ds_s[lw] = ds_s[lw] + (dsh[0].astype(F32) + dsh[1].astype(F32))
        return carry

    all_rows = slice(0, 64)
    def windows_back(pair, carry):
        attend_back(pair, carry)

        @pl.when(pair == 0)
        def _():
            arrived(g1p, 5)
            add_pair(g1s, g1p, g1h)
            g1r[chip] = g1h[chip]
            chips_all(lambda o: to_chip(g1h.at[o], g1r.at[chip], 6, o).start())

        @pl.when(pair == 2)
        def _():
            arrived(g1l.at[pl.ds(0, 3)], 7)
            g1l[4] = sum_of(g1l, 4, all_rows)
            to_band(g1l.at[4], g1l.at[5], 15, d_pair).start()

        return carry

    def second_gradients():
        summed = dot_tn(ni_s[...], dt_s[...])
        sections = [summed[:, 0:C], summed[:, 256:448], summed[:, 512:704], jnp.zeros((C, 64), F32)]
        g_triple = jnp.concatenate(sections, axis=1).astype(BF16)
        for i in range(3):
            for j in range(5):
                at = 5 * i + j
                g2s[at // 8, at % 8, 0:64] = g_triple[i * 64:(i + 1) * 64, j * 128:(j + 1) * 128]
        g2s[1, 7, 0:64] = jnp.zeros((64, 128), BF16)
        for lw in range(2):
            for h in range(HEADS):
                at = pl.ds(h * 2 + lw, WIN, stride=16)
                part = jnp.concatenate(
                [ds_s[lw, :, h * 128:(h + 1) * 128], ds_s[lw, :, 768 + h * 16:784 + h * 16]], axis=1
            ).T
                bs_s.at[0][at, :] = part[:, 0:128]
                bs_s.at[1][at, :] = jnp.concatenate([part[:, 128:144], jnp.zeros((WIN, 112), F32)], axis=1)

        def fold(s_i, carry):
            at = pl.ds(pl.multiple_of(s_i * 192, 192), 192)
            rows = jnp.concatenate([bs_s[0, at, :], bs_s[1, at, :]], axis=1)[:, 0:WIN].astype(BF16)
            return carry + dot_nt(rows, spread_s[s_i])

        folded = lax.fori_loop(0, 12, fold, jnp.zeros((192, 512), F32))
        pieces_t = []
        for p in range(2):
            for pk in range(2):
                for r in range(6):
                    at = (p * 6 + r) * 16
                    pieces_t.append(folded[at:at + 16, pk * 256:pk * 256 + 138])
        table = jnp.concatenate(pieces_t + [jnp.zeros((16, 4096 - POS), F32)], axis=1).astype(BF16)
        for o in range(32):
            g2s[o // 16, (o // 2) % 8, 64 + 16 * (o % 2):80 + 16 * (o % 2)] = table[:, o * 128:(o + 1) * 128]
        to_core(g2s.at[1 - core], g2p, 9).start()

    def project_back(i, carry):
        rows = chunk_rows(i)
        tmp[...] = (
            dot_nt(dt_s[rows, 0:C], wq[...])
            + dot_nt(dt_s[rows, 256:448], wk[...])
            + dot_nt(dt_s[rows, 512:704], wv[...])
        )
        for t in range(CHUNK // TILE):
            part = tile_rows(i, t)
            unit, inverse = statistics(x_w[part, :].astype(F32))
            back = norm_back(unit, inverse, tmp[t * TILE:(t + 1) * TILE, :] * attend_gain[...])
            gt_s[part, :] = (gm_s[part, :] + back).astype(BF16)
        return carry

    from_window = one_hot(HALF, orders[3:4, 0:HALF])

    def backward_windows(b, carry):
        lax.fori_loop(2 * b, 2 * b + 2, windows_back, 0)

        @pl.when(b == 1)
        def _():
            arrived(g1l.at[5], 15)
            g1f[chip] = (g1l[4].astype(F32) + g1l[5].astype(F32)).astype(BF16)
            chips_all(lambda o: to_chip(g1f.at[chip], g1f.at[chip], 8, o).start())
            second_gradients()

        lax.fori_loop(2 * b, 2 * b + 2, project_back, 0)

        @pl.when(b == 0)
        def _():
            arrived(g1r.at[others], 6)
            g1l[d // 2] = sum_of(g1r, NCHIP, all_rows)
            for step in range(1, 4):
                to_band(g1l.at[d // 2], g1l.at[d // 2], 7, lax.rem(d + 2 * step, NLAT)).start()

        @pl.when(b == 1)
        def _():
            arrived(g2p, 9)
            add_pair(g2s, g2p, g2h)
            g2r[chip] = g2h[chip]
            chips_all(lambda o: to_chip(g2h.at[o], g2r.at[chip], 10, o).start())

        quads = dot_nn(from_window, gt_s[half_rows(b), :])
        gq[b] = quads
        pack(quads, b, (c10, c01, c11))
        for copy in rows_behind(b):
            copy.start()
        return carry

    lax.fori_loop(0, 2, backward_windows, 0)

    arrived(g1f.at[others], 8)
    to_core(g1f, g1o, 11).start()

    arrived(g2r.at[others], 10)
    g2l[d] = sum_of(g2r, NCHIP, slice(0, 64))
    lat_all(lambda o: to_band(g2l.at[d], g2l.at[d], 12, o).start())
    g2f[chip, 64:96] = sum_of(g2r, NCHIP, slice(64, 96))

    to_natural = one_hot(HALF, orders[1:2, 0:HALF])

    def unsort_sample(b, carry):
        for copy in rows_behind(b):
            copy.wait()
        unpack(gq, b, (d10, d01, d11))
        out_fields[half_rows(b), :] = dot_nn(to_natural, gq[b].astype(BF16)).astype(BF16)
        return carry

    lax.fori_loop(0, 1, unsort_sample, 0)
    arrived(g2l.at[others], 12)
    g2f[chip, 0:64] = sum_of(g2l, NLAT, slice(0, 64))
    chips_all(lambda o: to_chip(g2f.at[chip], g2f.at[chip], 13, o).start())


    lax.fori_loop(1, 2, unsort_sample, 0)
    arrived(g1o, 11)
    out_g1[core] = g1f[...]
    out_g1[1 - core] = g1o[...]
    arrived(g2f.at[others], 13)
    to_core(g2f, g2o, 14).start()
    out_g2[core] = g2f[...]
    arrived(g2o, 14)
    out_g2[1 - core] = g2o[...]

    left(cs.at[others], 0)
    left(wa.at[others], 1)
    left(cf, 2)
    left(wb, 3)
    left(ch, 4)
    left(g1p, 5)
    left(g1r.at[others], 6)
    left(g1l.at[pl.ds(0, 3)], 7)
    left(g1l.at[4], 15)
    left(g1f.at[others], 8)
    left(g2p, 9)
    left(g2r.at[others], 10)
    left(g1o, 11)
    left(g2l.at[others], 12)
    left(g2f.at[others], 13)
    left(g2o, 14)


def results_kernel(
    fields, g1, g2, attend_gain, triple_w, feed_gain, expand_w,
    out_fields, out_triple, out_output, out_expand, out_shrink, out_attend, out_feed, out_table,
):
    out_fields[...] = fields[...]
    for i in range(4):
        for j in range(2):
            rows, cols = slice(i * 48, (i + 1) * 48), slice(j * 384, (j + 1) * 384)
            out_expand[rows, cols] = g1[0, 2 * i + j, 0:48].astype(F32)
            out_shrink[rows, cols] = g1[1, 2 * i + j, 0:48].astype(F32)
    for i in range(6):
        wide = g1[i % 2, i // 2, 48:64].astype(F32)
        out_output[i * 16:(i + 1) * 16, :] = wide[:, 0:C]
        out_output[96 + i * 16:96 + (i + 1) * 16, :] = wide[:, C:2 * C]
    for i in range(3):
        for j in range(5):
            at, size = 5 * i + j, 128 if j < 4 else 64
            part = g2[at // 8, at % 8, 0:64].astype(F32)
            out_triple[i * 64:(i + 1) * 64, j * 128:j * 128 + size] = part[:, 0:size]
    table = jnp.concatenate(
        [g2[o // 16, (o // 2) % 8, 64 + 16 * (o % 2):80 + 16 * (o % 2)] for o in range(32)], axis=1
    ).astype(F32)
    for h in range(HEADS):
        out_table[h] = table[2 * h:2 * h + 2, 0:POS]

    def gain_gradient(grad, weight, gain):
        product = (grad[...] * weight[...].astype(F32)).astype(BF16)
        total = dot_nt(jnp.ones((16, product.shape[1]), BF16), product)
        return total[0:1] / gain[...]

    out_attend[...] = gain_gradient(out_triple, triple_w, attend_gain)
    out_feed[...] = gain_gradient(out_expand, expand_w, feed_gain)


def scratch():
    def vmem(*shape, kind=BF16):
        return pltpu.VMEM(shape, kind)

    token = vmem(TOK, C)
    token_f = vmem(TOK, C, kind=F32)
    weight = vmem(C, C)
    quad = vmem(2, HALF, C, kind=F32)
    halves = [vmem(2, 336, 128), vmem(2, 112, 128), vmem(2, 112, 128)]
    stat = vmem(WIN, 128, kind=F32)
    small = vmem(2, 24, 128, kind=F32)
    buffers = [
        quad, quad, *halves, *halves, *halves, *halves, token, token, token, token, token, weight, weight, weight,
        vmem(NWIN, WIN, WIDE), token, token_f, token, vmem(TOK, FF), vmem(TOK, FF, kind=F32), token,
        vmem(16, POS, kind=F32), vmem(576, 512), vmem(2, 2304, 128, kind=F32),
        vmem(2, WIN, WIDE, kind=F32), vmem(2, WIN, WIDE, kind=F32),
        vmem(12, 512, WIN), vmem(2, WIN, 384),
        vmem(576, 256, kind=F32), vmem(8, 2, 3, 32, 128), vmem(2, 8, 3, 32, 128), vmem(8, 3, 32, 128), vmem(2, 384, 128),
        vmem(3, 384, 128), vmem(8, 32, 768), vmem(8, 32, 768), vmem(384, 768),
        vmem(12, 128, C), token, vmem(2, WIN, 128, kind=F32), stat, small, small, small, small, vmem(4, WIN, 128, kind=F32),
        token, vmem(TOK, FF), token_f, token, token, vmem(TOK, 768), token,
        vmem(2, WIN, WIDE, kind=F32), vmem(2, WIN, WIDE), vmem(2, WIDE, C), vmem(CHUNK, FF, kind=F32),
        vmem(CHUNK, C, kind=F32),
    ]
    for rows, cols in ((64, 384), (96, 128)):
        chunks = vmem(8, rows, cols)
        buffers += [vmem(2, 8, rows, cols), chunks, chunks, chunks, vmem(8, 64, cols), chunks, chunks]
    counts = [6, 6, 6, 6, 4, 4, 16, 16]
    return buffers + [pltpu.SemaphoreType.DMA((n,)) for n in counts]


def per_device(
    fields, merge_cotangent, attend_gain, triple_weight, bias_table, output_weight, feed_gain,
    expand_weight, shrink_weight, merge_gain, merge_weight,
):
    cot = jnp.transpose(merge_cotangent, (1, 2, 3, 4, 0)).reshape(576, 192)
    bias = jnp.transpose(bias_table[0], (1, 0, 2))
    def shaped(shapes):
        return [jax.ShapeDtypeStruct(shape, kind) for shape, kind in shapes]

    vmem_spec = pl.BlockSpec(memory_space=pltpu.VMEM)
    parts = pl.pallas_call(
        kernel,
        out_shape=shaped(
            [((TOK, C), BF16), ((2, 8, 64, 384), BF16), ((2, 8, 96, 128), BF16)]
        ),
        in_specs=[vmem_spec] * 12,
        out_specs=[vmem_spec] * 3,
        scratch_shapes=scratch(),
        compiler_params=pltpu.CompilerParams(
            collective_id=0, has_side_effects=True, vmem_limit_bytes=60 * 1024 * 1024
        ),
    )(
        fields.reshape(TOK, C), cot, attend_gain.reshape(1, C), triple_weight, bias, output_weight,
        feed_gain.reshape(1, C), expand_weight, shrink_weight.T, merge_gain,
        merge_weight.T, jnp.asarray(order_indices()),
    )
    g_fields, g_triple, g_output, g_expand, g_shrink, g_attend, g_feed, g_table = pl.pallas_call(
        results_kernel,
        out_shape=shaped(
            [
                ((TOK, C), BF16), ((C, 3 * C), F32), ((C, C), F32), ((C, FF), F32), ((C, FF), F32),
                ((1, C), F32), ((1, C), F32), ((HEADS, 2, POS), F32),
            ]
        ),
        in_specs=[vmem_spec] * 7,
        out_specs=[vmem_spec] * 8,
        compiler_params=pltpu.CompilerParams(vmem_limit_bytes=60 * 1024 * 1024),
    )(*parts, attend_gain.reshape(1, C), triple_weight, feed_gain.reshape(1, C), expand_weight)
    return (
        g_fields.reshape(fields.shape), g_triple, g_output, g_expand, g_shrink.T,
        g_attend.reshape(C), g_feed.reshape(C), jnp.transpose(g_table, (1, 0, 2))[None],
    )


def solution(mesh):
    placed = (
        P(None, None, "lat", "lon", None),
        P(None, None, None, "lat", "lon"),
        P(),
        P(),
        P("lat", None, None, None),
        P(),
        P(),
        P(),
        P(),
        P(),
        P(None, "lon"),
    )
    return jax.shard_map(
        per_device,
        mesh=mesh,
        in_specs=placed,
        out_specs=(
            P(None, None, "lat", "lon", None),
            P(),
            P(),
            P(),
            P(),
            P(),
            P(),
            P("lat", None, None, None),
        ),
        check_vma=False,
    )
```

```python
import functools
import math

import jax
import jax.numpy as jnp
import numpy as np
from jax import lax
from jax.experimental import pallas as pl
from jax.experimental.pallas import tpu as pltpu
from jax.sharding import PartitionSpec as P

F32 = jnp.float32
BF16 = jnp.bfloat16
I32 = jnp.int32
MESH = pl.DeviceIdType.MESH

EPS = 1e-05
MASKED = -1000000000.0
NLON = 16
NLAT = 8
NCHIP = 8
C = 192
HEADS = 6
FF = 768
WIN = 144
NWIN = 8
TOK = WIN * NWIN
HALF = TOK // 2
SIZES = ((216, 112), (72, 40), (72, 40))
POS = 3312
CHUNK = 288
NCHUNK = TOK // CHUNK
TILE = 48
WIDE = 896
FACTOR = 32 ** -0.5


def order_indices():
    natural_to_quad = np.full(640, -1, np.int32)
    quad_to_natural = np.full(640, -1, np.int32)
    quad_to_window = np.full(640, -1, np.int32)
    window_to_quad = np.full(640, -1, np.int32)
    for level in range(4):
        for row in range(6):
            for col in range(24):
                source = (level * 6 + row) * 24 + col
                if col >= 6:
                    place = (0 if row >= 3 else 216) + level * 54 + (row % 3) * 18 + col - 6
                else:
                    place = (432 if row >= 3 else 504) + level * 18 + (row % 3) * 6 + col
                natural_to_quad[source] = place
                quad_to_natural[place] = source
    index = 0
    for lev_win in range(2):
        for lon_win in range(2):
            for s in range(12):
                for p in range(2):
                    for r in range(6):
                        level = (lev_win * 2 + p + 1) % 4
                        col = lon_win * 12 + s
                        if col < 18:
                            place = (0 if r < 3 else 216) + level * 54 + (r % 3) * 18 + col
                        else:
                            place = (432 if r < 3 else 504) + level * 18 + (r % 3) * 6 + col - 18
                        window_to_quad[index] = place
                        quad_to_window[place] = index
                        index += 1
    cell_lane = np.full(640, -1, np.int32)
    bias_row = np.full(640, -1, np.int32)
    merged_token = np.full((2, 640), -1, np.int32)
    for lane in range(256):
        if lane % 16 < 12:
            cell_lane[lane] = (12 * (lane // 16) + 3 + lane % 16) % 192
    for k in range(WIN):
        s, p, r = k // 12, (k // 6) % 2, k % 6
        bias_row[k] = p * 256 + r * 23 + 11 - s
    for lon_win in range(2):
        for row in range(384):
            p, r, y, m = row // 192, (row // 32) % 6, (row // 16) % 2, row % 16
            if 0 <= m - lon_win * 6 < 6:
                merged_token[lon_win, row] = (2 * (m - lon_win * 6) + y) * 12 + p * 6 + r
    rows = [natural_to_quad, quad_to_natural, quad_to_window, window_to_quad]
    return np.stack(rows + [cell_lane, bias_row, merged_token[0], merged_token[1]])


def dot_nn(a, b):
    return lax.dot_general(a, b, (((1,), (0,)), ((), ())), preferred_element_type=F32)


def dot_nt(a, b):
    return lax.dot_general(a, b, (((1,), (1,)), ((), ())), preferred_element_type=F32)


def dot_tn(a, b):
    return lax.dot_general(a, b, (((0,), (0,)), ((), ())), preferred_element_type=F32)


def one_hot(rows, targets):
    ids = lax.broadcasted_iota(I32, (rows, targets.shape[1]), 0)
    return jnp.where(ids == targets, 1.0, 0.0).astype(BF16)


def statistics(values):
    centred = values - jnp.mean(values, axis=-1, keepdims=True)
    inverse = lax.rsqrt(jnp.mean(centred * centred, axis=-1, keepdims=True) + EPS)
    return centred * inverse, inverse


def norm_back(normed, inverse, scaled):
    centre = jnp.mean(scaled, axis=-1, keepdims=True)
    projected = jnp.mean(scaled * normed, axis=-1, keepdims=True)
    return inverse * (scaled - centre - normed * projected)


def gelu_parts(values):
    cumulative = 0.5 * (1.0 + lax.erf(values * (1.0 / math.sqrt(2.0))))
    density = jnp.exp(-0.5 * values * values) * (1.0 / math.sqrt(2.0 * math.pi))
    return values * cumulative, cumulative + values * density


def lanes(rows, cols):
    return lax.broadcasted_iota(I32, (rows, cols), 1)


def over_12(ids):
    return (ids * 5462) >> 16


def over_6(ids):
    return (ids * 10923) >> 16


def kernel(
    fields, cot, attend_gain, triple_w, bias, output_w, feed_gain, expand_w, shrink_t, merge_gain,
    merge_wt, orders,
    out_fields, out_g1, out_g2,
    sq, gq, a10, a01, a11, b10, b01, b11, c10, c01, c11, d10, d01, d11, x_w, ni_s, q_s, k_s, v_s, wq, wk, wv, p_s, att_s, mid_s, nm_s, act_s, slope_s, vo_s,
    b16, bl_s, bs_s, bx, ds_s, spread_s, pick_s,
    cells, cs, cx, cm, ch, planes, w_own, w_part, w_send, w_all, qry, qw, st, sx, sup, sdn, tup, tdn, cp_s, go_s, gh_s, gm_s, ga_s, gmh_s,
    dt_s, gt_s, raw, dsh, dam, hid, tmp, g1s, g1p, g1h, g1r, g1l, g1f, g1o, g2s, g2p, g2h, g2r, g2l, g2f, g2o,
    halo_ss, halo_rs, back_ss, back_rs, st_ss, st_rs, sends, recvs,
):
    e = lax.axis_index("lon")
    d = lax.axis_index("lat")
    e_up, e_dn = lax.rem(e + 1, NLON), lax.rem(e + NLON - 1, NLON)
    d_up, d_dn = lax.rem(d + 1, NLAT), lax.rem(d + NLAT - 1, NLAT)

    def remote(src, dst, ssem, rsem, device):
        return pltpu.make_async_remote_copy(
            src_ref=src, dst_ref=dst, send_sem=ssem, recv_sem=rsem, device_id=device,
            device_id_type=MESH,
        )

    core, chip = lax.rem(e, 2), e // 2
    partner = e + 1 - 2 * core
    d_pair = d + 1 - 2 * lax.rem(d, 2)

    def chips_all(action):
        def body(step, carry):
            action(lax.rem(chip + step, NCHIP))
            return carry

        lax.fori_loop(1, NCHIP, body, 0)

    def lat_all(action):
        def body(step, carry):
            action(lax.rem(d + step, NLAT))
            return carry

        lax.fori_loop(1, NLAT, body, 0)

    def to_chip(src, dst, phase, o):
        return remote(src, dst, sends.at[phase], recvs.at[phase], (2 * o + core, d))

    def to_band(src, dst, phase, o):
        return remote(src, dst, sends.at[phase], recvs.at[phase], (e, o))

    def to_core(src, dst, phase):
        return remote(src, dst, sends.at[phase], recvs.at[phase], (partner, d))

    def arrived(region, phase):
        remote(region, region, sends.at[phase], recvs.at[phase], (partner, d)).wait_recv()

    def left(region, phase):
        remote(region, region, sends.at[phase], recvs.at[phase], (partner, d)).wait_send()

    barrier = pltpu.get_barrier_semaphore()

    def greet(device):
        pl.semaphore_signal(barrier, inc=1, device_id=device, device_id_type=MESH)

    chips_all(lambda o: greet((2 * o + core, d)))
    lat_all(lambda o: greet((e, o)))
    for device in ((e_up, d), (e_dn, d), (e_up, d_up), (e_dn, d_dn)):
        greet(device)

    def half_rows(b):
        return pl.ds(pl.multiple_of(b * HALF, HALF), HALF)

    def pack(quads, b, out):
        at = 216
        for (size, cut), message in zip(SIZES, out):
            rows = quads[at:at + size]
            rest = jnp.concatenate([rows[cut:, 128:C], jnp.zeros((2 * cut - size, 64), F32)], axis=0)
            parts = [rows[:, 0:128], jnp.concatenate([rows[:cut, 128:C], rest], axis=1)]
            if (size + cut) % 16:
                parts.append(jnp.zeros((8, 128), F32))
            message[b] = jnp.concatenate(parts, axis=0).astype(BF16)
            at += size

    def unpack(quads, b, messages):
        at = 216
        for (size, cut), message in zip(SIZES, messages):
            rows = message[b].astype(F32)
            tails = rows[size:size + cut]
            tail = jnp.concatenate([tails[:, 0:64], tails[0:size - cut, 64:128]], axis=0)
            quads[b, at:at + size, :] = jnp.concatenate([rows[0:size], tail], axis=1)
            at += size

    def halo(sources, targets, ssem, rsem, step, b):
        devices = ((e, step[1]), (step[0], d), (step[0], step[1]))
        return [
            remote(src.at[b], dst.at[b], ssem.at[3 * b + i], rsem.at[3 * b + i], dev)
            for i, (src, dst, dev) in enumerate(zip(sources, targets, devices))
        ]

    def rows_ahead(b):
        return halo((a10, a01, a11), (b10, b01, b11), halo_ss, halo_rs, (e_dn, d_dn), b)

    def rows_behind(b):
        return halo((c10, c01, c11), (d10, d01, d11), back_ss, back_rs, (e_up, d_up), b)

    to_quad = one_hot(HALF, orders[0:1, 0:HALF])

    def sort_sample(b, carry):
        quads = dot_nn(to_quad, fields[half_rows(b), :])
        sq[b] = quads
        pack(quads, b, (a10, a01, a11))
        return carry

    lax.fori_loop(0, 2, sort_sample, 0)
    pl.semaphore_wait(barrier, NCHIP - 1 + NLAT - 1 + 4)
    for b in range(2):
        for copy in rows_ahead(b):
            copy.start()

    cells[...] = dot_nn(cot[...], one_hot(192, orders[4:5, 0:256]))
    block_of = lanes(72, 128) >> 4

    def gather_cells(o, carry):
        tile = pl.ds(pl.multiple_of((o // 8) * 128, 128), 128)
        inner = lax.rem(o, 8)
        piece = jnp.zeros((72, 128), F32)
        for bl in range(8):
            part = pltpu.roll(cells[bl * 72:(bl + 1) * 72, tile], lax.rem(16 * (bl - inner) + 128, 128), 1)
            piece = jnp.where(block_of == bl, part, piece)
        for a in range(3):
            padded = jnp.concatenate([piece[a * 24:(a + 1) * 24], jnp.zeros((8, 128), F32)], axis=0)
            cs[o // 2, lax.rem(o, 2), a] = padded.astype(BF16)
        return carry

    lax.fori_loop(0, NLON, gather_cells, 0)
    w_own[...] = jnp.concatenate(
        [merge_wt[...].astype(F32), jnp.zeros((8, 768), F32)], axis=0
    ).astype(BF16)
    to_core(cs.at[:, 1 - core], cx, 0).start()
    to_core(w_own, w_part, 2).start()

    for h in range(HEADS):
        b16[2 * h:2 * h + 2, :] = bias[h]
    b16[12:16, :] = jnp.zeros((4, POS), F32)
    zero_tail = jnp.zeros((16, 256 - 138), F32)
    for p in range(2):
        for r in range(6):
            parts = []
            for pk in range(2):
                at = (p * 2 + pk) * 828 + r * 138
                parts += [b16[:, at:at + 138], zero_tail]
            row = jnp.concatenate(parts, axis=1)
            high = row.astype(BF16)
            rest = row - high.astype(F32)
            middle = rest.astype(BF16)
            low = (rest - middle.astype(F32)).astype(BF16)
            at = (p * 6 + r) * 16
            bl_s[at:at + 16, :] = high
            bl_s[192 + at:192 + at + 16, :] = middle
            bl_s[384 + at:384 + at + 16, :] = low

    bias_row = orders[5:6, 0:WIN]

    def spread(s_i, carry):
        matrix = one_hot(512, bias_row + s_i)
        spread_s[s_i] = matrix
        split = dot_nn(bl_s[...], matrix)
        rows = split[0:192] + split[192:384] + split[384:576]
        at = pl.ds(pl.multiple_of(s_i * 192, 192), 192)
        bs_s[0, at, :] = rows[:, 0:128]
        bs_s[1, at, :] = jnp.concatenate([rows[:, 128:144], jnp.zeros((192, 112), F32)], axis=1)
        return carry

    lax.fori_loop(0, 12, spread, 0)

    def dense(mine, other):
        mine, other = mine.astype(F32)[0:24], other.astype(F32)[0:24]
        swapped = core == 1
        parts = [jnp.where(swapped, other, mine), jnp.where(swapped, mine, other)]
        return jnp.concatenate(parts, axis=0)

    def chip_rows(o):
        return pl.ds(pl.multiple_of(o * 48, 48), 48)

    def merge_pieces(o, carry):
        for a in range(3):
            cm[o, a] = dense(cs[o, core, a], cx[o, a]).astype(BF16)
        return carry

    arrived(cx, 0)
    lax.fori_loop(0, NCHIP, merge_pieces, 0)
    planes[:, chip_rows(chip)] = cm[chip]
    chips_all(lambda o: to_chip(cm.at[o], planes.at[:, chip_rows(chip)], 1, o).start())
    arrived(w_part, 2)
    both = dense(w_own[...], w_part[...])
    w_send[...] = jnp.where(core == 1, both[:, 384:768], both[:, 0:384]).astype(BF16)
    w_all[core, chip_rows(chip)] = w_send[...]
    chips_all(lambda o: to_chip(w_send, w_all.at[core, chip_rows(chip)], 3, o).start())
    seven = pl.ds(0, 48 * (NCHIP - 1))

    tok_i = lax.broadcasted_iota(I32, (WIN, WIN), 0)
    tok_k = lax.broadcasted_iota(I32, (WIN, WIN), 1)
    half_i, half_k = over_6(tok_i), over_6(tok_k)
    last_band = d == NLAT - 1
    lat_differs = ((tok_i - half_i * 6 >= 3) != (tok_k - half_k * 6 >= 3)) & last_band
    lev_differs = (half_i & 1) != (half_k & 1)
    bx[:, :, HEADS * WIN:WIDE] = jnp.zeros((2, WIN, WIDE - HEADS * WIN), F32)
    for lw in range(2):
        differs = (lat_differs | lev_differs) if lw else lat_differs
        for h in range(HEADS):
            at = pl.ds(h * 2 + lw, WIN, stride=16)
            full = jnp.concatenate([bs_s.at[0][at, :], bs_s.at[1][at, :]], axis=1)[:, 0:WIN]
            spread_bias = jnp.where(differs, MASKED, full).T
            bx[lw, :, h * 128:(h + 1) * 128] = spread_bias[:, 0:128]
            bx[lw, :, 768 + h * 16:784 + h * 16] = spread_bias[:, 128:WIN]

    wq[...] = triple_w[:, 0:192]
    wk[...] = triple_w[:, 192:384]
    wv[...] = triple_w[:, 384:576]

    head_of = lanes(1, C) >> 5
    head_f = [jnp.where(head_of == h, 1.0, 0.0) for h in range(HEADS)]
    head_b = [mask.astype(BF16) for mask in head_f]

    blank = jnp.zeros((WIDE - HEADS * WIN, C), BF16)

    def stacked(values):
        first, rest = values[0:128], values[128:WIN]
        parts = [first * mask for mask in head_b] + [rest * mask for mask in head_b]
        return jnp.concatenate(parts + [blank], axis=0)

    def per_head(left, right):
        turned = left.T
        wide = [dot_nn(turned[64 * i:64 * i + 64], right[:, 256 * i:256 * i + 256]) for i in range(3)]
        tail = dot_nn(turned, right[:, 768:WIDE])
        blocks = []
        for h in range(HEADS):
            at, row = 128 * (h % 2), 32 * (h % 2)
            blocks.append(
                jnp.concatenate(
                    [wide[h // 2][row:row + 32, at:at + 128], tail[32 * h:32 * h + 32, 16 * h:16 * h + 16]], axis=1
                )
            )
        return jnp.concatenate(blocks, axis=0).T

    to_window = one_hot(HALF, orders[2:3, 0:HALF])

    def window_rows(w):
        return pl.ds(pl.multiple_of(w * WIN, WIN), WIN)

    def chunk_rows(i):
        return pl.ds(pl.multiple_of(i * CHUNK, CHUNK), CHUNK)

    def tile_rows(i, t):
        return pl.ds(pl.multiple_of(i * CHUNK + t * TILE, 16), TILE)

    def project(i, carry):
        rows = chunk_rows(i)
        for t in range(CHUNK // TILE):
            part = tile_rows(i, t)
            normed = statistics(x_w[part, :].astype(F32))[0]
            ni_s[part, :] = (normed * attend_gain[...]).astype(BF16)
        normed_in = ni_s[rows, :]
        q_s[rows, :] = dot_nn(normed_in, wq[...]).astype(BF16)
        k_s[rows, :] = dot_nn(normed_in, wk[...]).astype(BF16)
        v_s[rows, :] = dot_nn(normed_in, wv[...]).astype(BF16)
        return carry


    def attend(pair, carry):
        lw = lax.rem(pair, 2)
        for i in range(2):
            rows = window_rows(2 * pair + i)
            raw[i] = dot_nt(k_s[rows, :], stacked(q_s[rows, :]))
        for i in range(2):
            for t in range(WIDE // 128):
                cols = slice(t * 128, (t + 1) * 128)
                scores = raw[i, :, cols] * FACTOR + bx[lw, :, cols]
                exponent = jnp.exp(scores - jnp.max(scores, axis=0, keepdims=True))
                chances = exponent * (1.0 / jnp.sum(exponent, axis=0, keepdims=True))
                p_s[2 * pair + i, :, cols] = chances.astype(BF16)
        for i in range(2):
            rows = window_rows(2 * pair + i)
            att_s[rows, :] = per_head(v_s[rows, :], p_s[2 * pair + i]).astype(BF16)
        return carry

    def forward_windows(b, carry):
        for copy in rows_ahead(b):
            copy.wait()

        unpack(sq, b, (b10, b01, b11))
        x_w[half_rows(b), :] = dot_nn(to_window, sq[b].astype(BF16)).astype(BF16)
        lax.fori_loop(2 * b, 2 * b + 2, project, 0)

        lax.fori_loop(2 * b, 2 * b + 2, attend, 0)

        @pl.when(b == 0)
        def _():
            arrived(planes.at[:, seven], 1)
            to_band(planes.at[pl.ds(0, 2)], ch, 4, d_dn).start()

        return carry

    lax.fori_loop(0, 2, forward_windows, 0)
    arrived(w_all.at[0, seven], 3)
    to_core(w_all.at[core], w_all.at[core], 16).start()

    def feed(i, carry):
        rows = chunk_rows(i)
        tmp[...] = x_w[rows, :].astype(F32) + dot_nn(att_s[rows, :], output_w[...])
        for t in range(CHUNK // TILE):
            part = tile_rows(i, t)
            middle = tmp[t * TILE:(t + 1) * TILE, :]
            mid_s[part, :] = middle
            nm_s[part, :] = (statistics(middle)[0] * feed_gain[...]).astype(BF16)
        hid[...] = dot_nn(nm_s[rows, :], expand_w[...])
        for t in range(CHUNK // 16):
            part = pl.ds(pl.multiple_of(i * CHUNK + t * 16, 16), 16)
            for j in range(FF // 256):
                cols = slice(j * 256, (j + 1) * 256)
                act, slope = gelu_parts(hid[t * 16:(t + 1) * 16, cols])
                act_s[part, cols] = act.astype(BF16)
                slope_s[part, cols] = slope
        vo_s[rows, :] = (tmp[...] + dot_nt(act_s[rows, :], shrink_t[...])).astype(BF16)
        return carry

    lax.fori_loop(0, NCHUNK, feed, 0)

    arrived(w_all.at[0], 16)
    gain_row = merge_gain[...].reshape(1, 4 * C)
    for r in range(6):
        x = (r + 1) % 2
        cell = (0, 1, 1, 2, 2, 3)[r]
        cols = slice(x * 384, (x + 1) * 384)
        if r == 3:
            arrived(ch, 4)
        plane = planes[cell + 1] if cell < 2 else ch[cell - 2]
        summed = dot_tn(plane, w_all[x])
        scaled = summed * gain_row[:, x * 384:(x + 1) * 384]
        qry[2 * r] = scaled[:, 0:192].astype(BF16)
        qry[2 * r + 1] = scaled[:, 192:384].astype(BF16)

    st[...] = jnp.zeros_like(st)
    for i in range(2):
        pick_s[i] = one_hot(WIN, orders[6 + i:7 + i, 0:384])
    stat_lane = lanes(WIN, 128)
    tile_lane = lanes(TILE, 128)

    def merge_sums(w, carry):
        rows = window_rows(w)
        b, lw, lon_win = w // 4, lax.rem(w // 2, 2), lax.rem(w, 2)
        parts = []
        for p in range(2):
            level = lax.rem(lw * 2 + p + 1, 4)
            at = pl.ds(pl.multiple_of((b * 4 + level) * 16, 16), 16)
            parts.append(qry[:, at, :].reshape(192, C))
        qw[rows, :] = dot_nn(pick_s[lon_win], jnp.concatenate(parts, axis=0)).astype(BF16)
        for t in range(WIN // TILE):
            part = pl.ds(pl.multiple_of(w * WIN + t * TILE, 16), TILE)
            at = slice(t * TILE, (t + 1) * TILE)
            q = qw[part, :].astype(F32)
            v = vo_s[part, :].astype(F32)
            mean = jnp.mean(v, axis=-1, keepdims=True)
            centred = v - mean
            squares = jnp.sum(centred * centred, axis=-1, keepdims=True)
            q_sum = jnp.sum(q, axis=-1, keepdims=True)
            qv_sum = jnp.sum(q * centred, axis=-1, keepdims=True)
            total = st[b, at, :]
            for j, value in enumerate((mean, squares, q_sum, qv_sum)):
                total = jnp.where(tile_lane == 32 * j + w, value, total)
            st[b, at, :] = total
        return carry

    def sums_copies(b):
        return (
            remote(tup.at[b], sup.at[b], st_ss.at[2 * b], st_rs.at[2 * b], (e, d_up)),
            remote(tdn.at[b], sdn.at[b], st_ss.at[2 * b + 1], st_rs.at[2 * b + 1], (e, d_dn)),
        )

    def exchange(b):
        tup[b] = st.at[b][pl.ds(5, 24, stride=6), :]
        tdn[b] = st.at[b][pl.ds(0, 24, stride=6), :]
        for copy in sums_copies(b):
            copy.start()

    even = (over_12(lax.broadcasted_iota(I32, (WIN, 128), 0)) & 1) == 0

    def pair_of(values):
        return jnp.where(even, pltpu.roll(values, WIN - 12, 0), pltpu.roll(values, 12, 0))

    def cell_norm(b):
        for r, other in ((1, 2), (2, 1), (3, 4), (4, 3)):
            sx[pl.ds(r, 24, stride=6), :] = st.at[b][pl.ds(other, 24, stride=6), :]
        for copy in sums_copies(b):
            copy.wait()
        sx[pl.ds(0, 24, stride=6), :] = sup[b]
        sx[pl.ds(5, 24, stride=6), :] = sdn[b]
        own, cross = st[b], sx[...]
        group = [own, cross, pair_of(own), pair_of(cross)]
        cell_mean = (group[0] + group[1] + group[2] + group[3]) * 0.25
        variance = jnp.zeros((WIN, 128), F32)
        q_total = jnp.zeros((WIN, 128), F32)
        qv_total = jnp.zeros((WIN, 128), F32)
        for values in group:
            offset = values - cell_mean
            q_sum = pltpu.roll(values, 64, 1)
            variance = variance + pltpu.roll(values, 96, 1) + 192.0 * offset * offset
            q_total = q_total + q_sum
            qv_total = qv_total + pltpu.roll(values, 32, 1) + offset * q_sum
        cell_inverse = lax.rsqrt(jnp.where(stat_lane < 8, variance, 0.0) * (1.0 / 768.0) + EPS)
        cp_s[0] = cell_mean
        cp_s[1] = cell_inverse
        cp_s[2] = q_total * (1.0 / 768.0)
        cp_s[3] = cell_inverse * cell_inverse * qv_total * (1.0 / 768.0)

    def merge_back(w, carry):
        for t in range(WIN // TILE):
            part = pl.ds(pl.multiple_of(w * WIN + t * TILE, 16), TILE)
            at = slice(t * TILE, (t + 1) * TILE)
            mean, inverse, q_mean, projected = [
                jnp.sum(jnp.where(tile_lane == w, cp_s[j, at, :], 0.0), axis=-1, keepdims=True) for j in range(4)
            ]
            v = vo_s[part, :].astype(F32) - mean
            go_s[part, :] = (inverse * (qw[part, :].astype(F32) - q_mean - v * projected)).astype(BF16)
        return carry

    def feed_back(i, carry):
        rows = chunk_rows(i)
        go = go_s[rows, :]
        gh = (dot_nn(go, shrink_t[...]) * slope_s[rows, :]).astype(BF16)
        gh_s[rows, :] = gh
        tmp[...] = dot_nt(gh, expand_w[...])
        for t in range(CHUNK // TILE):
            part = tile_rows(i, t)
            gnm = tmp[t * TILE:(t + 1) * TILE, :]
            unit, inverse = statistics(mid_s[part, :])
            gm = go_s[part, :].astype(F32) + norm_back(unit, inverse, gnm * feed_gain[...])
            gm_s[part, :] = gm
            gmh_s[part, :] = gm.astype(BF16)
        ga_s[rows, :] = dot_nt(gmh_s[rows, :], output_w[...]).astype(BF16)
        return carry

    def forward_sample(b, carry):
        lax.fori_loop(4 * b, 4 * b + 4, merge_sums, 0)
        exchange(b)
        return carry

    def backward_sample(b, carry):
        cell_norm(b)
        lax.fori_loop(4 * b, 4 * b + 4, merge_back, 0)
        lax.fori_loop(2 * b, 2 * b + 2, feed_back, 0)
        return carry

    lax.fori_loop(0, 2, forward_sample, 0)
    lax.fori_loop(0, 2, backward_sample, 0)

    g_expand = dot_tn(nm_s[...], gh_s[...]).astype(BF16)
    g_shrink = dot_tn(go_s[...], act_s[...]).astype(BF16)
    g_output = dot_tn(att_s[...], gmh_s[...]).astype(BF16)
    for i in range(4):
        for j in range(2):
            g1s[0, 2 * i + j, 0:48] = g_expand[i * 48:(i + 1) * 48, j * 384:(j + 1) * 384]
            g1s[1, 2 * i + j, 0:48] = g_shrink[i * 48:(i + 1) * 48, j * 384:(j + 1) * 384]
    wide = jnp.concatenate([g_output[0:96], g_output[96:192]], axis=1)
    for i in range(NCHIP):
        for j in range(2):
            at = (i * 2 + j) * 16
            g1s[j, i, 48:64] = wide[at:at + 16] if at < 96 else jnp.zeros((16, 384), BF16)

    def sum_of(ref, count, rows):
        total = ref[0, rows].astype(F32)
        for o in range(1, count):
            total = total + ref[o, rows].astype(F32)
        return total.astype(BF16)

    def add_pair(mine, other, out):
        def body(o, carry):
            out[o] = (mine[core, o].astype(F32) + other[o].astype(F32)).astype(BF16)
            return carry

        lax.fori_loop(0, NCHIP, body, 0)

    others = pl.ds(0, NCHIP - 1)
    to_core(g1s.at[1 - core], g1p, 5).start()

    ds_s[...] = jnp.zeros_like(ds_s)
    dt_s[...] = jnp.zeros_like(dt_s)

    def attend_back(pair, carry):
        lw = lax.rem(pair, 2)
        for i in range(2):
            rows = window_rows(2 * pair + i)
            dam[i] = stacked(ga_s[rows, :])
            raw[i] = dot_nt(v_s[rows, :], dam[i])
        for i in range(2):
            for t in range(WIDE // 128):
                cols = slice(t * 128, (t + 1) * 128)
                chances = p_s[2 * pair + i, :, cols].astype(F32)
                weighted = raw[i, :, cols]
                centre = jnp.sum(chances * weighted, axis=0, keepdims=True)
                dsh[i, :, cols] = (chances * (weighted - centre)).astype(BF16)
        for i in range(2):
            rows = window_rows(2 * pair + i)
            dt_s[rows, 512:704] = dot_nn(p_s[2 * pair + i], dam[i]).astype(BF16)
            dt_s[rows, 0:C] = (per_head(k_s[rows, :], dsh[i]) * FACTOR).astype(BF16)
            dt_s[rows, 256:448] = (dot_nn(dsh[i], stacked(q_s[rows, :])) * FACTOR).astype(BF16)
        ds_s[lw] = ds_s[lw] + (dsh[0].astype(F32) + dsh[1].astype(F32))
        return carry

    all_rows = slice(0, 64)
    def windows_back(pair, carry):
        attend_back(pair, carry)

        @pl.when(pair == 0)
        def _():
            arrived(g1p, 5)
            add_pair(g1s, g1p, g1h)
            g1r[chip] = g1h[chip]
            chips_all(lambda o: to_chip(g1h.at[o], g1r.at[chip], 6, o).start())

        @pl.when(pair == 2)
        def _():
            arrived(g1l.at[pl.ds(0, 3)], 7)
            g1l[4] = sum_of(g1l, 4, all_rows)
            to_band(g1l.at[4], g1l.at[5], 15, d_pair).start()

        return carry

    def second_gradients():
        summed = dot_tn(ni_s[...], dt_s[...])
        sections = [summed[:, 0:C], summed[:, 256:448], summed[:, 512:704], jnp.zeros((C, 64), F32)]
        g_triple = jnp.concatenate(sections, axis=1).astype(BF16)
        for i in range(3):
            for j in range(5):
                at = 5 * i + j
                g2s[at // 8, at % 8, 0:64] = g_triple[i * 64:(i + 1) * 64, j * 128:(j + 1) * 128]
        g2s[1, 7, 0:64] = jnp.zeros((64, 128), BF16)
        for lw in range(2):
            for h in range(HEADS):
                at = pl.ds(h * 2 + lw, WIN, stride=16)
                part = jnp.concatenate(
                [ds_s[lw, :, h * 128:(h + 1) * 128], ds_s[lw, :, 768 + h * 16:784 + h * 16]], axis=1
            ).T
                bs_s.at[0][at, :] = part[:, 0:128]
                bs_s.at[1][at, :] = jnp.concatenate([part[:, 128:144], jnp.zeros((WIN, 112), F32)], axis=1)

        def fold(s_i, carry):
            at = pl.ds(pl.multiple_of(s_i * 192, 192), 192)
            rows = jnp.concatenate([bs_s[0, at, :], bs_s[1, at, :]], axis=1)[:, 0:WIN].astype(BF16)
            return carry + dot_nt(rows, spread_s[s_i])

        folded = lax.fori_loop(0, 12, fold, jnp.zeros((192, 512), F32))
        pieces_t = []
        for p in range(2):
            for pk in range(2):
                for r in range(6):
                    at = (p * 6 + r) * 16
                    pieces_t.append(folded[at:at + 16, pk * 256:pk * 256 + 138])
        table = jnp.concatenate(pieces_t + [jnp.zeros((16, 4096 - POS), F32)], axis=1).astype(BF16)
        for o in range(32):
            g2s[o // 16, (o // 2) % 8, 64 + 16 * (o % 2):80 + 16 * (o % 2)] = table[:, o * 128:(o + 1) * 128]
        to_core(g2s.at[1 - core], g2p, 9).start()

    def project_back(i, carry):
        rows = chunk_rows(i)
        tmp[...] = (
            dot_nt(dt_s[rows, 0:C], wq[...])
            + dot_nt(dt_s[rows, 256:448], wk[...])
            + dot_nt(dt_s[rows, 512:704], wv[...])
        )
        for t in range(CHUNK // TILE):
            part = tile_rows(i, t)
            unit, inverse = statistics(x_w[part, :].astype(F32))
            back = norm_back(unit, inverse, tmp[t * TILE:(t + 1) * TILE, :] * attend_gain[...])
            gt_s[part, :] = (gm_s[part, :] + back).astype(BF16)
        return carry

    from_window = one_hot(HALF, orders[3:4, 0:HALF])

    def backward_windows(b, carry):
        lax.fori_loop(2 * b, 2 * b + 2, windows_back, 0)

        @pl.when(b == 1)
        def _():
            arrived(g1l.at[5], 15)
            g1f[chip] = (g1l[4].astype(F32) + g1l[5].astype(F32)).astype(BF16)
            chips_all(lambda o: to_chip(g1f.at[chip], g1f.at[chip], 8, o).start())
            second_gradients()

        lax.fori_loop(2 * b, 2 * b + 2, project_back, 0)

        @pl.when(b == 0)
        def _():
            arrived(g1r.at[others], 6)
            g1l[d // 2] = sum_of(g1r, NCHIP, all_rows)
            for step in range(1, 4):
                to_band(g1l.at[d // 2], g1l.at[d // 2], 7, lax.rem(d + 2 * step, NLAT)).start()

        @pl.when(b == 1)
        def _():
            arrived(g2p, 9)
            add_pair(g2s, g2p, g2h)
            g2r[chip] = g2h[chip]
            chips_all(lambda o: to_chip(g2h.at[o], g2r.at[chip], 10, o).start())

        quads = dot_nn(from_window, gt_s[half_rows(b), :])
        gq[b] = quads
        pack(quads, b, (c10, c01, c11))
        for copy in rows_behind(b):
            copy.start()
        return carry

    lax.fori_loop(0, 2, backward_windows, 0)

    arrived(g1f.at[others], 8)
    to_core(g1f, g1o, 11).start()

    arrived(g2r.at[others], 10)
    g2l[d] = sum_of(g2r, NCHIP, slice(0, 64))
    lat_all(lambda o: to_band(g2l.at[d], g2l.at[d], 12, o).start())
    g2f[chip, 64:96] = sum_of(g2r, NCHIP, slice(64, 96))

    to_natural = one_hot(HALF, orders[1:2, 0:HALF])

    def unsort_sample(b, carry):
        for copy in rows_behind(b):
            copy.wait()
        unpack(gq, b, (d10, d01, d11))
        out_fields[half_rows(b), :] = dot_nn(to_natural, gq[b].astype(BF16)).astype(BF16)
        return carry

    lax.fori_loop(0, 1, unsort_sample, 0)
    arrived(g2l.at[others], 12)
    g2f[chip, 0:64] = sum_of(g2l, NLAT, slice(0, 64))
    chips_all(lambda o: to_chip(g2f.at[chip], g2f.at[chip], 13, o).start())


    lax.fori_loop(1, 2, unsort_sample, 0)
    arrived(g1o, 11)
    out_g1[core] = g1f[...]
    out_g1[1 - core] = g1o[...]
    arrived(g2f.at[others], 13)
    to_core(g2f, g2o, 14).start()
    out_g2[core] = g2f[...]
    arrived(g2o, 14)
    out_g2[1 - core] = g2o[...]

    left(cx, 0)
    left(cm.at[others], 1)
    left(w_part, 2)
    left(w_all.at[0, seven], 3)
    left(w_all.at[0], 16)
    left(ch, 4)
    left(g1p, 5)
    left(g1r.at[others], 6)
    left(g1l.at[pl.ds(0, 3)], 7)
    left(g1l.at[4], 15)
    left(g1f.at[others], 8)
    left(g2p, 9)
    left(g2r.at[others], 10)
    left(g1o, 11)
    left(g2l.at[others], 12)
    left(g2f.at[others], 13)
    left(g2o, 14)


def results_kernel(
    fields, g1, g2, attend_gain, triple_w, feed_gain, expand_w,
    out_fields, out_triple, out_output, out_expand, out_shrink, out_attend, out_feed, out_table,
):
    out_fields[...] = fields[...]
    for i in range(4):
        for j in range(2):
            rows, cols = slice(i * 48, (i + 1) * 48), slice(j * 384, (j + 1) * 384)
            out_expand[rows, cols] = g1[0, 2 * i + j, 0:48].astype(F32)
            out_shrink[rows, cols] = g1[1, 2 * i + j, 0:48].astype(F32)
    for i in range(6):
        wide = g1[i % 2, i // 2, 48:64].astype(F32)
        out_output[i * 16:(i + 1) * 16, :] = wide[:, 0:C]
        out_output[96 + i * 16:96 + (i + 1) * 16, :] = wide[:, C:2 * C]
    for i in range(3):
        for j in range(5):
            at, size = 5 * i + j, 128 if j < 4 else 64
            part = g2[at // 8, at % 8, 0:64].astype(F32)
            out_triple[i * 64:(i + 1) * 64, j * 128:j * 128 + size] = part[:, 0:size]
    table = jnp.concatenate(
        [g2[o // 16, (o // 2) % 8, 64 + 16 * (o % 2):80 + 16 * (o % 2)] for o in range(32)], axis=1
    ).astype(F32)
    for h in range(HEADS):
        out_table[h] = table[2 * h:2 * h + 2, 0:POS]

    def gain_gradient(grad, weight, gain):
        product = (grad[...] * weight[...].astype(F32)).astype(BF16)
        total = dot_nt(jnp.ones((16, product.shape[1]), BF16), product)
        return total[0:1] / gain[...]

    out_attend[...] = gain_gradient(out_triple, triple_w, attend_gain)
    out_feed[...] = gain_gradient(out_expand, expand_w, feed_gain)


def scratch():
    def vmem(*shape, kind=BF16):
        return pltpu.VMEM(shape, kind)

    token = vmem(TOK, C)
    token_f = vmem(TOK, C, kind=F32)
    weight = vmem(C, C)
    quad = vmem(2, HALF, C, kind=F32)
    halves = [vmem(2, 336, 128), vmem(2, 112, 128), vmem(2, 112, 128)]
    stat = vmem(WIN, 128, kind=F32)
    small = vmem(2, 24, 128, kind=F32)
    buffers = [
        quad, quad, *halves, *halves, *halves, *halves, token, token, token, token, token, weight, weight, weight,
        vmem(NWIN, WIN, WIDE), token, token_f, token, vmem(TOK, FF), vmem(TOK, FF, kind=F32), token,
        vmem(16, POS, kind=F32), vmem(576, 512), vmem(2, 2304, 128, kind=F32),
        vmem(2, WIN, WIDE, kind=F32), vmem(2, WIN, WIDE, kind=F32),
        vmem(12, 512, WIN), vmem(2, WIN, 384),
        vmem(576, 256, kind=F32), vmem(8, 2, 3, 32, 128), vmem(8, 3, 32, 128),
        vmem(8, 3, 48, 128), vmem(2, 384, 128), vmem(3, 384, 128),
        vmem(32, 768), vmem(32, 768), vmem(48, 384), vmem(2, 384, 384),
        vmem(12, 128, C), token, vmem(2, WIN, 128, kind=F32), stat, small, small, small, small, vmem(4, WIN, 128, kind=F32),
        token, vmem(TOK, FF), token_f, token, token, vmem(TOK, 768), token,
        vmem(2, WIN, WIDE, kind=F32), vmem(2, WIN, WIDE), vmem(2, WIDE, C), vmem(CHUNK, FF, kind=F32),
        vmem(CHUNK, C, kind=F32),
    ]
    for rows, cols in ((64, 384), (96, 128)):
        chunks = vmem(8, rows, cols)
        buffers += [vmem(2, 8, rows, cols), chunks, chunks, chunks, vmem(8, 64, cols), chunks, chunks]
    counts = [6, 6, 6, 6, 4, 4, 17, 17]
    return buffers + [pltpu.SemaphoreType.DMA((n,)) for n in counts]


def per_device(
    fields, merge_cotangent, attend_gain, triple_weight, bias_table, output_weight, feed_gain,
    expand_weight, shrink_weight, merge_gain, merge_weight,
):
    cot = jnp.transpose(merge_cotangent, (1, 2, 3, 4, 0)).reshape(576, 192)
    bias = jnp.transpose(bias_table[0], (1, 0, 2))
    def shaped(shapes):
        return [jax.ShapeDtypeStruct(shape, kind) for shape, kind in shapes]

    vmem_spec = pl.BlockSpec(memory_space=pltpu.VMEM)
    parts = pl.pallas_call(
        kernel,
        out_shape=shaped(
            [((TOK, C), BF16), ((2, 8, 64, 384), BF16), ((2, 8, 96, 128), BF16)]
        ),
        in_specs=[vmem_spec] * 12,
        out_specs=[vmem_spec] * 3,
        scratch_shapes=scratch(),
        compiler_params=pltpu.CompilerParams(
            collective_id=0, has_side_effects=True, vmem_limit_bytes=60 * 1024 * 1024
        ),
    )(
        fields.reshape(TOK, C), cot, attend_gain.reshape(1, C), triple_weight, bias, output_weight,
        feed_gain.reshape(1, C), expand_weight, shrink_weight.T, merge_gain,
        merge_weight.T, jnp.asarray(order_indices()),
    )
    g_fields, g_triple, g_output, g_expand, g_shrink, g_attend, g_feed, g_table = pl.pallas_call(
        results_kernel,
        out_shape=shaped(
            [
                ((TOK, C), BF16), ((C, 3 * C), F32), ((C, C), F32), ((C, FF), F32), ((C, FF), F32),
                ((1, C), F32), ((1, C), F32), ((HEADS, 2, POS), F32),
            ]
        ),
        in_specs=[vmem_spec] * 7,
        out_specs=[vmem_spec] * 8,
        compiler_params=pltpu.CompilerParams(vmem_limit_bytes=60 * 1024 * 1024),
    )(*parts, attend_gain.reshape(1, C), triple_weight, feed_gain.reshape(1, C), expand_weight)
    return (
        g_fields.reshape(fields.shape), g_triple, g_output, g_expand, g_shrink.T,
        g_attend.reshape(C), g_feed.reshape(C), jnp.transpose(g_table, (1, 0, 2))[None],
    )


def solution(mesh):
    placed = (
        P(None, None, "lat", "lon", None),
        P(None, None, None, "lat", "lon"),
        P(),
        P(),
        P("lat", None, None, None),
        P(),
        P(),
        P(),
        P(),
        P(),
        P(None, "lon"),
    )
    return jax.shard_map(
        per_device,
        mesh=mesh,
        in_specs=placed,
        out_specs=(
            P(None, None, "lat", "lon", None),
            P(),
            P(),
            P(),
            P(),
            P(),
            P(),
            P("lat", None, None, None),
        ),
        check_vma=False,
    )
```

```python
import functools
import math

import jax
import jax.numpy as jnp
import numpy as np
from jax import lax
from jax.experimental import pallas as pl
from jax.experimental.pallas import tpu as pltpu
from jax.sharding import PartitionSpec as P

F32 = jnp.float32
BF16 = jnp.bfloat16
I32 = jnp.int32
MESH = pl.DeviceIdType.MESH

EPS = 1e-05
MASKED = -1000000000.0
NLON = 16
NLAT = 8
NCHIP = 8
C = 192
HEADS = 6
FF = 768
WIN = 144
NWIN = 8
TOK = WIN * NWIN
HALF = TOK // 2
SIZES = ((216, 112), (72, 40), (72, 40))
POS = 3312
CHUNK = 288
NCHUNK = TOK // CHUNK
TILE = 48
WIDE = 896
FACTOR = 32 ** -0.5


def order_indices():
    natural_to_quad = np.full(640, -1, np.int32)
    quad_to_natural = np.full(640, -1, np.int32)
    quad_to_window = np.full(640, -1, np.int32)
    window_to_quad = np.full(640, -1, np.int32)
    for level in range(4):
        for row in range(6):
            for col in range(24):
                source = (level * 6 + row) * 24 + col
                if col >= 6:
                    place = (0 if row >= 3 else 216) + level * 54 + (row % 3) * 18 + col - 6
                else:
                    place = (432 if row >= 3 else 504) + level * 18 + (row % 3) * 6 + col
                natural_to_quad[source] = place
                quad_to_natural[place] = source
    index = 0
    for lev_win in range(2):
        for lon_win in range(2):
            for s in range(12):
                for p in range(2):
                    for r in range(6):
                        level = (lev_win * 2 + p + 1) % 4
                        col = lon_win * 12 + s
                        if col < 18:
                            place = (0 if r < 3 else 216) + level * 54 + (r % 3) * 18 + col
                        else:
                            place = (432 if r < 3 else 504) + level * 18 + (r % 3) * 6 + col - 18
                        window_to_quad[index] = place
                        quad_to_window[place] = index
                        index += 1
    cell_lane = np.full(640, -1, np.int32)
    bias_row = np.full(640, -1, np.int32)
    merged_token = np.full((2, 640), -1, np.int32)
    for lane in range(256):
        if lane % 16 < 12:
            cell_lane[lane] = (12 * (lane // 16) + 3 + lane % 16) % 192
    for k in range(WIN):
        s, p, r = k // 12, (k // 6) % 2, k % 6
        bias_row[k] = p * 256 + r * 23 + 11 - s
    for lon_win in range(2):
        for row in range(384):
            p, r, y, m = row // 192, (row // 32) % 6, (row // 16) % 2, row % 16
            if 0 <= m - lon_win * 6 < 6:
                merged_token[lon_win, row] = (2 * (m - lon_win * 6) + y) * 12 + p * 6 + r
    rows = [natural_to_quad, quad_to_natural, quad_to_window, window_to_quad]
    return np.stack(rows + [cell_lane, bias_row, merged_token[0], merged_token[1]])


def dot_nn(a, b):
    return lax.dot_general(a, b, (((1,), (0,)), ((), ())), preferred_element_type=F32)


def dot_nt(a, b):
    return lax.dot_general(a, b, (((1,), (1,)), ((), ())), preferred_element_type=F32)


def dot_tn(a, b):
    return lax.dot_general(a, b, (((0,), (0,)), ((), ())), preferred_element_type=F32)


def one_hot(rows, targets):
    ids = lax.broadcasted_iota(I32, (rows, targets.shape[1]), 0)
    return jnp.where(ids == targets, 1.0, 0.0).astype(BF16)


def statistics(values):
    centred = values - jnp.mean(values, axis=-1, keepdims=True)
    inverse = lax.rsqrt(jnp.mean(centred * centred, axis=-1, keepdims=True) + EPS)
    return centred * inverse, inverse


def norm_back(normed, inverse, scaled):
    centre = jnp.mean(scaled, axis=-1, keepdims=True)
    projected = jnp.mean(scaled * normed, axis=-1, keepdims=True)
    return inverse * (scaled - centre - normed * projected)


def gelu_parts(values):
    cumulative = 0.5 * (1.0 + lax.erf(values * (1.0 / math.sqrt(2.0))))
    density = jnp.exp(-0.5 * values * values) * (1.0 / math.sqrt(2.0 * math.pi))
    return values * cumulative, cumulative + values * density


def lanes(rows, cols):
    return lax.broadcasted_iota(I32, (rows, cols), 1)


def over_12(ids):
    return (ids * 5462) >> 16


def over_6(ids):
    return (ids * 10923) >> 16


def kernel(
    fields, cot, attend_gain, triple_w, bias, output_w, feed_gain, expand_w, shrink_t, merge_gain,
    merge_wt, orders,
    out_fields, out_g1, out_g2,
    sq, gq, a10, a01, a11, b10, b01, b11, c10, c01, c11, d10, d01, d11, x_w, ni_s, q_s, k_s, v_s, wq, wk, wv, p_s, att_s, mid_s, nm_s, act_s, slope_s, vo_s,
    b16, bl_s, bs_s, bx, ds_s, spread_s, pick_s,
    cells, cs, cx, cm, ch, planes, w_own, w_part, w_send, w_all, qry, qw, st, sx, sup, sdn, tup, tdn, cp_s, go_s, gh_s, gm_s, ga_s, gmh_s,
    dt_s, gt_s, raw, dsh, dam, hid, tmp, g1s, g1p, g1h, g1r, g1l, g1f, g1o, g2s, g2p, g2h, g2r, g2l, g2f, g2o,
    halo_ss, halo_rs, back_ss, back_rs, st_ss, st_rs, sends, recvs,
):
    e = lax.axis_index("lon")
    d = lax.axis_index("lat")
    e_up, e_dn = lax.rem(e + 1, NLON), lax.rem(e + NLON - 1, NLON)
    d_up, d_dn = lax.rem(d + 1, NLAT), lax.rem(d + NLAT - 1, NLAT)

    def remote(src, dst, ssem, rsem, device):
        return pltpu.make_async_remote_copy(
            src_ref=src, dst_ref=dst, send_sem=ssem, recv_sem=rsem, device_id=device,
            device_id_type=MESH,
        )

    core, chip = lax.rem(e, 2), e // 2
    partner = e + 1 - 2 * core
    d_pair = d + 1 - 2 * lax.rem(d, 2)

    def chips_all(action):
        def body(step, carry):
            action(lax.rem(chip + step, NCHIP))
            return carry

        lax.fori_loop(1, NCHIP, body, 0)

    def lat_all(action):
        def body(step, carry):
            action(lax.rem(d + step, NLAT))
            return carry

        lax.fori_loop(1, NLAT, body, 0)

    def to_chip(src, dst, phase, o):
        return remote(src, dst, sends.at[phase], recvs.at[phase], (2 * o + core, d))

    def to_band(src, dst, phase, o):
        return remote(src, dst, sends.at[phase], recvs.at[phase], (e, o))

    def to_core(src, dst, phase):
        return remote(src, dst, sends.at[phase], recvs.at[phase], (partner, d))

    def arrived(region, phase):
        remote(region, region, sends.at[phase], recvs.at[phase], (partner, d)).wait_recv()

    def left(region, phase):
        remote(region, region, sends.at[phase], recvs.at[phase], (partner, d)).wait_send()

    barrier = pltpu.get_barrier_semaphore()

    def greet(device):
        pl.semaphore_signal(barrier, inc=1, device_id=device, device_id_type=MESH)

    chips_all(lambda o: greet((2 * o + core, d)))
    lat_all(lambda o: greet((e, o)))
    for device in ((e_up, d), (e_dn, d), (e_up, d_up), (e_dn, d_dn)):
        greet(device)

    def half_rows(b):
        return pl.ds(pl.multiple_of(b * HALF, HALF), HALF)

    def pack(quads, b, out):
        at = 216
        for (size, cut), message in zip(SIZES, out):
            rows = quads[at:at + size]
            rest = jnp.concatenate([rows[cut:, 128:C], jnp.zeros((2 * cut - size, 64), F32)], axis=0)
            parts = [rows[:, 0:128], jnp.concatenate([rows[:cut, 128:C], rest], axis=1)]
            if (size + cut) % 16:
                parts.append(jnp.zeros((8, 128), F32))
            message[b] = jnp.concatenate(parts, axis=0).astype(BF16)
            at += size

    def unpack(quads, b, messages):
        at = 216
        for (size, cut), message in zip(SIZES, messages):
            rows = message[b].astype(F32)
            tails = rows[size:size + cut]
            tail = jnp.concatenate([tails[:, 0:64], tails[0:size - cut, 64:128]], axis=0)
            quads[b, at:at + size, :] = jnp.concatenate([rows[0:size], tail], axis=1)
            at += size

    def halo(sources, targets, ssem, rsem, step, b):
        devices = ((e, step[1]), (step[0], d), (step[0], step[1]))
        return [
            remote(src.at[b], dst.at[b], ssem.at[3 * b + i], rsem.at[3 * b + i], dev)
            for i, (src, dst, dev) in enumerate(zip(sources, targets, devices))
        ]

    def rows_ahead(b):
        return halo((a10, a01, a11), (b10, b01, b11), halo_ss, halo_rs, (e_dn, d_dn), b)

    def rows_behind(b):
        return halo((c10, c01, c11), (d10, d01, d11), back_ss, back_rs, (e_up, d_up), b)

    to_quad = one_hot(HALF, orders[0:1, 0:HALF])

    def sort_sample(b, carry):
        quads = dot_nn(to_quad, fields[half_rows(b), :])
        sq[b] = quads
        pack(quads, b, (a10, a01, a11))
        return carry

    lax.fori_loop(0, 2, sort_sample, 0)
    pl.semaphore_wait(barrier, NCHIP - 1 + NLAT - 1 + 4)
    for b in range(2):
        for copy in rows_ahead(b):
            copy.start()

    cells[...] = dot_nn(cot[...], one_hot(192, orders[4:5, 0:256]))
    block_of = lanes(72, 128) >> 4

    def gather_cells(inner, carry):
        for tile in range(2):
            piece = jnp.zeros((72, 128), F32)
            for bl in range(8):
                part = cells[bl * 72:(bl + 1) * 72, tile * 128:(tile + 1) * 128]
                part = pltpu.roll(part, lax.rem(16 * (bl - inner) + 128, 128), 1)
                piece = jnp.where(block_of == bl, part, piece)
            for a in range(3):
                padded = jnp.concatenate([piece[a * 24:(a + 1) * 24], jnp.zeros((8, 128), F32)], axis=0)
                cs[4 * tile + inner // 2, lax.rem(inner, 2), a] = padded.astype(BF16)
        return carry

    lax.fori_loop(0, 8, gather_cells, 0)
    w_own[...] = jnp.concatenate(
        [merge_wt[...].astype(F32), jnp.zeros((8, 768), F32)], axis=0
    ).astype(BF16)
    to_core(cs.at[:, 1 - core], cx, 0).start()
    to_core(w_own, w_part, 2).start()

    for h in range(HEADS):
        b16[2 * h:2 * h + 2, :] = bias[h]
    b16[12:16, :] = jnp.zeros((4, POS), F32)
    zero_tail = jnp.zeros((16, 256 - 138), F32)
    for p in range(2):
        for r in range(6):
            parts = []
            for pk in range(2):
                at = (p * 2 + pk) * 828 + r * 138
                parts += [b16[:, at:at + 138], zero_tail]
            row = jnp.concatenate(parts, axis=1)
            high = row.astype(BF16)
            low = (row - high.astype(F32)).astype(BF16)
            at = (p * 6 + r) * 16
            bl_s[at:at + 16, :] = high
            bl_s[192 + at:192 + at + 16, :] = low

    bias_row = orders[5:6, 0:WIN]

    def spread(pair, carry):
        for i in range(2):
            s_i = 2 * pair + i
            matrix = one_hot(512, bias_row + s_i)
            spread_s[s_i] = matrix
            split = dot_nn(bl_s[...], matrix)
            rows = split[0:192] + split[192:384]
            at = pl.ds(pl.multiple_of(s_i * 192, 192), 192)
            bs_s[0, at, :] = rows[:, 0:128]
            bs_s[1, at, :] = jnp.concatenate([rows[:, 128:144], jnp.zeros((192, 112), F32)], axis=1)
        return carry

    lax.fori_loop(0, 6, spread, 0)

    def dense(mine, other):
        mine, other = mine.astype(F32)[0:24], other.astype(F32)[0:24]
        swapped = core == 1
        parts = [jnp.where(swapped, other, mine), jnp.where(swapped, mine, other)]
        return jnp.concatenate(parts, axis=0)

    def chip_rows(o):
        return pl.ds(pl.multiple_of(o * 48, 48), 48)

    def merge_pieces(o, carry):
        for a in range(3):
            cm[o, a] = dense(cs[o, core, a], cx[o, a]).astype(BF16)
        return carry

    arrived(cx, 0)
    lax.fori_loop(0, NCHIP, merge_pieces, 0)
    planes[:, chip_rows(chip)] = cm[chip]
    chips_all(lambda o: to_chip(cm.at[o], planes.at[:, chip_rows(chip)], 1, o).start())
    arrived(w_part, 2)
    both = dense(w_own[...], w_part[...])
    w_send[...] = jnp.where(core == 1, both[:, 384:768], both[:, 0:384]).astype(BF16)
    w_all[core, chip_rows(chip)] = w_send[...]
    chips_all(lambda o: to_chip(w_send, w_all.at[core, chip_rows(chip)], 3, o).start())
    seven = pl.ds(0, 48 * (NCHIP - 1))

    tok_i = lax.broadcasted_iota(I32, (WIN, WIN), 0)
    tok_k = lax.broadcasted_iota(I32, (WIN, WIN), 1)
    half_i, half_k = over_6(tok_i), over_6(tok_k)
    last_band = d == NLAT - 1
    lat_differs = ((tok_i - half_i * 6 >= 3) != (tok_k - half_k * 6 >= 3)) & last_band
    lev_differs = (half_i & 1) != (half_k & 1)
    bx[:, :, HEADS * WIN:WIDE] = jnp.zeros((2, WIN, WIDE - HEADS * WIN), F32)
    for lw in range(2):
        differs = (lat_differs | lev_differs) if lw else lat_differs
        for h in range(HEADS):
            at = pl.ds(h * 2 + lw, WIN, stride=16)
            full = jnp.concatenate([bs_s.at[0][at, :], bs_s.at[1][at, :]], axis=1)[:, 0:WIN]
            spread_bias = jnp.where(differs, MASKED, full).T
            bx[lw, :, h * 128:(h + 1) * 128] = spread_bias[:, 0:128]
            bx[lw, :, 768 + h * 16:784 + h * 16] = spread_bias[:, 128:WIN]

    wq[...] = triple_w[:, 0:192]
    wk[...] = triple_w[:, 192:384]
    wv[...] = triple_w[:, 384:576]

    head_of = lanes(1, C) >> 5
    head_f = [jnp.where(head_of == h, 1.0, 0.0) for h in range(HEADS)]
    head_b = [mask.astype(BF16) for mask in head_f]

    blank = jnp.zeros((WIDE - HEADS * WIN, C), BF16)

    def stacked(values):
        first, rest = values[0:128], values[128:WIN]
        parts = [first * mask for mask in head_b] + [rest * mask for mask in head_b]
        return jnp.concatenate(parts + [blank], axis=0)

    def per_head(left, right):
        turned = left.T
        wide = [dot_nn(turned[64 * i:64 * i + 64], right[:, 256 * i:256 * i + 256]) for i in range(3)]
        tail = dot_nn(turned, right[:, 768:WIDE])
        blocks = []
        for h in range(HEADS):
            at, row = 128 * (h % 2), 32 * (h % 2)
            blocks.append(
                jnp.concatenate(
                    [wide[h // 2][row:row + 32, at:at + 128], tail[32 * h:32 * h + 32, 16 * h:16 * h + 16]], axis=1
                )
            )
        return jnp.concatenate(blocks, axis=0).T

    to_window = one_hot(HALF, orders[2:3, 0:HALF])

    def window_rows(w):
        return pl.ds(pl.multiple_of(w * WIN, WIN), WIN)

    def chunk_rows(i):
        return pl.ds(pl.multiple_of(i * CHUNK, CHUNK), CHUNK)

    def tile_rows(i, t):
        return pl.ds(pl.multiple_of(i * CHUNK + t * TILE, 16), TILE)

    def project(i, carry):
        rows = chunk_rows(i)
        for t in range(CHUNK // TILE):
            part = tile_rows(i, t)
            normed = statistics(x_w[part, :].astype(F32))[0]
            ni_s[part, :] = (normed * attend_gain[...]).astype(BF16)
        normed_in = ni_s[rows, :]
        q_s[rows, :] = dot_nn(normed_in, wq[...]).astype(BF16)
        k_s[rows, :] = dot_nn(normed_in, wk[...]).astype(BF16)
        v_s[rows, :] = dot_nn(normed_in, wv[...]).astype(BF16)
        return carry


    def attend(pair, carry):
        lw = lax.rem(pair, 2)
        for i in range(2):
            rows = window_rows(2 * pair + i)
            raw[i] = dot_nt(k_s[rows, :], stacked(q_s[rows, :]))
        for i in range(2):
            for t in range(WIDE // 128):
                cols = slice(t * 128, (t + 1) * 128)
                scores = raw[i, :, cols] * FACTOR + bx[lw, :, cols]
                exponent = jnp.exp(scores - jnp.max(scores, axis=0, keepdims=True))
                chances = exponent * (1.0 / jnp.sum(exponent, axis=0, keepdims=True))
                p_s[2 * pair + i, :, cols] = chances.astype(BF16)
        for i in range(2):
            rows = window_rows(2 * pair + i)
            att_s[rows, :] = per_head(v_s[rows, :], p_s[2 * pair + i]).astype(BF16)
        return carry

    def forward_windows(b, carry):
        for copy in rows_ahead(b):
            copy.wait()

        unpack(sq, b, (b10, b01, b11))
        x_w[half_rows(b), :] = dot_nn(to_window, sq[b].astype(BF16)).astype(BF16)
        lax.fori_loop(2 * b, 2 * b + 2, project, 0)

        lax.fori_loop(2 * b, 2 * b + 2, attend, 0)

        @pl.when(b == 0)
        def _():
            arrived(planes.at[:, seven], 1)
            to_band(planes.at[pl.ds(0, 2)], ch, 4, d_dn).start()

        return carry

    lax.fori_loop(0, 2, forward_windows, 0)
    arrived(w_all.at[0, seven], 3)
    to_core(w_all.at[core], w_all.at[core], 16).start()

    def feed(i, carry):
        rows = chunk_rows(i)
        tmp[...] = x_w[rows, :].astype(F32) + dot_nn(att_s[rows, :], output_w[...])
        for t in range(CHUNK // TILE):
            part = tile_rows(i, t)
            middle = tmp[t * TILE:(t + 1) * TILE, :]
            mid_s[part, :] = middle
            nm_s[part, :] = (statistics(middle)[0] * feed_gain[...]).astype(BF16)
        hid[...] = dot_nn(nm_s[rows, :], expand_w[...])
        for t in range(CHUNK // 16):
            part = pl.ds(pl.multiple_of(i * CHUNK + t * 16, 16), 16)
            for j in range(FF // 256):
                cols = slice(j * 256, (j + 1) * 256)
                act, slope = gelu_parts(hid[t * 16:(t + 1) * 16, cols])
                act_s[part, cols] = act.astype(BF16)
                slope_s[part, cols] = slope
        vo_s[rows, :] = (tmp[...] + dot_nt(act_s[rows, :], shrink_t[...])).astype(BF16)
        return carry

    lax.fori_loop(0, NCHUNK, feed, 0)

    arrived(w_all.at[0], 16)
    gain_row = merge_gain[...].reshape(1, 4 * C)
    for r in range(6):
        x = (r + 1) % 2
        cell = (0, 1, 1, 2, 2, 3)[r]
        cols = slice(x * 384, (x + 1) * 384)
        if r == 3:
            arrived(ch, 4)
        plane = planes[cell + 1] if cell < 2 else ch[cell - 2]
        summed = dot_tn(plane, w_all[x])
        scaled = summed * gain_row[:, x * 384:(x + 1) * 384]
        qry[2 * r] = scaled[:, 0:192].astype(BF16)
        qry[2 * r + 1] = scaled[:, 192:384].astype(BF16)

    st[...] = jnp.zeros_like(st)
    for i in range(2):
        pick_s[i] = one_hot(WIN, orders[6 + i:7 + i, 0:384])
    stat_lane = lanes(WIN, 128)
    tile_lane = lanes(TILE, 128)

    def merge_sums(w, carry):
        rows = window_rows(w)
        b, lw, lon_win = w // 4, lax.rem(w // 2, 2), lax.rem(w, 2)
        parts = []
        for p in range(2):
            level = lax.rem(lw * 2 + p + 1, 4)
            at = pl.ds(pl.multiple_of((b * 4 + level) * 16, 16), 16)
            parts.append(qry[:, at, :].reshape(192, C))
        qw[rows, :] = dot_nn(pick_s[lon_win], jnp.concatenate(parts, axis=0)).astype(BF16)
        for t in range(WIN // TILE):
            part = pl.ds(pl.multiple_of(w * WIN + t * TILE, 16), TILE)
            at = slice(t * TILE, (t + 1) * TILE)
            q = qw[part, :].astype(F32)
            v = vo_s[part, :].astype(F32)
            mean = jnp.mean(v, axis=-1, keepdims=True)
            centred = v - mean
            squares = jnp.sum(centred * centred, axis=-1, keepdims=True)
            q_sum = jnp.sum(q, axis=-1, keepdims=True)
            qv_sum = jnp.sum(q * centred, axis=-1, keepdims=True)
            total = st[b, at, :]
            for j, value in enumerate((mean, squares, q_sum, qv_sum)):
                total = jnp.where(tile_lane == 32 * j + w, value, total)
            st[b, at, :] = total
        return carry

    def sums_copies(b):
        return (
            remote(tup.at[b], sup.at[b], st_ss.at[2 * b], st_rs.at[2 * b], (e, d_up)),
            remote(tdn.at[b], sdn.at[b], st_ss.at[2 * b + 1], st_rs.at[2 * b + 1], (e, d_dn)),
        )

    def exchange(b):
        tup[b] = st.at[b][pl.ds(5, 24, stride=6), :]
        tdn[b] = st.at[b][pl.ds(0, 24, stride=6), :]
        for copy in sums_copies(b):
            copy.start()

    even = (over_12(lax.broadcasted_iota(I32, (WIN, 128), 0)) & 1) == 0

    def pair_of(values):
        return jnp.where(even, pltpu.roll(values, WIN - 12, 0), pltpu.roll(values, 12, 0))

    def cell_norm(b):
        for r, other in ((1, 2), (2, 1), (3, 4), (4, 3)):
            sx[pl.ds(r, 24, stride=6), :] = st.at[b][pl.ds(other, 24, stride=6), :]
        for copy in sums_copies(b):
            copy.wait()
        sx[pl.ds(0, 24, stride=6), :] = sup[b]
        sx[pl.ds(5, 24, stride=6), :] = sdn[b]
        own, cross = st[b], sx[...]
        group = [own, cross, pair_of(own), pair_of(cross)]
        cell_mean = (group[0] + group[1] + group[2] + group[3]) * 0.25
        variance = jnp.zeros((WIN, 128), F32)
        q_total = jnp.zeros((WIN, 128), F32)
        qv_total = jnp.zeros((WIN, 128), F32)
        for values in group:
            offset = values - cell_mean
            q_sum = pltpu.roll(values, 64, 1)
            variance = variance + pltpu.roll(values, 96, 1) + 192.0 * offset * offset
            q_total = q_total + q_sum
            qv_total = qv_total + pltpu.roll(values, 32, 1) + offset * q_sum
        cell_inverse = lax.rsqrt(jnp.where(stat_lane < 8, variance, 0.0) * (1.0 / 768.0) + EPS)
        cp_s[0] = cell_mean
        cp_s[1] = cell_inverse
        cp_s[2] = q_total * (1.0 / 768.0)
        cp_s[3] = cell_inverse * cell_inverse * qv_total * (1.0 / 768.0)

    def merge_back(w, carry):
        for t in range(WIN // TILE):
            part = pl.ds(pl.multiple_of(w * WIN + t * TILE, 16), TILE)
            at = slice(t * TILE, (t + 1) * TILE)
            mean, inverse, q_mean, projected = [
                jnp.sum(jnp.where(tile_lane == w, cp_s[j, at, :], 0.0), axis=-1, keepdims=True) for j in range(4)
            ]
            v = vo_s[part, :].astype(F32) - mean
            go_s[part, :] = (inverse * (qw[part, :].astype(F32) - q_mean - v * projected)).astype(BF16)
        return carry

    def feed_back(i, carry):
        rows = chunk_rows(i)
        go = go_s[rows, :]
        gh = (dot_nn(go, shrink_t[...]) * slope_s[rows, :]).astype(BF16)
        gh_s[rows, :] = gh
        tmp[...] = dot_nt(gh, expand_w[...])
        for t in range(CHUNK // TILE):
            part = tile_rows(i, t)
            gnm = tmp[t * TILE:(t + 1) * TILE, :]
            unit, inverse = statistics(mid_s[part, :])
            gm = go_s[part, :].astype(F32) + norm_back(unit, inverse, gnm * feed_gain[...])
            gm_s[part, :] = gm
            gmh_s[part, :] = gm.astype(BF16)
        ga_s[rows, :] = dot_nt(gmh_s[rows, :], output_w[...]).astype(BF16)
        return carry

    def forward_sample(b, carry):
        lax.fori_loop(4 * b, 4 * b + 4, merge_sums, 0)
        exchange(b)
        return carry

    def backward_sample(b, carry):
        cell_norm(b)
        lax.fori_loop(4 * b, 4 * b + 4, merge_back, 0)
        lax.fori_loop(2 * b, 2 * b + 2, feed_back, 0)
        return carry

    lax.fori_loop(0, 2, forward_sample, 0)
    ds_s[...] = jnp.zeros_like(ds_s)
    dt_s[...] = jnp.zeros_like(dt_s)
    from_window = one_hot(HALF, orders[3:4, 0:HALF])
    lax.fori_loop(0, 2, backward_sample, 0)

    g_expand = dot_tn(nm_s[...], gh_s[...]).astype(BF16)
    g_shrink = dot_tn(go_s[...], act_s[...]).astype(BF16)
    g_output = dot_tn(att_s[...], gmh_s[...]).astype(BF16)
    for i in range(4):
        for j in range(2):
            g1s[0, 2 * i + j, 0:48] = g_expand[i * 48:(i + 1) * 48, j * 384:(j + 1) * 384]
            g1s[1, 2 * i + j, 0:48] = g_shrink[i * 48:(i + 1) * 48, j * 384:(j + 1) * 384]
    wide = jnp.concatenate([g_output[0:96], g_output[96:192]], axis=1)
    for i in range(NCHIP):
        for j in range(2):
            at = (i * 2 + j) * 16
            g1s[j, i, 48:64] = wide[at:at + 16] if at < 96 else jnp.zeros((16, 384), BF16)

    def sum_of(ref, count, rows):
        total = ref[0, rows].astype(F32)
        for o in range(1, count):
            total = total + ref[o, rows].astype(F32)
        return total.astype(BF16)

    def add_pair(mine, other, out):
        def body(o, carry):
            out[o] = (mine[core, o].astype(F32) + other[o].astype(F32)).astype(BF16)
            return carry

        lax.fori_loop(0, NCHIP, body, 0)

    others = pl.ds(0, NCHIP - 1)
    to_core(g1s.at[1 - core], g1p, 5).start()


    def attend_back(pair, carry):
        lw = lax.rem(pair, 2)
        for i in range(2):
            rows = window_rows(2 * pair + i)
            dam[i] = stacked(ga_s[rows, :])
            raw[i] = dot_nt(v_s[rows, :], dam[i])
        for i in range(2):
            for t in range(WIDE // 128):
                cols = slice(t * 128, (t + 1) * 128)
                chances = p_s[2 * pair + i, :, cols].astype(F32)
                weighted = raw[i, :, cols]
                centre = jnp.sum(chances * weighted, axis=0, keepdims=True)
                dsh[i, :, cols] = (chances * (weighted - centre)).astype(BF16)
        for i in range(2):
            rows = window_rows(2 * pair + i)
            dt_s[rows, 512:704] = dot_nn(p_s[2 * pair + i], dam[i]).astype(BF16)
            dt_s[rows, 0:C] = (per_head(k_s[rows, :], dsh[i]) * FACTOR).astype(BF16)
            dt_s[rows, 256:448] = (dot_nn(dsh[i], stacked(q_s[rows, :])) * FACTOR).astype(BF16)
        ds_s[lw] = ds_s[lw] + (dsh[0].astype(F32) + dsh[1].astype(F32))
        return carry

    all_rows = slice(0, 64)
    def windows_back(pair, carry):
        attend_back(pair, carry)

        @pl.when(pair == 0)
        def _():
            arrived(g1p, 5)
            add_pair(g1s, g1p, g1h)
            g1r[chip] = g1h[chip]
            chips_all(lambda o: to_chip(g1h.at[o], g1r.at[chip], 6, o).start())

        @pl.when(pair == 2)
        def _():
            arrived(g1l.at[pl.ds(0, 3)], 7)
            g1l[4] = sum_of(g1l, 4, all_rows)
            to_band(g1l.at[4], g1l.at[5], 15, d_pair).start()

        return carry

    def second_gradients():
        summed = dot_tn(ni_s[...], dt_s[...])
        sections = [summed[:, 0:C], summed[:, 256:448], summed[:, 512:704], jnp.zeros((C, 64), F32)]
        g_triple = jnp.concatenate(sections, axis=1).astype(BF16)
        for i in range(3):
            for j in range(5):
                at = 5 * i + j
                g2s[at // 8, at % 8, 0:64] = g_triple[i * 64:(i + 1) * 64, j * 128:(j + 1) * 128]
        g2s[1, 7, 0:64] = jnp.zeros((64, 128), BF16)
        arrived(g1l.at[5], 15)
        g1f[chip] = (g1l[4].astype(F32) + g1l[5].astype(F32)).astype(BF16)
        chips_all(lambda o: to_chip(g1f.at[chip], g1f.at[chip], 8, o).start())
        for lw in range(2):
            for h in range(HEADS):
                at = pl.ds(h * 2 + lw, WIN, stride=16)
                part = jnp.concatenate(
                [ds_s[lw, :, h * 128:(h + 1) * 128], ds_s[lw, :, 768 + h * 16:784 + h * 16]], axis=1
            ).T
                bs_s.at[0][at, :] = part[:, 0:128]
                bs_s.at[1][at, :] = jnp.concatenate([part[:, 128:144], jnp.zeros((WIN, 112), F32)], axis=1)

        def fold(s_i):
            at = slice(s_i * 192, (s_i + 1) * 192)
            rows = jnp.concatenate([bs_s[0, at, :], bs_s[1, at, :]], axis=1)[:, 0:WIN].astype(BF16)
            return dot_nt(rows, spread_s[s_i])

        folded = fold(0)
        for s_i in range(1, 12):
            folded = folded + fold(s_i)
        pieces_t = []
        for p in range(2):
            for pk in range(2):
                for r in range(6):
                    at = (p * 6 + r) * 16
                    pieces_t.append(folded[at:at + 16, pk * 256:pk * 256 + 138])
        table = jnp.concatenate(pieces_t + [jnp.zeros((16, 4096 - POS), F32)], axis=1).astype(BF16)
        for o in range(32):
            g2s[o // 16, (o // 2) % 8, 64 + 16 * (o % 2):80 + 16 * (o % 2)] = table[:, o * 128:(o + 1) * 128]
        to_core(g2s.at[1 - core], g2p, 9).start()

    def project_back(i, carry):
        rows = chunk_rows(i)
        tmp[...] = (
            dot_nt(dt_s[rows, 0:C], wq[...])
            + dot_nt(dt_s[rows, 256:448], wk[...])
            + dot_nt(dt_s[rows, 512:704], wv[...])
        )
        for t in range(CHUNK // TILE):
            part = tile_rows(i, t)
            unit, inverse = statistics(x_w[part, :].astype(F32))
            back = norm_back(unit, inverse, tmp[t * TILE:(t + 1) * TILE, :] * attend_gain[...])
            gt_s[part, :] = (gm_s[part, :] + back).astype(BF16)
        return carry

    def backward_windows(b, carry):
        lax.fori_loop(2 * b, 2 * b + 2, windows_back, 0)

        @pl.when(b == 1)
        def _():
            second_gradients()

        lax.fori_loop(2 * b, 2 * b + 2, project_back, 0)

        @pl.when(b == 1)
        def _():
            arrived(g2p, 9)
            add_pair(g2s, g2p, g2h)
            g2r[chip] = g2h[chip]
            chips_all(lambda o: to_chip(g2h.at[o], g2r.at[chip], 10, o).start())

        quads = dot_nn(from_window, gt_s[half_rows(b), :])
        gq[b] = quads
        pack(quads, b, (c10, c01, c11))
        for copy in rows_behind(b):
            copy.start()

        @pl.when(b == 0)
        def _():
            arrived(g1r.at[others], 6)
            g1l[d // 2] = sum_of(g1r, NCHIP, all_rows)
            for step in range(1, 4):
                to_band(g1l.at[d // 2], g1l.at[d // 2], 7, lax.rem(d + 2 * step, NLAT)).start()

        return carry

    lax.fori_loop(0, 2, backward_windows, 0)

    arrived(g1f.at[others], 8)
    to_core(g1f, g1o, 11).start()

    arrived(g2r.at[others], 10)
    g2l[d] = sum_of(g2r, NCHIP, slice(0, 64))
    lat_all(lambda o: to_band(g2l.at[d], g2l.at[d], 12, o).start())
    g2f[chip, 64:96] = sum_of(g2r, NCHIP, slice(64, 96))

    to_natural = one_hot(HALF, orders[1:2, 0:HALF])

    def unsort_sample(b, carry):
        for copy in rows_behind(b):
            copy.wait()
        unpack(gq, b, (d10, d01, d11))
        out_fields[half_rows(b), :] = dot_nn(to_natural, gq[b].astype(BF16)).astype(BF16)
        return carry

    lax.fori_loop(0, 1, unsort_sample, 0)
    arrived(g2l.at[others], 12)
    g2f[chip, 0:64] = sum_of(g2l, NLAT, slice(0, 64))
    chips_all(lambda o: to_chip(g2f.at[chip], g2f.at[chip], 13, o).start())


    lax.fori_loop(1, 2, unsort_sample, 0)
    arrived(g1o, 11)
    out_g1[core] = g1f[...]
    out_g1[1 - core] = g1o[...]
    arrived(g2f.at[others], 13)
    to_core(g2f, g2o, 14).start()
    out_g2[core] = g2f[...]
    arrived(g2o, 14)
    out_g2[1 - core] = g2o[...]

    left(cx, 0)
    left(cm.at[others], 1)
    left(w_part, 2)
    left(w_all.at[0, seven], 3)
    left(w_all.at[0], 16)
    left(ch, 4)
    left(g1p, 5)
    left(g1r.at[others], 6)
    left(g1l.at[pl.ds(0, 3)], 7)
    left(g1l.at[4], 15)
    left(g1f.at[others], 8)
    left(g2p, 9)
    left(g2r.at[others], 10)
    left(g1o, 11)
    left(g2l.at[others], 12)
    left(g2f.at[others], 13)
    left(g2o, 14)


def results_kernel(
    fields, g1, g2, attend_gain, triple_w, feed_gain, expand_w,
    out_fields, out_triple, out_output, out_expand, out_shrink, out_attend, out_feed, out_table,
):
    out_fields[...] = fields[...]
    for i in range(4):
        for j in range(2):
            rows, cols = slice(i * 48, (i + 1) * 48), slice(j * 384, (j + 1) * 384)
            out_expand[rows, cols] = g1[0, 2 * i + j, 0:48].astype(F32)
            out_shrink[rows, cols] = g1[1, 2 * i + j, 0:48].astype(F32)
    for i in range(6):
        wide = g1[i % 2, i // 2, 48:64].astype(F32)
        out_output[i * 16:(i + 1) * 16, :] = wide[:, 0:C]
        out_output[96 + i * 16:96 + (i + 1) * 16, :] = wide[:, C:2 * C]
    for i in range(3):
        for j in range(5):
            at, size = 5 * i + j, 128 if j < 4 else 64
            part = g2[at // 8, at % 8, 0:64].astype(F32)
            out_triple[i * 64:(i + 1) * 64, j * 128:j * 128 + size] = part[:, 0:size]
    table = jnp.concatenate(
        [g2[o // 16, (o // 2) % 8, 64 + 16 * (o % 2):80 + 16 * (o % 2)] for o in range(32)], axis=1
    ).astype(F32)
    for h in range(HEADS):
        out_table[h] = table[2 * h:2 * h + 2, 0:POS]

    def gain_gradient(grad, weight, gain):
        product = (grad[...] * weight[...].astype(F32)).astype(BF16)
        total = dot_nt(jnp.ones((16, product.shape[1]), BF16), product)
        return total[0:1] / gain[...]

    out_attend[...] = gain_gradient(out_triple, triple_w, attend_gain)
    out_feed[...] = gain_gradient(out_expand, expand_w, feed_gain)


def scratch():
    def vmem(*shape, kind=BF16):
        return pltpu.VMEM(shape, kind)

    token = vmem(TOK, C)
    token_f = vmem(TOK, C, kind=F32)
    weight = vmem(C, C)
    quad = vmem(2, HALF, C, kind=F32)
    halves = [vmem(2, 336, 128), vmem(2, 112, 128), vmem(2, 112, 128)]
    stat = vmem(WIN, 128, kind=F32)
    small = vmem(2, 24, 128, kind=F32)
    buffers = [
        quad, quad, *halves, *halves, *halves, *halves, token, token, token, token, token, weight, weight, weight,
        vmem(NWIN, WIN, WIDE), token, token_f, token, vmem(TOK, FF), vmem(TOK, FF, kind=F32), token,
        vmem(16, POS, kind=F32), vmem(384, 512), vmem(2, 2304, 128, kind=F32),
        vmem(2, WIN, WIDE, kind=F32), vmem(2, WIN, WIDE, kind=F32),
        vmem(12, 512, WIN), vmem(2, WIN, 384),
        vmem(576, 256, kind=F32), vmem(8, 2, 3, 32, 128), vmem(8, 3, 32, 128),
        vmem(8, 3, 48, 128), vmem(2, 384, 128), vmem(3, 384, 128),
        vmem(32, 768), vmem(32, 768), vmem(48, 384), vmem(2, 384, 384),
        vmem(12, 128, C), token, vmem(2, WIN, 128, kind=F32), stat, small, small, small, small, vmem(4, WIN, 128, kind=F32),
        token, vmem(TOK, FF), token_f, token, token, vmem(TOK, 768), token,
        vmem(2, WIN, WIDE, kind=F32), vmem(2, WIN, WIDE), vmem(2, WIDE, C), vmem(CHUNK, FF, kind=F32),
        vmem(CHUNK, C, kind=F32),
    ]
    for rows, cols in ((64, 384), (96, 128)):
        chunks = vmem(8, rows, cols)
        buffers += [vmem(2, 8, rows, cols), chunks, chunks, chunks, vmem(8, 64, cols), chunks, chunks]
    counts = [6, 6, 6, 6, 4, 4, 17, 17]
    return buffers + [pltpu.SemaphoreType.DMA((n,)) for n in counts]


def per_device(
    fields, merge_cotangent, attend_gain, triple_weight, bias_table, output_weight, feed_gain,
    expand_weight, shrink_weight, merge_gain, merge_weight,
):
    cot = jnp.transpose(merge_cotangent, (1, 2, 3, 4, 0)).reshape(576, 192)
    bias = jnp.transpose(bias_table[0], (1, 0, 2))
    def shaped(shapes):
        return [jax.ShapeDtypeStruct(shape, kind) for shape, kind in shapes]

    vmem_spec = pl.BlockSpec(memory_space=pltpu.VMEM)
    parts = pl.pallas_call(
        kernel,
        out_shape=shaped(
            [((TOK, C), BF16), ((2, 8, 64, 384), BF16), ((2, 8, 96, 128), BF16)]
        ),
        in_specs=[vmem_spec] * 12,
        out_specs=[vmem_spec] * 3,
        scratch_shapes=scratch(),
        compiler_params=pltpu.CompilerParams(
            collective_id=0, has_side_effects=True, vmem_limit_bytes=60 * 1024 * 1024
        ),
    )(
        fields.reshape(TOK, C), cot, attend_gain.reshape(1, C), triple_weight, bias, output_weight,
        feed_gain.reshape(1, C), expand_weight, shrink_weight.T, merge_gain,
        merge_weight.T, jnp.asarray(order_indices()),
    )
    g_fields, g_triple, g_output, g_expand, g_shrink, g_attend, g_feed, g_table = pl.pallas_call(
        results_kernel,
        out_shape=shaped(
            [
                ((TOK, C), BF16), ((C, 3 * C), F32), ((C, C), F32), ((C, FF), F32), ((C, FF), F32),
                ((1, C), F32), ((1, C), F32), ((HEADS, 2, POS), F32),
            ]
        ),
        in_specs=[vmem_spec] * 7,
        out_specs=[vmem_spec] * 8,
        compiler_params=pltpu.CompilerParams(vmem_limit_bytes=60 * 1024 * 1024),
    )(*parts, attend_gain.reshape(1, C), triple_weight, feed_gain.reshape(1, C), expand_weight)
    return (
        g_fields.reshape(fields.shape), g_triple, g_output, g_expand, g_shrink.T,
        g_attend.reshape(C), g_feed.reshape(C), jnp.transpose(g_table, (1, 0, 2))[None],
    )


def solution(mesh):
    placed = (
        P(None, None, "lat", "lon", None),
        P(None, None, None, "lat", "lon"),
        P(),
        P(),
        P("lat", None, None, None),
        P(),
        P(),
        P(),
        P(),
        P(),
        P(None, "lon"),
    )
    return jax.shard_map(
        per_device,
        mesh=mesh,
        in_specs=placed,
        out_specs=(
            P(None, None, "lat", "lon", None),
            P(),
            P(),
            P(),
            P(),
            P(),
            P(),
            P("lat", None, None, None),
        ),
        check_vma=False,
    )
```

```python
import functools
import math

import jax
import jax.numpy as jnp
import numpy as np
from jax import lax
from jax.experimental import pallas as pl
from jax.experimental.pallas import tpu as pltpu
from jax.sharding import PartitionSpec as P

F32 = jnp.float32
BF16 = jnp.bfloat16
I32 = jnp.int32
MESH = pl.DeviceIdType.MESH

EPS = 1e-05
MASKED = -1000000000.0
NLON = 16
NLAT = 8
NCHIP = 8
C = 192
HEADS = 6
FF = 768
WIN = 144
NWIN = 8
TOK = WIN * NWIN
HALF = TOK // 2
SIZES = ((216, 112), (72, 40), (72, 40))
POS = 3312
CHUNK = 576
NCHUNK = TOK // CHUNK
TILE = 48
WIDE = 896
FACTOR = 32 ** -0.5


def order_indices():
    natural_to_quad = np.full(640, -1, np.int32)
    quad_to_natural = np.full(640, -1, np.int32)
    quad_to_window = np.full(640, -1, np.int32)
    window_to_quad = np.full(640, -1, np.int32)
    for level in range(4):
        for row in range(6):
            for col in range(24):
                source = (level * 6 + row) * 24 + col
                if col >= 6:
                    place = (0 if row >= 3 else 216) + level * 54 + (row % 3) * 18 + col - 6
                else:
                    place = (432 if row >= 3 else 504) + level * 18 + (row % 3) * 6 + col
                natural_to_quad[source] = place
                quad_to_natural[place] = source
    index = 0
    for lev_win in range(2):
        for lon_win in range(2):
            for s in range(12):
                for p in range(2):
                    for r in range(6):
                        level = (lev_win * 2 + p + 1) % 4
                        col = lon_win * 12 + s
                        if col < 18:
                            place = (0 if r < 3 else 216) + level * 54 + (r % 3) * 18 + col
                        else:
                            place = (432 if r < 3 else 504) + level * 18 + (r % 3) * 6 + col - 18
                        window_to_quad[index] = place
                        quad_to_window[place] = index
                        index += 1
    cell_lane = np.full(640, -1, np.int32)
    bias_row = np.full(640, -1, np.int32)
    merged_token = np.full((2, 640), -1, np.int32)
    for lane in range(256):
        if lane % 16 < 12:
            cell_lane[lane] = (12 * (lane // 16) + 3 + lane % 16) % 192
    for k in range(WIN):
        s, p, r = k // 12, (k // 6) % 2, k % 6
        bias_row[k] = p * 256 + r * 23 + 11 - s
    for lon_win in range(2):
        for row in range(384):
            p, r, y, m = row // 192, (row // 32) % 6, (row // 16) % 2, row % 16
            if 0 <= m - lon_win * 6 < 6:
                merged_token[lon_win, row] = (2 * (m - lon_win * 6) + y) * 12 + p * 6 + r
    rows = [natural_to_quad, quad_to_natural, quad_to_window, window_to_quad]
    return np.stack(rows + [cell_lane, bias_row, merged_token[0], merged_token[1]])


def dot_nn(a, b):
    return lax.dot_general(a, b, (((1,), (0,)), ((), ())), preferred_element_type=F32)


def dot_nt(a, b):
    return lax.dot_general(a, b, (((1,), (1,)), ((), ())), preferred_element_type=F32)


def dot_tn(a, b):
    return lax.dot_general(a, b, (((0,), (0,)), ((), ())), preferred_element_type=F32)


def one_hot(rows, targets):
    ids = lax.broadcasted_iota(I32, (rows, targets.shape[1]), 0)
    return jnp.where(ids == targets, 1.0, 0.0).astype(BF16)


def statistics(values):
    centred = values - jnp.mean(values, axis=-1, keepdims=True)
    inverse = lax.rsqrt(jnp.mean(centred * centred, axis=-1, keepdims=True) + EPS)
    return centred * inverse, inverse


def norm_back(normed, inverse, scaled):
    centre = jnp.mean(scaled, axis=-1, keepdims=True)
    projected = jnp.mean(scaled * normed, axis=-1, keepdims=True)
    return inverse * (scaled - centre - normed * projected)


def gelu_parts(values):
    cumulative = 0.5 * (1.0 + lax.erf(values * (1.0 / math.sqrt(2.0))))
    density = jnp.exp(-0.5 * values * values) * (1.0 / math.sqrt(2.0 * math.pi))
    return values * cumulative, cumulative + values * density


def lanes(rows, cols):
    return lax.broadcasted_iota(I32, (rows, cols), 1)


def over_12(ids):
    return (ids * 5462) >> 16


def over_6(ids):
    return (ids * 10923) >> 16


def kernel(
    fields, cot, attend_gain, triple_w, bias, output_w, feed_gain, expand_w, shrink_t, merge_gain,
    merge_wt, orders,
    out_fields, out_g1, out_g2,
    sq, gq, a10, a01, a11, b10, b01, b11, c10, c01, c11, d10, d01, d11, x_w, ni_s, q_s, k_s, v_s, wq, wk, wv, p_s, att_s, mid_s, nm_s, act_s, slope_s, vo_s,
    b16, bl_s, bs_s, bx, ds_s, spread_s, pick_s,
    cells, cs, cx, cm, ch, planes, w_own, w_part, w_send, w_all, qry, qw, st, sx, sup, sdn, tup, tdn, cp_s, go_s, gh_s, gm_s, ga_s, gmh_s,
    dt_s, gt_s, raw, dsh, dam, hid, tmp, g1s, g1p, g1h, g1r, g1l, g1f, g1o, g2s, g2p, g2h, g2r, g2l, g2f, g2o,
    halo_ss, halo_rs, back_ss, back_rs, st_ss, st_rs, sends, recvs,
):
    e = lax.axis_index("lon")
    d = lax.axis_index("lat")
    e_up, e_dn = lax.rem(e + 1, NLON), lax.rem(e + NLON - 1, NLON)
    d_up, d_dn = lax.rem(d + 1, NLAT), lax.rem(d + NLAT - 1, NLAT)

    def remote(src, dst, ssem, rsem, device):
        return pltpu.make_async_remote_copy(
            src_ref=src, dst_ref=dst, send_sem=ssem, recv_sem=rsem, device_id=device,
            device_id_type=MESH,
        )

    core, chip = lax.rem(e, 2), e // 2
    partner = e + 1 - 2 * core
    d_pair = d + 1 - 2 * lax.rem(d, 2)

    def chips_all(action):
        def body(step, carry):
            action(lax.rem(chip + step, NCHIP))
            return carry

        lax.fori_loop(1, NCHIP, body, 0)

    def lat_all(action):
        def body(step, carry):
            action(lax.rem(d + step, NLAT))
            return carry

        lax.fori_loop(1, NLAT, body, 0)

    def to_chip(src, dst, phase, o):
        return remote(src, dst, sends.at[phase], recvs.at[phase], (2 * o + core, d))

    def to_band(src, dst, phase, o):
        return remote(src, dst, sends.at[phase], recvs.at[phase], (e, o))

    def to_core(src, dst, phase):
        return remote(src, dst, sends.at[phase], recvs.at[phase], (partner, d))

    def arrived(region, phase):
        remote(region, region, sends.at[phase], recvs.at[phase], (partner, d)).wait_recv()

    def left(region, phase):
        remote(region, region, sends.at[phase], recvs.at[phase], (partner, d)).wait_send()

    barrier = pltpu.get_barrier_semaphore()

    def greet(device):
        pl.semaphore_signal(barrier, inc=1, device_id=device, device_id_type=MESH)

    chips_all(lambda o: greet((2 * o + core, d)))
    lat_all(lambda o: greet((e, o)))
    for device in ((e_up, d), (e_dn, d), (e_up, d_up), (e_dn, d_dn)):
        greet(device)

    def half_rows(b):
        return pl.ds(pl.multiple_of(b * HALF, HALF), HALF)

    def pack(quads, b, out):
        at = 216
        for (size, cut), message in zip(SIZES, out):
            rows = quads[at:at + size]
            rest = jnp.concatenate([rows[cut:, 128:C], jnp.zeros((2 * cut - size, 64), F32)], axis=0)
            parts = [rows[:, 0:128], jnp.concatenate([rows[:cut, 128:C], rest], axis=1)]
            if (size + cut) % 16:
                parts.append(jnp.zeros((8, 128), F32))
            message[b] = jnp.concatenate(parts, axis=0).astype(BF16)
            at += size

    def unpack(quads, b, messages):
        at = 216
        for (size, cut), message in zip(SIZES, messages):
            rows = message[b].astype(F32)
            tails = rows[size:size + cut]
            tail = jnp.concatenate([tails[:, 0:64], tails[0:size - cut, 64:128]], axis=0)
            quads[b, at:at + size, :] = jnp.concatenate([rows[0:size], tail], axis=1)
            at += size

    def halo(sources, targets, ssem, rsem, step, b):
        devices = ((e, step[1]), (step[0], d), (step[0], step[1]))
        return [
            remote(src.at[b], dst.at[b], ssem.at[3 * b + i], rsem.at[3 * b + i], dev)
            for i, (src, dst, dev) in enumerate(zip(sources, targets, devices))
        ]

    def rows_ahead(b):
        return halo((a10, a01, a11), (b10, b01, b11), halo_ss, halo_rs, (e_dn, d_dn), b)

    def rows_behind(b):
        return halo((c10, c01, c11), (d10, d01, d11), back_ss, back_rs, (e_up, d_up), b)

    to_quad = one_hot(HALF, orders[0:1, 0:HALF])

    def sort_sample(b, carry):
        quads = dot_nn(to_quad, fields[half_rows(b), :])
        sq[b] = quads
        pack(quads, b, (a10, a01, a11))
        return carry

    lax.fori_loop(0, 2, sort_sample, 0)
    pl.semaphore_wait(barrier, NCHIP - 1 + NLAT - 1 + 4)
    for b in range(2):
        for copy in rows_ahead(b):
            copy.start()

    cells[...] = dot_nn(cot[...], one_hot(192, orders[4:5, 0:256]))
    block_of = lanes(72, 128) >> 4

    def gather_cells(inner, carry):
        for tile in range(2):
            piece = jnp.zeros((72, 128), F32)
            for bl in range(8):
                part = cells[bl * 72:(bl + 1) * 72, tile * 128:(tile + 1) * 128]
                part = pltpu.roll(part, lax.rem(16 * (bl - inner) + 128, 128), 1)
                piece = jnp.where(block_of == bl, part, piece)
            for a in range(3):
                padded = jnp.concatenate([piece[a * 24:(a + 1) * 24], jnp.zeros((8, 128), F32)], axis=0)
                cs[4 * tile + inner // 2, lax.rem(inner, 2), a] = padded.astype(BF16)
        return carry

    lax.fori_loop(0, 8, gather_cells, 0)
    w_own[...] = jnp.concatenate(
        [merge_wt[...].astype(F32), jnp.zeros((8, 768), F32)], axis=0
    ).astype(BF16)
    to_core(cs.at[:, 1 - core], cx, 0).start()
    to_core(w_own, w_part, 2).start()

    for h in range(HEADS):
        b16[2 * h:2 * h + 2, :] = bias[h]
    b16[12:16, :] = jnp.zeros((4, POS), F32)
    zero_tail = jnp.zeros((16, 256 - 138), F32)
    for p in range(2):
        for r in range(6):
            parts = []
            for pk in range(2):
                at = (p * 2 + pk) * 828 + r * 138
                parts += [b16[:, at:at + 138], zero_tail]
            row = jnp.concatenate(parts, axis=1)
            high = row.astype(BF16)
            low = (row - high.astype(F32)).astype(BF16)
            at = (p * 6 + r) * 16
            bl_s[at:at + 16, :] = high
            bl_s[192 + at:192 + at + 16, :] = low

    bias_row = orders[5:6, 0:WIN]

    def spread(pair, carry):
        for i in range(2):
            s_i = 2 * pair + i
            matrix = one_hot(512, bias_row + s_i)
            spread_s[s_i] = matrix
            split = dot_nn(bl_s[...], matrix)
            rows = split[0:192] + split[192:384]
            at = pl.ds(pl.multiple_of(s_i * 192, 192), 192)
            bs_s[0, at, :] = rows[:, 0:128]
            bs_s[1, at, :] = jnp.concatenate([rows[:, 128:144], jnp.zeros((192, 112), F32)], axis=1)
        return carry

    lax.fori_loop(0, 6, spread, 0)

    def dense(mine, other):
        mine, other = mine.astype(F32)[0:24], other.astype(F32)[0:24]
        swapped = core == 1
        parts = [jnp.where(swapped, other, mine), jnp.where(swapped, mine, other)]
        return jnp.concatenate(parts, axis=0)

    def chip_rows(o):
        return pl.ds(pl.multiple_of(o * 48, 48), 48)

    def merge_pieces(o, carry):
        for a in range(3):
            cm[o, a] = dense(cs[o, core, a], cx[o, a]).astype(BF16)
        return carry

    arrived(cx, 0)
    lax.fori_loop(0, NCHIP, merge_pieces, 0)
    planes[:, chip_rows(chip)] = cm[chip]
    chips_all(lambda o: to_chip(cm.at[o], planes.at[:, chip_rows(chip)], 1, o).start())
    arrived(w_part, 2)
    both = dense(w_own[...], w_part[...])
    w_send[...] = jnp.where(core == 1, both[:, 384:768], both[:, 0:384]).astype(BF16)
    w_all[core, chip_rows(chip)] = w_send[...]
    chips_all(lambda o: to_chip(w_send, w_all.at[core, chip_rows(chip)], 3, o).start())
    seven = pl.ds(0, 48 * (NCHIP - 1))

    tok_i = lax.broadcasted_iota(I32, (WIN, WIN), 0)
    tok_k = lax.broadcasted_iota(I32, (WIN, WIN), 1)
    half_i, half_k = over_6(tok_i), over_6(tok_k)
    last_band = d == NLAT - 1
    lat_differs = ((tok_i - half_i * 6 >= 3) != (tok_k - half_k * 6 >= 3)) & last_band
    lev_differs = (half_i & 1) != (half_k & 1)
    bx[:, :, HEADS * WIN:WIDE] = jnp.zeros((2, WIN, WIDE - HEADS * WIN), F32)
    for lw in range(2):
        differs = (lat_differs | lev_differs) if lw else lat_differs
        for h in range(HEADS):
            at = pl.ds(h * 2 + lw, WIN, stride=16)
            full = jnp.concatenate([bs_s.at[0][at, :], bs_s.at[1][at, :]], axis=1)[:, 0:WIN]
            spread_bias = jnp.where(differs, MASKED, full).T
            bx[lw, :, h * 128:(h + 1) * 128] = spread_bias[:, 0:128]
            bx[lw, :, 768 + h * 16:784 + h * 16] = spread_bias[:, 128:WIN]

    wq[...] = triple_w[:, 0:192]
    wk[...] = triple_w[:, 192:384]
    wv[...] = triple_w[:, 384:576]

    head_of = lanes(1, C) >> 5
    head_f = [jnp.where(head_of == h, 1.0, 0.0) for h in range(HEADS)]
    head_b = [mask.astype(BF16) for mask in head_f]

    blank = jnp.zeros((WIDE - HEADS * WIN, C), BF16)

    def stacked(values):
        first, rest = values[0:128], values[128:WIN]
        parts = [first * mask for mask in head_b] + [rest * mask for mask in head_b]
        return jnp.concatenate(parts + [blank], axis=0)

    def per_head(left, right):
        turned = left.T
        wide = [dot_nn(turned[64 * i:64 * i + 64], right[:, 256 * i:256 * i + 256]) for i in range(3)]
        tail = dot_nn(turned, right[:, 768:WIDE])
        blocks = []
        for h in range(HEADS):
            at, row = 128 * (h % 2), 32 * (h % 2)
            blocks.append(
                jnp.concatenate(
                    [wide[h // 2][row:row + 32, at:at + 128], tail[32 * h:32 * h + 32, 16 * h:16 * h + 16]], axis=1
                )
            )
        return jnp.concatenate(blocks, axis=0).T

    to_window = one_hot(HALF, orders[2:3, 0:HALF])

    def window_rows(w):
        return pl.ds(pl.multiple_of(w * WIN, WIN), WIN)

    def chunk_rows(i):
        return pl.ds(pl.multiple_of(i * CHUNK, CHUNK), CHUNK)

    def tile_rows(i, t):
        return pl.ds(pl.multiple_of(i * CHUNK + t * TILE, 16), TILE)

    def project(i, carry):
        rows = chunk_rows(i)
        for t in range(CHUNK // TILE):
            part = tile_rows(i, t)
            normed = statistics(x_w[part, :].astype(F32))[0]
            ni_s[part, :] = (normed * attend_gain[...]).astype(BF16)
        normed_in = ni_s[rows, :]
        q_s[rows, :] = dot_nn(normed_in, wq[...]).astype(BF16)
        k_s[rows, :] = dot_nn(normed_in, wk[...]).astype(BF16)
        v_s[rows, :] = dot_nn(normed_in, wv[...]).astype(BF16)
        return carry


    def attend(pair, carry):
        lw = lax.rem(pair, 2)
        for i in range(2):
            rows = window_rows(2 * pair + i)
            raw[i] = dot_nt(k_s[rows, :], stacked(q_s[rows, :]))
        for i in range(2):
            for t in range(WIDE // 128):
                cols = slice(t * 128, (t + 1) * 128)
                scores = raw[i, :, cols] * FACTOR + bx[lw, :, cols]
                exponent = jnp.exp(scores - jnp.max(scores, axis=0, keepdims=True))
                chances = exponent * (1.0 / jnp.sum(exponent, axis=0, keepdims=True))
                p_s[2 * pair + i, :, cols] = chances.astype(BF16)
        for i in range(2):
            rows = window_rows(2 * pair + i)
            att_s[rows, :] = per_head(v_s[rows, :], p_s[2 * pair + i]).astype(BF16)
        return carry

    def forward_windows(b, carry):
        for copy in rows_ahead(b):
            copy.wait()

        unpack(sq, b, (b10, b01, b11))
        x_w[half_rows(b), :] = dot_nn(to_window, sq[b].astype(BF16)).astype(BF16)
        project(b, carry)

        lax.fori_loop(2 * b, 2 * b + 2, attend, 0)

        @pl.when(b == 0)
        def _():
            arrived(planes.at[:, seven], 1)
            to_band(planes.at[pl.ds(0, 2)], ch, 4, d_dn).start()

        return carry

    lax.fori_loop(0, 2, forward_windows, 0)
    arrived(w_all.at[0, seven], 3)
    to_core(w_all.at[core], w_all.at[core], 16).start()

    def feed(i, carry):
        rows = chunk_rows(i)
        tmp[...] = x_w[rows, :].astype(F32) + dot_nn(att_s[rows, :], output_w[...])
        for t in range(CHUNK // TILE):
            part = tile_rows(i, t)
            middle = tmp[t * TILE:(t + 1) * TILE, :]
            mid_s[part, :] = middle
            nm_s[part, :] = (statistics(middle)[0] * feed_gain[...]).astype(BF16)
        hid[...] = dot_nn(nm_s[rows, :], expand_w[...])
        for t in range(CHUNK // 16):
            part = pl.ds(pl.multiple_of(i * CHUNK + t * 16, 16), 16)
            for j in range(FF // 256):
                cols = slice(j * 256, (j + 1) * 256)
                act, slope = gelu_parts(hid[t * 16:(t + 1) * 16, cols])
                act_s[part, cols] = act.astype(BF16)
                slope_s[part, cols] = slope
        vo_s[rows, :] = (tmp[...] + dot_nt(act_s[rows, :], shrink_t[...])).astype(BF16)
        return carry

    lax.fori_loop(0, NCHUNK, feed, 0)

    arrived(w_all.at[0], 16)
    gain_row = merge_gain[...].reshape(1, 4 * C)
    for r in range(6):
        x = (r + 1) % 2
        cell = (0, 1, 1, 2, 2, 3)[r]
        cols = slice(x * 384, (x + 1) * 384)
        if r == 3:
            arrived(ch, 4)
        plane = planes[cell + 1] if cell < 2 else ch[cell - 2]
        summed = dot_tn(plane, w_all[x])
        scaled = summed * gain_row[:, x * 384:(x + 1) * 384]
        qry[2 * r] = scaled[:, 0:192].astype(BF16)
        qry[2 * r + 1] = scaled[:, 192:384].astype(BF16)

    st[...] = jnp.zeros_like(st)
    for i in range(2):
        pick_s[i] = one_hot(WIN, orders[6 + i:7 + i, 0:384])
    stat_lane = lanes(WIN, 128)
    tile_lane = lanes(TILE, 128)

    def merge_sums(pair, carry):
        b, lw = pair // 2, lax.rem(pair, 2)
        parts = []
        for p in range(2):
            level = lax.rem(lw * 2 + p + 1, 4)
            at = pl.ds(pl.multiple_of((b * 4 + level) * 16, 16), 16)
            parts.append(qry[:, at, :].reshape(192, C))
        cells_q = jnp.concatenate(parts, axis=0)
        for i in range(2):
            qw[window_rows(2 * pair + i), :] = dot_nn(pick_s[i], cells_q).astype(BF16)
        for t in range(WIN // TILE):
            at = slice(t * TILE, (t + 1) * TILE)
            total = st[b, at, :]
            for i in range(2):
                w = 2 * pair + i
                part = pl.ds(pl.multiple_of(w * WIN + t * TILE, 16), TILE)
                q = qw[part, :].astype(F32)
                v = vo_s[part, :].astype(F32)
                mean = jnp.mean(v, axis=-1, keepdims=True)
                centred = v - mean
                squares = jnp.sum(centred * centred, axis=-1, keepdims=True)
                q_sum = jnp.sum(q, axis=-1, keepdims=True)
                qv_sum = jnp.sum(q * centred, axis=-1, keepdims=True)
                for j, value in enumerate((mean, squares, q_sum, qv_sum)):
                    total = jnp.where(tile_lane == 32 * j + w, value, total)
            st[b, at, :] = total
        return carry

    def sums_copies(b):
        return (
            remote(tup.at[b], sup.at[b], st_ss.at[2 * b], st_rs.at[2 * b], (e, d_up)),
            remote(tdn.at[b], sdn.at[b], st_ss.at[2 * b + 1], st_rs.at[2 * b + 1], (e, d_dn)),
        )

    def exchange(b):
        tup[b] = st.at[b][pl.ds(5, 24, stride=6), :]
        tdn[b] = st.at[b][pl.ds(0, 24, stride=6), :]
        for copy in sums_copies(b):
            copy.start()

    even = (over_12(lax.broadcasted_iota(I32, (WIN, 128), 0)) & 1) == 0

    def pair_of(values):
        return jnp.where(even, pltpu.roll(values, WIN - 12, 0), pltpu.roll(values, 12, 0))

    def cell_norm(b):
        for r, other in ((1, 2), (2, 1), (3, 4), (4, 3)):
            sx[pl.ds(r, 24, stride=6), :] = st.at[b][pl.ds(other, 24, stride=6), :]
        for copy in sums_copies(b):
            copy.wait()
        sx[pl.ds(0, 24, stride=6), :] = sup[b]
        sx[pl.ds(5, 24, stride=6), :] = sdn[b]
        own, cross = st[b], sx[...]
        group = [own, cross, pair_of(own), pair_of(cross)]
        cell_mean = (group[0] + group[1] + group[2] + group[3]) * 0.25
        variance = jnp.zeros((WIN, 128), F32)
        q_total = jnp.zeros((WIN, 128), F32)
        qv_total = jnp.zeros((WIN, 128), F32)
        for values in group:
            offset = values - cell_mean
            q_sum = pltpu.roll(values, 64, 1)
            variance = variance + pltpu.roll(values, 96, 1) + 192.0 * offset * offset
            q_total = q_total + q_sum
            qv_total = qv_total + pltpu.roll(values, 32, 1) + offset * q_sum
        cell_inverse = lax.rsqrt(jnp.where(stat_lane < 8, variance, 0.0) * (1.0 / 768.0) + EPS)
        cp_s[0] = cell_mean
        cp_s[1] = cell_inverse
        cp_s[2] = q_total * (1.0 / 768.0)
        cp_s[3] = cell_inverse * cell_inverse * qv_total * (1.0 / 768.0)

    def merge_back(pair, carry):
        for i in range(2):
            w = 2 * pair + i
            for t in range(WIN // TILE):
                part = pl.ds(pl.multiple_of(w * WIN + t * TILE, 16), TILE)
                at = slice(t * TILE, (t + 1) * TILE)
                mean, inverse, q_mean, projected = [
                    jnp.sum(jnp.where(tile_lane == w, cp_s[j, at, :], 0.0), axis=-1, keepdims=True) for j in range(4)
                ]
                v = vo_s[part, :].astype(F32) - mean
                go_s[part, :] = (inverse * (qw[part, :].astype(F32) - q_mean - v * projected)).astype(BF16)
        return carry

    def feed_back(i, carry):
        rows = chunk_rows(i)
        go = go_s[rows, :]
        gh = (dot_nn(go, shrink_t[...]) * slope_s[rows, :]).astype(BF16)
        gh_s[rows, :] = gh
        tmp[...] = dot_nt(gh, expand_w[...])
        for t in range(CHUNK // TILE):
            part = tile_rows(i, t)
            gnm = tmp[t * TILE:(t + 1) * TILE, :]
            unit, inverse = statistics(mid_s[part, :])
            gm = go_s[part, :].astype(F32) + norm_back(unit, inverse, gnm * feed_gain[...])
            gm_s[part, :] = gm
            gmh_s[part, :] = gm.astype(BF16)
        ga_s[rows, :] = dot_nt(gmh_s[rows, :], output_w[...]).astype(BF16)
        return carry

    def forward_sample(b, carry):
        lax.fori_loop(2 * b, 2 * b + 2, merge_sums, 0)
        exchange(b)
        return carry

    def backward_sample(b, carry):
        cell_norm(b)
        lax.fori_loop(2 * b, 2 * b + 2, merge_back, 0)
        feed_back(b, carry)
        return carry

    lax.fori_loop(0, 2, forward_sample, 0)
    ds_s[...] = jnp.zeros_like(ds_s)
    dt_s[...] = jnp.zeros_like(dt_s)
    from_window = one_hot(HALF, orders[3:4, 0:HALF])
    lax.fori_loop(0, 2, backward_sample, 0)

    g_expand = dot_tn(nm_s[...], gh_s[...]).astype(BF16)
    g_shrink = dot_tn(go_s[...], act_s[...]).astype(BF16)
    g_output = dot_tn(att_s[...], gmh_s[...]).astype(BF16)
    for i in range(4):
        for j in range(2):
            g1s[0, 2 * i + j, 0:48] = g_expand[i * 48:(i + 1) * 48, j * 384:(j + 1) * 384]
            g1s[1, 2 * i + j, 0:48] = g_shrink[i * 48:(i + 1) * 48, j * 384:(j + 1) * 384]
    wide = jnp.concatenate([g_output[0:96], g_output[96:192]], axis=1)
    for i in range(NCHIP):
        for j in range(2):
            at = (i * 2 + j) * 16
            g1s[j, i, 48:64] = wide[at:at + 16] if at < 96 else jnp.zeros((16, 384), BF16)

    def sum_of(ref, count, rows):
        total = ref[0, rows].astype(F32)
        for o in range(1, count):
            total = total + ref[o, rows].astype(F32)
        return total.astype(BF16)

    def add_pair(mine, other, out):
        def body(o, carry):
            out[o] = (mine[core, o].astype(F32) + other[o].astype(F32)).astype(BF16)
            return carry

        lax.fori_loop(0, NCHIP, body, 0)

    others = pl.ds(0, NCHIP - 1)
    to_core(g1s.at[1 - core], g1p, 5).start()


    def attend_back(pair, carry):
        lw = lax.rem(pair, 2)
        for i in range(2):
            rows = window_rows(2 * pair + i)
            dam[i] = stacked(ga_s[rows, :])
            raw[i] = dot_nt(v_s[rows, :], dam[i])
        for i in range(2):
            for t in range(WIDE // 128):
                cols = slice(t * 128, (t + 1) * 128)
                chances = p_s[2 * pair + i, :, cols].astype(F32)
                weighted = raw[i, :, cols]
                centre = jnp.sum(chances * weighted, axis=0, keepdims=True)
                dsh[i, :, cols] = (chances * (weighted - centre)).astype(BF16)
        for i in range(2):
            rows = window_rows(2 * pair + i)
            dt_s[rows, 512:704] = dot_nn(p_s[2 * pair + i], dam[i]).astype(BF16)
            dt_s[rows, 0:C] = (per_head(k_s[rows, :], dsh[i]) * FACTOR).astype(BF16)
            dt_s[rows, 256:448] = (dot_nn(dsh[i], stacked(q_s[rows, :])) * FACTOR).astype(BF16)
        ds_s[lw] = ds_s[lw] + (dsh[0].astype(F32) + dsh[1].astype(F32))
        return carry

    all_rows = slice(0, 64)
    def windows_back(pair, carry):
        attend_back(pair, carry)

        @pl.when(pair == 0)
        def _():
            arrived(g1p, 5)
            add_pair(g1s, g1p, g1h)
            g1r[chip] = g1h[chip]
            chips_all(lambda o: to_chip(g1h.at[o], g1r.at[chip], 6, o).start())

        @pl.when(pair == 2)
        def _():
            arrived(g1l.at[pl.ds(0, 3)], 7)
            g1l[4] = sum_of(g1l, 4, all_rows)
            to_band(g1l.at[4], g1l.at[5], 15, d_pair).start()

        return carry

    def second_gradients():
        summed = dot_tn(ni_s[...], dt_s[...])
        sections = [summed[:, 0:C], summed[:, 256:448], summed[:, 512:704], jnp.zeros((C, 64), F32)]
        g_triple = jnp.concatenate(sections, axis=1).astype(BF16)
        for i in range(3):
            for j in range(5):
                at = 5 * i + j
                g2s[at // 8, at % 8, 0:64] = g_triple[i * 64:(i + 1) * 64, j * 128:(j + 1) * 128]
        g2s[1, 7, 0:64] = jnp.zeros((64, 128), BF16)
        arrived(g1l.at[5], 15)
        g1f[chip] = (g1l[4].astype(F32) + g1l[5].astype(F32)).astype(BF16)
        chips_all(lambda o: to_chip(g1f.at[chip], g1f.at[chip], 8, o).start())
        for lw in range(2):
            for h in range(HEADS):
                at = pl.ds(h * 2 + lw, WIN, stride=16)
                part = jnp.concatenate(
                [ds_s[lw, :, h * 128:(h + 1) * 128], ds_s[lw, :, 768 + h * 16:784 + h * 16]], axis=1
            ).T
                bs_s.at[0][at, :] = part[:, 0:128]
                bs_s.at[1][at, :] = jnp.concatenate([part[:, 128:144], jnp.zeros((WIN, 112), F32)], axis=1)

        def fold(s_i):
            at = slice(s_i * 192, (s_i + 1) * 192)
            rows = jnp.concatenate([bs_s[0, at, :], bs_s[1, at, :]], axis=1)[:, 0:WIN].astype(BF16)
            return dot_nt(rows, spread_s[s_i])

        folded = fold(0)
        for s_i in range(1, 12):
            folded = folded + fold(s_i)
        pieces_t = []
        for p in range(2):
            for pk in range(2):
                for r in range(6):
                    at = (p * 6 + r) * 16
                    pieces_t.append(folded[at:at + 16, pk * 256:pk * 256 + 138])
        table = jnp.concatenate(pieces_t + [jnp.zeros((16, 4096 - POS), F32)], axis=1).astype(BF16)
        for o in range(32):
            g2s[o // 16, (o // 2) % 8, 64 + 16 * (o % 2):80 + 16 * (o % 2)] = table[:, o * 128:(o + 1) * 128]
        to_core(g2s.at[1 - core], g2p, 9).start()

    def project_back(i, carry):
        rows = chunk_rows(i)
        tmp[...] = (
            dot_nt(dt_s[rows, 0:C], wq[...])
            + dot_nt(dt_s[rows, 256:448], wk[...])
            + dot_nt(dt_s[rows, 512:704], wv[...])
        )
        for t in range(CHUNK // TILE):
            part = tile_rows(i, t)
            unit, inverse = statistics(x_w[part, :].astype(F32))
            back = norm_back(unit, inverse, tmp[t * TILE:(t + 1) * TILE, :] * attend_gain[...])
            gt_s[part, :] = (gm_s[part, :] + back).astype(BF16)
        return carry

    def backward_windows(b, carry):
        lax.fori_loop(2 * b, 2 * b + 2, windows_back, 0)

        @pl.when(b == 1)
        def _():
            second_gradients()

        project_back(b, carry)

        @pl.when(b == 1)
        def _():
            arrived(g2p, 9)
            add_pair(g2s, g2p, g2h)
            g2r[chip] = g2h[chip]
            chips_all(lambda o: to_chip(g2h.at[o], g2r.at[chip], 10, o).start())

        quads = dot_nn(from_window, gt_s[half_rows(b), :])
        gq[b] = quads
        pack(quads, b, (c10, c01, c11))
        for copy in rows_behind(b):
            copy.start()

        @pl.when(b == 0)
        def _():
            arrived(g1r.at[others], 6)
            g1l[d // 2] = sum_of(g1r, NCHIP, all_rows)
            for step in range(1, 4):
                to_band(g1l.at[d // 2], g1l.at[d // 2], 7, lax.rem(d + 2 * step, NLAT)).start()

        return carry

    lax.fori_loop(0, 2, backward_windows, 0)

    arrived(g1f.at[others], 8)
    to_core(g1f, g1o, 11).start()

    arrived(g2r.at[others], 10)
    g2l[d] = sum_of(g2r, NCHIP, slice(0, 64))
    lat_all(lambda o: to_band(g2l.at[d], g2l.at[d], 12, o).start())
    g2f[chip, 64:96] = sum_of(g2r, NCHIP, slice(64, 96))

    to_natural = one_hot(HALF, orders[1:2, 0:HALF])

    def unsort_sample(b, carry):
        for copy in rows_behind(b):
            copy.wait()
        unpack(gq, b, (d10, d01, d11))
        out_fields[half_rows(b), :] = dot_nn(to_natural, gq[b].astype(BF16)).astype(BF16)
        return carry

    lax.fori_loop(0, 1, unsort_sample, 0)
    arrived(g2l.at[others], 12)
    g2f[chip, 0:64] = sum_of(g2l, NLAT, slice(0, 64))
    chips_all(lambda o: to_chip(g2f.at[chip], g2f.at[chip], 13, o).start())


    lax.fori_loop(1, 2, unsort_sample, 0)
    arrived(g1o, 11)
    out_g1[core] = g1f[...]
    out_g1[1 - core] = g1o[...]
    arrived(g2f.at[others], 13)
    to_core(g2f, g2o, 14).start()
    out_g2[core] = g2f[...]
    arrived(g2o, 14)
    out_g2[1 - core] = g2o[...]

    left(cx, 0)
    left(cm.at[others], 1)
    left(w_part, 2)
    left(w_all.at[0, seven], 3)
    left(w_all.at[0], 16)
    left(ch, 4)
    left(g1p, 5)
    left(g1r.at[others], 6)
    left(g1l.at[pl.ds(0, 3)], 7)
    left(g1l.at[4], 15)
    left(g1f.at[others], 8)
    left(g2p, 9)
    left(g2r.at[others], 10)
    left(g1o, 11)
    left(g2l.at[others], 12)
    left(g2f.at[others], 13)
    left(g2o, 14)


def results_kernel(
    fields, g1, g2, attend_gain, triple_w, feed_gain, expand_w,
    out_fields, out_triple, out_output, out_expand, out_shrink, out_attend, out_feed, out_table,
):
    out_fields[...] = fields[...]
    for i in range(4):
        for j in range(2):
            rows, cols = slice(i * 48, (i + 1) * 48), slice(j * 384, (j + 1) * 384)
            out_expand[rows, cols] = g1[0, 2 * i + j, 0:48].astype(F32)
            out_shrink[rows, cols] = g1[1, 2 * i + j, 0:48].astype(F32)
    for i in range(6):
        wide = g1[i % 2, i // 2, 48:64].astype(F32)
        out_output[i * 16:(i + 1) * 16, :] = wide[:, 0:C]
        out_output[96 + i * 16:96 + (i + 1) * 16, :] = wide[:, C:2 * C]
    for i in range(3):
        for j in range(5):
            at, size = 5 * i + j, 128 if j < 4 else 64
            part = g2[at // 8, at % 8, 0:64].astype(F32)
            out_triple[i * 64:(i + 1) * 64, j * 128:j * 128 + size] = part[:, 0:size]
    table = jnp.concatenate(
        [g2[o // 16, (o // 2) % 8, 64 + 16 * (o % 2):80 + 16 * (o % 2)] for o in range(32)], axis=1
    ).astype(F32)
    for h in range(HEADS):
        out_table[h] = table[2 * h:2 * h + 2, 0:POS]

    def gain_gradient(grad, weight, gain):
        product = (grad[...] * weight[...].astype(F32)).astype(BF16)
        total = dot_nt(jnp.ones((16, product.shape[1]), BF16), product)
        return total[0:1] / gain[...]

    out_attend[...] = gain_gradient(out_triple, triple_w, attend_gain)
    out_feed[...] = gain_gradient(out_expand, expand_w, feed_gain)


def scratch():
    def vmem(*shape, kind=BF16):
        return pltpu.VMEM(shape, kind)

    token = vmem(TOK, C)
    token_f = vmem(TOK, C, kind=F32)
    weight = vmem(C, C)
    quad = vmem(2, HALF, C, kind=F32)
    halves = [vmem(2, 336, 128), vmem(2, 112, 128), vmem(2, 112, 128)]
    stat = vmem(WIN, 128, kind=F32)
    small = vmem(2, 24, 128, kind=F32)
    buffers = [
        quad, quad, *halves, *halves, *halves, *halves, token, token, token, token, token, weight, weight, weight,
        vmem(NWIN, WIN, WIDE), token, token_f, token, vmem(TOK, FF), vmem(TOK, FF, kind=F32), token,
        vmem(16, POS, kind=F32), vmem(384, 512), vmem(2, 2304, 128, kind=F32),
        vmem(2, WIN, WIDE, kind=F32), vmem(2, WIN, WIDE, kind=F32),
        vmem(12, 512, WIN), vmem(2, WIN, 384),
        vmem(576, 256, kind=F32), vmem(8, 2, 3, 32, 128), vmem(8, 3, 32, 128),
        vmem(8, 3, 48, 128), vmem(2, 384, 128), vmem(3, 384, 128),
        vmem(32, 768), vmem(32, 768), vmem(48, 384), vmem(2, 384, 384),
        vmem(12, 128, C), token, vmem(2, WIN, 128, kind=F32), stat, small, small, small, small, vmem(4, WIN, 128, kind=F32),
        token, vmem(TOK, FF), token_f, token, token, vmem(TOK, 768), token,
        vmem(2, WIN, WIDE, kind=F32), vmem(2, WIN, WIDE), vmem(2, WIDE, C), vmem(CHUNK, FF, kind=F32),
        vmem(CHUNK, C, kind=F32),
    ]
    for rows, cols in ((64, 384), (96, 128)):
        chunks = vmem(8, rows, cols)
        buffers += [vmem(2, 8, rows, cols), chunks, chunks, chunks, vmem(8, 64, cols), chunks, chunks]
    counts = [6, 6, 6, 6, 4, 4, 17, 17]
    return buffers + [pltpu.SemaphoreType.DMA((n,)) for n in counts]


def per_device(
    fields, merge_cotangent, attend_gain, triple_weight, bias_table, output_weight, feed_gain,
    expand_weight, shrink_weight, merge_gain, merge_weight,
):
    cot = jnp.transpose(merge_cotangent, (1, 2, 3, 4, 0)).reshape(576, 192)
    bias = jnp.transpose(bias_table[0], (1, 0, 2))
    def shaped(shapes):
        return [jax.ShapeDtypeStruct(shape, kind) for shape, kind in shapes]

    vmem_spec = pl.BlockSpec(memory_space=pltpu.VMEM)
    parts = pl.pallas_call(
        kernel,
        out_shape=shaped(
            [((TOK, C), BF16), ((2, 8, 64, 384), BF16), ((2, 8, 96, 128), BF16)]
        ),
        in_specs=[vmem_spec] * 12,
        out_specs=[vmem_spec] * 3,
        scratch_shapes=scratch(),
        compiler_params=pltpu.CompilerParams(
            collective_id=0, has_side_effects=True, vmem_limit_bytes=60 * 1024 * 1024
        ),
    )(
        fields.reshape(TOK, C), cot, attend_gain.reshape(1, C), triple_weight, bias, output_weight,
        feed_gain.reshape(1, C), expand_weight, shrink_weight.T, merge_gain,
        merge_weight.T, jnp.asarray(order_indices()),
    )
    g_fields, g_triple, g_output, g_expand, g_shrink, g_attend, g_feed, g_table = pl.pallas_call(
        results_kernel,
        out_shape=shaped(
            [
                ((TOK, C), BF16), ((C, 3 * C), F32), ((C, C), F32), ((C, FF), F32), ((C, FF), F32),
                ((1, C), F32), ((1, C), F32), ((HEADS, 2, POS), F32),
            ]
        ),
        in_specs=[vmem_spec] * 7,
        out_specs=[vmem_spec] * 8,
        compiler_params=pltpu.CompilerParams(vmem_limit_bytes=60 * 1024 * 1024),
    )(*parts, attend_gain.reshape(1, C), triple_weight, feed_gain.reshape(1, C), expand_weight)
    return (
        g_fields.reshape(fields.shape), g_triple, g_output, g_expand, g_shrink.T,
        g_attend.reshape(C), g_feed.reshape(C), jnp.transpose(g_table, (1, 0, 2))[None],
    )


def solution(mesh):
    placed = (
        P(None, None, "lat", "lon", None),
        P(None, None, None, "lat", "lon"),
        P(),
        P(),
        P("lat", None, None, None),
        P(),
        P(),
        P(),
        P(),
        P(),
        P(None, "lon"),
    )
    return jax.shard_map(
        per_device,
        mesh=mesh,
        in_specs=placed,
        out_specs=(
            P(None, None, "lat", "lon", None),
            P(),
            P(),
            P(),
            P(),
            P(),
            P(),
            P("lat", None, None, None),
        ),
        check_vma=False,
    )
```

```python
import functools
import math

import jax
import jax.numpy as jnp
import numpy as np
from jax import lax
from jax.experimental import pallas as pl
from jax.experimental.pallas import tpu as pltpu
from jax.sharding import PartitionSpec as P

F32 = jnp.float32
BF16 = jnp.bfloat16
I32 = jnp.int32
MESH = pl.DeviceIdType.MESH

EPS = 1e-05
MASKED = -1000000000.0
NLON = 16
NLAT = 8
NCHIP = 8
C = 192
HEADS = 6
FF = 768
WIN = 144
NWIN = 8
TOK = WIN * NWIN
HALF = TOK // 2
SIZES = ((216, 112), (72, 40), (72, 40))
POS = 3312
CHUNK = 576
NCHUNK = TOK // CHUNK
TILE = 48
WIDE = 896
FACTOR = 32 ** -0.5


def order_indices():
    natural_to_quad = np.full(640, -1, np.int32)
    quad_to_natural = np.full(640, -1, np.int32)
    quad_to_window = np.full(640, -1, np.int32)
    window_to_quad = np.full(640, -1, np.int32)
    for level in range(4):
        for row in range(6):
            for col in range(24):
                source = (level * 6 + row) * 24 + col
                if col >= 6:
                    place = (0 if row >= 3 else 216) + level * 54 + (row % 3) * 18 + col - 6
                else:
                    place = (432 if row >= 3 else 504) + level * 18 + (row % 3) * 6 + col
                natural_to_quad[source] = place
                quad_to_natural[place] = source
    index = 0
    for lev_win in range(2):
        for lon_win in range(2):
            for s in range(12):
                for p in range(2):
                    for r in range(6):
                        level = (lev_win * 2 + p + 1) % 4
                        col = lon_win * 12 + s
                        if col < 18:
                            place = (0 if r < 3 else 216) + level * 54 + (r % 3) * 18 + col
                        else:
                            place = (432 if r < 3 else 504) + level * 18 + (r % 3) * 6 + col - 18
                        window_to_quad[index] = place
                        quad_to_window[place] = index
                        index += 1
    cell_lane = np.full(640, -1, np.int32)
    bias_row = np.full(640, -1, np.int32)
    merged_token = np.full((2, 640), -1, np.int32)
    for lane in range(256):
        if lane % 16 < 12:
            cell_lane[lane] = (12 * (lane // 16) + 3 + lane % 16) % 192
    for k in range(WIN):
        s, p, r = k // 12, (k // 6) % 2, k % 6
        bias_row[k] = p * 256 + r * 23 + 11 - s
    for lon_win in range(2):
        for row in range(384):
            p, r, y, m = row // 192, (row // 32) % 6, (row // 16) % 2, row % 16
            if 0 <= m - lon_win * 6 < 6:
                merged_token[lon_win, row] = (2 * (m - lon_win * 6) + y) * 12 + p * 6 + r
    rows = [natural_to_quad, quad_to_natural, quad_to_window, window_to_quad]
    return np.stack(rows + [cell_lane, bias_row, merged_token[0], merged_token[1]])


def dot_nn(a, b):
    return lax.dot_general(a, b, (((1,), (0,)), ((), ())), preferred_element_type=F32)


def dot_nt(a, b):
    return lax.dot_general(a, b, (((1,), (1,)), ((), ())), preferred_element_type=F32)


def dot_tn(a, b):
    return lax.dot_general(a, b, (((0,), (0,)), ((), ())), preferred_element_type=F32)


def one_hot(rows, targets):
    ids = lax.broadcasted_iota(I32, (rows, targets.shape[1]), 0)
    return jnp.where(ids == targets, 1.0, 0.0).astype(BF16)


def statistics(values):
    centred = values - jnp.mean(values, axis=-1, keepdims=True)
    inverse = lax.rsqrt(jnp.mean(centred * centred, axis=-1, keepdims=True) + EPS)
    return centred * inverse, inverse


def norm_back(normed, inverse, scaled):
    centre = jnp.mean(scaled, axis=-1, keepdims=True)
    projected = jnp.mean(scaled * normed, axis=-1, keepdims=True)
    return inverse * (scaled - centre - normed * projected)


def gelu_parts(values):
    cumulative = 0.5 * (1.0 + lax.erf(values * (1.0 / math.sqrt(2.0))))
    density = jnp.exp(-0.5 * values * values) * (1.0 / math.sqrt(2.0 * math.pi))
    return values * cumulative, cumulative + values * density


def lanes(rows, cols):
    return lax.broadcasted_iota(I32, (rows, cols), 1)


def over_12(ids):
    return (ids * 5462) >> 16


def over_6(ids):
    return (ids * 10923) >> 16


def kernel(
    fields, cot, attend_gain, triple_w, bias, output_w, feed_gain, expand_w, shrink_t, merge_gain,
    merge_wt, orders,
    out_fields, out_g1, out_g2,
    sq, gq, a10, a01, a11, b10, b01, b11, c10, c01, c11, d10, d01, d11, x_w, ni_s, q_s, k_s, v_s, wq, wk, wv, p_s, att_s, mid_s, nm_s, act_s, slope_s, vo_s,
    b16, bl_s, bs_s, bx, ds_s, spread_s, pick_s,
    cells, cs, cx, cm, ch, planes, w_own, w_part, w_send, w_all, qry, qw, st, sx, sup, sdn, tup, tdn, cp_s, go_s, gh_s, gm_s, ga_s, gmh_s,
    dt_s, gt_s, raw, dsh, dam, hid, tmp, g1s, g1p, g1h, g1r, g1l, g1f, g1o, g2s, g2p, g2h, g2r, g2l, g2f, g2o,
    halo_ss, halo_rs, back_ss, back_rs, st_ss, st_rs, sends, recvs,
):
    e = lax.axis_index("lon")
    d = lax.axis_index("lat")
    e_up, e_dn = lax.rem(e + 1, NLON), lax.rem(e + NLON - 1, NLON)
    d_up, d_dn = lax.rem(d + 1, NLAT), lax.rem(d + NLAT - 1, NLAT)

    def remote(src, dst, ssem, rsem, device):
        return pltpu.make_async_remote_copy(
            src_ref=src, dst_ref=dst, send_sem=ssem, recv_sem=rsem, device_id=device,
            device_id_type=MESH,
        )

    core, chip = lax.rem(e, 2), e // 2
    partner = e + 1 - 2 * core
    d_pair = d + 1 - 2 * lax.rem(d, 2)

    def chips_all(action):
        def body(step, carry):
            action(lax.rem(chip + step, NCHIP))
            return carry

        lax.fori_loop(1, NCHIP, body, 0)

    def lat_all(action):
        def body(step, carry):
            action(lax.rem(d + step, NLAT))
            return carry

        lax.fori_loop(1, NLAT, body, 0)

    def to_chip(src, dst, phase, o):
        return remote(src, dst, sends.at[phase], recvs.at[phase], (2 * o + core, d))

    def to_band(src, dst, phase, o):
        return remote(src, dst, sends.at[phase], recvs.at[phase], (e, o))

    def to_core(src, dst, phase):
        return remote(src, dst, sends.at[phase], recvs.at[phase], (partner, d))

    def arrived(region, phase):
        remote(region, region, sends.at[phase], recvs.at[phase], (partner, d)).wait_recv()

    def left(region, phase):
        remote(region, region, sends.at[phase], recvs.at[phase], (partner, d)).wait_send()

    barrier = pltpu.get_barrier_semaphore()

    def greet(device):
        pl.semaphore_signal(barrier, inc=1, device_id=device, device_id_type=MESH)

    chips_all(lambda o: greet((2 * o + core, d)))
    lat_all(lambda o: greet((e, o)))
    for device in ((e_up, d), (e_dn, d), (e_up, d_up), (e_dn, d_dn)):
        greet(device)

    def half_rows(b):
        return pl.ds(pl.multiple_of(b * HALF, HALF), HALF)

    def pack(quads, b, out):
        at = 216
        for (size, cut), message in zip(SIZES, out):
            rows = quads[at:at + size]
            rest = jnp.concatenate([rows[cut:, 128:C], jnp.zeros((2 * cut - size, 64), F32)], axis=0)
            parts = [rows[:, 0:128], jnp.concatenate([rows[:cut, 128:C], rest], axis=1)]
            if (size + cut) % 16:
                parts.append(jnp.zeros((8, 128), F32))
            message[b] = jnp.concatenate(parts, axis=0).astype(BF16)
            at += size

    def unpack(quads, b, messages):
        at = 216
        for (size, cut), message in zip(SIZES, messages):
            rows = message[b].astype(F32)
            tails = rows[size:size + cut]
            tail = jnp.concatenate([tails[:, 0:64], tails[0:size - cut, 64:128]], axis=0)
            quads[b, at:at + size, :] = jnp.concatenate([rows[0:size], tail], axis=1)
            at += size

    def halo(sources, targets, ssem, rsem, step, b):
        devices = ((e, step[1]), (step[0], d), (step[0], step[1]))
        return [
            remote(src.at[b], dst.at[b], ssem.at[3 * b + i], rsem.at[3 * b + i], dev)
            for i, (src, dst, dev) in enumerate(zip(sources, targets, devices))
        ]

    def rows_ahead(b):
        return halo((a10, a01, a11), (b10, b01, b11), halo_ss, halo_rs, (e_dn, d_dn), b)

    def rows_behind(b):
        return halo((c10, c01, c11), (d10, d01, d11), back_ss, back_rs, (e_up, d_up), b)

    to_quad = one_hot(HALF, orders[0:1, 0:HALF])

    for b in range(2):
        quads = dot_nn(to_quad, fields[b * HALF:(b + 1) * HALF, :])
        sq[b] = quads
        pack(quads, b, (a10, a01, a11))
    pl.semaphore_wait(barrier, NCHIP - 1 + NLAT - 1 + 4)
    for b in range(2):
        for copy in rows_ahead(b):
            copy.start()

    cells[...] = dot_nn(cot[...], one_hot(192, orders[4:5, 0:256]))
    block_of = lanes(72, 128) >> 4

    def gather_cells(inner, carry):
        for tile in range(2):
            piece = jnp.zeros((72, 128), F32)
            for bl in range(8):
                part = cells[bl * 72:(bl + 1) * 72, tile * 128:(tile + 1) * 128]
                part = pltpu.roll(part, lax.rem(16 * (bl - inner) + 128, 128), 1)
                piece = jnp.where(block_of == bl, part, piece)
            for a in range(3):
                padded = jnp.concatenate([piece[a * 24:(a + 1) * 24], jnp.zeros((8, 128), F32)], axis=0)
                cs[4 * tile + inner // 2, lax.rem(inner, 2), a] = padded.astype(BF16)
        return carry

    lax.fori_loop(0, 8, gather_cells, 0)
    w_own[...] = jnp.concatenate(
        [merge_wt[...].astype(F32), jnp.zeros((8, 768), F32)], axis=0
    ).astype(BF16)
    to_core(cs.at[:, 1 - core], cx, 0).start()
    to_core(w_own, w_part, 2).start()

    for h in range(HEADS):
        b16[2 * h:2 * h + 2, :] = bias[h]
    b16[12:16, :] = jnp.zeros((4, POS), F32)
    zero_tail = jnp.zeros((16, 256 - 138), F32)
    for p in range(2):
        for r in range(6):
            parts = []
            for pk in range(2):
                at = (p * 2 + pk) * 828 + r * 138
                parts += [b16[:, at:at + 138], zero_tail]
            row = jnp.concatenate(parts, axis=1)
            high = row.astype(BF16)
            low = (row - high.astype(F32)).astype(BF16)
            at = (p * 6 + r) * 16
            bl_s[at:at + 16, :] = high
            bl_s[192 + at:192 + at + 16, :] = low

    bias_row = orders[5:6, 0:WIN]

    def spread(pair, carry):
        for i in range(2):
            s_i = 2 * pair + i
            matrix = one_hot(512, bias_row + s_i)
            spread_s[s_i] = matrix
            split = dot_nn(bl_s[...], matrix)
            rows = split[0:192] + split[192:384]
            at = pl.ds(pl.multiple_of(s_i * 192, 192), 192)
            bs_s[0, at, :] = rows[:, 0:128]
            bs_s[1, at, :] = jnp.concatenate([rows[:, 128:144], jnp.zeros((192, 112), F32)], axis=1)
        return carry

    lax.fori_loop(0, 6, spread, 0)

    def dense(mine, other):
        mine, other = mine.astype(F32)[0:24], other.astype(F32)[0:24]
        swapped = core == 1
        parts = [jnp.where(swapped, other, mine), jnp.where(swapped, mine, other)]
        return jnp.concatenate(parts, axis=0)

    def chip_rows(o):
        return pl.ds(pl.multiple_of(o * 48, 48), 48)

    def merge_pieces(o, carry):
        for a in range(3):
            cm[o, a] = dense(cs[o, core, a], cx[o, a]).astype(BF16)
        return carry

    arrived(cx, 0)
    lax.fori_loop(0, NCHIP, merge_pieces, 0)
    planes[:, chip_rows(chip)] = cm[chip]
    chips_all(lambda o: to_chip(cm.at[o], planes.at[:, chip_rows(chip)], 1, o).start())
    arrived(w_part, 2)
    both = dense(w_own[...], w_part[...])
    w_send[...] = jnp.where(core == 1, both[:, 384:768], both[:, 0:384]).astype(BF16)
    w_all[core, chip_rows(chip)] = w_send[...]
    chips_all(lambda o: to_chip(w_send, w_all.at[core, chip_rows(chip)], 3, o).start())
    seven = pl.ds(0, 48 * (NCHIP - 1))

    tok_i = lax.broadcasted_iota(I32, (WIN, WIN), 0)
    tok_k = lax.broadcasted_iota(I32, (WIN, WIN), 1)
    half_i, half_k = over_6(tok_i), over_6(tok_k)
    last_band = d == NLAT - 1
    lat_differs = ((tok_i - half_i * 6 >= 3) != (tok_k - half_k * 6 >= 3)) & last_band
    lev_differs = (half_i & 1) != (half_k & 1)
    bx[:, :, HEADS * WIN:WIDE] = jnp.zeros((2, WIN, WIDE - HEADS * WIN), F32)
    for lw in range(2):
        differs = (lat_differs | lev_differs) if lw else lat_differs
        for h in range(HEADS):
            at = pl.ds(h * 2 + lw, WIN, stride=16)
            full = jnp.concatenate([bs_s.at[0][at, :], bs_s.at[1][at, :]], axis=1)[:, 0:WIN]
            spread_bias = jnp.where(differs, MASKED, full).T
            bx[lw, :, h * 128:(h + 1) * 128] = spread_bias[:, 0:128]
            bx[lw, :, 768 + h * 16:784 + h * 16] = spread_bias[:, 128:WIN]

    wq[...] = triple_w[:, 0:192]
    wk[...] = triple_w[:, 192:384]
    wv[...] = triple_w[:, 384:576]

    head_of = lanes(1, C) >> 5
    head_f = [jnp.where(head_of == h, 1.0, 0.0) for h in range(HEADS)]
    head_b = [mask.astype(BF16) for mask in head_f]

    blank = jnp.zeros((WIDE - HEADS * WIN, C), BF16)

    def stacked(values):
        first, rest = values[0:128], values[128:WIN]
        parts = [first * mask for mask in head_b] + [rest * mask for mask in head_b]
        return jnp.concatenate(parts + [blank], axis=0)

    def per_head(left, right):
        turned = left.T
        wide = [dot_nn(turned[64 * i:64 * i + 64], right[:, 256 * i:256 * i + 256]) for i in range(3)]
        tail = dot_nn(turned, right[:, 768:WIDE])
        blocks = []
        for h in range(HEADS):
            at, row = 128 * (h % 2), 32 * (h % 2)
            blocks.append(
                jnp.concatenate(
                    [wide[h // 2][row:row + 32, at:at + 128], tail[32 * h:32 * h + 32, 16 * h:16 * h + 16]], axis=1
                )
            )
        return jnp.concatenate(blocks, axis=0).T

    to_window = one_hot(HALF, orders[2:3, 0:HALF])

    def window_rows(w):
        return pl.ds(pl.multiple_of(w * WIN, WIN), WIN)

    def chunk_rows(i):
        return pl.ds(pl.multiple_of(i * CHUNK, CHUNK), CHUNK)

    def tile_rows(i, t):
        return pl.ds(pl.multiple_of(i * CHUNK + t * TILE, 16), TILE)

    def project(i, carry):
        rows = chunk_rows(i)
        for t in range(CHUNK // TILE):
            part = tile_rows(i, t)
            normed = statistics(x_w[part, :].astype(F32))[0]
            ni_s[part, :] = (normed * attend_gain[...]).astype(BF16)
        normed_in = ni_s[rows, :]
        q_s[rows, :] = dot_nn(normed_in, wq[...]).astype(BF16)
        k_s[rows, :] = dot_nn(normed_in, wk[...]).astype(BF16)
        v_s[rows, :] = dot_nn(normed_in, wv[...]).astype(BF16)
        return carry


    def attend(b):
        for i in range(4):
            rows = window_rows(4 * b + i)
            raw[i] = dot_nt(k_s[rows, :], stacked(q_s[rows, :]))
        for i in range(4):
            for t in range(WIDE // 128):
                cols = slice(t * 128, (t + 1) * 128)
                scores = raw[i, :, cols] * FACTOR + bx[i // 2, :, cols]
                exponent = jnp.exp(scores - jnp.max(scores, axis=0, keepdims=True))
                chances = exponent * (1.0 / jnp.sum(exponent, axis=0, keepdims=True))
                p_s[4 * b + i, :, cols] = chances.astype(BF16)
        for i in range(4):
            rows = window_rows(4 * b + i)
            att_s[rows, :] = per_head(v_s[rows, :], p_s[4 * b + i]).astype(BF16)

    def forward_windows(b, carry):
        for copy in rows_ahead(b):
            copy.wait()

        unpack(sq, b, (b10, b01, b11))
        x_w[half_rows(b), :] = dot_nn(to_window, sq[b].astype(BF16)).astype(BF16)
        project(b, carry)

        attend(b)

        @pl.when(b == 0)
        def _():
            arrived(planes.at[:, seven], 1)
            to_band(planes.at[pl.ds(0, 2)], ch, 4, d_dn).start()

        return carry

    lax.fori_loop(0, 2, forward_windows, 0)
    arrived(w_all.at[0, seven], 3)
    to_core(w_all.at[core], w_all.at[core], 16).start()

    def feed(i, carry):
        rows = chunk_rows(i)
        tmp[...] = x_w[rows, :].astype(F32) + dot_nn(att_s[rows, :], output_w[...])
        for t in range(CHUNK // TILE):
            part = tile_rows(i, t)
            middle = tmp[t * TILE:(t + 1) * TILE, :]
            mid_s[part, :] = middle
            nm_s[part, :] = (statistics(middle)[0] * feed_gain[...]).astype(BF16)
        hid[...] = dot_nn(nm_s[rows, :], expand_w[...])
        for t in range(CHUNK // 16):
            part = pl.ds(pl.multiple_of(i * CHUNK + t * 16, 16), 16)
            for j in range(FF // 256):
                cols = slice(j * 256, (j + 1) * 256)
                act, slope = gelu_parts(hid[t * 16:(t + 1) * 16, cols])
                act_s[part, cols] = act.astype(BF16)
                slope_s[part, cols] = slope
        vo_s[rows, :] = (tmp[...] + dot_nt(act_s[rows, :], shrink_t[...])).astype(BF16)
        return carry

    lax.fori_loop(0, NCHUNK, feed, 0)

    arrived(w_all.at[0], 16)
    gain_row = merge_gain[...].reshape(1, 4 * C)
    for r in range(6):
        x = (r + 1) % 2
        cell = (0, 1, 1, 2, 2, 3)[r]
        cols = slice(x * 384, (x + 1) * 384)
        if r == 3:
            arrived(ch, 4)
        plane = planes[cell + 1] if cell < 2 else ch[cell - 2]
        summed = dot_tn(plane, w_all[x])
        scaled = summed * gain_row[:, x * 384:(x + 1) * 384]
        qry[2 * r] = scaled[:, 0:192].astype(BF16)
        qry[2 * r + 1] = scaled[:, 192:384].astype(BF16)

    st[...] = jnp.zeros_like(st)
    for i in range(2):
        pick_s[i] = one_hot(WIN, orders[6 + i:7 + i, 0:384])
    stat_lane = lanes(WIN, 128)
    tile_lane = lanes(TILE, 128)

    def merge_sums(pair, carry):
        b, lw = pair // 2, lax.rem(pair, 2)
        parts = []
        for p in range(2):
            level = lax.rem(lw * 2 + p + 1, 4)
            at = pl.ds(pl.multiple_of((b * 4 + level) * 16, 16), 16)
            parts.append(qry[:, at, :].reshape(192, C))
        cells_q = jnp.concatenate(parts, axis=0)
        for i in range(2):
            qw[window_rows(2 * pair + i), :] = dot_nn(pick_s[i], cells_q).astype(BF16)
        for t in range(WIN // TILE):
            at = slice(t * TILE, (t + 1) * TILE)
            total = st[b, at, :]
            for i in range(2):
                w = 2 * pair + i
                part = pl.ds(pl.multiple_of(w * WIN + t * TILE, 16), TILE)
                q = qw[part, :].astype(F32)
                v = vo_s[part, :].astype(F32)
                mean = jnp.mean(v, axis=-1, keepdims=True)
                centred = v - mean
                squares = jnp.sum(centred * centred, axis=-1, keepdims=True)
                q_sum = jnp.sum(q, axis=-1, keepdims=True)
                qv_sum = jnp.sum(q * centred, axis=-1, keepdims=True)
                for j, value in enumerate((mean, squares, q_sum, qv_sum)):
                    total = jnp.where(tile_lane == 32 * j + w, value, total)
            st[b, at, :] = total
        return carry

    def sums_copies(b):
        return (
            remote(tup.at[b], sup.at[b], st_ss.at[2 * b], st_rs.at[2 * b], (e, d_up)),
            remote(tdn.at[b], sdn.at[b], st_ss.at[2 * b + 1], st_rs.at[2 * b + 1], (e, d_dn)),
        )

    def exchange(b):
        tup[b] = st.at[b][pl.ds(5, 24, stride=6), :]
        tdn[b] = st.at[b][pl.ds(0, 24, stride=6), :]
        for copy in sums_copies(b):
            copy.start()

    even = (over_12(lax.broadcasted_iota(I32, (WIN, 128), 0)) & 1) == 0

    def pair_of(values):
        return jnp.where(even, pltpu.roll(values, WIN - 12, 0), pltpu.roll(values, 12, 0))

    def cell_norm(b):
        for r, other in ((1, 2), (2, 1), (3, 4), (4, 3)):
            sx[pl.ds(r, 24, stride=6), :] = st.at[b][pl.ds(other, 24, stride=6), :]
        for copy in sums_copies(b):
            copy.wait()
        sx[pl.ds(0, 24, stride=6), :] = sup[b]
        sx[pl.ds(5, 24, stride=6), :] = sdn[b]
        own, cross = st[b], sx[...]
        group = [own, cross, pair_of(own), pair_of(cross)]
        cell_mean = (group[0] + group[1] + group[2] + group[3]) * 0.25
        variance = jnp.zeros((WIN, 128), F32)
        q_total = jnp.zeros((WIN, 128), F32)
        qv_total = jnp.zeros((WIN, 128), F32)
        for values in group:
            offset = values - cell_mean
            q_sum = pltpu.roll(values, 64, 1)
            variance = variance + pltpu.roll(values, 96, 1) + 192.0 * offset * offset
            q_total = q_total + q_sum
            qv_total = qv_total + pltpu.roll(values, 32, 1) + offset * q_sum
        cell_inverse = lax.rsqrt(jnp.where(stat_lane < 8, variance, 0.0) * (1.0 / 768.0) + EPS)
        cp_s[0] = cell_mean
        cp_s[1] = cell_inverse
        cp_s[2] = q_total * (1.0 / 768.0)
        cp_s[3] = cell_inverse * cell_inverse * qv_total * (1.0 / 768.0)

    def merge_back(pair, carry):
        for i in range(2):
            w = 2 * pair + i
            for t in range(WIN // TILE):
                part = pl.ds(pl.multiple_of(w * WIN + t * TILE, 16), TILE)
                at = slice(t * TILE, (t + 1) * TILE)
                mean, inverse, q_mean, projected = [
                    jnp.sum(jnp.where(tile_lane == w, cp_s[j, at, :], 0.0), axis=-1, keepdims=True) for j in range(4)
                ]
                v = vo_s[part, :].astype(F32) - mean
                go_s[part, :] = (inverse * (qw[part, :].astype(F32) - q_mean - v * projected)).astype(BF16)
        return carry

    def feed_back(i, carry):
        rows = chunk_rows(i)
        go = go_s[rows, :]
        gh = (dot_nn(go, shrink_t[...]) * slope_s[rows, :]).astype(BF16)
        gh_s[rows, :] = gh
        tmp[...] = dot_nt(gh, expand_w[...])
        for t in range(CHUNK // TILE):
            part = tile_rows(i, t)
            gnm = tmp[t * TILE:(t + 1) * TILE, :]
            unit, inverse = statistics(mid_s[part, :])
            gm = go_s[part, :].astype(F32) + norm_back(unit, inverse, gnm * feed_gain[...])
            gm_s[part, :] = gm
            gmh_s[part, :] = gm.astype(BF16)
        ga_s[rows, :] = dot_nt(gmh_s[rows, :], output_w[...]).astype(BF16)
        return carry

    def forward_sample(b, carry):
        lax.fori_loop(2 * b, 2 * b + 2, merge_sums, 0)
        exchange(b)
        return carry

    def backward_sample(b, carry):
        cell_norm(b)
        lax.fori_loop(2 * b, 2 * b + 2, merge_back, 0)
        feed_back(b, carry)
        return carry

    lax.fori_loop(0, 2, forward_sample, 0)
    ds_s[...] = jnp.zeros_like(ds_s)
    dt_s[...] = jnp.zeros_like(dt_s)
    from_window = one_hot(HALF, orders[3:4, 0:HALF])
    lax.fori_loop(0, 2, backward_sample, 0)

    g_expand = dot_tn(nm_s[...], gh_s[...]).astype(BF16)
    g_shrink = dot_tn(go_s[...], act_s[...]).astype(BF16)
    g_output = dot_tn(att_s[...], gmh_s[...]).astype(BF16)
    for i in range(4):
        for j in range(2):
            g1s[0, 2 * i + j, 0:48] = g_expand[i * 48:(i + 1) * 48, j * 384:(j + 1) * 384]
            g1s[1, 2 * i + j, 0:48] = g_shrink[i * 48:(i + 1) * 48, j * 384:(j + 1) * 384]
    wide = jnp.concatenate([g_output[0:96], g_output[96:192]], axis=1)
    for i in range(NCHIP):
        for j in range(2):
            at = (i * 2 + j) * 16
            g1s[j, i, 48:64] = wide[at:at + 16] if at < 96 else jnp.zeros((16, 384), BF16)

    def sum_of(ref, count, rows):
        total = ref[0, rows].astype(F32)
        for o in range(1, count):
            total = total + ref[o, rows].astype(F32)
        return total.astype(BF16)

    def add_pair(mine, other, out):
        def body(o, carry):
            out[o] = (mine[core, o].astype(F32) + other[o].astype(F32)).astype(BF16)
            return carry

        lax.fori_loop(0, NCHIP, body, 0)

    others = pl.ds(0, NCHIP - 1)
    to_core(g1s.at[1 - core], g1p, 5).start()


    def attend_back(pair, carry):
        lw = lax.rem(pair, 2)
        for i in range(2):
            rows = window_rows(2 * pair + i)
            dam[i] = stacked(ga_s[rows, :])
            raw[i] = dot_nt(v_s[rows, :], dam[i])
        for i in range(2):
            for t in range(WIDE // 128):
                cols = slice(t * 128, (t + 1) * 128)
                chances = p_s[2 * pair + i, :, cols].astype(F32)
                weighted = raw[i, :, cols]
                centre = jnp.sum(chances * weighted, axis=0, keepdims=True)
                dsh[i, :, cols] = (chances * (weighted - centre)).astype(BF16)
        for i in range(2):
            rows = window_rows(2 * pair + i)
            dt_s[rows, 512:704] = dot_nn(p_s[2 * pair + i], dam[i]).astype(BF16)
            dt_s[rows, 0:C] = (per_head(k_s[rows, :], dsh[i]) * FACTOR).astype(BF16)
            dt_s[rows, 256:448] = (dot_nn(dsh[i], stacked(q_s[rows, :])) * FACTOR).astype(BF16)
        ds_s[lw] = ds_s[lw] + (dsh[0].astype(F32) + dsh[1].astype(F32))
        return carry

    all_rows = slice(0, 64)
    def windows_back(pair, carry):
        attend_back(pair, carry)

        @pl.when(pair == 0)
        def _():
            arrived(g1p, 5)
            add_pair(g1s, g1p, g1h)
            g1r[chip] = g1h[chip]
            chips_all(lambda o: to_chip(g1h.at[o], g1r.at[chip], 6, o).start())

        @pl.when(pair == 2)
        def _():
            arrived(g1l.at[pl.ds(0, 3)], 7)
            g1l[4] = sum_of(g1l, 4, all_rows)
            to_band(g1l.at[4], g1l.at[5], 15, d_pair).start()

        return carry

    def second_gradients():
        summed = dot_tn(ni_s[...], dt_s[...])
        sections = [summed[:, 0:C], summed[:, 256:448], summed[:, 512:704], jnp.zeros((C, 64), F32)]
        g_triple = jnp.concatenate(sections, axis=1).astype(BF16)
        for i in range(3):
            for j in range(5):
                at = 5 * i + j
                g2s[at // 8, at % 8, 0:64] = g_triple[i * 64:(i + 1) * 64, j * 128:(j + 1) * 128]
        g2s[1, 7, 0:64] = jnp.zeros((64, 128), BF16)
        arrived(g1l.at[5], 15)
        g1f[chip] = (g1l[4].astype(F32) + g1l[5].astype(F32)).astype(BF16)
        chips_all(lambda o: to_chip(g1f.at[chip], g1f.at[chip], 8, o).start())
        for lw in range(2):
            for h in range(HEADS):
                at = pl.ds(h * 2 + lw, WIN, stride=16)
                part = jnp.concatenate(
                [ds_s[lw, :, h * 128:(h + 1) * 128], ds_s[lw, :, 768 + h * 16:784 + h * 16]], axis=1
            ).T
                bs_s.at[0][at, :] = part[:, 0:128]
                bs_s.at[1][at, :] = jnp.concatenate([part[:, 128:144], jnp.zeros((WIN, 112), F32)], axis=1)

        def fold(s_i):
            at = slice(s_i * 192, (s_i + 1) * 192)
            rows = jnp.concatenate([bs_s[0, at, :], bs_s[1, at, :]], axis=1)[:, 0:WIN].astype(BF16)
            return dot_nt(rows, spread_s[s_i])

        folded = fold(0)
        for s_i in range(1, 12):
            folded = folded + fold(s_i)
        pieces_t = []
        for p in range(2):
            for pk in range(2):
                for r in range(6):
                    at = (p * 6 + r) * 16
                    pieces_t.append(folded[at:at + 16, pk * 256:pk * 256 + 138])
        table = jnp.concatenate(pieces_t + [jnp.zeros((16, 4096 - POS), F32)], axis=1).astype(BF16)
        for o in range(32):
            g2s[o // 16, (o // 2) % 8, 64 + 16 * (o % 2):80 + 16 * (o % 2)] = table[:, o * 128:(o + 1) * 128]
        to_core(g2s.at[1 - core], g2p, 9).start()

    def project_back(i, carry):
        rows = chunk_rows(i)
        tmp[...] = (
            dot_nt(dt_s[rows, 0:C], wq[...])
            + dot_nt(dt_s[rows, 256:448], wk[...])
            + dot_nt(dt_s[rows, 512:704], wv[...])
        )
        for t in range(CHUNK // TILE):
            part = tile_rows(i, t)
            unit, inverse = statistics(x_w[part, :].astype(F32))
            back = norm_back(unit, inverse, tmp[t * TILE:(t + 1) * TILE, :] * attend_gain[...])
            gt_s[part, :] = (gm_s[part, :] + back).astype(BF16)
        return carry

    def backward_windows(b, carry):
        lax.fori_loop(2 * b, 2 * b + 2, windows_back, 0)

        @pl.when(b == 1)
        def _():
            second_gradients()

        project_back(b, carry)

        @pl.when(b == 1)
        def _():
            arrived(g2p, 9)
            add_pair(g2s, g2p, g2h)
            g2r[chip] = g2h[chip]
            chips_all(lambda o: to_chip(g2h.at[o], g2r.at[chip], 10, o).start())

        quads = dot_nn(from_window, gt_s[half_rows(b), :])
        gq[b] = quads
        pack(quads, b, (c10, c01, c11))
        for copy in rows_behind(b):
            copy.start()

        @pl.when(b == 0)
        def _():
            arrived(g1r.at[others], 6)
            g1l[d // 2] = sum_of(g1r, NCHIP, all_rows)
            for step in range(1, 4):
                to_band(g1l.at[d // 2], g1l.at[d // 2], 7, lax.rem(d + 2 * step, NLAT)).start()

        return carry

    lax.fori_loop(0, 2, backward_windows, 0)

    arrived(g1f.at[others], 8)
    to_core(g1f, g1o, 11).start()

    arrived(g2r.at[others], 10)
    g2l[d] = sum_of(g2r, NCHIP, slice(0, 64))
    lat_all(lambda o: to_band(g2l.at[d], g2l.at[d], 12, o).start())
    g2f[chip, 64:96] = sum_of(g2r, NCHIP, slice(64, 96))

    to_natural = one_hot(HALF, orders[1:2, 0:HALF])

    def unsort_sample(b, carry):
        for copy in rows_behind(b):
            copy.wait()
        unpack(gq, b, (d10, d01, d11))
        out_fields[half_rows(b), :] = dot_nn(to_natural, gq[b].astype(BF16)).astype(BF16)
        return carry

    lax.fori_loop(0, 1, unsort_sample, 0)
    arrived(g2l.at[others], 12)
    g2f[chip, 0:64] = sum_of(g2l, NLAT, slice(0, 64))
    chips_all(lambda o: to_chip(g2f.at[chip], g2f.at[chip], 13, o).start())


    lax.fori_loop(1, 2, unsort_sample, 0)
    arrived(g1o, 11)
    out_g1[core] = g1f[...]
    out_g1[1 - core] = g1o[...]
    arrived(g2f.at[others], 13)
    to_core(g2f, g2o, 14).start()
    out_g2[core] = g2f[...]
    arrived(g2o, 14)
    out_g2[1 - core] = g2o[...]

    left(cx, 0)
    left(cm.at[others], 1)
    left(w_part, 2)
    left(w_all.at[0, seven], 3)
    left(w_all.at[0], 16)
    left(ch, 4)
    left(g1p, 5)
    left(g1r.at[others], 6)
    left(g1l.at[pl.ds(0, 3)], 7)
    left(g1l.at[4], 15)
    left(g1f.at[others], 8)
    left(g2p, 9)
    left(g2r.at[others], 10)
    left(g1o, 11)
    left(g2l.at[others], 12)
    left(g2f.at[others], 13)
    left(g2o, 14)


def results_kernel(
    fields, g1, g2, attend_gain, triple_w, feed_gain, expand_w,
    out_fields, out_triple, out_output, out_expand, out_shrink, out_attend, out_feed, out_table,
):
    out_fields[...] = fields[...]
    for i in range(4):
        for j in range(2):
            rows, cols = slice(i * 48, (i + 1) * 48), slice(j * 384, (j + 1) * 384)
            out_expand[rows, cols] = g1[0, 2 * i + j, 0:48].astype(F32)
            out_shrink[rows, cols] = g1[1, 2 * i + j, 0:48].astype(F32)
    for i in range(6):
        wide = g1[i % 2, i // 2, 48:64].astype(F32)
        out_output[i * 16:(i + 1) * 16, :] = wide[:, 0:C]
        out_output[96 + i * 16:96 + (i + 1) * 16, :] = wide[:, C:2 * C]
    for i in range(3):
        for j in range(5):
            at, size = 5 * i + j, 128 if j < 4 else 64
            part = g2[at // 8, at % 8, 0:64].astype(F32)
            out_triple[i * 64:(i + 1) * 64, j * 128:j * 128 + size] = part[:, 0:size]
    table = jnp.concatenate(
        [g2[o // 16, (o // 2) % 8, 64 + 16 * (o % 2):80 + 16 * (o % 2)] for o in range(32)], axis=1
    ).astype(F32)
    for h in range(HEADS):
        out_table[h] = table[2 * h:2 * h + 2, 0:POS]

    def gain_gradient(grad, weight, gain):
        product = (grad[...] * weight[...].astype(F32)).astype(BF16)
        total = dot_nt(jnp.ones((16, product.shape[1]), BF16), product)
        return total[0:1] / gain[...]

    out_attend[...] = gain_gradient(out_triple, triple_w, attend_gain)
    out_feed[...] = gain_gradient(out_expand, expand_w, feed_gain)


def scratch():
    def vmem(*shape, kind=BF16):
        return pltpu.VMEM(shape, kind)

    token = vmem(TOK, C)
    token_f = vmem(TOK, C, kind=F32)
    weight = vmem(C, C)
    quad = vmem(2, HALF, C, kind=F32)
    halves = [vmem(2, 336, 128), vmem(2, 112, 128), vmem(2, 112, 128)]
    stat = vmem(WIN, 128, kind=F32)
    small = vmem(2, 24, 128, kind=F32)
    buffers = [
        quad, quad, *halves, *halves, *halves, *halves, token, token, token, token, token, weight, weight, weight,
        vmem(NWIN, WIN, WIDE), token, token_f, token, vmem(TOK, FF), vmem(TOK, FF, kind=F32), token,
        vmem(16, POS, kind=F32), vmem(384, 512), vmem(2, 2304, 128, kind=F32),
        vmem(2, WIN, WIDE, kind=F32), vmem(2, WIN, WIDE, kind=F32),
        vmem(12, 512, WIN), vmem(2, WIN, 384),
        vmem(576, 256, kind=F32), vmem(8, 2, 3, 32, 128), vmem(8, 3, 32, 128),
        vmem(8, 3, 48, 128), vmem(2, 384, 128), vmem(3, 384, 128),
        vmem(32, 768), vmem(32, 768), vmem(48, 384), vmem(2, 384, 384),
        vmem(12, 128, C), token, vmem(2, WIN, 128, kind=F32), stat, small, small, small, small, vmem(4, WIN, 128, kind=F32),
        token, vmem(TOK, FF), token_f, token, token, vmem(TOK, 768), token,
        vmem(4, WIN, WIDE, kind=F32), vmem(2, WIN, WIDE), vmem(2, WIDE, C), vmem(CHUNK, FF, kind=F32),
        vmem(CHUNK, C, kind=F32),
    ]
    for rows, cols in ((64, 384), (96, 128)):
        chunks = vmem(8, rows, cols)
        buffers += [vmem(2, 8, rows, cols), chunks, chunks, chunks, vmem(8, 64, cols), chunks, chunks]
    counts = [6, 6, 6, 6, 4, 4, 17, 17]
    return buffers + [pltpu.SemaphoreType.DMA((n,)) for n in counts]


def per_device(
    fields, merge_cotangent, attend_gain, triple_weight, bias_table, output_weight, feed_gain,
    expand_weight, shrink_weight, merge_gain, merge_weight,
):
    cot = jnp.transpose(merge_cotangent, (1, 2, 3, 4, 0)).reshape(576, 192)
    bias = jnp.transpose(bias_table[0], (1, 0, 2))
    def shaped(shapes):
        return [jax.ShapeDtypeStruct(shape, kind) for shape, kind in shapes]

    vmem_spec = pl.BlockSpec(memory_space=pltpu.VMEM)
    parts = pl.pallas_call(
        kernel,
        out_shape=shaped(
            [((TOK, C), BF16), ((2, 8, 64, 384), BF16), ((2, 8, 96, 128), BF16)]
        ),
        in_specs=[vmem_spec] * 12,
        out_specs=[vmem_spec] * 3,
        scratch_shapes=scratch(),
        compiler_params=pltpu.CompilerParams(
            collective_id=0, has_side_effects=True, vmem_limit_bytes=60 * 1024 * 1024
        ),
    )(
        fields.reshape(TOK, C), cot, attend_gain.reshape(1, C), triple_weight, bias, output_weight,
        feed_gain.reshape(1, C), expand_weight, shrink_weight.T, merge_gain,
        merge_weight.T, jnp.asarray(order_indices()),
    )
    g_fields, g_triple, g_output, g_expand, g_shrink, g_attend, g_feed, g_table = pl.pallas_call(
        results_kernel,
        out_shape=shaped(
            [
                ((TOK, C), BF16), ((C, 3 * C), F32), ((C, C), F32), ((C, FF), F32), ((C, FF), F32),
                ((1, C), F32), ((1, C), F32), ((HEADS, 2, POS), F32),
            ]
        ),
        in_specs=[vmem_spec] * 7,
        out_specs=[vmem_spec] * 8,
        compiler_params=pltpu.CompilerParams(vmem_limit_bytes=60 * 1024 * 1024),
    )(*parts, attend_gain.reshape(1, C), triple_weight, feed_gain.reshape(1, C), expand_weight)
    return (
        g_fields.reshape(fields.shape), g_triple, g_output, g_expand, g_shrink.T,
        g_attend.reshape(C), g_feed.reshape(C), jnp.transpose(g_table, (1, 0, 2))[None],
    )


def solution(mesh):
    placed = (
        P(None, None, "lat", "lon", None),
        P(None, None, None, "lat", "lon"),
        P(),
        P(),
        P("lat", None, None, None),
        P(),
        P(),
        P(),
        P(),
        P(),
        P(None, "lon"),
    )
    return jax.shard_map(
        per_device,
        mesh=mesh,
        in_specs=placed,
        out_specs=(
            P(None, None, "lat", "lon", None),
            P(),
            P(),
            P(),
            P(),
            P(),
            P(),
            P("lat", None, None, None),
        ),
        check_vma=False,
    )
```

```python
import functools
import math

import jax
import jax.numpy as jnp
import numpy as np
from jax import lax
from jax.experimental import pallas as pl
from jax.experimental.pallas import tpu as pltpu
from jax.sharding import PartitionSpec as P

F32 = jnp.float32
BF16 = jnp.bfloat16
I32 = jnp.int32
MESH = pl.DeviceIdType.MESH

EPS = 1e-05
MASKED = -1000000000.0
NLON = 16
NLAT = 8
NCHIP = 8
C = 192
HEADS = 6
FF = 768
WIN = 144
NWIN = 8
TOK = WIN * NWIN
HALF = TOK // 2
SIZES = ((216, 112), (72, 40), (72, 40))
POS = 3312
CHUNK = 576
NCHUNK = TOK // CHUNK
TILE = 48
WIDE = 896
FACTOR = 32 ** -0.5


def order_indices():
    natural_to_quad = np.full(640, -1, np.int32)
    quad_to_natural = np.full(640, -1, np.int32)
    quad_to_window = np.full(640, -1, np.int32)
    window_to_quad = np.full(640, -1, np.int32)
    for level in range(4):
        for row in range(6):
            for col in range(24):
                source = (level * 6 + row) * 24 + col
                if col >= 6:
                    place = (0 if row >= 3 else 216) + level * 54 + (row % 3) * 18 + col - 6
                else:
                    place = (432 if row >= 3 else 504) + level * 18 + (row % 3) * 6 + col
                natural_to_quad[source] = place
                quad_to_natural[place] = source
    index = 0
    for lev_win in range(2):
        for lon_win in range(2):
            for s in range(12):
                for p in range(2):
                    for r in range(6):
                        level = (lev_win * 2 + p + 1) % 4
                        col = lon_win * 12 + s
                        if col < 18:
                            place = (0 if r < 3 else 216) + level * 54 + (r % 3) * 18 + col
                        else:
                            place = (432 if r < 3 else 504) + level * 18 + (r % 3) * 6 + col - 18
                        window_to_quad[index] = place
                        quad_to_window[place] = index
                        index += 1
    cell_lane = np.full(640, -1, np.int32)
    bias_row = np.full(640, -1, np.int32)
    merged_token = np.full((2, 640), -1, np.int32)
    for lane in range(256):
        if lane % 16 < 12:
            cell_lane[lane] = (12 * (lane // 16) + 3 + lane % 16) % 192
    for k in range(WIN):
        s, p, r = k // 12, (k // 6) % 2, k % 6
        bias_row[k] = p * 256 + r * 23 + 11 - s
    for lon_win in range(2):
        for row in range(384):
            p, r, y, m = row // 192, (row // 32) % 6, (row // 16) % 2, row % 16
            if 0 <= m - lon_win * 6 < 6:
                merged_token[lon_win, row] = (2 * (m - lon_win * 6) + y) * 12 + p * 6 + r
    rows = [natural_to_quad, quad_to_natural, quad_to_window, window_to_quad]
    return np.stack(rows + [cell_lane, bias_row, merged_token[0], merged_token[1]])


def dot_nn(a, b):
    return lax.dot_general(a, b, (((1,), (0,)), ((), ())), preferred_element_type=F32)


def dot_nt(a, b):
    return lax.dot_general(a, b, (((1,), (1,)), ((), ())), preferred_element_type=F32)


def dot_tn(a, b):
    return lax.dot_general(a, b, (((0,), (0,)), ((), ())), preferred_element_type=F32)


def one_hot(rows, targets):
    ids = lax.broadcasted_iota(I32, (rows, targets.shape[1]), 0)
    return jnp.where(ids == targets, 1.0, 0.0).astype(BF16)


def statistics(values):
    centred = values - jnp.mean(values, axis=-1, keepdims=True)
    inverse = lax.rsqrt(jnp.mean(centred * centred, axis=-1, keepdims=True) + EPS)
    return centred * inverse, inverse


def norm_back(normed, inverse, scaled):
    centre = jnp.mean(scaled, axis=-1, keepdims=True)
    projected = jnp.mean(scaled * normed, axis=-1, keepdims=True)
    return inverse * (scaled - centre - normed * projected)


def gelu_parts(values):
    cumulative = 0.5 * (1.0 + lax.erf(values * (1.0 / math.sqrt(2.0))))
    density = jnp.exp(-0.5 * values * values) * (1.0 / math.sqrt(2.0 * math.pi))
    return values * cumulative, cumulative + values * density


def lanes(rows, cols):
    return lax.broadcasted_iota(I32, (rows, cols), 1)


def over_12(ids):
    return (ids * 5462) >> 16


def over_6(ids):
    return (ids * 10923) >> 16


def kernel(
    fields, cot, attend_gain, triple_w, bias, output_w, feed_gain, expand_w, shrink_t, merge_gain,
    merge_wt, orders,
    out_fields, out_g1, out_g2,
    sq, gq, a10, a01, a11, b10, b01, b11, c10, c01, c11, d10, d01, d11, x_w, ni_s, q_s, k_s, v_s, wq, wk, wv, p_s, att_s, mid_s, nm_s, act_s, slope_s, vo_s,
    b16, bl_s, bs_s, bx, ds_s, spread_s, pick_s,
    cells, cs, cx, cm, ch, planes, w_own, w_part, w_send, w_all, qry, qw, st, sx, sup, sdn, tup, tdn, cp_s, go_s, gh_s, gm_s, ga_s, gmh_s,
    dt_s, gt_s, raw, dsh, dam, hid, tmp, g1s, g1p, g1h, g1r, g1l, g1f, g1o, g2s, g2p, g2h, g2r, g2l, g2f, g2o,
    halo_ss, halo_rs, back_ss, back_rs, st_ss, st_rs, sends, recvs,
):
    e = lax.axis_index("lon")
    d = lax.axis_index("lat")
    e_up, e_dn = lax.rem(e + 1, NLON), lax.rem(e + NLON - 1, NLON)
    d_up, d_dn = lax.rem(d + 1, NLAT), lax.rem(d + NLAT - 1, NLAT)

    def remote(src, dst, ssem, rsem, device):
        return pltpu.make_async_remote_copy(
            src_ref=src, dst_ref=dst, send_sem=ssem, recv_sem=rsem, device_id=device,
            device_id_type=MESH,
        )

    core, chip = lax.rem(e, 2), e // 2
    partner = e + 1 - 2 * core
    d_pair = d + 1 - 2 * lax.rem(d, 2)

    def chips_all(action):
        def body(step, carry):
            action(lax.rem(chip + step, NCHIP))
            return carry

        lax.fori_loop(1, NCHIP, body, 0)

    def lat_all(action):
        def body(step, carry):
            action(lax.rem(d + step, NLAT))
            return carry

        lax.fori_loop(1, NLAT, body, 0)

    def to_chip(src, dst, phase, o):
        return remote(src, dst, sends.at[phase], recvs.at[phase], (2 * o + core, d))

    def to_band(src, dst, phase, o):
        return remote(src, dst, sends.at[phase], recvs.at[phase], (e, o))

    def to_core(src, dst, phase):
        return remote(src, dst, sends.at[phase], recvs.at[phase], (partner, d))

    def arrived(region, phase):
        remote(region, region, sends.at[phase], recvs.at[phase], (partner, d)).wait_recv()

    def left(region, phase):
        remote(region, region, sends.at[phase], recvs.at[phase], (partner, d)).wait_send()

    barrier = pltpu.get_barrier_semaphore()

    def greet(device):
        pl.semaphore_signal(barrier, inc=1, device_id=device, device_id_type=MESH)

    chips_all(lambda o: greet((2 * o + core, d)))
    lat_all(lambda o: greet((e, o)))
    for device in ((e_up, d), (e_dn, d), (e_up, d_up), (e_dn, d_dn)):
        greet(device)

    def half_rows(b):
        return pl.ds(pl.multiple_of(b * HALF, HALF), HALF)

    def pack(quads, b, out):
        at = 216
        for (size, cut), message in zip(SIZES, out):
            rows = quads[at:at + size]
            rest = jnp.concatenate([rows[cut:, 128:C], jnp.zeros((2 * cut - size, 64), F32)], axis=0)
            parts = [rows[:, 0:128], jnp.concatenate([rows[:cut, 128:C], rest], axis=1)]
            if (size + cut) % 16:
                parts.append(jnp.zeros((8, 128), F32))
            message[b] = jnp.concatenate(parts, axis=0).astype(BF16)
            at += size

    def unpack(quads, b, messages):
        at = 216
        for (size, cut), message in zip(SIZES, messages):
            rows = message[b].astype(F32)
            tails = rows[size:size + cut]
            tail = jnp.concatenate([tails[:, 0:64], tails[0:size - cut, 64:128]], axis=0)
            quads[b, at:at + size, :] = jnp.concatenate([rows[0:size], tail], axis=1)
            at += size

    def halo(sources, targets, ssem, rsem, step, b):
        devices = ((e, step[1]), (step[0], d), (step[0], step[1]))
        return [
            remote(src.at[b], dst.at[b], ssem.at[3 * b + i], rsem.at[3 * b + i], dev)
            for i, (src, dst, dev) in enumerate(zip(sources, targets, devices))
        ]

    def rows_ahead(b):
        return halo((a10, a01, a11), (b10, b01, b11), halo_ss, halo_rs, (e_dn, d_dn), b)

    def rows_behind(b):
        return halo((c10, c01, c11), (d10, d01, d11), back_ss, back_rs, (e_up, d_up), b)

    to_quad = one_hot(HALF, orders[0:1, 0:HALF])

    for b in range(2):
        quads = dot_nn(to_quad, fields[b * HALF:(b + 1) * HALF, :])
        sq[b] = quads
        pack(quads, b, (a10, a01, a11))
    pl.semaphore_wait(barrier, NCHIP - 1 + NLAT - 1 + 4)
    for b in range(2):
        for copy in rows_ahead(b):
            copy.start()

    cells[...] = dot_nn(cot[...], one_hot(192, orders[4:5, 0:256]))
    block_of = lanes(72, 128) >> 4

    def gather_cells(inner, carry):
        for tile in range(2):
            piece = jnp.zeros((72, 128), F32)
            for bl in range(8):
                part = cells[bl * 72:(bl + 1) * 72, tile * 128:(tile + 1) * 128]
                part = pltpu.roll(part, lax.rem(16 * (bl - inner) + 128, 128), 1)
                piece = jnp.where(block_of == bl, part, piece)
            for a in range(3):
                padded = jnp.concatenate([piece[a * 24:(a + 1) * 24], jnp.zeros((8, 128), F32)], axis=0)
                cs[4 * tile + inner // 2, lax.rem(inner, 2), a] = padded.astype(BF16)
        return carry

    lax.fori_loop(0, 8, gather_cells, 0)
    w_own[...] = jnp.concatenate(
        [merge_wt[...].astype(F32), jnp.zeros((8, 768), F32)], axis=0
    ).astype(BF16)
    to_core(cs.at[:, 1 - core], cx, 0).start()
    to_core(w_own, w_part, 2).start()

    for h in range(HEADS):
        b16[2 * h:2 * h + 2, :] = bias[h]
    b16[12:16, :] = jnp.zeros((4, POS), F32)
    zero_tail = jnp.zeros((16, 256 - 138), F32)
    for p in range(2):
        for r in range(6):
            parts = []
            for pk in range(2):
                at = (p * 2 + pk) * 828 + r * 138
                parts += [b16[:, at:at + 138], zero_tail]
            row = jnp.concatenate(parts, axis=1)
            high = row.astype(BF16)
            low = (row - high.astype(F32)).astype(BF16)
            at = (p * 6 + r) * 16
            bl_s[at:at + 16, :] = high
            bl_s[192 + at:192 + at + 16, :] = low

    bias_row = orders[5:6, 0:WIN]

    def spread(pair, carry):
        for i in range(2):
            s_i = 2 * pair + i
            matrix = one_hot(512, bias_row + s_i)
            spread_s[s_i] = matrix
            split = dot_nn(bl_s[...], matrix)
            rows = split[0:192] + split[192:384]
            at = pl.ds(pl.multiple_of(s_i * 192, 192), 192)
            bs_s[0, at, :] = rows[:, 0:128]
            bs_s[1, at, :] = jnp.concatenate([rows[:, 128:144], jnp.zeros((192, 112), F32)], axis=1)
        return carry

    lax.fori_loop(0, 6, spread, 0)

    def dense(mine, other):
        mine, other = mine.astype(F32)[0:24], other.astype(F32)[0:24]
        swapped = core == 1
        parts = [jnp.where(swapped, other, mine), jnp.where(swapped, mine, other)]
        return jnp.concatenate(parts, axis=0)

    def chip_rows(o):
        return pl.ds(pl.multiple_of(o * 48, 48), 48)

    def merge_pieces(o, carry):
        for a in range(3):
            cm[o, a] = dense(cs[o, core, a], cx[o, a]).astype(BF16)
        return carry

    arrived(cx, 0)
    lax.fori_loop(0, NCHIP, merge_pieces, 0)
    planes[:, chip_rows(chip)] = cm[chip]
    chips_all(lambda o: to_chip(cm.at[o], planes.at[:, chip_rows(chip)], 1, o).start())
    arrived(w_part, 2)
    both = dense(w_own[...], w_part[...])
    w_send[...] = jnp.where(core == 1, both[:, 384:768], both[:, 0:384]).astype(BF16)
    w_all[core, chip_rows(chip)] = w_send[...]
    chips_all(lambda o: to_chip(w_send, w_all.at[core, chip_rows(chip)], 3, o).start())
    seven = pl.ds(0, 48 * (NCHIP - 1))

    tok_i = lax.broadcasted_iota(I32, (WIN, WIN), 0)
    tok_k = lax.broadcasted_iota(I32, (WIN, WIN), 1)
    half_i, half_k = over_6(tok_i), over_6(tok_k)
    last_band = d == NLAT - 1
    lat_differs = ((tok_i - half_i * 6 >= 3) != (tok_k - half_k * 6 >= 3)) & last_band
    lev_differs = (half_i & 1) != (half_k & 1)
    bx[:, :, HEADS * WIN:WIDE] = jnp.zeros((2, WIN, WIDE - HEADS * WIN), F32)
    for lw in range(2):
        differs = (lat_differs | lev_differs) if lw else lat_differs
        for h in range(HEADS):
            at = pl.ds(h * 2 + lw, WIN, stride=16)
            full = jnp.concatenate([bs_s.at[0][at, :], bs_s.at[1][at, :]], axis=1)[:, 0:WIN]
            spread_bias = jnp.where(differs, MASKED, full).T
            bx[lw, :, h * 128:(h + 1) * 128] = spread_bias[:, 0:128]
            bx[lw, :, 768 + h * 16:784 + h * 16] = spread_bias[:, 128:WIN]

    wq[...] = triple_w[:, 0:192]
    wk[...] = triple_w[:, 192:384]
    wv[...] = triple_w[:, 384:576]

    head_of = lanes(1, C) >> 5
    head_f = [jnp.where(head_of == h, 1.0, 0.0) for h in range(HEADS)]
    head_b = [mask.astype(BF16) for mask in head_f]

    blank = jnp.zeros((WIDE - HEADS * WIN, C), BF16)

    def stacked(values):
        first, rest = values[0:128], values[128:WIN]
        parts = [first * mask for mask in head_b] + [rest * mask for mask in head_b]
        return jnp.concatenate(parts + [blank], axis=0)

    def per_head(left, right):
        turned = left.T
        wide = [dot_nn(turned[64 * i:64 * i + 64], right[:, 256 * i:256 * i + 256]) for i in range(3)]
        tail = dot_nn(turned, right[:, 768:WIDE])
        blocks = []
        for h in range(HEADS):
            at, row = 128 * (h % 2), 32 * (h % 2)
            blocks.append(
                jnp.concatenate(
                    [wide[h // 2][row:row + 32, at:at + 128], tail[32 * h:32 * h + 32, 16 * h:16 * h + 16]], axis=1
                )
            )
        return jnp.concatenate(blocks, axis=0).T

    to_window = one_hot(HALF, orders[2:3, 0:HALF])

    def window_rows(w):
        return pl.ds(pl.multiple_of(w * WIN, WIN), WIN)

    def chunk_rows(i):
        return pl.ds(pl.multiple_of(i * CHUNK, CHUNK), CHUNK)

    def tile_rows(i, t):
        return pl.ds(pl.multiple_of(i * CHUNK + t * TILE, 16), TILE)

    def project(i, carry):
        rows = chunk_rows(i)
        for t in range(CHUNK // TILE):
            part = tile_rows(i, t)
            normed = statistics(x_w[part, :].astype(F32))[0]
            ni_s[part, :] = (normed * attend_gain[...]).astype(BF16)
        normed_in = ni_s[rows, :]
        q_s[rows, :] = dot_nn(normed_in, wq[...]).astype(BF16)
        k_s[rows, :] = dot_nn(normed_in, wk[...]).astype(BF16)
        v_s[rows, :] = dot_nn(normed_in, wv[...]).astype(BF16)
        return carry


    def attend(b):
        for i in range(4):
            rows = window_rows(4 * b + i)
            raw[i] = dot_nt(k_s[rows, :], stacked(q_s[rows, :]))
        for i in range(4):
            for t in range(WIDE // 128):
                cols = slice(t * 128, (t + 1) * 128)
                scores = raw[i, :, cols] * FACTOR + bx[i // 2, :, cols]
                exponent = jnp.exp(scores - jnp.max(scores, axis=0, keepdims=True))
                chances = exponent * (1.0 / jnp.sum(exponent, axis=0, keepdims=True))
                p_s[4 * b + i, :, cols] = chances.astype(BF16)
        for i in range(4):
            rows = window_rows(4 * b + i)
            att_s[rows, :] = per_head(v_s[rows, :], p_s[4 * b + i]).astype(BF16)

    def forward_windows(b, carry):
        for copy in rows_ahead(b):
            copy.wait()

        unpack(sq, b, (b10, b01, b11))
        x_w[half_rows(b), :] = dot_nn(to_window, sq[b].astype(BF16)).astype(BF16)
        project(b, carry)

        @pl.when(b == 0)
        def _():
            arrived(planes.at[:, seven], 1)
            to_band(planes.at[pl.ds(0, 2)], ch, 4, d_dn).start()

        @pl.when(b == 1)
        def _():
            arrived(w_all.at[0, seven], 3)
            to_core(w_all.at[core], w_all.at[core], 16).start()

        attend(b)
        return carry

    lax.fori_loop(0, 2, forward_windows, 0)

    def feed(i, carry):
        rows = chunk_rows(i)
        tmp[...] = x_w[rows, :].astype(F32) + dot_nn(att_s[rows, :], output_w[...])
        for t in range(CHUNK // TILE):
            part = tile_rows(i, t)
            middle = tmp[t * TILE:(t + 1) * TILE, :]
            mid_s[part, :] = middle
            nm_s[part, :] = (statistics(middle)[0] * feed_gain[...]).astype(BF16)
        hid[...] = dot_nn(nm_s[rows, :], expand_w[...])
        for t in range(CHUNK // 16):
            part = pl.ds(pl.multiple_of(i * CHUNK + t * 16, 16), 16)
            for j in range(FF // 256):
                cols = slice(j * 256, (j + 1) * 256)
                act, slope = gelu_parts(hid[t * 16:(t + 1) * 16, cols])
                act_s[part, cols] = act.astype(BF16)
                slope_s[part, cols] = slope
        vo_s[rows, :] = (tmp[...] + dot_nt(act_s[rows, :], shrink_t[...])).astype(BF16)
        return carry

    lax.fori_loop(0, NCHUNK, feed, 0)

    arrived(w_all.at[0], 16)
    gain_row = merge_gain[...].reshape(1, 4 * C)
    for r in range(6):
        x = (r + 1) % 2
        cell = (0, 1, 1, 2, 2, 3)[r]
        cols = slice(x * 384, (x + 1) * 384)
        if r == 3:
            arrived(ch, 4)
        plane = planes[cell + 1] if cell < 2 else ch[cell - 2]
        summed = dot_tn(plane, w_all[x])
        scaled = summed * gain_row[:, x * 384:(x + 1) * 384]
        qry[2 * r] = scaled[:, 0:192].astype(BF16)
        qry[2 * r + 1] = scaled[:, 192:384].astype(BF16)

    st[...] = jnp.zeros_like(st)
    for i in range(2):
        pick_s[i] = one_hot(WIN, orders[6 + i:7 + i, 0:384])
    stat_lane = lanes(WIN, 128)
    tile_lane = lanes(TILE, 128)

    def merge_sums(pair, carry):
        b, lw = pair // 2, lax.rem(pair, 2)
        parts = []
        for p in range(2):
            level = lax.rem(lw * 2 + p + 1, 4)
            at = pl.ds(pl.multiple_of((b * 4 + level) * 16, 16), 16)
            parts.append(qry[:, at, :].reshape(192, C))
        cells_q = jnp.concatenate(parts, axis=0)
        for i in range(2):
            qw[window_rows(2 * pair + i), :] = dot_nn(pick_s[i], cells_q).astype(BF16)
        for t in range(WIN // TILE):
            at = slice(t * TILE, (t + 1) * TILE)
            total = st[b, at, :]
            for i in range(2):
                w = 2 * pair + i
                part = pl.ds(pl.multiple_of(w * WIN + t * TILE, 16), TILE)
                q = qw[part, :].astype(F32)
                v = vo_s[part, :].astype(F32)
                mean = jnp.mean(v, axis=-1, keepdims=True)
                centred = v - mean
                squares = jnp.sum(centred * centred, axis=-1, keepdims=True)
                q_sum = jnp.sum(q, axis=-1, keepdims=True)
                qv_sum = jnp.sum(q * centred, axis=-1, keepdims=True)
                for j, value in enumerate((mean, squares, q_sum, qv_sum)):
                    total = jnp.where(tile_lane == 32 * j + w, value, total)
            st[b, at, :] = total
        return carry

    def sums_copies(b):
        return (
            remote(tup.at[b], sup.at[b], st_ss.at[2 * b], st_rs.at[2 * b], (e, d_up)),
            remote(tdn.at[b], sdn.at[b], st_ss.at[2 * b + 1], st_rs.at[2 * b + 1], (e, d_dn)),
        )

    def exchange(b):
        tup[b] = st.at[b][pl.ds(5, 24, stride=6), :]
        tdn[b] = st.at[b][pl.ds(0, 24, stride=6), :]
        for copy in sums_copies(b):
            copy.start()

    even = (over_12(lax.broadcasted_iota(I32, (WIN, 128), 0)) & 1) == 0

    def pair_of(values):
        return jnp.where(even, pltpu.roll(values, WIN - 12, 0), pltpu.roll(values, 12, 0))

    def cell_norm(b):
        for r, other in ((1, 2), (2, 1), (3, 4), (4, 3)):
            sx[pl.ds(r, 24, stride=6), :] = st.at[b][pl.ds(other, 24, stride=6), :]
        for copy in sums_copies(b):
            copy.wait()
        sx[pl.ds(0, 24, stride=6), :] = sup[b]
        sx[pl.ds(5, 24, stride=6), :] = sdn[b]
        own, cross = st[b], sx[...]
        group = [own, cross, pair_of(own), pair_of(cross)]
        cell_mean = (group[0] + group[1] + group[2] + group[3]) * 0.25
        variance = jnp.zeros((WIN, 128), F32)
        q_total = jnp.zeros((WIN, 128), F32)
        qv_total = jnp.zeros((WIN, 128), F32)
        for values in group:
            offset = values - cell_mean
            q_sum = pltpu.roll(values, 64, 1)
            variance = variance + pltpu.roll(values, 96, 1) + 192.0 * offset * offset
            q_total = q_total + q_sum
            qv_total = qv_total + pltpu.roll(values, 32, 1) + offset * q_sum
        cell_inverse = lax.rsqrt(jnp.where(stat_lane < 8, variance, 0.0) * (1.0 / 768.0) + EPS)
        cp_s[0] = cell_mean
        cp_s[1] = cell_inverse
        cp_s[2] = q_total * (1.0 / 768.0)
        cp_s[3] = cell_inverse * cell_inverse * qv_total * (1.0 / 768.0)

    def merge_back(pair, carry):
        for i in range(2):
            w = 2 * pair + i
            for t in range(WIN // TILE):
                part = pl.ds(pl.multiple_of(w * WIN + t * TILE, 16), TILE)
                at = slice(t * TILE, (t + 1) * TILE)
                mean, inverse, q_mean, projected = [
                    jnp.sum(jnp.where(tile_lane == w, cp_s[j, at, :], 0.0), axis=-1, keepdims=True) for j in range(4)
                ]
                v = vo_s[part, :].astype(F32) - mean
                go_s[part, :] = (inverse * (qw[part, :].astype(F32) - q_mean - v * projected)).astype(BF16)
        return carry

    def feed_back(i, carry):
        rows = chunk_rows(i)
        go = go_s[rows, :]
        gh = (dot_nn(go, shrink_t[...]) * slope_s[rows, :]).astype(BF16)
        gh_s[rows, :] = gh
        tmp[...] = dot_nt(gh, expand_w[...])
        for t in range(CHUNK // TILE):
            part = tile_rows(i, t)
            gnm = tmp[t * TILE:(t + 1) * TILE, :]
            unit, inverse = statistics(mid_s[part, :])
            gm = go_s[part, :].astype(F32) + norm_back(unit, inverse, gnm * feed_gain[...])
            gm_s[part, :] = gm
            gmh_s[part, :] = gm.astype(BF16)
        ga_s[rows, :] = dot_nt(gmh_s[rows, :], output_w[...]).astype(BF16)
        return carry

    def forward_sample(b, carry):
        lax.fori_loop(2 * b, 2 * b + 2, merge_sums, 0)
        exchange(b)
        return carry

    def backward_sample(b, carry):
        cell_norm(b)
        lax.fori_loop(2 * b, 2 * b + 2, merge_back, 0)
        feed_back(b, carry)
        return carry

    lax.fori_loop(0, 2, forward_sample, 0)
    ds_s[...] = jnp.zeros_like(ds_s)
    dt_s[...] = jnp.zeros_like(dt_s)
    from_window = one_hot(HALF, orders[3:4, 0:HALF])
    lax.fori_loop(0, 2, backward_sample, 0)

    g_expand = dot_tn(nm_s[...], gh_s[...]).astype(BF16)
    g_shrink = dot_tn(go_s[...], act_s[...]).astype(BF16)
    g_output = dot_tn(att_s[...], gmh_s[...]).astype(BF16)
    for i in range(4):
        for j in range(2):
            g1s[0, 2 * i + j, 0:48] = g_expand[i * 48:(i + 1) * 48, j * 384:(j + 1) * 384]
            g1s[1, 2 * i + j, 0:48] = g_shrink[i * 48:(i + 1) * 48, j * 384:(j + 1) * 384]
    wide = jnp.concatenate([g_output[0:96], g_output[96:192]], axis=1)
    for i in range(NCHIP):
        for j in range(2):
            at = (i * 2 + j) * 16
            g1s[j, i, 48:64] = wide[at:at + 16] if at < 96 else jnp.zeros((16, 384), BF16)

    def sum_of(ref, count, rows):
        total = ref[0, rows].astype(F32)
        for o in range(1, count):
            total = total + ref[o, rows].astype(F32)
        return total.astype(BF16)

    def add_pair(mine, other, out):
        def body(o, carry):
            out[o] = (mine[core, o].astype(F32) + other[o].astype(F32)).astype(BF16)
            return carry

        lax.fori_loop(0, NCHIP, body, 0)

    others = pl.ds(0, NCHIP - 1)
    to_core(g1s.at[1 - core], g1p, 5).start()


    def attend_back(pair, carry):
        lw = lax.rem(pair, 2)
        for i in range(2):
            rows = window_rows(2 * pair + i)
            dam[i] = stacked(ga_s[rows, :])
            raw[i] = dot_nt(v_s[rows, :], dam[i])
        for i in range(2):
            for t in range(WIDE // 128):
                cols = slice(t * 128, (t + 1) * 128)
                chances = p_s[2 * pair + i, :, cols].astype(F32)
                weighted = raw[i, :, cols]
                centre = jnp.sum(chances * weighted, axis=0, keepdims=True)
                dsh[i, :, cols] = (chances * (weighted - centre)).astype(BF16)
        for i in range(2):
            rows = window_rows(2 * pair + i)
            dt_s[rows, 512:704] = dot_nn(p_s[2 * pair + i], dam[i]).astype(BF16)
            dt_s[rows, 0:C] = (per_head(k_s[rows, :], dsh[i]) * FACTOR).astype(BF16)
            dt_s[rows, 256:448] = (dot_nn(dsh[i], stacked(q_s[rows, :])) * FACTOR).astype(BF16)
        ds_s[lw] = ds_s[lw] + (dsh[0].astype(F32) + dsh[1].astype(F32))
        return carry

    all_rows = slice(0, 64)
    def windows_back(pair, carry):
        attend_back(pair, carry)

        @pl.when(pair == 0)
        def _():
            arrived(g1p, 5)
            add_pair(g1s, g1p, g1h)
            g1r[chip] = g1h[chip]
            chips_all(lambda o: to_chip(g1h.at[o], g1r.at[chip], 6, o).start())

        @pl.when(pair == 2)
        def _():
            arrived(g1l.at[pl.ds(0, 3)], 7)
            g1l[4] = sum_of(g1l, 4, all_rows)
            to_band(g1l.at[4], g1l.at[5], 15, d_pair).start()

        return carry

    def second_gradients():
        summed = dot_tn(ni_s[...], dt_s[...])
        sections = [summed[:, 0:C], summed[:, 256:448], summed[:, 512:704], jnp.zeros((C, 64), F32)]
        g_triple = jnp.concatenate(sections, axis=1).astype(BF16)
        for i in range(3):
            for j in range(5):
                at = 5 * i + j
                g2s[at // 8, at % 8, 0:64] = g_triple[i * 64:(i + 1) * 64, j * 128:(j + 1) * 128]
        g2s[1, 7, 0:64] = jnp.zeros((64, 128), BF16)
        arrived(g1l.at[5], 15)
        g1f[chip] = (g1l[4].astype(F32) + g1l[5].astype(F32)).astype(BF16)
        chips_all(lambda o: to_chip(g1f.at[chip], g1f.at[chip], 8, o).start())
        for lw in range(2):
            for h in range(HEADS):
                at = pl.ds(h * 2 + lw, WIN, stride=16)
                part = jnp.concatenate(
                [ds_s[lw, :, h * 128:(h + 1) * 128], ds_s[lw, :, 768 + h * 16:784 + h * 16]], axis=1
            ).T
                bs_s.at[0][at, :] = part[:, 0:128]
                bs_s.at[1][at, :] = jnp.concatenate([part[:, 128:144], jnp.zeros((WIN, 112), F32)], axis=1)

        def fold(s_i):
            at = slice(s_i * 192, (s_i + 1) * 192)
            rows = jnp.concatenate([bs_s[0, at, :], bs_s[1, at, :]], axis=1)[:, 0:WIN].astype(BF16)
            return dot_nt(rows, spread_s[s_i])

        folded = fold(0)
        for s_i in range(1, 12):
            folded = folded + fold(s_i)
        pieces_t = []
        for p in range(2):
            for pk in range(2):
                for r in range(6):
                    at = (p * 6 + r) * 16
                    pieces_t.append(folded[at:at + 16, pk * 256:pk * 256 + 138])
        table = jnp.concatenate(pieces_t + [jnp.zeros((16, 4096 - POS), F32)], axis=1).astype(BF16)
        for o in range(32):
            g2s[o // 16, (o // 2) % 8, 64 + 16 * (o % 2):80 + 16 * (o % 2)] = table[:, o * 128:(o + 1) * 128]
        to_core(g2s.at[1 - core], g2p, 9).start()

    def project_back(i, carry):
        rows = chunk_rows(i)
        tmp[...] = (
            dot_nt(dt_s[rows, 0:C], wq[...])
            + dot_nt(dt_s[rows, 256:448], wk[...])
            + dot_nt(dt_s[rows, 512:704], wv[...])
        )
        for t in range(CHUNK // TILE):
            part = tile_rows(i, t)
            unit, inverse = statistics(x_w[part, :].astype(F32))
            back = norm_back(unit, inverse, tmp[t * TILE:(t + 1) * TILE, :] * attend_gain[...])
            gt_s[part, :] = (gm_s[part, :] + back).astype(BF16)
        return carry

    def backward_windows(b, carry):
        lax.fori_loop(2 * b, 2 * b + 2, windows_back, 0)

        @pl.when(b == 1)
        def _():
            second_gradients()

        project_back(b, carry)

        @pl.when(b == 1)
        def _():
            arrived(g2p, 9)
            add_pair(g2s, g2p, g2h)
            g2r[chip] = g2h[chip]
            chips_all(lambda o: to_chip(g2h.at[o], g2r.at[chip], 10, o).start())

        quads = dot_nn(from_window, gt_s[half_rows(b), :])
        gq[b] = quads
        pack(quads, b, (c10, c01, c11))
        for copy in rows_behind(b):
            copy.start()

        @pl.when(b == 0)
        def _():
            arrived(g1r.at[others], 6)
            g1l[d // 2] = sum_of(g1r, NCHIP, all_rows)
            for step in range(1, 4):
                to_band(g1l.at[d // 2], g1l.at[d // 2], 7, lax.rem(d + 2 * step, NLAT)).start()

        return carry

    lax.fori_loop(0, 2, backward_windows, 0)

    arrived(g1f.at[others], 8)
    to_core(g1f, g1o, 11).start()

    arrived(g2r.at[others], 10)
    g2l[d] = sum_of(g2r, NCHIP, slice(0, 64))
    lat_all(lambda o: to_band(g2l.at[d], g2l.at[d], 12, o).start())
    g2f[chip, 64:96] = sum_of(g2r, NCHIP, slice(64, 96))

    to_natural = one_hot(HALF, orders[1:2, 0:HALF])

    def unsort_sample(b, carry):
        for copy in rows_behind(b):
            copy.wait()
        unpack(gq, b, (d10, d01, d11))
        out_fields[half_rows(b), :] = dot_nn(to_natural, gq[b].astype(BF16)).astype(BF16)
        return carry

    lax.fori_loop(0, 1, unsort_sample, 0)
    arrived(g2l.at[others], 12)
    g2f[chip, 0:64] = sum_of(g2l, NLAT, slice(0, 64))
    chips_all(lambda o: to_chip(g2f.at[chip], g2f.at[chip], 13, o).start())


    lax.fori_loop(1, 2, unsort_sample, 0)
    arrived(g1o, 11)
    out_g1[core] = g1f[...]
    out_g1[1 - core] = g1o[...]
    arrived(g2f.at[others], 13)
    to_core(g2f, g2o, 14).start()
    out_g2[core] = g2f[...]
    arrived(g2o, 14)
    out_g2[1 - core] = g2o[...]

    left(cx, 0)
    left(cm.at[others], 1)
    left(w_part, 2)
    left(w_all.at[0, seven], 3)
    left(w_all.at[0], 16)
    left(ch, 4)
    left(g1p, 5)
    left(g1r.at[others], 6)
    left(g1l.at[pl.ds(0, 3)], 7)
    left(g1l.at[4], 15)
    left(g1f.at[others], 8)
    left(g2p, 9)
    left(g2r.at[others], 10)
    left(g1o, 11)
    left(g2l.at[others], 12)
    left(g2f.at[others], 13)
    left(g2o, 14)


def results_kernel(
    fields, g1, g2, attend_gain, triple_w, feed_gain, expand_w,
    out_fields, out_triple, out_output, out_expand, out_shrink, out_attend, out_feed, out_table,
):
    out_fields[...] = fields[...]
    for i in range(4):
        for j in range(2):
            rows, cols = slice(i * 48, (i + 1) * 48), slice(j * 384, (j + 1) * 384)
            out_expand[rows, cols] = g1[0, 2 * i + j, 0:48].astype(F32)
            out_shrink[rows, cols] = g1[1, 2 * i + j, 0:48].astype(F32)
    for i in range(6):
        wide = g1[i % 2, i // 2, 48:64].astype(F32)
        out_output[i * 16:(i + 1) * 16, :] = wide[:, 0:C]
        out_output[96 + i * 16:96 + (i + 1) * 16, :] = wide[:, C:2 * C]
    for i in range(3):
        for j in range(5):
            at, size = 5 * i + j, 128 if j < 4 else 64
            part = g2[at // 8, at % 8, 0:64].astype(F32)
            out_triple[i * 64:(i + 1) * 64, j * 128:j * 128 + size] = part[:, 0:size]
    table = jnp.concatenate(
        [g2[o // 16, (o // 2) % 8, 64 + 16 * (o % 2):80 + 16 * (o % 2)] for o in range(32)], axis=1
    ).astype(F32)
    for h in range(HEADS):
        out_table[h] = table[2 * h:2 * h + 2, 0:POS]

    def gain_gradient(grad, weight, gain):
        product = (grad[...] * weight[...].astype(F32)).astype(BF16)
        total = dot_nt(jnp.ones((16, product.shape[1]), BF16), product)
        return total[0:1] / gain[...]

    out_attend[...] = gain_gradient(out_triple, triple_w, attend_gain)
    out_feed[...] = gain_gradient(out_expand, expand_w, feed_gain)


def scratch():
    def vmem(*shape, kind=BF16):
        return pltpu.VMEM(shape, kind)

    token = vmem(TOK, C)
    token_f = vmem(TOK, C, kind=F32)
    weight = vmem(C, C)
    quad = vmem(2, HALF, C, kind=F32)
    halves = [vmem(2, 336, 128), vmem(2, 112, 128), vmem(2, 112, 128)]
    stat = vmem(WIN, 128, kind=F32)
    small = vmem(2, 24, 128, kind=F32)
    buffers = [
        quad, quad, *halves, *halves, *halves, *halves, token, token, token, token, token, weight, weight, weight,
        vmem(NWIN, WIN, WIDE), token, token_f, token, vmem(TOK, FF), vmem(TOK, FF, kind=F32), token,
        vmem(16, POS, kind=F32), vmem(384, 512), vmem(2, 2304, 128, kind=F32),
        vmem(2, WIN, WIDE, kind=F32), vmem(2, WIN, WIDE, kind=F32),
        vmem(12, 512, WIN), vmem(2, WIN, 384),
        vmem(576, 256, kind=F32), vmem(8, 2, 3, 32, 128), vmem(8, 3, 32, 128),
        vmem(8, 3, 48, 128), vmem(2, 384, 128), vmem(3, 384, 128),
        vmem(32, 768), vmem(32, 768), vmem(48, 384), vmem(2, 384, 384),
        vmem(12, 128, C), token, vmem(2, WIN, 128, kind=F32), stat, small, small, small, small, vmem(4, WIN, 128, kind=F32),
        token, vmem(TOK, FF), token_f, token, token, vmem(TOK, 768), token,
        vmem(4, WIN, WIDE, kind=F32), vmem(2, WIN, WIDE), vmem(2, WIDE, C), vmem(CHUNK, FF, kind=F32),
        vmem(CHUNK, C, kind=F32),
    ]
    for rows, cols in ((64, 384), (96, 128)):
        chunks = vmem(8, rows, cols)
        buffers += [vmem(2, 8, rows, cols), chunks, chunks, chunks, vmem(8, 64, cols), chunks, chunks]
    counts = [6, 6, 6, 6, 4, 4, 17, 17]
    return buffers + [pltpu.SemaphoreType.DMA((n,)) for n in counts]


def per_device(
    fields, merge_cotangent, attend_gain, triple_weight, bias_table, output_weight, feed_gain,
    expand_weight, shrink_weight, merge_gain, merge_weight,
):
    cot = jnp.transpose(merge_cotangent, (1, 2, 3, 4, 0)).reshape(576, 192)
    bias = jnp.transpose(bias_table[0], (1, 0, 2))
    def shaped(shapes):
        return [jax.ShapeDtypeStruct(shape, kind) for shape, kind in shapes]

    vmem_spec = pl.BlockSpec(memory_space=pltpu.VMEM)
    parts = pl.pallas_call(
        kernel,
        out_shape=shaped(
            [((TOK, C), BF16), ((2, 8, 64, 384), BF16), ((2, 8, 96, 128), BF16)]
        ),
        in_specs=[vmem_spec] * 12,
        out_specs=[vmem_spec] * 3,
        scratch_shapes=scratch(),
        compiler_params=pltpu.CompilerParams(
            collective_id=0, has_side_effects=True, vmem_limit_bytes=60 * 1024 * 1024
        ),
    )(
        fields.reshape(TOK, C), cot, attend_gain.reshape(1, C), triple_weight, bias, output_weight,
        feed_gain.reshape(1, C), expand_weight, shrink_weight.T, merge_gain,
        merge_weight.T, jnp.asarray(order_indices()),
    )
    g_fields, g_triple, g_output, g_expand, g_shrink, g_attend, g_feed, g_table = pl.pallas_call(
        results_kernel,
        out_shape=shaped(
            [
                ((TOK, C), BF16), ((C, 3 * C), F32), ((C, C), F32), ((C, FF), F32), ((C, FF), F32),
                ((1, C), F32), ((1, C), F32), ((HEADS, 2, POS), F32),
            ]
        ),
        in_specs=[vmem_spec] * 7,
        out_specs=[vmem_spec] * 8,
        compiler_params=pltpu.CompilerParams(vmem_limit_bytes=60 * 1024 * 1024),
    )(*parts, attend_gain.reshape(1, C), triple_weight, feed_gain.reshape(1, C), expand_weight)
    return (
        g_fields.reshape(fields.shape), g_triple, g_output, g_expand, g_shrink.T,
        g_attend.reshape(C), g_feed.reshape(C), jnp.transpose(g_table, (1, 0, 2))[None],
    )


def solution(mesh):
    placed = (
        P(None, None, "lat", "lon", None),
        P(None, None, None, "lat", "lon"),
        P(),
        P(),
        P("lat", None, None, None),
        P(),
        P(),
        P(),
        P(),
        P(),
        P(None, "lon"),
    )
    return jax.shard_map(
        per_device,
        mesh=mesh,
        in_specs=placed,
        out_specs=(
            P(None, None, "lat", "lon", None),
            P(),
            P(),
            P(),
            P(),
            P(),
            P(),
            P("lat", None, None, None),
        ),
        check_vma=False,
    )
```
